128 devices in a mesh: dp: 8 (over x, core), expert: 16 (over z, y).
Axes of the slice: x: 4, y: 4, z: 4, core: 2. Of those that a mesh axis runs over, the one named last changes fastest.
Arguments:
- tokens: bfloat16 [16, 2048, 1024], P('expert', 'dp'), may hold values from -6 to 6
- cotangent: bfloat16 [16, 2048, 1024], P('expert', 'dp'), may hold values from -6 to 6
- lengths: int32 [16], P('expert'), may hold values from 1793 to 2048, as said below
- routes: int32 [16, 2048, 8], P('expert', 'dp'), may hold values from 0 to 31, all different within a row; in each aligned block of 256 rows (0 to 255, 256 to 511, ..., all dimensions but the last counted through in order) at most 80 rows name the same one
- attn_gain: bfloat16 [1024], replicated, may hold values from 0.099609375 to 1.8984375
- w_query: bfloat16 [1024, 1024], replicated, may hold values from -0.1875 to 0.1875
- w_key: bfloat16 [1024, 512], replicated, may hold values from -0.1875 to 0.1875
- w_value: bfloat16 [1024, 512], replicated, may hold values from -0.1875 to 0.1875
- query_gain: bfloat16 [1024], replicated, may hold values from 0.099609375 to 1.8984375
- key_gain: bfloat16 [512], replicated, may hold values from 0.099609375 to 1.8984375
- w_output: bfloat16 [1024, 1024], replicated, may hold values from -2 to 2
- ffn_gain: bfloat16 [1024], replicated, may hold values from 0.099609375 to 1.8984375
- w_router: bfloat16 [1024, 32], replicated, may hold values from -0.09375 to 0.09375
- w_gate: bfloat16 [32, 1024, 512], P('expert'), may hold values from -0.1875 to 0.1875
- w_up: bfloat16 [32, 1024, 512], P('expert'), may hold values from -0.1875 to 0.1875
- w_down: bfloat16 [32, 512, 1024], P('expert'), may hold values from -1 to 1
Outputs:
- mixed_out: bfloat16 [16, 2048, 1024], P('expert', 'dp')
- token_grad: bfloat16 [16, 2048, 1024], P('expert', 'dp')
- attn_gain_grad: float32 [1024], replicated
- w_query_grad: float32 [1024, 1024], replicated
- w_key_grad: float32 [1024, 512], replicated
- w_value_grad: float32 [1024, 512], replicated
- query_gain_grad: float32 [1024], replicated
- key_gain_grad: float32 [512], replicated
- w_output_grad: float32 [1024, 1024], replicated
- ffn_gain_grad: float32 [1024], replicated
- w_router_grad: float32 [1024, 32], replicated
- w_gate_grad: float32 [32, 1024, 512], P('expert')
- w_up_grad: float32 [32, 1024, 512], P('expert')
- w_down_grad: float32 [32, 512, 1024], P('expert')
The draws below stay inside these ranges and needn't reach their ends.
Inputs may be any that keep to these rules, and one draw needn't show every extreme that they name: `lengths`: one of the 16 sequences is full; positions at or past a sequence's length are padding. `routes`: each row names 8 different experts; among the 256 rows of one device no expert is named by more than 80 rows, and in some devices' rows one expert is named by exactly 80.
All inputs are finite; a program needn't handle non-finite values.
Results may differ from the reference program's by a relative error of at most 0.025.
Values may be sent and summed in bfloat16 or wider, within the bound.
A program may use at most 192 MiB of HBM per device.

```python
import math
import jax
import jax.numpy as jnp
import numpy as np
from jax import lax

D = 1024
HEADS = 16
KV_HEADS = 8
HEAD_DIM = 64
EXPERTS = 32
TOPK = 8
EFF = 512
TOK_DEV = 256
SEQ = 2048
SEQS = 16
CAP = 80
N_DP = 8


def draw_lengths(key, part):
    key = jax.random.fold_in(key, 7)
    first_key, second_key = jax.random.split(key)
    shortest = (N_DP - 1) * TOK_DEV + 1
    drawn = jax.random.randint(first_key, (SEQS,), shortest, SEQ + 1)
    chosen = jax.random.randint(second_key, (), 0, SEQS)
    return drawn.at[chosen].set(SEQ).astype(jnp.int32)


def steps_of(own_key, extent, shards, least, top_value):
    level, own = 1.0, jax.random.fold_in(own_key, 6)
    for dim, parts in shards:
        steps = jnp.exp(jax.random.uniform(jax.random.fold_in(own, dim), (parts,), jnp.float32, least / len(shards), top_value / len(shards)))
        level = level * jnp.repeat(steps, extent[dim] // parts).reshape([-1 if axis == dim else 1 for axis in range(len(extent))])
    return level


def routed_block(stream_key, own, number, rows, amount, top, reach, lean):
    ranking = jax.random.permutation(stream_key, amount)
    heavy_load, ordinary = load_shares(amount, rows * top, reach, lean, True), load_shares(amount, rows * top, reach, lean, False)
    places = jnp.arange(amount)

    def named(sizes, rotation):
        used = int((sizes > 0).sum())
        fixed = max(1, used // 4)
        shifted = fixed + (places - fixed + rotation * (used - fixed)) % max(1, amount - fixed)
        return jnp.zeros((amount,), jnp.int32).at[ranking[jnp.where(places < fixed, places, shifted)]].set(jnp.asarray(sizes, jnp.int32))

    sizes = jnp.where(number % 4 == 0, named(heavy_load, number // 4), named(ordinary, number - number // 4 - 1))
    mixed = jax.random.permutation(jax.random.fold_in(own, 3), amount)
    source_of, taker = mixed[0:amount // 2 * 2:2], mixed[1:amount // 2 * 2:2]
    room = jnp.minimum(sizes[source_of] - 1, reach - sizes[taker]) // 2
    room = jnp.where((source_of == ranking[0]) | (taker == ranking[0]) | (sizes[taker] == 0), 0, jnp.maximum(room, 0))
    shifted = jax.random.randint(jax.random.fold_in(own, 4), (amount // 2,), 0, 1 << 20) % (room + 1)
    sizes = sizes.at[source_of].add(-shifted).at[taker].add(shifted)
    items = jnp.searchsorted(jnp.cumsum(sizes), jnp.arange(rows * top), side="right").astype(jnp.int32)
    listing = items.reshape(top, rows).T
    listing = listing[jax.random.permutation(jax.random.fold_in(own, 1), rows)]
    rotation = jax.random.randint(jax.random.fold_in(own, 2), (rows, 1), 0, top)
    return jnp.take_along_axis(listing, (jnp.arange(top)[None, :] + rotation) % top, axis=1)


def load_shares(count, total, limit, skew, full):
    loads = [(1 << 20) // math.isqrt(rank ** skew) + 1 for rank in range(1, count + 1)]
    largest = limit if full else min(limit, max(-(-total // count), total * loads[0] // sum(loads)))
    least = 1 if total - largest >= count - 1 else 0
    given, surplus = [largest] + [least] * (count - 1), total - largest - least * (count - 1)
    while surplus > 0:
        free = [i for i in range(1, count) if given[i] < largest] or [i for i in range(1, count) if given[i] < limit]
        mass, remaining = sum([loads[i] for i in free]), surplus
        for i in free:
            more = min(limit - given[i], max(1, remaining * loads[i] // mass), surplus)
            given[i] = given[i] + more
            surplus = surplus - more
    return np.array(given)


def centred(own_key, shape, scale, most, cuts=(), held_as=jnp.bfloat16):
    entries = jax.random.normal(own_key, shape, jnp.float32) * scale
    if len(cuts) > 0:
        entries = steps_of(own_key, shape, cuts, -0.22, 0.18) * entries
    return jnp.clip(entries, min=-most, max=most).astype(held_as)


def setup_inputs(seed: int = 0) -> dict:
    seeds = jax.random.split(jax.random.key(seed), 17)
    tokens = centred(seeds[0], (SEQS, SEQ, D), 1.0, 6.0, ((0, 16), (1, 8)))
    cotangent = centred(seeds[1], (SEQS, SEQ, D), 1.0, 6.0, ((0, 16), (1, 8)))
    lengths = draw_lengths(jax.random.fold_in(seeds[16], 71), 0)
    routes_keys = jax.random.split(jax.random.fold_in(seeds[3], 1), SEQS * SEQ // TOK_DEV)
    routes_turns = jax.random.permutation(jax.random.fold_in(seeds[3], 3), SEQS * SEQ // TOK_DEV)
    routes = jax.vmap(lambda own, number: routed_block(jax.random.fold_in(seeds[3], 2), own, number, TOK_DEV, EXPERTS, TOPK, CAP, 2))(routes_keys, routes_turns).reshape((SEQS, SEQ, TOPK))
    attn_gain = jnp.clip(1.0 + 0.18 * jax.random.normal(seeds[4], (D,), jnp.float32), 0.099609375, 1.8984375).astype(jnp.bfloat16)
    w_query = centred(seeds[5], (D, D), D ** -0.5, 0.1875)
    w_key = centred(seeds[6], (D, KV_HEADS * HEAD_DIM), D ** -0.5, 0.1875)
    w_value = centred(seeds[7], (D, KV_HEADS * HEAD_DIM), D ** -0.5, 0.1875)
    query_gain = jnp.clip(1.0 + 0.18 * jax.random.normal(seeds[8], (D,), jnp.float32), 0.099609375, 1.8984375).astype(jnp.bfloat16)
    key_gain = jnp.clip(1.0 + 0.18 * jax.random.normal(seeds[9], (KV_HEADS * HEAD_DIM,), jnp.float32), 0.099609375, 1.8984375).astype(jnp.bfloat16)
    w_output = centred(seeds[10], (D, D), (max(D // 128, 1)) ** -0.5, 2.0)
    ffn_gain = jnp.clip(1.0 + 0.18 * jax.random.normal(seeds[11], (D,), jnp.float32), 0.099609375, 1.8984375).astype(jnp.bfloat16)
    w_router = centred(seeds[12], (D, EXPERTS), (4 * D) ** -0.5, 0.09375)
    w_gate = centred(seeds[13], (EXPERTS, D, EFF), D ** -0.5, 0.1875, ((0, 16),))
    w_up = centred(seeds[14], (EXPERTS, D, EFF), D ** -0.5, 0.1875, ((0, 16),))
    w_down = centred(seeds[15], (EXPERTS, EFF, D), (max(EFF // 16, 1)) ** -0.5, 1.0, ((0, 16),))
    return dict(tokens=tokens, cotangent=cotangent, lengths=lengths, routes=routes, attn_gain=attn_gain, w_query=w_query, w_key=w_key, w_value=w_value, query_gain=query_gain, key_gain=key_gain, w_output=w_output, ffn_gain=ffn_gain, w_router=w_router, w_gate=w_gate, w_up=w_up, w_down=w_down)


epsilon = 1e-06
HIGHEST = lax.Precision.HIGHEST

@jax.custom_vjp
def low(v):
    return lax.optimization_barrier(v.astype(jnp.bfloat16)).astype(jnp.float32)

@jax.custom_vjp
def low_back(v):
    return v

def low_keep(v):
    return (low(v), None)

def low_pass(kept, grad):
    return (grad,)

def back_keep(v):
    return (v, None)

def back_low(kept, grad):
    return (low(grad),)
low.defvjp(low_keep, low_pass)
low_back.defvjp(back_keep, back_low)

def product(left, right):
    return jnp.dot(left, right, precision=HIGHEST)

def norm_rows(values, norm_gain):
    return values * lax.rsqrt(lax.optimization_barrier(jnp.mean(values * values, axis=-1, keepdims=True)) + epsilon) * norm_gain

def rope_tables(positions):
    steps_half = jnp.arange(HEAD_DIM // 2).astype(jnp.float32)
    inverse = jnp.exp(steps_half * (-2.0 * math.log(10000.0) / HEAD_DIM))
    angles = positions.astype(jnp.float32)[:, None] * inverse[None, :]
    return (jnp.cos(angles), jnp.sin(angles))

def rotate(values, cosine, sine_table):
    count_rows = values.shape[0]
    heads_view = values.reshape(count_rows, -1, HEAD_DIM)
    front_half = heads_view[..., :HEAD_DIM // 2]
    back_half = heads_view[..., HEAD_DIM // 2:]
    cosine_rows = cosine[:, None, :]
    sine_rows = sine_table[:, None, :]
    turned = jnp.concatenate([front_half * cosine_rows - back_half * sine_rows, back_half * cosine_rows + front_half * sine_rows], axis=-1)
    return turned.reshape(count_rows, -1)

def head_block(operands, key_valid):
    query_pair, key_head, value_head = operands
    scores = jnp.einsum('trd,sd->rts', query_pair, key_head, precision=HIGHEST) * HEAD_DIM ** (-0.5)
    scores = low_back(scores)
    scores = jnp.where(key_valid[None], scores, -1e+30)
    probs = low(jax.nn.softmax(scores, axis=-1))
    return jnp.einsum('rts,sd->trd', probs, value_head, precision=HIGHEST)

def place_rows(pair_values, target):
    filled = jnp.zeros((EXPERTS * CAP + 1, D), pair_values.dtype).at[target].set(pair_values)
    return filled[:EXPERTS * CAP]

def layer_sequence(weights, token_rows, length, route_rows):
    attn_gain, w_query, w_key, w_value, query_gain, key_gain, w_output, ffn_gain, w_router, w_gate, w_up, w_down = weights
    positions = jnp.arange(SEQ, dtype=jnp.int32)
    cosine, sine_table = rope_tables(positions)
    normed = low(norm_rows(token_rows, attn_gain))
    query_raw = low_back(product(normed, w_query))
    key_raw = low_back(product(normed, w_key))
    value_raw = low_back(product(normed, w_value))
    queries = low(rotate(norm_rows(query_raw, query_gain), cosine, sine_table))
    keys_all = low(rotate(norm_rows(key_raw, key_gain), cosine, sine_table))
    values_all = low(value_raw)
    key_valid = (positions[None, :] <= positions[:, None]) & (positions[None, :] < length)
    query_groups = queries.reshape(SEQ, KV_HEADS, HEADS // KV_HEADS, HEAD_DIM).transpose(1, 0, 2, 3)
    key_groups = keys_all.reshape(SEQ, KV_HEADS, HEAD_DIM).transpose(1, 0, 2)
    value_groups = values_all.reshape(SEQ, KV_HEADS, HEAD_DIM).transpose(1, 0, 2)
    head_step = jax.checkpoint(lambda operands: head_block(operands, key_valid))
    mixed_heads = lax.map(head_step, (query_groups, key_groups, value_groups))
    attended = low(low_back(mixed_heads.transpose(1, 0, 2, 3).reshape(SEQ, D)))
    hidden_res = token_rows + low_back(product(attended, w_output))
    ffn_in = low(norm_rows(hidden_res, ffn_gain))
    logits = low_back(product(ffn_in, w_router))
    choose = (route_rows[:, :, None] == jnp.arange(EXPERTS, dtype=jnp.int32)[None, None, :]).astype(jnp.float32)
    gates = jax.nn.softmax(jnp.einsum('tke,te->tk', choose, logits, precision=HIGHEST), axis=-1)
    blocks = SEQ // TOK_DEV
    block_routes = route_rows.reshape(blocks, TOK_DEV * TOPK)
    member = (block_routes[:, :, None] == jnp.arange(EXPERTS, dtype=jnp.int32)[None, None, :]).astype(jnp.int32)
    earlier = jnp.cumsum(member, axis=1) - member
    slots = lax.optimization_barrier(jnp.sum(earlier * member, axis=-1))
    target = jnp.where(slots < CAP, block_routes * CAP + slots, EXPERTS * CAP).astype(jnp.int32)
    spread_rows = jnp.broadcast_to(ffn_in.reshape(blocks, TOK_DEV, 1, D), (blocks, TOK_DEV, TOPK, D))
    pair_rows = low_back(spread_rows.reshape(blocks, TOK_DEV * TOPK, D))
    filled = jax.vmap(place_rows)(pair_rows, target)
    expert_in = filled.reshape(blocks, EXPERTS, CAP, D).transpose(1, 0, 2, 3).reshape(EXPERTS, blocks * CAP, D)
    gate_pre = low_back(jnp.einsum('erd,edf->erf', expert_in, w_gate, precision=HIGHEST))
    up_pre = low_back(jnp.einsum('erd,edf->erf', expert_in, w_up, precision=HIGHEST))
    inner = low(jax.nn.silu(gate_pre) * up_pre)
    expert_out = low(low_back(jnp.einsum('erf,efd->erd', inner, w_down, precision=HIGHEST)))
    back_rows = expert_out.reshape(EXPERTS, blocks, CAP, D).transpose(1, 0, 2, 3).reshape(blocks, EXPERTS * CAP, D)
    padded = jnp.concatenate([back_rows, jnp.zeros((blocks, 1, D), back_rows.dtype)], axis=1)
    returned = jnp.take_along_axis(padded, target[:, :, None], axis=1).reshape(SEQ, TOPK, D)
    return hidden_res + jnp.einsum('tk,tkd->td', gates, returned, precision=HIGHEST)

def reference(tokens, cotangent, lengths, routes, attn_gain, w_query, w_key, w_value, query_gain, key_gain, w_output, ffn_gain, w_router, w_gate, w_up, w_down):
    weights = tuple((weight_arg.astype(jnp.float32) for weight_arg in (attn_gain, w_query, w_key, w_value, query_gain, key_gain, w_output, ffn_gain, w_router, w_gate, w_up, w_down)))

    def whole_layer(token_values, weight_values):
        seq_step = jax.checkpoint(lambda operands: layer_sequence(weight_values, operands[0], operands[1], operands[2]))
        return lax.map(seq_step, (token_values, lengths, routes))
    mixed, pullback = jax.vjp(whole_layer, tokens.astype(jnp.float32), weights)
    token_grad, weight_grads = pullback(cotangent.astype(jnp.float32))
    return (mixed.astype(jnp.bfloat16), token_grad.astype(jnp.bfloat16), weight_grads[0], weight_grads[1], weight_grads[2], weight_grads[3], weight_grads[4], weight_grads[5], weight_grads[6], weight_grads[7], weight_grads[8], weight_grads[9], weight_grads[10], weight_grads[11])
```

```python
import math

import jax
import jax.numpy as jnp
from jax import lax
from jax.experimental import pallas as pl
from jax.experimental.pallas import tpu as pltpu
from jax.sharding import PartitionSpec as P

HEADS = 16
KV_HEADS = 8
HEAD_DIM = 64
EXPERTS = 32
TOPK = 8
CAP = 80


epsilon = 1e-06
HIGHEST = lax.Precision.HIGHEST


def in_one_piece(arrays, axis, dim, along):
    widths = [a.shape[along] for a in arrays]
    both = jnp.concatenate(arrays, axis=along)
    whole = lax.all_gather(both, axis, axis=dim, tiled=True)
    return tuple(jnp.split(whole, [sum(widths[:k]) for k in range(1, len(widths))], axis=along))


def sent_together(arrays, axis, dim, along):
    widths = [a.shape[along] for a in arrays]
    both = jnp.concatenate(arrays, axis=along)
    whole = lax.psum_scatter(both, axis, scatter_dimension=dim, tiled=True)
    return tuple(jnp.split(whole, [sum(widths[:k]) for k in range(1, len(widths))], axis=along))


def together(arrays, axis):
    vector, at, finished = (jnp.concatenate([a.reshape(-1) for a in arrays]), 0, [])
    so_far = lax.psum(vector, axis)
    for a in arrays:
        finished.append(so_far[at : at + a.size].reshape(a.shape))
        at += a.size
    return tuple(finished)


def norm_rows(values, norm_gain):
    return (
        values * lax.rsqrt(jnp.mean(values * values, axis=-1, keepdims=True) + epsilon) * norm_gain
    )


def rope_tables(positions):
    steps_half = jnp.arange(HEAD_DIM // 2).astype(jnp.float32)
    inverse = jnp.exp(steps_half * (-2.0 * math.log(10000.0) / HEAD_DIM))
    angles = positions.astype(jnp.float32)[:, None] * inverse[None, :]
    return (jnp.cos(angles), jnp.sin(angles))


def rotate(values, cosine, sine_table):
    count_rows = values.shape[0]
    heads_view = values.reshape(count_rows, -1, HEAD_DIM)
    front_half = heads_view[..., : HEAD_DIM // 2]
    back_half = heads_view[..., HEAD_DIM // 2 :]
    cosine_rows = cosine[:, None, :]
    sine_rows = sine_table[:, None, :]
    turned = jnp.concatenate(
        [
            front_half * cosine_rows - back_half * sine_rows,
            back_half * cosine_rows + front_half * sine_rows,
        ],
        axis=-1,
    )
    return turned.reshape(count_rows, -1)


def contract_rows(left, right):
    return lax.dot_general(
        left, right, (((0,), (0,)), ((), ())), preferred_element_type=jnp.float32
    )


def times_transposed(left, right):
    return lax.dot_general(
        left, right, (((1,), (1,)), ((), ())), preferred_element_type=jnp.float32
    )


def masked_scores(query_pair, key_head, key_valid):
    scores = jnp.einsum(
        "trd,sd->rts", query_pair, key_head, preferred_element_type=jnp.float32
    ) * HEAD_DIM ** (-0.5)
    return jnp.where(key_valid[None], scores, -1e30)


def forward_head(operands, key_valid):
    query_pair, key_head, value_head = operands
    scores = masked_scores(query_pair, key_head, key_valid)
    top_score = jnp.max(scores, axis=-1, keepdims=True)
    log_total = top_score + jnp.log(jnp.sum(jnp.exp(scores - top_score), axis=-1, keepdims=True))
    probs = jnp.exp(scores - log_total).astype(jnp.bfloat16)
    mixed = jnp.einsum("rts,sd->trd", probs, value_head, preferred_element_type=jnp.float32)
    return (mixed, log_total[..., 0])


def backward_head(operands, key_valid):
    query_pair, key_head, value_head, grad_pair, log_total = operands
    scores = masked_scores(query_pair, key_head, key_valid)
    probs = jnp.exp(scores - log_total[..., None])
    grad_probs = jnp.einsum(
        "trd,sd->rts", grad_pair, value_head, preferred_element_type=jnp.float32
    )
    score_grad = (
        probs * (grad_probs - jnp.sum(probs * grad_probs, axis=-1, keepdims=True))
    ).astype(jnp.bfloat16)
    query_grad = jnp.einsum(
        "rts,sd->trd", score_grad, key_head, preferred_element_type=jnp.float32
    ) * HEAD_DIM ** (-0.5)
    key_grad = jnp.einsum(
        "rts,trd->sd", score_grad, query_pair, preferred_element_type=jnp.float32
    ) * HEAD_DIM ** (-0.5)
    value_grad = jnp.einsum(
        "rts,trd->sd", probs.astype(jnp.bfloat16), grad_pair, preferred_element_type=jnp.float32
    )
    return (query_grad, key_grad, value_grad)


RING = 4
ROWS = 256
EXTRA = 16
FULL = ROWS + EXTRA
GROUP = 4 * CAP
MESH = pl.DeviceIdType.MESH


def dot_nn(a, b):
    return jnp.dot(a, b, preferred_element_type=jnp.float32)


def dot_nt(a, b):
    return lax.dot_general(a, b, (((1,), (1,)), ((), ())), preferred_element_type=jnp.float32)


def dot_tn(a, b):
    return lax.dot_general(a, b, (((0,), (0,)), ((), ())), preferred_element_type=jnp.float32)


class Torus:
    def __init__(self):
        self.dp = lax.axis_index("dp")
        expert = lax.axis_index("expert")
        self.expert = expert
        self.z, self.y = expert // RING, expert % RING

    def block(self, dz, dy):
        return ((self.z + dz + RING) % RING) * RING + (self.y + dy + RING) % RING

    def near(self, axis, step):
        return (self.dp, self.block(step, 0) if axis == "z" else self.block(0, step))

    def along(self, axis, other, step):
        return self.block(step, other) if axis == "z" else self.block(other, step)

    def neighbours(self):
        return [self.near(axis, step) for axis in "yz" for step in (1, -1)]


class Gather:
    def __init__(self, torus, buffer, send, recv, number, axis, other, low, size):
        self.torus, self.buffer, self.send, self.recv = torus, buffer, send, recv
        self.number, self.axis, self.other, self.low, self.size = number, axis, other, low, size

    def copy(self, which, offset, start, size, step):
        at = self.torus.along(self.axis, self.other, offset) * ROWS + start
        rows = self.buffer.at[pl.ds(pl.multiple_of(at, 16), size)]
        return pltpu.make_async_remote_copy(
            src_ref=rows,
            dst_ref=rows,
            send_sem=self.send.at[self.number, which],
            recv_sem=self.recv.at[self.number, which],
            device_id=self.torus.near(self.axis, step),
            device_id_type=MESH,
        )

    def first(self):
        self.copy(0, 0, self.low, self.size, 1).start()
        self.copy(1, 0, self.low, self.size, -1).start()

    def second(self):
        half = self.size // 2
        self.copy(0, -1, self.low, self.size, 1).wait_recv()
        self.copy(2, -1, self.low, half, 1).start()
        self.copy(1, 1, self.low, self.size, -1).wait_recv()
        self.copy(3, 1, self.low + half, half, -1).start()

    def third(self):
        half = self.size // 2
        self.copy(2, 2, self.low, half, 1).wait_recv()
        self.copy(3, 2, self.low + half, half, -1).wait_recv()

    def drain(self):
        half = self.size // 2
        self.copy(0, 0, self.low, self.size, 1).wait_send()
        self.copy(1, 0, self.low, self.size, -1).wait_send()
        self.copy(2, -1, self.low, half, 1).wait_send()
        self.copy(3, 1, self.low + half, half, -1).wait_send()


class Scatter:
    def __init__(self, torus, sums, landing, send, recv, number, base, axis, other, low, first, second):
        self.torus, self.sums, self.landing, self.send, self.recv = torus, sums, landing, send, recv
        self.number, self.axis, self.other = number, axis, other
        self.low, self.parts = low, (first, second)
        self.size = first + second
        self.slots = (base, base + first, base + self.size, base + 2 * self.size)

    def rows(self, which):
        if which == 0:
            return self.low, self.parts[0]
        if which == 1:
            return self.low + self.parts[0], self.parts[1]
        return self.low, self.size

    def at(self, offset):
        return self.torus.along(self.axis, self.other, offset)

    def copy(self, which):
        start, size = self.rows(which)
        offset = (2, 2, 1, -1)[which]
        return pltpu.make_async_remote_copy(
            src_ref=self.sums.at[self.at(offset), pl.ds(start, size)],
            dst_ref=self.landing.at[pl.ds(self.slots[which], size)],
            send_sem=self.send.at[self.number, which],
            recv_sem=self.recv.at[self.number, which],
            device_id=self.torus.near(self.axis, (1, -1, 1, -1)[which]),
            device_id_type=MESH,
        )

    def add(self, which, offset):
        start, size = self.rows(which)
        block = self.at(offset)

        @pl.loop(0, size // 16)
        def _(k):
            here = pl.ds(pl.multiple_of(start + k * 16, 16), 16)
            there = pl.ds(pl.multiple_of(self.slots[which] + k * 16, 16), 16)
            total = self.sums[block, here].astype(jnp.float32) + self.landing[there].astype(jnp.float32)
            self.sums[block, here] = total.astype(jnp.bfloat16)

    def first(self):
        self.copy(0).start()
        self.copy(1).start()

    def second(self):
        self.copy(0).wait_recv()
        self.add(0, 1)
        self.copy(2).start()
        self.copy(1).wait_recv()
        self.add(1, -1)
        self.copy(3).start()

    def third(self, result=None):
        self.copy(2).wait_recv()
        self.copy(3).wait_recv()
        block = self.at(0)

        @pl.loop(0, self.size // 16)
        def _(k):
            here = pl.ds(pl.multiple_of(self.low + k * 16, 16), 16)
            left = pl.ds(pl.multiple_of(self.slots[2] + k * 16, 16), 16)
            right = pl.ds(pl.multiple_of(self.slots[3] + k * 16, 16), 16)
            total = (
                self.sums[block, here].astype(jnp.float32)
                + self.landing[left].astype(jnp.float32)
                + self.landing[right].astype(jnp.float32)
            )
            if result is None:
                self.sums[block, here] = total.astype(jnp.bfloat16)
            else:
                result[here] = total

    def drain(self):
        for which in range(4):
            self.copy(which).wait_send()


def moe_kernel(
    ffn, cot, sel, mem, wr, w_gate, w_up, w_down,
    ret, mixed, grad_gu, grad_d,
    rows, sums, wgu, wd, held, pair, inner, dgu, mixing, back, cotv, gate_rows, grad_rows, stage,
    ag_send, ag_recv, rs_send, rs_recv, w_sem, cot_sem, stage_sem, credit,
):
    torus = Torus()
    barrier = pltpu.get_barrier_semaphore()
    for device in torus.neighbours():
        pl.semaphore_signal(barrier, inc=1, device_id=device, device_id_type=MESH)

    weights = [
        pltpu.make_async_copy(w_gate, wgu.at[:, :, pl.ds(0, 512)], w_sem.at[0]),
        pltpu.make_async_copy(w_up, wgu.at[:, :, pl.ds(512, 512)], w_sem.at[1]),
        pltpu.make_async_copy(w_down, wd, w_sem.at[2]),
    ]
    for copy in weights:
        copy.start()

    def group_z(g):
        return (torus.z + g + (g // 2) * (1 - 2 * (g % 2))) % RING

    def cot_copy(g):
        return pltpu.make_async_copy(cot.at[pl.ds(group_z(g) * RING, RING)], cotv, cot_sem)

    cot_copy(0).start()
    rows[pl.ds(pl.multiple_of(torus.expert * ROWS, ROWS), ROWS)] = ffn[...]
    pl.semaphore_wait(barrier, 4)

    def gather(number, axis, other, low):
        return Gather(torus, rows, ag_send, ag_recv, number, axis, other, low, ROWS // 2)

    a_first = gather(0, "y", 0, 0)
    b_first = gather(1, "z", 0, ROWS // 2)
    a_second = {d: gather(2 + d % RING, "z", d, 0) for d in (0, 1, -1, 2)}
    b_second = {d: gather(6 + d % RING, "y", d, ROWS // 2) for d in (0, 1, -1, 2)}
    gathers = [a_first, b_first, *a_second.values(), *b_second.values()]

    a_first.first()
    b_first.first()
    b_second[0].first()
    a_second[0].first()
    a_first.second()
    b_first.second()
    for d in (1, -1):
        b_second[d].first()
        a_second[d].first()
    a_first.third()
    b_first.third()
    b_second[2].first()
    a_second[2].first()
    for copy in weights:
        copy.wait()

    def choice(source, e):
        return lax.broadcasted_iota(jnp.int32, (CAP, ROWS), 0) == sel[source, pl.ds(e, 1), :]

    def choices(source):
        picked = [choice(source, e) for e in range(2)]
        both = jnp.concatenate([p.astype(jnp.float32) for p in picked], axis=0)
        return picked, both.astype(jnp.bfloat16)

    def stage_copy(slot, target):
        return pltpu.make_async_copy(stage.at[slot], target, stage_sem.at[slot])

    expert_rows = lax.broadcasted_iota(jnp.int32, (EXPERTS, ROWS), 0)

    @pl.loop(0, 4)
    def _(g):
        @pl.when(g == 0)
        def _():
            b_second[0].second()
            a_second[0].second()
            b_second[0].third()

        @pl.when(g == 1)
        def _():
            for d in (1, -1):
                b_second[d].second()
                a_second[d].second()
            a_second[2].second()
            b_second[1].third()

        @pl.when(g == 2)
        def _():
            b_second[2].second()
            b_second[-1].third()

        @pl.when(g == 3)
        def _():
            for d in (0, 1, -1, 2):
                a_second[d].third()
            b_second[2].third()

        cot_copy(g).wait()
        first_source = group_z(g) * RING

        @pl.loop(0, 4)
        def _(j):
            source = first_source + j
            block = rows[pl.ds(pl.multiple_of(source * ROWS, ROWS), ROWS)]
            named = mem[source].astype(jnp.float32) > 0.5
            logits = jnp.where(named, dot_nt(wr[...], block), -1e30)
            weight = jnp.where(named, jnp.exp(logits - jnp.max(logits, axis=0, keepdims=True)), 0.0)
            gates = weight / jnp.sum(weight, axis=0, keepdims=True)
            picked, both = choices(source)
            took = dot_nn(both, block).astype(jnp.bfloat16)
            took_grad = dot_nn(both, cotv[j]).astype(jnp.bfloat16)
            here = pl.ds(pl.multiple_of(j * CAP, 16), CAP)
            there = pl.ds(pl.multiple_of(g * GROUP + j * CAP, 16), CAP)
            for e in range(2):
                own = jnp.sum(
                    jnp.where(expert_rows == torus.expert * 2 + e, gates, 0.0), axis=0, keepdims=True
                )
                of_rows = jnp.sum(jnp.where(picked[e], own, 0.0), axis=1, keepdims=True)
                gate_rows[e, here] = jnp.broadcast_to(of_rows, (CAP, 128))
                held[e, there] = took[e * CAP : (e + 1) * CAP]
                mixing[e, here] = took_grad[e * CAP : (e + 1) * CAP]

        @pl.when(g < 3)
        def _():
            cot_copy(g + 1).start()

        @pl.when(g == 3)
        def _():
            for one in gathers:
                one.drain()
            for device in torus.neighbours():
                pl.semaphore_signal(credit, inc=1, device_id=device, device_id_type=MESH)

        @pl.loop(0, 2)
        def _(e):
            there = pl.ds(pl.multiple_of(g * GROUP, 16), GROUP)
            both = dot_nn(held[e, there], wgu[e])
            gate, up = both[:, :512], both[:, 512:]
            sig = jax.nn.sigmoid(gate)
            silu = gate * sig
            act = (silu * up).astype(jnp.bfloat16)
            inner[e, there] = act
            out = dot_nn(act, wd[e]).astype(jnp.bfloat16).astype(jnp.float32)
            grad = mixing[e].astype(jnp.float32)
            weight = gate_rows[e][:, :1]
            grad_rows[e] = jnp.broadcast_to(jnp.sum(grad * out, axis=1, keepdims=True), (GROUP, 128))
            pair[e, there] = (weight * grad).astype(jnp.bfloat16)
            mixing[e] = (weight * out).astype(jnp.bfloat16)
            inner_grad = dot_nt(pair[e, there], wd[e])
            dgu[e, there, :512] = (inner_grad * up * sig * (1.0 + gate * (1.0 - sig))).astype(jnp.bfloat16)
            dgu[e, there, 512:] = (inner_grad * silu).astype(jnp.bfloat16)
            back[e] = dot_nt(dgu[e, there], wgu[e]).astype(jnp.bfloat16)

        @pl.loop(0, 4)
        def _(j):
            source = first_source + j
            picked, both = choices(source)
            here = pl.ds(pl.multiple_of(j * CAP, 16), CAP)
            part = dot_tn(both, jnp.concatenate([back[0, here], back[1, here]], axis=0))
            sums[source, pl.ds(EXTRA, ROWS)] = part.astype(jnp.bfloat16)
            grads = jnp.zeros((EXPERTS, ROWS), jnp.float32)
            for e in range(2):
                own = jnp.sum(
                    jnp.where(picked[e], grad_rows[e, here][:, :1], 0.0), axis=0, keepdims=True
                )
                grads = grads + jnp.where(expert_rows == torus.expert * 2 + e, own, 0.0)
            laid = jnp.concatenate([grads[8 * q : 8 * q + 8] for q in range(4)], axis=1)
            sums[source, pl.ds(0, EXTRA)] = jnp.concatenate([laid, jnp.zeros_like(laid)], axis=0).astype(
                jnp.bfloat16
            )
            slot = j % 2

            @pl.when((g > 0) | (j > 1))
            def _():
                stage_copy(slot, mixed.at[source]).wait()

            result = dot_tn(both, jnp.concatenate([mixing[0, here], mixing[1, here]], axis=0))
            stage[slot] = result.astype(jnp.bfloat16)
            stage_copy(slot, mixed.at[source]).start()

    pl.semaphore_wait(credit, 4)

    order = (2, 1, -1, 0)
    a_lead = {}
    b_lead = {}
    for n, d in enumerate(order):
        a_lead[d] = Scatter(
            torus, sums, rows, rs_send, rs_recv, n, n * 384, "z", d, 0, 64, 64
        )
        b_lead[d] = Scatter(
            torus, sums, rows, rs_send, rs_recv, 4 + n, 1920 + n * 432, "y", d, 128, 80, 64
        )
    a_last = Scatter(torus, sums, rows, rs_send, rs_recv, 8, 4 * 384, "y", 0, 0, 64, 64)
    b_last = Scatter(torus, sums, rows, rs_send, rs_recv, 9, 1920 + 4 * 432, "z", 0, 128, 80, 64)

    def write_grads(low, high):
        @pl.loop(low, high)
        def _(k):
            slot = k % 2
            e, c = k // 6, k % 6
            stage_copy(slot, grad_d.at[0, pl.ds(0, 256)]).wait()

            @pl.when(c < 4)
            def _():
                columns = pl.ds(pl.multiple_of(c * 256, 256), 256)
                stage[slot] = dot_tn(held[e, :, columns], dgu[e]).astype(jnp.bfloat16)
                stage_copy(slot, grad_gu.at[e, columns]).start()

            @pl.when(c >= 4)
            def _():
                columns = pl.ds(pl.multiple_of((c - 4) * 256, 256), 256)
                stage[slot] = dot_tn(inner[e, :, columns], pair[e]).astype(jnp.bfloat16)
                stage_copy(slot, grad_d.at[e, columns]).start()

    for d in order:
        b_lead[d].first()
        a_lead[d].first()
    write_grads(0, 4)
    for d in order:
        b_lead[d].second()
        a_lead[d].second()
    write_grads(4, 12)
    for slot in range(2):
        stage_copy(slot, grad_d.at[0, pl.ds(0, 256)]).wait()
    for d in order:
        b_lead[d].third()
        a_lead[d].third()
        if d == 2:
            b_last.first()
            a_last.first()
    b_last.second()
    a_last.second()
    b_last.third(ret)
    a_last.third(ret)
    for one in [*a_lead.values(), *b_lead.values(), a_last, b_last]:
        one.drain()


def moe(ffn_in, cot_all, sel, mem, router_rows, w_gate, w_up, w_down):
    vmem, hbm = pl.BlockSpec(memory_space=pltpu.VMEM), pl.BlockSpec(memory_space=pl.ANY)
    low, total = jnp.bfloat16, 4 * GROUP
    return pl.pallas_call(
        moe_kernel,
        name="moe",
        out_shape=(
            jax.ShapeDtypeStruct((FULL, 1024), jnp.float32),
            jax.ShapeDtypeStruct((16, ROWS, 1024), low),
            jax.ShapeDtypeStruct((2, 1024, 1024), low),
            jax.ShapeDtypeStruct((2, 512, 1024), low),
        ),
        in_specs=[vmem, hbm, vmem, vmem, vmem, hbm, hbm, hbm],
        out_specs=(vmem, hbm, hbm, hbm),
        scratch_shapes=[
            pltpu.VMEM((16 * ROWS, 1024), low),
            pltpu.VMEM((16, FULL, 1024), low),
            pltpu.VMEM((2, 1024, 1024), low),
            pltpu.VMEM((2, 512, 1024), low),
            pltpu.VMEM((2, total, 1024), low),
            pltpu.VMEM((2, total, 1024), low),
            pltpu.VMEM((2, total, 512), low),
            pltpu.VMEM((2, total, 1024), low),
            pltpu.VMEM((2, GROUP, 1024), low),
            pltpu.VMEM((2, GROUP, 1024), low),
            pltpu.VMEM((4, ROWS, 1024), low),
            pltpu.VMEM((2, GROUP, 128), jnp.float32),
            pltpu.VMEM((2, GROUP, 128), jnp.float32),
            pltpu.VMEM((2, ROWS, 1024), low),
            pltpu.SemaphoreType.DMA((10, 4)),
            pltpu.SemaphoreType.DMA((10, 4)),
            pltpu.SemaphoreType.DMA((10, 4)),
            pltpu.SemaphoreType.DMA((10, 4)),
            pltpu.SemaphoreType.DMA((3,)),
            pltpu.SemaphoreType.DMA,
            pltpu.SemaphoreType.DMA((2,)),
            pltpu.SemaphoreType.REGULAR,
        ],
        compiler_params=pltpu.CompilerParams(
            collective_id=1, has_side_effects=True, vmem_limit_bytes=63 * 2**20
        ),
        cost_estimate=pl.CostEstimate(flops=50 * 10**9, bytes_accessed=40 * 10**6, transcendentals=2 * 10**6),
    )(ffn_in, cot_all, sel, mem, router_rows, w_gate, w_up, w_down)


def body(
    tokens,
    cotangent,
    lengths,
    routes,
    attn_gain,
    w_query,
    w_key,
    w_value,
    query_gain,
    key_gain,
    w_output,
    ffn_gain,
    w_router,
    w_gate,
    w_up,
    w_down,
):
    local_experts = w_gate.shape[0]
    cot_all = lax.all_gather(cotangent[0], "expert", axis=0)
    routes_all = lax.all_gather(routes[0], "expert", axis=0)
    member = (
        (routes_all[:, :, :, None] == jnp.arange(EXPERTS, dtype=jnp.int32)).any(axis=2).astype(jnp.bfloat16)
    )
    mem = member.transpose(0, 2, 1)
    before = jnp.triu(jnp.ones((ROWS, ROWS), jnp.bfloat16), 1)
    own_mem = lax.dynamic_slice_in_dim(mem, lax.axis_index("expert") * local_experts, local_experts, 1)
    slots = jnp.einsum("seu,ut->set", own_mem, before, preferred_element_type=jnp.float32).astype(jnp.int32)
    sel = jnp.where((own_mem > 0) & (slots < CAP), slots, -1)
    token_rows = tokens[0].astype(jnp.float32)
    tok_count = token_rows.shape[0]
    width = token_rows.shape[1]
    kv_width = w_key.shape[1]
    seq_total = tok_count * lax.axis_size("dp")
    query_pos = lax.axis_index("dp") * tok_count + jnp.arange(tok_count, dtype=jnp.int32)
    key_pos = jnp.arange(seq_total, dtype=jnp.int32)
    key_valid = (key_pos[None, :] <= query_pos[:, None]) & (key_pos[None, :] < lengths[0])
    cosine, sine_table = rope_tables(query_pos)
    normed_value, attn_pull = jax.vjp(norm_rows, token_rows, attn_gain.astype(jnp.float32))
    normed = normed_value.astype(jnp.bfloat16)
    query_raw = jnp.dot(normed, w_query, preferred_element_type=jnp.float32)
    key_raw = jnp.dot(normed, w_key, preferred_element_type=jnp.float32)
    value_raw = jnp.dot(normed, w_value, preferred_element_type=jnp.float32)

    def post_norm(query_in, key_in, gain_query, gain_key):
        return (
            rotate(norm_rows(query_in, gain_query), cosine, sine_table),
            rotate(norm_rows(key_in, gain_key), cosine, sine_table),
        )

    post_values, post_pull = jax.vjp(
        post_norm, query_raw, key_raw, query_gain.astype(jnp.float32), key_gain.astype(jnp.float32)
    )
    queries = post_values[0].astype(jnp.bfloat16)
    keys_own = post_values[1].astype(jnp.bfloat16)
    values_own = value_raw.astype(jnp.bfloat16)
    keys_full, values_full = in_one_piece((keys_own, values_own), "dp", 0, 1)
    query_groups = queries.reshape(tok_count, KV_HEADS, HEADS // KV_HEADS, HEAD_DIM).transpose(
        1, 0, 2, 3
    )
    key_groups = keys_full.reshape(seq_total, KV_HEADS, HEAD_DIM).transpose(1, 0, 2)
    value_groups = values_full.reshape(seq_total, KV_HEADS, HEAD_DIM).transpose(1, 0, 2)
    mixed_heads, log_totals = lax.map(
        lambda operands: forward_head(operands, key_valid), (query_groups, key_groups, value_groups)
    )
    attended = mixed_heads.transpose(1, 0, 2, 3).reshape(tok_count, width).astype(jnp.bfloat16)
    hidden_res = token_rows + jnp.dot(attended, w_output, preferred_element_type=jnp.float32)
    ffn_value, ffn_pull = jax.vjp(norm_rows, hidden_res, ffn_gain.astype(jnp.float32))
    ffn_in = ffn_value.astype(jnp.bfloat16)
    logits = jnp.dot(ffn_in, w_router, preferred_element_type=jnp.float32)
    own_routes = (routes[0][:, :, None] == jnp.arange(EXPERTS, dtype=jnp.int32)).any(axis=1)
    gates = jax.nn.softmax(jnp.where(own_routes, logits, -1e30), axis=-1)
    gates = jnp.where(own_routes, gates, 0.0)
    returned, mixed_parts, gate_up_w_grad, down_grad = moe(
        ffn_in, cot_all, sel, mem, w_router.T, w_gate, w_up, w_down
    )
    mixed_sum = lax.psum_scatter(
        mixed_parts.reshape(16 * ROWS, width), "expert", scatter_dimension=0, tiled=True
    )
    mixed_out = (hidden_res + mixed_sum.astype(jnp.float32)).astype(jnp.bfloat16)
    grad_out = cotangent[0].astype(jnp.float32)
    gate_grad = returned[:8].reshape(8, 4, ROWS).transpose(1, 0, 2).reshape(EXPERTS, ROWS).T
    pair_sum = returned[EXTRA:]
    logit_grad = (
        gates * (gate_grad - jnp.sum(gates * gate_grad, axis=-1, keepdims=True))
    ).astype(jnp.bfloat16)
    router_grad = contract_rows(ffn_in, logit_grad)
    ffn_in_grad = times_transposed(logit_grad, w_router) + pair_sum
    res_part, ffn_gain_grad = ffn_pull(ffn_in_grad)
    hidden_grad = grad_out + res_part
    branch_grad = hidden_grad.astype(jnp.bfloat16)
    output_w_grad = contract_rows(attended, branch_grad)
    attended_grad = times_transposed(branch_grad, w_output).astype(jnp.bfloat16)
    grad_groups = attended_grad.reshape(tok_count, KV_HEADS, HEADS // KV_HEADS, HEAD_DIM).transpose(
        1, 0, 2, 3
    )
    query_grad_heads, key_grad_heads, value_grad_heads = lax.map(
        lambda operands: backward_head(operands, key_valid),
        (query_groups, key_groups, value_groups, grad_groups, log_totals),
    )
    query_grad = query_grad_heads.transpose(1, 0, 2, 3).reshape(tok_count, width)
    key_grad_full = key_grad_heads.transpose(1, 0, 2).reshape(seq_total, kv_width)
    value_grad_full = value_grad_heads.transpose(1, 0, 2).reshape(seq_total, kv_width)
    key_grad, value_grad = tuple(
        (
            part.astype(jnp.float32)
            for part in sent_together(
                (key_grad_full.astype(jnp.bfloat16), value_grad_full.astype(jnp.bfloat16)),
                "dp",
                0,
                1,
            )
        )
    )
    query_raw_grad, key_raw_grad, query_gain_grad, key_gain_grad = post_pull((query_grad, key_grad))
    query_raw_low = query_raw_grad.astype(jnp.bfloat16)
    key_raw_low = key_raw_grad.astype(jnp.bfloat16)
    value_raw_low = value_grad.astype(jnp.bfloat16)
    query_w_grad = contract_rows(normed, query_raw_low)
    key_w_grad = contract_rows(normed, key_raw_low)
    value_w_grad = contract_rows(normed, value_raw_low)
    normed_grad = (
        times_transposed(query_raw_low, w_query)
        + times_transposed(key_raw_low, w_key)
        + times_transposed(value_raw_low, w_value)
    )
    token_part, attn_gain_grad = attn_pull(normed_grad)
    token_grad = (hidden_grad + token_part).astype(jnp.bfloat16)
    (
        attn_gain_sum,
        query_w_sum,
        key_w_sum,
        value_w_sum,
        query_gain_sum,
        key_gain_sum,
        output_w_sum,
        ffn_gain_sum,
        router_sum,
    ) = lax.psum(
        (
            attn_gain_grad,
            query_w_grad,
            key_w_grad,
            value_w_grad,
            query_gain_grad,
            key_gain_grad,
            output_w_grad,
            ffn_gain_grad,
            router_grad,
        ),
        ("dp", "expert"),
    )
    gate_up_sum, down_w_sum = lax.psum((gate_up_w_grad, down_grad), "dp")
    gate_w_sum = gate_up_sum[:, :, :512].astype(jnp.float32)
    up_w_sum = gate_up_sum[:, :, 512:].astype(jnp.float32)
    down_w_sum = down_w_sum.astype(jnp.float32)
    return (
        mixed_out[None],
        token_grad[None],
        attn_gain_sum,
        query_w_sum,
        key_w_sum,
        value_w_sum,
        query_gain_sum,
        key_gain_sum,
        output_w_sum,
        ffn_gain_sum,
        router_sum,
        gate_w_sum,
        up_w_sum,
        down_w_sum,
    )


def solution(mesh):
    return jax.shard_map(
        body,
        mesh=mesh,
        in_specs=(
            P("expert", "dp", None),
            P("expert", "dp", None),
            P("expert"),
            P("expert", "dp", None),
            P(),
            P(),
            P(),
            P(),
            P(),
            P(),
            P(),
            P(),
            P(),
            P("expert", None, None),
            P("expert", None, None),
            P("expert", None, None),
        ),
        out_specs=(
            P("expert", "dp", None),
            P("expert", "dp", None),
            P(),
            P(),
            P(),
            P(),
            P(),
            P(),
            P(),
            P(),
            P(),
            P("expert", None, None),
            P("expert", None, None),
            P("expert", None, None),
        ),
        check_vma=False,
    )
```

```python
import math

import jax
import jax.numpy as jnp
from jax import lax
from jax.experimental import pallas as pl
from jax.experimental.pallas import tpu as pltpu
from jax.sharding import PartitionSpec as P

HEADS = 16
KV_HEADS = 8
HEAD_DIM = 64
EXPERTS = 32
TOPK = 8
CAP = 80


epsilon = 1e-06
HIGHEST = lax.Precision.HIGHEST


def in_one_piece(arrays, axis, dim, along):
    widths = [a.shape[along] for a in arrays]
    both = jnp.concatenate(arrays, axis=along)
    whole = lax.all_gather(both, axis, axis=dim, tiled=True)
    return tuple(jnp.split(whole, [sum(widths[:k]) for k in range(1, len(widths))], axis=along))


def sent_together(arrays, axis, dim, along):
    widths = [a.shape[along] for a in arrays]
    both = jnp.concatenate(arrays, axis=along)
    whole = lax.psum_scatter(both, axis, scatter_dimension=dim, tiled=True)
    return tuple(jnp.split(whole, [sum(widths[:k]) for k in range(1, len(widths))], axis=along))


def together(arrays, axis):
    vector, at, finished = (jnp.concatenate([a.reshape(-1) for a in arrays]), 0, [])
    so_far = lax.psum(vector, axis)
    for a in arrays:
        finished.append(so_far[at : at + a.size].reshape(a.shape))
        at += a.size
    return tuple(finished)


def norm_rows(values, norm_gain):
    return (
        values * lax.rsqrt(jnp.mean(values * values, axis=-1, keepdims=True) + epsilon) * norm_gain
    )


def rope_tables(positions):
    steps_half = jnp.arange(HEAD_DIM // 2).astype(jnp.float32)
    inverse = jnp.exp(steps_half * (-2.0 * math.log(10000.0) / HEAD_DIM))
    angles = positions.astype(jnp.float32)[:, None] * inverse[None, :]
    return (jnp.cos(angles), jnp.sin(angles))


def rotate(values, cosine, sine_table):
    count_rows = values.shape[0]
    heads_view = values.reshape(count_rows, -1, HEAD_DIM)
    front_half = heads_view[..., : HEAD_DIM // 2]
    back_half = heads_view[..., HEAD_DIM // 2 :]
    cosine_rows = cosine[:, None, :]
    sine_rows = sine_table[:, None, :]
    turned = jnp.concatenate(
        [
            front_half * cosine_rows - back_half * sine_rows,
            back_half * cosine_rows + front_half * sine_rows,
        ],
        axis=-1,
    )
    return turned.reshape(count_rows, -1)


def contract_rows(left, right):
    return lax.dot_general(
        left, right, (((0,), (0,)), ((), ())), preferred_element_type=jnp.float32
    )


def times_transposed(left, right):
    return lax.dot_general(
        left, right, (((1,), (1,)), ((), ())), preferred_element_type=jnp.float32
    )


def masked_scores(query_pair, key_head, key_valid):
    scores = jnp.einsum(
        "trd,sd->rts", query_pair, key_head, preferred_element_type=jnp.float32
    ) * HEAD_DIM ** (-0.5)
    return jnp.where(key_valid[None], scores, -1e30)


def forward_head(operands, key_valid):
    query_pair, key_head, value_head = operands
    scores = masked_scores(query_pair, key_head, key_valid)
    top_score = jnp.max(scores, axis=-1, keepdims=True)
    log_total = top_score + jnp.log(jnp.sum(jnp.exp(scores - top_score), axis=-1, keepdims=True))
    probs = jnp.exp(scores - log_total).astype(jnp.bfloat16)
    mixed = jnp.einsum("rts,sd->trd", probs, value_head, preferred_element_type=jnp.float32)
    return (mixed, log_total[..., 0])


def backward_head(operands, key_valid):
    query_pair, key_head, value_head, grad_pair, log_total = operands
    scores = masked_scores(query_pair, key_head, key_valid)
    probs = jnp.exp(scores - log_total[..., None])
    grad_probs = jnp.einsum(
        "trd,sd->rts", grad_pair, value_head, preferred_element_type=jnp.float32
    )
    score_grad = (
        probs * (grad_probs - jnp.sum(probs * grad_probs, axis=-1, keepdims=True))
    ).astype(jnp.bfloat16)
    query_grad = jnp.einsum(
        "rts,sd->trd", score_grad, key_head, preferred_element_type=jnp.float32
    ) * HEAD_DIM ** (-0.5)
    key_grad = jnp.einsum(
        "rts,trd->sd", score_grad, query_pair, preferred_element_type=jnp.float32
    ) * HEAD_DIM ** (-0.5)
    value_grad = jnp.einsum(
        "rts,trd->sd", probs.astype(jnp.bfloat16), grad_pair, preferred_element_type=jnp.float32
    )
    return (query_grad, key_grad, value_grad)


RING = 4
ROWS = 256
EXTRA = 16
FULL = ROWS + EXTRA
GROUP = 4 * CAP
MESH = pl.DeviceIdType.MESH


def dot_nn(a, b):
    return jnp.dot(a, b, preferred_element_type=jnp.float32)


def dot_nt(a, b):
    return lax.dot_general(a, b, (((1,), (1,)), ((), ())), preferred_element_type=jnp.float32)


def dot_tn(a, b):
    return lax.dot_general(a, b, (((0,), (0,)), ((), ())), preferred_element_type=jnp.float32)


class Torus:
    def __init__(self):
        self.dp = lax.axis_index("dp")
        expert = lax.axis_index("expert")
        self.expert = expert
        self.z, self.y = expert // RING, expert % RING

    def block(self, dz, dy):
        return ((self.z + dz + RING) % RING) * RING + (self.y + dy + RING) % RING

    def near(self, axis, step):
        return (self.dp, self.block(step, 0) if axis == "z" else self.block(0, step))

    def along(self, axis, other, step):
        return self.block(step, other) if axis == "z" else self.block(other, step)

    def neighbours(self):
        return [self.near(axis, step) for axis in "yz" for step in (1, -1)]


class Gather:
    def __init__(self, torus, buffer, send, recv, number, axis, other, low, first, second, stride):
        self.torus, self.buffer, self.send, self.recv = torus, buffer, send, recv
        self.number, self.axis, self.other, self.stride = number, axis, other, stride
        self.whole, self.front, self.rear = (low, first + second), (low, first), (low + first, second)

    def copy(self, which, offset, part, step):
        at = self.torus.along(self.axis, self.other, offset) * self.stride + part[0]
        rows = self.buffer.at[pl.ds(pl.multiple_of(at, 16), part[1])]
        return pltpu.make_async_remote_copy(
            src_ref=rows,
            dst_ref=rows,
            send_sem=self.send.at[self.number, which],
            recv_sem=self.recv.at[self.number, which],
            device_id=self.torus.near(self.axis, step),
            device_id_type=MESH,
        )

    def first(self):
        self.copy(0, 0, self.whole, 1).start()
        self.copy(1, 0, self.whole, -1).start()

    def second(self):
        self.copy(0, -1, self.whole, 1).wait_recv()
        self.copy(2, -1, self.front, 1).start()
        self.copy(1, 1, self.whole, -1).wait_recv()
        self.copy(3, 1, self.rear, -1).start()

    def third(self):
        self.copy(2, 2, self.front, 1).wait_recv()
        self.copy(3, 2, self.rear, -1).wait_recv()

    def drain(self):
        self.copy(0, 0, self.whole, 1).wait_send()
        self.copy(1, 0, self.whole, -1).wait_send()
        self.copy(2, -1, self.front, 1).wait_send()
        self.copy(3, 1, self.rear, -1).wait_send()


class Scatter:
    def __init__(self, torus, sums, landing, send, recv, number, base, axis, other, low, first, second):
        self.torus, self.sums, self.landing, self.send, self.recv = torus, sums, landing, send, recv
        self.number, self.axis, self.other = number, axis, other
        self.low, self.parts = low, (first, second)
        self.size = first + second
        self.slots = (base, base + first, base + self.size, base + 2 * self.size)

    def rows(self, which):
        if which == 0:
            return self.low, self.parts[0]
        if which == 1:
            return self.low + self.parts[0], self.parts[1]
        return self.low, self.size

    def at(self, offset):
        return self.torus.along(self.axis, self.other, offset)

    def copy(self, which):
        start, size = self.rows(which)
        offset = (2, 2, 1, -1)[which]
        return pltpu.make_async_remote_copy(
            src_ref=self.sums.at[self.at(offset), pl.ds(start, size)],
            dst_ref=self.landing.at[pl.ds(self.slots[which], size)],
            send_sem=self.send.at[self.number, which],
            recv_sem=self.recv.at[self.number, which],
            device_id=self.torus.near(self.axis, (1, -1, 1, -1)[which]),
            device_id_type=MESH,
        )

    def add(self, which, offset):
        start, size = self.rows(which)
        block = self.at(offset)

        @pl.loop(0, size // 16)
        def _(k):
            here = pl.ds(pl.multiple_of(start + k * 16, 16), 16)
            there = pl.ds(pl.multiple_of(self.slots[which] + k * 16, 16), 16)
            total = self.sums[block, here].astype(jnp.float32) + self.landing[there].astype(jnp.float32)
            self.sums[block, here] = total.astype(jnp.bfloat16)

    def first(self):
        self.copy(0).start()
        self.copy(1).start()

    def second(self):
        self.copy(0).wait_recv()
        self.add(0, 1)
        self.copy(2).start()
        self.copy(1).wait_recv()
        self.add(1, -1)
        self.copy(3).start()

    def third(self, result=None):
        self.copy(2).wait_recv()
        self.copy(3).wait_recv()
        block = self.at(0)

        @pl.loop(0, self.size // 16)
        def _(k):
            here = pl.ds(pl.multiple_of(self.low + k * 16, 16), 16)
            left = pl.ds(pl.multiple_of(self.slots[2] + k * 16, 16), 16)
            right = pl.ds(pl.multiple_of(self.slots[3] + k * 16, 16), 16)
            total = (
                self.sums[block, here].astype(jnp.float32)
                + self.landing[left].astype(jnp.float32)
                + self.landing[right].astype(jnp.float32)
            )
            if result is None:
                self.sums[block, here] = total.astype(jnp.bfloat16)
            else:
                result[here] = total

    def drain(self):
        for which in range(4):
            self.copy(which).wait_send()


def moe_kernel(
    ffn, cot, wr, w_gate, w_up, w_down,
    ret, mixed, grad_gu, grad_d,
    rows, sums, wgu, wd, held, pair, inner, dgu, mixing, back, cotv, before, chosen, gate_rows, grad_rows, stage,
    ag_send, ag_recv, rs_send, rs_recv, w_sem, cot_sem, stage_sem, credit,
):
    torus = Torus()
    barrier = pltpu.get_barrier_semaphore()
    for device in torus.neighbours():
        pl.semaphore_signal(barrier, inc=1, device_id=device, device_id_type=MESH)

    weights = [
        pltpu.make_async_copy(w_gate, wgu.at[:, :, pl.ds(0, 512)], w_sem.at[0]),
        pltpu.make_async_copy(w_up, wgu.at[:, :, pl.ds(512, 512)], w_sem.at[1]),
        pltpu.make_async_copy(w_down, wd, w_sem.at[2]),
    ]
    for copy in weights:
        copy.start()

    def group_z(g):
        return (torus.z + g + (g // 2) * (1 - 2 * (g % 2))) % RING

    def cot_copy(g):
        return pltpu.make_async_copy(cot.at[pl.ds(pl.multiple_of(group_z(g) * RING * FULL, 16), RING * FULL)], cotv, cot_sem)

    cot_copy(0).start()
    rows[pl.ds(pl.multiple_of(torus.expert * ROWS, ROWS), ROWS)] = ffn[...]
    pl.semaphore_wait(barrier, 4)

    def gather(number, axis, other, low):
        return Gather(torus, rows, ag_send, ag_recv, number, axis, other, low, ROWS // 4, ROWS // 4, ROWS)

    a_first = gather(0, "y", 0, 0)
    b_first = gather(1, "z", 0, ROWS // 2)
    a_second = {d: gather(2 + d % RING, "z", d, 0) for d in (0, 1, -1, 2)}
    b_second = {d: gather(6 + d % RING, "y", d, ROWS // 2) for d in (0, 1, -1, 2)}
    gathers = [a_first, b_first, *a_second.values(), *b_second.values()]

    a_first.first()
    b_first.first()
    b_second[0].first()
    a_second[0].first()
    a_first.second()
    b_first.second()
    for d in (1, -1):
        b_second[d].first()
        a_second[d].first()
    a_first.third()
    b_first.third()
    b_second[2].first()
    a_second[2].first()
    for copy in weights:
        copy.wait()

    earlier = lax.broadcasted_iota(jnp.int32, (ROWS, ROWS), 0) < lax.broadcasted_iota(jnp.int32, (ROWS, ROWS), 1)
    before[...] = jnp.where(earlier, 1.0, 0.0).astype(jnp.bfloat16)
    slot_at = lax.broadcasted_iota(jnp.int32, (CAP, ROWS), 0).astype(jnp.float32)

    def stage_copy(slot, target):
        return pltpu.make_async_copy(stage.at[slot], target, stage_sem.at[slot])

    expert_rows = lax.broadcasted_iota(jnp.int32, (EXPERTS, ROWS), 0)

    @pl.loop(0, 4)
    def _(g):
        @pl.when(g == 0)
        def _():
            b_second[0].second()
            a_second[0].second()
            b_second[0].third()

        @pl.when(g == 1)
        def _():
            for d in (1, -1):
                b_second[d].second()
                a_second[d].second()
            a_second[2].second()
            b_second[1].third()

        @pl.when(g == 2)
        def _():
            b_second[2].second()
            b_second[-1].third()

        @pl.when(g == 3)
        def _():
            for d in (0, 1, -1, 2):
                a_second[d].third()
            b_second[2].third()

        cot_copy(g).wait()
        first_source = group_z(g) * RING

        @pl.loop(0, 4)
        def _(j):
            source = first_source + j
            block = rows[pl.ds(pl.multiple_of(source * ROWS, ROWS), ROWS)]
            laid = cotv[pl.ds(pl.multiple_of(j * FULL, 16), EXTRA)].astype(jnp.float32)
            member = jnp.concatenate([laid[:8, q * ROWS : (q + 1) * ROWS] for q in range(4)], axis=0)
            named = member > 0.5
            slots = dot_nn(member.astype(jnp.bfloat16), before[...])
            slots = jnp.where(named, slots, -1.0)
            logits = jnp.where(named, dot_nt(wr[...], block), -1e30)
            weight = jnp.where(named, jnp.exp(logits - jnp.max(logits, axis=0, keepdims=True)), 0.0)
            gates = weight / jnp.sum(weight, axis=0, keepdims=True)
            picked = []
            for e in range(2):
                own = jnp.sum(
                    jnp.where(expert_rows == torus.expert * 2 + e, slots, 0.0), axis=0, keepdims=True
                )
                picked.append(jnp.where(slot_at == own, 1.0, 0.0))
            both = jnp.concatenate(picked, axis=0).astype(jnp.bfloat16)
            chosen[j] = both
            took = dot_nn(both, block).astype(jnp.bfloat16)
            took_grad = dot_nn(both, cotv[pl.ds(pl.multiple_of(j * FULL + EXTRA, 16), ROWS)]).astype(jnp.bfloat16)
            here = pl.ds(pl.multiple_of(j * CAP, 16), CAP)
            there = pl.ds(pl.multiple_of(g * GROUP + j * CAP, 16), CAP)
            for e in range(2):
                own = jnp.sum(
                    jnp.where(expert_rows == torus.expert * 2 + e, gates, 0.0), axis=0, keepdims=True
                )
                of_rows = jnp.sum(picked[e] * own, axis=1, keepdims=True)
                gate_rows[e, here] = jnp.broadcast_to(of_rows, (CAP, 128))
                held[e, there] = took[e * CAP : (e + 1) * CAP]
                mixing[e, here] = took_grad[e * CAP : (e + 1) * CAP]

        @pl.when(g < 3)
        def _():
            cot_copy(g + 1).start()

        @pl.when(g == 3)
        def _():
            for one in gathers:
                one.drain()
            for device in torus.neighbours():
                pl.semaphore_signal(credit, inc=1, device_id=device, device_id_type=MESH)

        @pl.loop(0, 2)
        def _(e):
            there = pl.ds(pl.multiple_of(g * GROUP, 16), GROUP)
            both = dot_nn(held[e, there], wgu[e])
            gate, up = both[:, :512], both[:, 512:]
            sig = jax.nn.sigmoid(gate)
            silu = gate * sig
            act = (silu * up).astype(jnp.bfloat16)
            inner[e, there] = act
            out = dot_nn(act, wd[e]).astype(jnp.bfloat16).astype(jnp.float32)
            grad = mixing[e].astype(jnp.float32)
            weight = gate_rows[e][:, :1]
            grad_rows[e] = jnp.broadcast_to(jnp.sum(grad * out, axis=1, keepdims=True), (GROUP, 128))
            pair[e, there] = (weight * grad).astype(jnp.bfloat16)
            mixing[e] = (weight * out).astype(jnp.bfloat16)
            inner_grad = dot_nt(pair[e, there], wd[e])
            dgu[e, there, :512] = (inner_grad * up * sig * (1.0 + gate * (1.0 - sig))).astype(jnp.bfloat16)
            dgu[e, there, 512:] = (inner_grad * silu).astype(jnp.bfloat16)
            back[e] = dot_nt(dgu[e, there], wgu[e]).astype(jnp.bfloat16)

        @pl.loop(0, 4)
        def _(j):
            source = first_source + j
            both = chosen[j]
            picked = both.astype(jnp.float32)
            here = pl.ds(pl.multiple_of(j * CAP, 16), CAP)
            part = dot_tn(both, jnp.concatenate([back[0, here], back[1, here]], axis=0))
            sums[source, pl.ds(EXTRA, ROWS)] = part.astype(jnp.bfloat16)
            grads = jnp.zeros((EXPERTS, ROWS), jnp.float32)
            for e in range(2):
                own = jnp.sum(
                    picked[e * CAP : (e + 1) * CAP] * grad_rows[e, here][:, :1], axis=0, keepdims=True
                )
                grads = grads + jnp.where(expert_rows == torus.expert * 2 + e, own, 0.0)
            laid = jnp.concatenate([grads[8 * q : 8 * q + 8] for q in range(4)], axis=1)
            sums[source, pl.ds(0, EXTRA)] = jnp.concatenate([laid, jnp.zeros_like(laid)], axis=0).astype(
                jnp.bfloat16
            )
            slot = j % 2

            @pl.when((g > 0) | (j > 1))
            def _():
                stage_copy(slot, mixed.at[source]).wait()

            result = dot_tn(both, jnp.concatenate([mixing[0, here], mixing[1, here]], axis=0))
            stage[slot] = result.astype(jnp.bfloat16)
            stage_copy(slot, mixed.at[source]).start()

    pl.semaphore_wait(credit, 4)

    order = (2, 1, -1, 0)
    a_lead = {}
    b_lead = {}
    for n, d in enumerate(order):
        a_lead[d] = Scatter(
            torus, sums, rows, rs_send, rs_recv, n, n * 384, "z", d, 0, 64, 64
        )
        b_lead[d] = Scatter(
            torus, sums, rows, rs_send, rs_recv, 4 + n, 1920 + n * 432, "y", d, 128, 80, 64
        )
    a_last = Scatter(torus, sums, rows, rs_send, rs_recv, 8, 4 * 384, "y", 0, 0, 64, 64)
    b_last = Scatter(torus, sums, rows, rs_send, rs_recv, 9, 1920 + 4 * 432, "z", 0, 128, 80, 64)

    def write_grads(low, high):
        @pl.loop(low, high)
        def _(k):
            slot = k % 2
            e, c = k // 6, k % 6
            stage_copy(slot, grad_d.at[0, pl.ds(0, 256)]).wait()

            @pl.when(c < 4)
            def _():
                columns = pl.ds(pl.multiple_of(c * 256, 256), 256)
                stage[slot] = dot_tn(held[e, :, columns], dgu[e]).astype(jnp.bfloat16)
                stage_copy(slot, grad_gu.at[e, columns]).start()

            @pl.when(c >= 4)
            def _():
                columns = pl.ds(pl.multiple_of((c - 4) * 256, 256), 256)
                stage[slot] = dot_tn(inner[e, :, columns], pair[e]).astype(jnp.bfloat16)
                stage_copy(slot, grad_d.at[e, columns]).start()

    for d in order:
        b_lead[d].first()
        a_lead[d].first()
    write_grads(0, 4)
    for d in order:
        b_lead[d].second()
        a_lead[d].second()
    write_grads(4, 12)
    for slot in range(2):
        stage_copy(slot, grad_d.at[0, pl.ds(0, 256)]).wait()
    for d in order:
        b_lead[d].third()
        a_lead[d].third()
        if d == 2:
            b_last.first()
            a_last.first()
    b_last.second()
    a_last.second()
    b_last.third(ret)
    a_last.third(ret)
    for one in [*a_lead.values(), *b_lead.values(), a_last, b_last]:
        one.drain()


def moe(ffn_in, cot_all, router_rows, w_gate, w_up, w_down):
    vmem, hbm = pl.BlockSpec(memory_space=pltpu.VMEM), pl.BlockSpec(memory_space=pl.ANY)
    low, total = jnp.bfloat16, 4 * GROUP
    return pl.pallas_call(
        moe_kernel,
        name="moe",
        out_shape=(
            jax.ShapeDtypeStruct((FULL, 1024), jnp.float32),
            jax.ShapeDtypeStruct((16, ROWS, 1024), low),
            jax.ShapeDtypeStruct((2, 1024, 1024), low),
            jax.ShapeDtypeStruct((2, 512, 1024), low),
        ),
        in_specs=[vmem, hbm, vmem, hbm, hbm, hbm],
        out_specs=(vmem, hbm, hbm, hbm),
        scratch_shapes=[
            pltpu.VMEM((16 * ROWS, 1024), low),
            pltpu.VMEM((16, FULL, 1024), low),
            pltpu.VMEM((2, 1024, 1024), low),
            pltpu.VMEM((2, 512, 1024), low),
            pltpu.VMEM((2, total, 1024), low),
            pltpu.VMEM((2, total, 1024), low),
            pltpu.VMEM((2, total, 512), low),
            pltpu.VMEM((2, total, 1024), low),
            pltpu.VMEM((2, GROUP, 1024), low),
            pltpu.VMEM((2, GROUP, 1024), low),
            pltpu.VMEM((4 * FULL, 1024), low),
            pltpu.VMEM((ROWS, ROWS), low),
            pltpu.VMEM((4, 2 * CAP, ROWS), low),
            pltpu.VMEM((2, GROUP, 128), jnp.float32),
            pltpu.VMEM((2, GROUP, 128), jnp.float32),
            pltpu.VMEM((2, ROWS, 1024), low),
            pltpu.SemaphoreType.DMA((10, 4)),
            pltpu.SemaphoreType.DMA((10, 4)),
            pltpu.SemaphoreType.DMA((10, 4)),
            pltpu.SemaphoreType.DMA((10, 4)),
            pltpu.SemaphoreType.DMA((3,)),
            pltpu.SemaphoreType.DMA,
            pltpu.SemaphoreType.DMA((2,)),
            pltpu.SemaphoreType.REGULAR,
        ],
        compiler_params=pltpu.CompilerParams(
            collective_id=1, has_side_effects=True, vmem_limit_bytes=63 * 2**20
        ),
        cost_estimate=pl.CostEstimate(flops=50 * 10**9, bytes_accessed=40 * 10**6, transcendentals=2 * 10**6),
    )(ffn_in, cot_all, router_rows, w_gate, w_up, w_down)


def everywhere():
    dp, expert = lax.axis_index("dp"), lax.axis_index("expert")
    here = {"x": dp // 2, "core": dp % 2, "z": expert // RING, "y": expert % RING}

    def device(axis, step):
        there = dict(here)
        size = 2 if axis == "core" else RING
        there[axis] = (here[axis] + step + size) % size
        return (there["x"] * 2 + there["core"], there["z"] * RING + there["y"])

    return here, device


def rms_scale(values):
    return lax.rsqrt(jnp.mean(values * values, axis=-1, keepdims=True) + epsilon)


def turned_rows(values, cosine, sine):
    front, back = values[: HEAD_DIM // 2], values[HEAD_DIM // 2 :]
    return jnp.concatenate([front * cosine - back * sine, back * cosine + front * sine], axis=0)


def kv_order(here, step):
    turn = step // 2
    return (turn % 2) * (3 - turn // 2) + (1 - turn % 2) * (turn // 2)


class Keys:
    def __init__(self, here, device, blocks, send, recv):
        self.here, self.device, self.blocks, self.send, self.recv = here, device, blocks, send, recv
        self.lines = blocks.shape[1]

    def copy(self, which):
        half = self.lines // 2
        offset, start, size, axis, step = (
            (0, 0, self.lines, "core", 1),
            (0, 0, self.lines, "x", 1),
            (0, 0, self.lines, "x", -1),
            (-1, 0, half, "x", 1),
            (1, half, half, "x", -1),
            (-1, 0, self.lines, "core", 1),
            (1, 0, self.lines, "core", 1),
            (2, 0, self.lines, "core", 1),
        )[which]
        block = (self.here["x"] + offset + RING) % RING * 2 + self.here["core"]
        part = self.blocks.at[block, pl.ds(start, size)]
        return pltpu.make_async_remote_copy(
            src_ref=part,
            dst_ref=part,
            send_sem=self.send.at[which],
            recv_sem=self.recv.at[which],
            device_id=self.device(axis, step),
            device_id_type=MESH,
        )

    def start(self, *which):
        for one in which:
            self.copy(one).start()

    def arrive(self, *which):
        for one in which:
            self.copy(one).wait_recv()

    def drain(self):
        for one in range(8):
            self.copy(one).wait_send()


def forward_kernel(
    tokens, cot, routes_t, length, cosine, sine, attn_gain, query_gain, key_gain, ffn_gain,
    w_query, w_key, w_value, w_output,
    ffn_in, hidden, mixed_t, queries, log_total, normed, query_raw, key_raw, kv_all, cot_all,
    wq, wk, wv, wo, kv, turned, most, total, mixed, packed,
    ag_send, ag_recv, kv_send, kv_recv, w_sem, kv_sem, own_sem,
):
    torus = Torus()
    here, device = everywhere()
    me = here["x"] * 2 + here["core"]
    barrier = pltpu.get_barrier_semaphore()
    peers = [*torus.neighbours(), device("core", 1), device("x", 1), device("x", -1)]
    for peer in peers:
        pl.semaphore_signal(barrier, inc=1, device_id=peer, device_id_type=MESH)
    loads = [
        pltpu.make_async_copy(source, target, w_sem.at[n])
        for n, (source, target) in enumerate(((w_query, wq), (w_key, wk), (w_value, wv), (w_output, wo)))
    ]
    for load in loads:
        load.start()

    expert_rows = lax.broadcasted_iota(jnp.int32, (EXPERTS, ROWS), 0)
    member = jnp.zeros((EXPERTS, ROWS), jnp.float32)
    for k in range(TOPK):
        member = member + jnp.where(expert_rows == routes_t[pl.ds(k, 1), :], 1.0, 0.0)
    laid = jnp.concatenate([member[8 * q : 8 * q + 8] for q in range(4)], axis=1)
    packed[...] = jnp.concatenate([laid, jnp.zeros_like(laid)], axis=0).astype(jnp.bfloat16)
    first_row = pl.multiple_of(torus.expert * FULL, 16)
    owns = [
        pltpu.make_async_copy(packed, cot_all.at[pl.ds(first_row, EXTRA)], own_sem.at[0]),
        pltpu.make_async_copy(cot, cot_all.at[pl.ds(pl.multiple_of(first_row + EXTRA, 16), ROWS)], own_sem.at[1]),
    ]
    for copy in owns:
        copy.start()
    for copy in owns:
        copy.wait()
    pl.semaphore_wait(barrier, len(peers))

    def gather(number, axis, other, low, first, second):
        return Gather(torus, cot_all, ag_send, ag_recv, number, axis, other, low, first, second, FULL)

    a_first = gather(0, "y", 0, 0, 64, 64)
    b_first = gather(1, "z", 0, 128, 80, 64)
    a_second = {d: gather(2 + d % RING, "z", d, 0, 64, 64) for d in (0, 1, -1, 2)}
    b_second = {d: gather(6 + d % RING, "y", d, 128, 80, 64) for d in (0, 1, -1, 2)}
    gathers = [a_first, b_first, *a_second.values(), *b_second.values()]
    a_first.first()
    b_first.first()
    b_second[0].first()
    a_second[0].first()

    @pl.loop(0, 4)
    def _(n):
        at = pl.ds(pl.multiple_of(n * 64, 64), 64)
        rows = tokens[at].astype(jnp.float32)
        normed[at] = (rows * rms_scale(rows) * attn_gain[...].astype(jnp.float32)).astype(jnp.bfloat16)

    for load in loads:
        load.wait()

    keys = Keys(here, device, kv, kv_send, kv_recv)
    key_raw[...] = dot_nn(normed[...], wk[...])
    scaled = key_raw[...]
    scaled = (scaled * rms_scale(scaled) * key_gain[...].astype(jnp.float32)).T
    for j in range(KV_HEADS):
        head = turned_rows(scaled[j * 64 : j * 64 + 64], cosine[...], sine[...])
        kv[me, pl.ds(j * 64, 64)] = head.astype(jnp.bfloat16)
    kv[me, pl.ds(512, 512)] = dot_nn(normed[...], wv[...]).T.astype(jnp.bfloat16)
    keys.start(0, 1, 2)
    query_raw[...] = dot_nn(normed[...], wq[...])
    scaled = query_raw[...]
    turned[...] = (scaled * rms_scale(scaled) * query_gain[...].astype(jnp.float32)).T

    @pl.loop(0, KV_HEADS)
    def _(j):
        for r in range(2):
            head = turned[pl.ds(pl.multiple_of(j * 128 + r * 64, 64), 64)]
            head = turned_rows(head, cosine[...], sine[...])
            queries[j, :, r * ROWS : (r + 1) * ROWS] = (head * HEAD_DIM**-0.5).astype(jnp.bfloat16)

    a_first.second()
    b_first.second()
    for d in (1, -1):
        b_second[d].first()
        a_second[d].first()

    key_at = lax.broadcasted_iota(jnp.int32, (ROWS, 2 * ROWS), 0)
    query_at = lax.broadcasted_iota(jnp.int32, (ROWS, 2 * ROWS), 1) % ROWS
    valid = (key_at <= query_at) & (key_at + me * ROWS < length[...])

    @pl.loop(0, KV_HEADS)
    def _(j):
        key_head = kv[me, pl.ds(pl.multiple_of(j * 64, 64), 64)]
        value_head = kv[me, pl.ds(pl.multiple_of(512 + j * 64, 64), 64)]
        scores = jnp.where(valid, dot_tn(key_head, queries[j]), -1e30)
        top = jnp.max(scores, axis=0, keepdims=True)
        probs = jnp.exp(scores - top)
        most[j] = top
        total[j] = jnp.sum(probs, axis=0, keepdims=True)
        mixed[j] = dot_nn(value_head, probs.astype(jnp.bfloat16))

    @pl.loop(1, 8)
    def _(step):
        @pl.when(step == 1)
        def _():
            a_first.third()
            b_first.third()
            b_second[2].first()
            a_second[2].first()
            keys.arrive(0)

        @pl.when(step == 2)
        def _():
            keys.arrive(1)
            keys.start(3, 5)
            keys.arrive(2)
            keys.start(4, 6)
            b_second[0].second()
            a_second[0].second()

        @pl.when(step == 3)
        def _():
            keys.arrive(5)
            for d in (1, -1):
                b_second[d].second()
                a_second[d].second()

        @pl.when(step == 5)
        def _():
            keys.arrive(3, 4)
            keys.start(7)
            keys.arrive(6)
            b_second[2].second()
            a_second[2].second()

        @pl.when(step == 7)
        def _():
            keys.arrive(7)

        block = (here["x"] + kv_order(here, step) + RING) % RING * 2 + (here["core"] + step) % 2

        @pl.when(block < me)
        def _():
            @pl.loop(0, KV_HEADS)
            def _(j):
                key_head = kv[block, pl.ds(pl.multiple_of(j * 64, 64), 64)]
                value_head = kv[block, pl.ds(pl.multiple_of(512 + j * 64, 64), 64)]
                scores = dot_tn(key_head, queries[j])
                before = most[j]
                top = jnp.maximum(before, jnp.max(scores, axis=0, keepdims=True))
                probs = jnp.exp(scores - top)
                less = jnp.exp(before - top)
                most[j] = top
                total[j] = total[j] * less + jnp.sum(probs, axis=0, keepdims=True)
                mixed[j] = mixed[j] * less + dot_nn(value_head, probs.astype(jnp.bfloat16))

    save = pltpu.make_async_copy(kv, kv_all, kv_sem)
    save.start()

    @pl.loop(0, KV_HEADS)
    def _(j):
        share = total[j]
        log_total[j] = most[j] + jnp.log(share)
        head = (mixed[j] / share).astype(jnp.bfloat16)
        for r in range(2):
            mixed_t[pl.ds(pl.multiple_of(j * 128 + r * 64, 64), 64), :] = head[:, r * ROWS : (r + 1) * ROWS]

    hidden[...] = dot_tn(mixed_t[...], wo[...])

    @pl.loop(0, 4)
    def _(n):
        at = pl.ds(pl.multiple_of(n * 64, 64), 64)
        rows = hidden[at] + tokens[at].astype(jnp.float32)
        hidden[at] = rows
        ffn_in[at] = (rows * rms_scale(rows) * ffn_gain[...].astype(jnp.float32)).astype(jnp.bfloat16)

    for d in (0, 1, -1, 2):
        a_second[d].third()
        b_second[d].third()
    save.wait()
    keys.drain()
    for one in gathers:
        one.drain()


def forward(tokens, cot, routes_t, length, cosine, sine, gains, weights):
    vmem, hbm = pl.BlockSpec(memory_space=pltpu.VMEM), pl.BlockSpec(memory_space=pl.ANY)
    low, wide = jnp.bfloat16, jnp.float32
    shape = jax.ShapeDtypeStruct
    return pl.pallas_call(
        forward_kernel,
        name="forward",
        out_shape=(
            shape((ROWS, 1024), low),
            shape((ROWS, 1024), wide),
            shape((1024, ROWS), low),
            shape((KV_HEADS, HEAD_DIM, 2 * ROWS), low),
            shape((KV_HEADS, 1, 2 * ROWS), wide),
            shape((ROWS, 1024), low),
            shape((ROWS, 1024), wide),
            shape((ROWS, 512), wide),
            shape((8, 1024, ROWS), low),
            shape((16 * FULL, 1024), low),
        ),
        in_specs=[vmem] * 10 + [hbm] * 4,
        out_specs=(vmem,) * 8 + (hbm, hbm),
        scratch_shapes=[
            pltpu.VMEM((1024, 1024), low),
            pltpu.VMEM((1024, 512), low),
            pltpu.VMEM((1024, 512), low),
            pltpu.VMEM((1024, 1024), low),
            pltpu.VMEM((8, 1024, ROWS), low),
            pltpu.VMEM((1024, ROWS), wide),
            pltpu.VMEM((KV_HEADS, 1, 2 * ROWS), wide),
            pltpu.VMEM((KV_HEADS, 1, 2 * ROWS), wide),
            pltpu.VMEM((KV_HEADS, HEAD_DIM, 2 * ROWS), wide),
            pltpu.VMEM((EXTRA, 1024), low),
            pltpu.SemaphoreType.DMA((10, 4)),
            pltpu.SemaphoreType.DMA((10, 4)),
            pltpu.SemaphoreType.DMA((8,)),
            pltpu.SemaphoreType.DMA((8,)),
            pltpu.SemaphoreType.DMA((4,)),
            pltpu.SemaphoreType.DMA,
            pltpu.SemaphoreType.DMA((2,)),
        ],
        compiler_params=pltpu.CompilerParams(
            collective_id=3, has_side_effects=True, vmem_limit_bytes=56 * 2**20
        ),
    )(tokens, cot, routes_t, length, cosine, sine, *gains, *weights)


ORDERS = (("x", "y", "z"), ("y", "z", "x"), ("z", "x", "y"))


class Total:
    def __init__(self, here, device, buffer, final, landing, work, send, recv, number, half, start, rows, base, order):
        self.here, self.device, self.buffer, self.final = here, device, buffer, final
        self.landing, self.work = landing, work
        self.send, self.recv, self.number, self.order = send, recv, number, order
        self.half, self.start, self.rows, self.base = half, start, rows, base

    def own(self):
        return self.here["core"] * self.half + self.start

    def copy(self, which, source, target, axis, step):
        return pltpu.make_async_remote_copy(
            src_ref=source,
            dst_ref=target,
            send_sem=self.send.at[self.number, which],
            recv_sem=self.recv.at[self.number, which],
            device_id=self.device(axis, step),
            device_id_type=MESH,
        )

    def part(self, ref, at, size):
        return ref.at[pl.ds(pl.multiple_of(at, 16), size)]

    def copies(self, stage):
        r, own = self.rows, self.own()
        a, b, c = self.order
        ia, ib = self.here[a], self.here[b]
        second = own + ia * (r // 4)
        third = second + ib * (r // 16)
        land1, land2, land3 = self.base + r, self.base + r + 3 * (r // 4), self.base + r + 3 * (r // 4) + 3 * (r // 16)
        if stage == 0:
            there = (1 - self.here["core"]) * self.half + self.start
            return [self.copy(0, self.part(self.buffer, there, r), self.part(self.landing, self.base, r), "core", 1)]
        if stage == 6:
            whole = self.part(self.final, own, r)
            return [self.copy(16, whole, whole, "core", 1)]
        found = []
        for d in (1, 2, 3):
            if stage == 1:
                source = self.part(self.buffer, own + (ia + d) % RING * (r // 4), r // 4)
                target, axis = self.part(self.landing, land1 + (d - 1) * (r // 4), r // 4), a
            elif stage == 2:
                source = self.part(self.buffer, second + (ib + d) % RING * (r // 16), r // 16)
                target, axis = self.part(self.landing, land2 + (d - 1) * (r // 16), r // 16), b
            elif stage == 3:
                source = self.work.at[self.number, pl.ds(0, r // 16)]
                target, axis = self.part(self.landing, land3 + (d - 1) * (r // 16), r // 16), c
            elif stage == 4:
                source = self.part(self.final, third, r // 16)
                target, axis = source, b
            else:
                source = self.part(self.final, second, r // 4)
                target, axis = source, a
            found.append(self.copy(1 + (stage - 1) * 3 + d - 1, source, target, axis, d))
        return found

    def begin(self, stage):
        for copy in self.copies(stage):
            copy.start()

    def add(self, target, start, size, lands):
        @pl.loop(0, size // 16)
        def _(k):
            here = pl.ds(pl.multiple_of(start + k * 16, 16), 16)
            total = self.buffer[here].astype(jnp.float32)
            for land in lands:
                total = total + self.landing[pl.ds(pl.multiple_of(land + k * 16, 16), 16)].astype(jnp.float32)
            if target is None:
                self.buffer[here] = total.astype(jnp.bfloat16)
            else:
                target[pl.ds(pl.multiple_of(k * 16, 16), 16)] = total.astype(jnp.bfloat16)

    def finish(self, stage):
        for copy in self.copies(stage):
            copy.wait_recv()
        r, own = self.rows, self.own()
        a, b, _ = self.order
        second = own + self.here[a] * (r // 4)
        third = second + self.here[b] * (r // 16)
        land1, land2, land3 = self.base + r, self.base + r + 3 * (r // 4), self.base + r + 3 * (r // 4) + 3 * (r // 16)
        if stage == 0:
            self.add(None, own, r, [self.base])
        elif stage == 1:
            self.add(None, second, r // 4, [land1 + d * (r // 4) for d in range(3)])
        elif stage == 2:
            self.add(self.work.at[self.number], third, r // 16, [land2 + d * (r // 16) for d in range(3)])
        elif stage == 3:
            r16 = r // 16

            @pl.loop(0, r16 // 16)
            def _(k):
                total = self.work[self.number, pl.ds(pl.multiple_of(k * 16, 16), 16)].astype(jnp.float32)
                for d in range(3):
                    at = land3 + d * r16 + k * 16
                    total = total + self.landing[pl.ds(pl.multiple_of(at, 16), 16)].astype(jnp.float32)
                self.final[pl.ds(pl.multiple_of(third + k * 16, 16), 16)] = total.astype(jnp.bfloat16)

    def drain(self):
        for stage in range(7):
            for copy in self.copies(stage):
                copy.wait_send()


class Small:
    STAGES = (("core", (1,)), ("x", (1, 2, 3)), ("y", (1, 2, 3)), ("z", (1, 2, 3)))

    def __init__(self, device, value, landing, send, recv):
        self.device, self.value, self.landing, self.send, self.recv = device, value, landing, send, recv

    def copies(self, stage):
        axis, steps = self.STAGES[stage]
        first = sum(len(s) for _, s in self.STAGES[:stage])
        return [
            pltpu.make_async_remote_copy(
                src_ref=self.value.at[stage],
                dst_ref=self.landing.at[first + n],
                send_sem=self.send.at[first + n],
                recv_sem=self.recv.at[first + n],
                device_id=self.device(axis, step),
                device_id_type=MESH,
            )
            for n, step in enumerate(steps)
        ]

    def begin(self, stage):
        for copy in self.copies(stage):
            copy.start()

    def finish(self, stage):
        for copy in self.copies(stage):
            copy.wait_recv()
        first = sum(len(s) for _, s in self.STAGES[:stage])
        total = self.value[stage]
        for n in range(len(self.STAGES[stage][1])):
            total = total + self.landing[first + n]
        self.value[stage + 1] = total

    def drain(self):
        for stage in range(4):
            for copy in self.copies(stage):
                copy.wait_send()


def total_kernel(parts, small, whole, small_whole, held, landing, work, values, small_landing, send, recv, small_send, small_recv, load_sem):
    here, device = everywhere()
    barrier = pltpu.get_barrier_semaphore()
    peers = [device("core", 1)] + [device(axis, d) for axis in "xyz" for d in (1, 2, 3)]
    for peer in peers:
        pl.semaphore_signal(barrier, inc=1, device_id=peer, device_id_type=MESH)
    load = pltpu.make_async_copy(parts, held, load_sem)
    load.start()
    values[0] = small[...]
    load.wait()
    pl.semaphore_wait(barrier, len(peers))
    half = whole.shape[0] // 2
    rows = half // 3
    room = rows + 3 * (rows // 4) + 6 * (rows // 16)
    streams = [
        Total(here, device, held, whole, landing, work, send, recv, s, half, s * rows, rows, s * room, ORDERS[s])
        for s in range(3)
    ]
    few = Small(device, values, small_landing, small_send, small_recv)
    for one in streams:
        one.begin(0)
    few.begin(0)
    for stage in range(7):
        for one in streams:
            one.finish(stage)
            if stage < 6:
                one.begin(stage + 1)
        if stage < 4:
            few.finish(stage)
            if stage < 3:
                few.begin(stage + 1)
    small_whole[...] = values[4]
    for one in streams:
        one.drain()
    few.drain()


def total_everywhere(parts, small):
    vmem, hbm = pl.BlockSpec(memory_space=pltpu.VMEM), pl.BlockSpec(memory_space=pl.ANY)
    low = jnp.bfloat16
    rows, width = parts.shape
    third = rows // 6
    room = third + 3 * (third // 4) + 6 * (third // 16)
    return pl.pallas_call(
        total_kernel,
        name="total",
        out_shape=(
            jax.ShapeDtypeStruct(parts.shape, low),
            jax.ShapeDtypeStruct(small.shape, jnp.float32),
        ),
        in_specs=[hbm, vmem],
        out_specs=(vmem, vmem),
        scratch_shapes=[
            pltpu.VMEM((rows, width), low),
            pltpu.VMEM((3 * room, width), low),
            pltpu.VMEM((3, third // 16, width), low),
            pltpu.VMEM((5, *small.shape), jnp.float32),
            pltpu.VMEM((10, *small.shape), jnp.float32),
            pltpu.SemaphoreType.DMA((3, 17)),
            pltpu.SemaphoreType.DMA((3, 17)),
            pltpu.SemaphoreType.DMA((10,)),
            pltpu.SemaphoreType.DMA((10,)),
            pltpu.SemaphoreType.DMA,
        ],
        compiler_params=pltpu.CompilerParams(
            collective_id=2, has_side_effects=True, vmem_limit_bytes=56 * 2**20
        ),
    )(parts, small)


def body(
    tokens,
    cotangent,
    lengths,
    routes,
    attn_gain,
    w_query,
    w_key,
    w_value,
    query_gain,
    key_gain,
    w_output,
    ffn_gain,
    w_router,
    w_gate,
    w_up,
    w_down,
):
    token_rows = tokens[0].astype(jnp.float32)
    tok_count = token_rows.shape[0]
    width = token_rows.shape[1]
    kv_width = w_key.shape[1]
    seq_total = tok_count * lax.axis_size("dp")
    query_pos = lax.axis_index("dp") * tok_count + jnp.arange(tok_count, dtype=jnp.int32)
    key_pos = jnp.arange(seq_total, dtype=jnp.int32)
    key_valid = (key_pos[None, :] <= query_pos[:, None]) & (key_pos[None, :] < lengths[0])
    cosine, sine_table = rope_tables(query_pos)
    ffn_in, hidden_res, mixed_t, queries_t, log_totals, normed, query_raw, key_raw, kv_all, cot_all = forward(
        tokens[0],
        cotangent[0],
        routes[0].T,
        lengths.reshape(1, 1),
        cosine.T,
        sine_table.T,
        [gain.reshape(1, -1) for gain in (attn_gain, query_gain, key_gain, ffn_gain)],
        (w_query, w_key, w_value, w_output),
    )
    _, attn_pull = jax.vjp(norm_rows, token_rows, attn_gain.astype(jnp.float32))

    def post_norm(query_in, key_in, gain_query, gain_key):
        return (
            rotate(norm_rows(query_in, gain_query), cosine, sine_table),
            rotate(norm_rows(key_in, gain_key), cosine, sine_table),
        )

    _, post_pull = jax.vjp(
        post_norm, query_raw, key_raw, query_gain.astype(jnp.float32), key_gain.astype(jnp.float32)
    )
    query_groups = queries_t.reshape(KV_HEADS, HEAD_DIM, 2, tok_count).transpose(0, 3, 2, 1) * 8
    key_groups = kv_all[:, :512].reshape(8, KV_HEADS, HEAD_DIM, ROWS).transpose(1, 0, 3, 2).reshape(KV_HEADS, seq_total, HEAD_DIM)
    value_groups = kv_all[:, 512:].reshape(8, KV_HEADS, HEAD_DIM, ROWS).transpose(1, 0, 3, 2).reshape(KV_HEADS, seq_total, HEAD_DIM)
    log_totals = log_totals.reshape(KV_HEADS, 2, tok_count)
    attended = mixed_t.T
    _, ffn_pull = jax.vjp(norm_rows, hidden_res, ffn_gain.astype(jnp.float32))
    logits = jnp.dot(ffn_in, w_router, preferred_element_type=jnp.float32)
    own_routes = (routes[0][:, :, None] == jnp.arange(EXPERTS, dtype=jnp.int32)).any(axis=1)
    gates = jax.nn.softmax(jnp.where(own_routes, logits, -1e30), axis=-1)
    gates = jnp.where(own_routes, gates, 0.0)
    returned, mixed_parts, gate_up_w_grad, down_grad = moe(
        ffn_in, cot_all, w_router.T, w_gate, w_up, w_down
    )
    mixed_sum = lax.psum_scatter(
        mixed_parts.reshape(16 * ROWS, width), "expert", scatter_dimension=0, tiled=True
    )
    mixed_out = (hidden_res + mixed_sum.astype(jnp.float32)).astype(jnp.bfloat16)
    grad_out = cotangent[0].astype(jnp.float32)
    gate_grad = returned[:8].reshape(8, 4, ROWS).transpose(1, 0, 2).reshape(EXPERTS, ROWS).T
    pair_sum = returned[EXTRA:]
    logit_grad = (
        gates * (gate_grad - jnp.sum(gates * gate_grad, axis=-1, keepdims=True))
    ).astype(jnp.bfloat16)
    router_grad = contract_rows(ffn_in, logit_grad)
    ffn_in_grad = times_transposed(logit_grad, w_router) + pair_sum
    res_part, ffn_gain_grad = ffn_pull(ffn_in_grad)
    hidden_grad = grad_out + res_part
    branch_grad = hidden_grad.astype(jnp.bfloat16)
    output_w_grad = contract_rows(attended, branch_grad)
    attended_grad = times_transposed(branch_grad, w_output).astype(jnp.bfloat16)
    grad_groups = attended_grad.reshape(tok_count, KV_HEADS, HEADS // KV_HEADS, HEAD_DIM).transpose(
        1, 0, 2, 3
    )
    query_grad_heads, key_grad_heads, value_grad_heads = lax.map(
        lambda operands: backward_head(operands, key_valid),
        (query_groups, key_groups, value_groups, grad_groups, log_totals),
    )
    query_grad = query_grad_heads.transpose(1, 0, 2, 3).reshape(tok_count, width)
    key_grad_full = key_grad_heads.transpose(1, 0, 2).reshape(seq_total, kv_width)
    value_grad_full = value_grad_heads.transpose(1, 0, 2).reshape(seq_total, kv_width)
    key_grad, value_grad = tuple(
        (
            part.astype(jnp.float32)
            for part in sent_together(
                (key_grad_full.astype(jnp.bfloat16), value_grad_full.astype(jnp.bfloat16)),
                "dp",
                0,
                1,
            )
        )
    )
    query_raw_grad, key_raw_grad, query_gain_grad, key_gain_grad = post_pull((query_grad, key_grad))
    query_raw_low = query_raw_grad.astype(jnp.bfloat16)
    key_raw_low = key_raw_grad.astype(jnp.bfloat16)
    value_raw_low = value_grad.astype(jnp.bfloat16)
    query_w_grad = contract_rows(normed, query_raw_low)
    key_w_grad = contract_rows(normed, key_raw_low)
    value_w_grad = contract_rows(normed, value_raw_low)
    normed_grad = (
        times_transposed(query_raw_low, w_query)
        + times_transposed(key_raw_low, w_key)
        + times_transposed(value_raw_low, w_value)
    )
    token_part, attn_gain_grad = attn_pull(normed_grad)
    token_grad = (hidden_grad + token_part).astype(jnp.bfloat16)
    weight_parts = [
        query_w_grad[:, :512],
        query_w_grad[:, 512:],
        key_w_grad,
        value_w_grad,
        output_w_grad[:, :512],
        output_w_grad[:, 512:],
    ]
    small_parts = [
        router_grad.reshape(32, 1024),
        attn_gain_grad.reshape(1, 1024),
        query_gain_grad.reshape(1, 1024),
        jnp.pad(key_gain_grad, (0, 512)).reshape(1, 1024),
        ffn_gain_grad.reshape(1, 1024),
        jnp.zeros((4, 1024), jnp.float32),
    ]
    weight_sums, small_sums = total_everywhere(
        jnp.concatenate([part.astype(jnp.bfloat16) for part in weight_parts], axis=0),
        jnp.concatenate(small_parts, axis=0),
    )
    weight_sums = weight_sums.astype(jnp.float32)
    query_w_sum = jnp.concatenate([weight_sums[:1024], weight_sums[1024:2048]], axis=1)
    key_w_sum, value_w_sum = weight_sums[2048:3072], weight_sums[3072:4096]
    output_w_sum = jnp.concatenate([weight_sums[4096:5120], weight_sums[5120:]], axis=1)
    router_sum = small_sums[:32].reshape(1024, 32)
    attn_gain_sum, query_gain_sum, ffn_gain_sum = small_sums[32], small_sums[33], small_sums[35]
    key_gain_sum = small_sums[34, :512]
    gate_up_sum, down_w_sum = lax.psum((gate_up_w_grad, down_grad), "dp")
    gate_w_sum = gate_up_sum[:, :, :512].astype(jnp.float32)
    up_w_sum = gate_up_sum[:, :, 512:].astype(jnp.float32)
    down_w_sum = down_w_sum.astype(jnp.float32)
    return (
        mixed_out[None],
        token_grad[None],
        attn_gain_sum,
        query_w_sum,
        key_w_sum,
        value_w_sum,
        query_gain_sum,
        key_gain_sum,
        output_w_sum,
        ffn_gain_sum,
        router_sum,
        gate_w_sum,
        up_w_sum,
        down_w_sum,
    )


def solution(mesh):
    return jax.shard_map(
        body,
        mesh=mesh,
        in_specs=(
            P("expert", "dp", None),
            P("expert", "dp", None),
            P("expert"),
            P("expert", "dp", None),
            P(),
            P(),
            P(),
            P(),
            P(),
            P(),
            P(),
            P(),
            P(),
            P("expert", None, None),
            P("expert", None, None),
            P("expert", None, None),
        ),
        out_specs=(
            P("expert", "dp", None),
            P("expert", "dp", None),
            P(),
            P(),
            P(),
            P(),
            P(),
            P(),
            P(),
            P(),
            P(),
            P("expert", None, None),
            P("expert", None, None),
            P("expert", None, None),
        ),
        check_vma=False,
    )
```

```python
import math

import jax
import jax.numpy as jnp
from jax import lax
from jax.experimental import pallas as pl
from jax.experimental.pallas import tpu as pltpu
from jax.sharding import PartitionSpec as P

HEADS = 16
KV_HEADS = 8
HEAD_DIM = 64
EXPERTS = 32
TOPK = 8
CAP = 80


epsilon = 1e-06


def rope_tables(positions):
    steps_half = jnp.arange(HEAD_DIM // 2).astype(jnp.float32)
    inverse = jnp.exp(steps_half * (-2.0 * math.log(10000.0) / HEAD_DIM))
    angles = positions.astype(jnp.float32)[:, None] * inverse[None, :]
    return (jnp.cos(angles), jnp.sin(angles))


RING = 4
ROWS = 256
EXTRA = 16
FULL = ROWS + EXTRA
GROUP = 4 * CAP
MESH = pl.DeviceIdType.MESH


def dot_nn(a, b):
    return jnp.dot(a, b, preferred_element_type=jnp.float32)


def dot_nt(a, b):
    return lax.dot_general(a, b, (((1,), (1,)), ((), ())), preferred_element_type=jnp.float32)


def dot_tn(a, b):
    return lax.dot_general(a, b, (((0,), (0,)), ((), ())), preferred_element_type=jnp.float32)


class Torus:
    def __init__(self):
        self.dp = lax.axis_index("dp")
        expert = lax.axis_index("expert")
        self.expert = expert
        self.z, self.y = expert // RING, expert % RING

    def block(self, dz, dy):
        return ((self.z + dz + RING) % RING) * RING + (self.y + dy + RING) % RING

    def near(self, axis, step):
        return (self.dp, self.block(step, 0) if axis == "z" else self.block(0, step))

    def along(self, axis, other, step):
        return self.block(step, other) if axis == "z" else self.block(other, step)

    def neighbours(self):
        return [self.near(axis, step) for axis in "yz" for step in (1, -1)]


class Gather:
    def __init__(self, torus, buffer, send, recv, number, axis, other, low, first, second, stride):
        self.torus, self.buffer, self.send, self.recv = torus, buffer, send, recv
        self.number, self.axis, self.other, self.stride = number, axis, other, stride
        self.whole, self.front, self.rear = (low, first + second), (low, first), (low + first, second)

    def copy(self, which, offset, part, step):
        at = self.torus.along(self.axis, self.other, offset) * self.stride + part[0]
        rows = self.buffer.at[pl.ds(pl.multiple_of(at, 16), part[1])]
        return pltpu.make_async_remote_copy(
            src_ref=rows,
            dst_ref=rows,
            send_sem=self.send.at[self.number, which],
            recv_sem=self.recv.at[self.number, which],
            device_id=self.torus.near(self.axis, step),
            device_id_type=MESH,
        )

    def first(self):
        self.copy(0, 0, self.whole, 1).start()
        self.copy(1, 0, self.whole, -1).start()

    def second(self):
        self.copy(0, -1, self.whole, 1).wait_recv()
        self.copy(2, -1, self.front, 1).start()
        self.copy(1, 1, self.whole, -1).wait_recv()
        self.copy(3, 1, self.rear, -1).start()

    def third(self):
        self.copy(2, 2, self.front, 1).wait_recv()
        self.copy(3, 2, self.rear, -1).wait_recv()

    def drain(self):
        self.copy(0, 0, self.whole, 1).wait_send()
        self.copy(1, 0, self.whole, -1).wait_send()
        self.copy(2, -1, self.front, 1).wait_send()
        self.copy(3, 1, self.rear, -1).wait_send()


class Scatter:
    def __init__(self, torus, sums, landing, send, recv, number, base, axis, other, low, first, second):
        self.torus, self.sums, self.landing, self.send, self.recv = torus, sums, landing, send, recv
        self.number, self.axis, self.other = number, axis, other
        self.low, self.parts = low, (first, second)
        self.size = first + second
        self.slots = (base, base + first, base + self.size, base + 2 * self.size)

    def rows(self, which):
        if which == 0:
            return self.low, self.parts[0]
        if which == 1:
            return self.low + self.parts[0], self.parts[1]
        return self.low, self.size

    def at(self, offset):
        return self.torus.along(self.axis, self.other, offset)

    def copy(self, which):
        start, size = self.rows(which)
        offset = (2, 2, 1, -1)[which]
        return pltpu.make_async_remote_copy(
            src_ref=self.sums.at[self.at(offset), pl.ds(start, size)],
            dst_ref=self.landing.at[pl.ds(self.slots[which], size)],
            send_sem=self.send.at[self.number, which],
            recv_sem=self.recv.at[self.number, which],
            device_id=self.torus.near(self.axis, (1, -1, 1, -1)[which]),
            device_id_type=MESH,
        )

    def add(self, which, offset):
        start, size = self.rows(which)
        block = self.at(offset)

        @pl.loop(0, size // 16)
        def _(k):
            here = pl.ds(pl.multiple_of(start + k * 16, 16), 16)
            there = pl.ds(pl.multiple_of(self.slots[which] + k * 16, 16), 16)
            total = self.sums[block, here].astype(jnp.float32) + self.landing[there].astype(jnp.float32)
            self.sums[block, here] = total.astype(jnp.bfloat16)

    def first(self):
        self.copy(0).start()
        self.copy(1).start()

    def second(self):
        self.copy(0).wait_recv()
        self.add(0, 1)
        self.copy(2).start()
        self.copy(1).wait_recv()
        self.add(1, -1)
        self.copy(3).start()

    def third(self, result=None):
        self.copy(2).wait_recv()
        self.copy(3).wait_recv()
        block = self.at(0)

        @pl.loop(0, self.size // 16)
        def _(k):
            here = pl.ds(pl.multiple_of(self.low + k * 16, 16), 16)
            left = pl.ds(pl.multiple_of(self.slots[2] + k * 16, 16), 16)
            right = pl.ds(pl.multiple_of(self.slots[3] + k * 16, 16), 16)
            total = (
                self.sums[block, here].astype(jnp.float32)
                + self.landing[left].astype(jnp.float32)
                + self.landing[right].astype(jnp.float32)
            )
            if result is None:
                self.sums[block, here] = total.astype(jnp.bfloat16)
            else:
                result[here] = total

    def drain(self):
        for which in range(4):
            self.copy(which).wait_send()


def moe_kernel(
    ffn, cot, wr, w_gate, w_up, w_down,
    ret, mixed, grad_gu, grad_d,
    rows, sums, wgu, wd, held, pair, inner, dgu, mixing, back, cotv, before, chosen, gate_rows, grad_rows, stage,
    ag_send, ag_recv, rs_send, rs_recv, w_sem, cot_sem, stage_sem, credit,
):
    torus = Torus()
    barrier = pltpu.get_barrier_semaphore()
    for device in torus.neighbours():
        pl.semaphore_signal(barrier, inc=1, device_id=device, device_id_type=MESH)

    weights = [
        pltpu.make_async_copy(w_gate, wgu.at[:, :, pl.ds(0, 512)], w_sem.at[0]),
        pltpu.make_async_copy(w_up, wgu.at[:, :, pl.ds(512, 512)], w_sem.at[1]),
        pltpu.make_async_copy(w_down, wd, w_sem.at[2]),
    ]
    for copy in weights:
        copy.start()

    def group_z(g):
        return (torus.z + g + (g // 2) * (1 - 2 * (g % 2))) % RING

    def cot_copy(g):
        return pltpu.make_async_copy(cot.at[pl.ds(pl.multiple_of(group_z(g) * RING * FULL, 16), RING * FULL)], cotv, cot_sem)

    cot_copy(0).start()
    rows[pl.ds(pl.multiple_of(torus.expert * ROWS, ROWS), ROWS)] = ffn[...]
    pl.semaphore_wait(barrier, 4)

    def gather(number, axis, other, low):
        return Gather(torus, rows, ag_send, ag_recv, number, axis, other, low, ROWS // 4, ROWS // 4, ROWS)

    a_first = gather(0, "y", 0, 0)
    b_first = gather(1, "z", 0, ROWS // 2)
    a_second = {d: gather(2 + d % RING, "z", d, 0) for d in (0, 1, -1, 2)}
    b_second = {d: gather(6 + d % RING, "y", d, ROWS // 2) for d in (0, 1, -1, 2)}
    gathers = [a_first, b_first, *a_second.values(), *b_second.values()]

    a_first.first()
    b_first.first()
    b_second[0].first()
    a_second[0].first()
    a_first.second()
    b_first.second()
    for d in (1, -1):
        b_second[d].first()
        a_second[d].first()
    a_first.third()
    b_first.third()
    b_second[2].first()
    a_second[2].first()
    for copy in weights:
        copy.wait()

    earlier = lax.broadcasted_iota(jnp.int32, (ROWS, ROWS), 0) < lax.broadcasted_iota(jnp.int32, (ROWS, ROWS), 1)
    before[...] = jnp.where(earlier, 1.0, 0.0).astype(jnp.bfloat16)
    slot_at = lax.broadcasted_iota(jnp.int32, (CAP, ROWS), 0).astype(jnp.float32)

    def stage_copy(slot, target):
        return pltpu.make_async_copy(stage.at[slot], target, stage_sem.at[slot])

    expert_rows = lax.broadcasted_iota(jnp.int32, (EXPERTS, ROWS), 0)

    @pl.loop(0, 4)
    def _(g):
        @pl.when(g == 0)
        def _():
            b_second[0].second()
            a_second[0].second()
            b_second[0].third()

        @pl.when(g == 1)
        def _():
            for d in (1, -1):
                b_second[d].second()
                a_second[d].second()
            a_second[2].second()
            b_second[1].third()

        @pl.when(g == 2)
        def _():
            b_second[2].second()
            b_second[-1].third()

        @pl.when(g == 3)
        def _():
            for d in (0, 1, -1, 2):
                a_second[d].third()
            b_second[2].third()

        cot_copy(g).wait()
        first_source = group_z(g) * RING

        @pl.loop(0, 4)
        def _(j):
            source = first_source + j
            block = rows[pl.ds(pl.multiple_of(source * ROWS, ROWS), ROWS)]
            laid = cotv[pl.ds(pl.multiple_of(j * FULL, 16), EXTRA)].astype(jnp.float32)
            member = jnp.concatenate([laid[:8, q * ROWS : (q + 1) * ROWS] for q in range(4)], axis=0)
            named = member > 0.5
            slots = dot_nn(member.astype(jnp.bfloat16), before[...])
            slots = jnp.where(named, slots, -1.0)
            logits = jnp.where(named, dot_nt(wr[...], block), -1e30)
            weight = jnp.where(named, jnp.exp(logits - jnp.max(logits, axis=0, keepdims=True)), 0.0)
            gates = weight / jnp.sum(weight, axis=0, keepdims=True)
            picked = []
            for e in range(2):
                own = jnp.sum(
                    jnp.where(expert_rows == torus.expert * 2 + e, slots, 0.0), axis=0, keepdims=True
                )
                picked.append(jnp.where(slot_at == own, 1.0, 0.0))
            both = jnp.concatenate(picked, axis=0).astype(jnp.bfloat16)
            chosen[j] = both
            took = dot_nn(both, block).astype(jnp.bfloat16)
            took_grad = dot_nn(both, cotv[pl.ds(pl.multiple_of(j * FULL + EXTRA, 16), ROWS)]).astype(jnp.bfloat16)
            here = pl.ds(pl.multiple_of(j * CAP, 16), CAP)
            there = pl.ds(pl.multiple_of(g * GROUP + j * CAP, 16), CAP)
            for e in range(2):
                own = jnp.sum(
                    jnp.where(expert_rows == torus.expert * 2 + e, gates, 0.0), axis=0, keepdims=True
                )
                of_rows = jnp.sum(picked[e] * own, axis=1, keepdims=True)
                gate_rows[e, here] = jnp.broadcast_to(of_rows, (CAP, 128))
                held[e, there] = took[e * CAP : (e + 1) * CAP]
                mixing[e, here] = took_grad[e * CAP : (e + 1) * CAP]

        @pl.when(g < 3)
        def _():
            cot_copy(g + 1).start()

        @pl.when(g == 3)
        def _():
            for one in gathers:
                one.drain()
            for device in torus.neighbours():
                pl.semaphore_signal(credit, inc=1, device_id=device, device_id_type=MESH)

        @pl.loop(0, 2)
        def _(e):
            there = pl.ds(pl.multiple_of(g * GROUP, 16), GROUP)
            both = dot_nn(held[e, there], wgu[e])
            gate, up = both[:, :512], both[:, 512:]
            sig = jax.nn.sigmoid(gate)
            silu = gate * sig
            act = (silu * up).astype(jnp.bfloat16)
            inner[e, there] = act
            out = dot_nn(act, wd[e]).astype(jnp.bfloat16).astype(jnp.float32)
            grad = mixing[e].astype(jnp.float32)
            weight = gate_rows[e][:, :1]
            grad_rows[e] = jnp.broadcast_to(jnp.sum(grad * out, axis=1, keepdims=True), (GROUP, 128))
            pair[e, there] = (weight * grad).astype(jnp.bfloat16)
            mixing[e] = (weight * out).astype(jnp.bfloat16)
            inner_grad = dot_nt(pair[e, there], wd[e])
            dgu[e, there, :512] = (inner_grad * up * sig * (1.0 + gate * (1.0 - sig))).astype(jnp.bfloat16)
            dgu[e, there, 512:] = (inner_grad * silu).astype(jnp.bfloat16)
            back[e] = dot_nt(dgu[e, there], wgu[e]).astype(jnp.bfloat16)

        @pl.loop(0, 4)
        def _(j):
            source = first_source + j
            both = chosen[j]
            picked = both.astype(jnp.float32)
            here = pl.ds(pl.multiple_of(j * CAP, 16), CAP)
            part = dot_tn(both, jnp.concatenate([back[0, here], back[1, here]], axis=0))
            sums[source, pl.ds(EXTRA, ROWS)] = part.astype(jnp.bfloat16)
            grads = jnp.zeros((EXPERTS, ROWS), jnp.float32)
            for e in range(2):
                own = jnp.sum(
                    picked[e * CAP : (e + 1) * CAP] * grad_rows[e, here][:, :1], axis=0, keepdims=True
                )
                grads = grads + jnp.where(expert_rows == torus.expert * 2 + e, own, 0.0)
            laid = jnp.concatenate([grads[8 * q : 8 * q + 8] for q in range(4)], axis=1)
            sums[source, pl.ds(0, EXTRA)] = jnp.concatenate([laid, jnp.zeros_like(laid)], axis=0).astype(
                jnp.bfloat16
            )
            slot = j % 2

            @pl.when((g > 0) | (j > 1))
            def _():
                stage_copy(slot, mixed.at[source]).wait()

            result = dot_tn(both, jnp.concatenate([mixing[0, here], mixing[1, here]], axis=0))
            stage[slot] = result.astype(jnp.bfloat16)
            stage_copy(slot, mixed.at[source]).start()

    pl.semaphore_wait(credit, 4)

    order = (2, 1, -1, 0)
    a_lead = {}
    b_lead = {}
    for n, d in enumerate(order):
        a_lead[d] = Scatter(
            torus, sums, rows, rs_send, rs_recv, n, n * 384, "z", d, 0, 64, 64
        )
        b_lead[d] = Scatter(
            torus, sums, rows, rs_send, rs_recv, 4 + n, 1920 + n * 432, "y", d, 128, 80, 64
        )
    a_last = Scatter(torus, sums, rows, rs_send, rs_recv, 8, 4 * 384, "y", 0, 0, 64, 64)
    b_last = Scatter(torus, sums, rows, rs_send, rs_recv, 9, 1920 + 4 * 432, "z", 0, 128, 80, 64)

    def write_grads(low, high):
        @pl.loop(low, high)
        def _(k):
            slot = k % 2
            e, c = k // 6, k % 6
            stage_copy(slot, grad_d.at[0, pl.ds(0, 256)]).wait()

            @pl.when(c < 4)
            def _():
                columns = pl.ds(pl.multiple_of(c * 256, 256), 256)
                stage[slot] = dot_tn(held[e, :, columns], dgu[e]).astype(jnp.bfloat16)
                stage_copy(slot, grad_gu.at[e, columns]).start()

            @pl.when(c >= 4)
            def _():
                columns = pl.ds(pl.multiple_of((c - 4) * 256, 256), 256)
                stage[slot] = dot_tn(inner[e, :, columns], pair[e]).astype(jnp.bfloat16)
                stage_copy(slot, grad_d.at[e, columns]).start()

    for d in order:
        b_lead[d].first()
        a_lead[d].first()
    write_grads(0, 4)
    for d in order:
        b_lead[d].second()
        a_lead[d].second()
    write_grads(4, 12)
    for slot in range(2):
        stage_copy(slot, grad_d.at[0, pl.ds(0, 256)]).wait()
    for d in order:
        b_lead[d].third()
        a_lead[d].third()
        if d == 2:
            b_last.first()
            a_last.first()
    b_last.second()
    a_last.second()
    b_last.third(ret)
    a_last.third(ret)
    for one in [*a_lead.values(), *b_lead.values(), a_last, b_last]:
        one.drain()


def moe(ffn_in, cot_all, router_rows, w_gate, w_up, w_down):
    vmem, hbm = pl.BlockSpec(memory_space=pltpu.VMEM), pl.BlockSpec(memory_space=pl.ANY)
    low, total = jnp.bfloat16, 4 * GROUP
    return pl.pallas_call(
        moe_kernel,
        name="moe",
        out_shape=(
            jax.ShapeDtypeStruct((FULL, 1024), jnp.float32),
            jax.ShapeDtypeStruct((16, ROWS, 1024), low),
            jax.ShapeDtypeStruct((2, 1024, 1024), low),
            jax.ShapeDtypeStruct((2, 512, 1024), low),
        ),
        in_specs=[vmem, hbm, vmem, hbm, hbm, hbm],
        out_specs=(vmem, hbm, hbm, hbm),
        scratch_shapes=[
            pltpu.VMEM((16 * ROWS, 1024), low),
            pltpu.VMEM((16, FULL, 1024), low),
            pltpu.VMEM((2, 1024, 1024), low),
            pltpu.VMEM((2, 512, 1024), low),
            pltpu.VMEM((2, total, 1024), low),
            pltpu.VMEM((2, total, 1024), low),
            pltpu.VMEM((2, total, 512), low),
            pltpu.VMEM((2, total, 1024), low),
            pltpu.VMEM((2, GROUP, 1024), low),
            pltpu.VMEM((2, GROUP, 1024), low),
            pltpu.VMEM((4 * FULL, 1024), low),
            pltpu.VMEM((ROWS, ROWS), low),
            pltpu.VMEM((4, 2 * CAP, ROWS), low),
            pltpu.VMEM((2, GROUP, 128), jnp.float32),
            pltpu.VMEM((2, GROUP, 128), jnp.float32),
            pltpu.VMEM((2, ROWS, 1024), low),
            pltpu.SemaphoreType.DMA((10, 4)),
            pltpu.SemaphoreType.DMA((10, 4)),
            pltpu.SemaphoreType.DMA((10, 4)),
            pltpu.SemaphoreType.DMA((10, 4)),
            pltpu.SemaphoreType.DMA((3,)),
            pltpu.SemaphoreType.DMA,
            pltpu.SemaphoreType.DMA((2,)),
            pltpu.SemaphoreType.REGULAR,
        ],
        compiler_params=pltpu.CompilerParams(
            collective_id=1, has_side_effects=True, vmem_limit_bytes=63 * 2**20
        ),
        cost_estimate=pl.CostEstimate(flops=50 * 10**9, bytes_accessed=40 * 10**6, transcendentals=2 * 10**6),
    )(ffn_in, cot_all, router_rows, w_gate, w_up, w_down)


def everywhere():
    dp, expert = lax.axis_index("dp"), lax.axis_index("expert")
    here = {"x": dp // 2, "core": dp % 2, "z": expert // RING, "y": expert % RING}

    def device(axis, step):
        there = dict(here)
        size = 2 if axis == "core" else RING
        there[axis] = (here[axis] + step + size) % size
        return (there["x"] * 2 + there["core"], there["z"] * RING + there["y"])

    return here, device


def rms_scale(values):
    return lax.rsqrt(jnp.mean(values * values, axis=-1, keepdims=True) + epsilon)


def turned_rows(values, cosine, sine):
    front, back = values[: HEAD_DIM // 2], values[HEAD_DIM // 2 :]
    return jnp.concatenate([front * cosine - back * sine, back * cosine + front * sine], axis=0)


def kv_order(here, step):
    turn = step // 2
    return (turn % 2) * (3 - turn // 2) + (1 - turn % 2) * (turn // 2)


class Keys:
    def __init__(self, here, device, blocks, send, recv):
        self.here, self.device, self.blocks, self.send, self.recv = here, device, blocks, send, recv
        self.lines = blocks.shape[1]

    def copy(self, which):
        half = self.lines // 2
        offset, start, size, axis, step = (
            (0, 0, self.lines, "core", 1),
            (0, 0, self.lines, "x", 1),
            (0, 0, self.lines, "x", -1),
            (-1, 0, half, "x", 1),
            (1, half, half, "x", -1),
            (-1, 0, self.lines, "core", 1),
            (1, 0, self.lines, "core", 1),
            (2, 0, self.lines, "core", 1),
        )[which]
        block = (self.here["x"] + offset + RING) % RING * 2 + self.here["core"]
        part = self.blocks.at[block, pl.ds(start, size)]
        return pltpu.make_async_remote_copy(
            src_ref=part,
            dst_ref=part,
            send_sem=self.send.at[which],
            recv_sem=self.recv.at[which],
            device_id=self.device(axis, step),
            device_id_type=MESH,
        )

    def start(self, *which):
        for one in which:
            self.copy(one).start()

    def arrive(self, *which):
        for one in which:
            self.copy(one).wait_recv()

    def drain(self):
        for one in range(8):
            self.copy(one).wait_send()


def forward_kernel(
    tokens, cot, routes_t, length, cosine, sine, attn_gain, query_gain, key_gain, ffn_gain,
    w_query, w_key, w_value, w_output,
    ffn_in, hidden, mixed_t, queries, log_total, normed, query_raw, key_raw, kv_all, cot_all,
    wq, wk, wv, wo, kv, turned, most, total, mixed, packed,
    ag_send, ag_recv, kv_send, kv_recv, w_sem, kv_sem, own_sem,
):
    torus = Torus()
    here, device = everywhere()
    me = here["x"] * 2 + here["core"]
    barrier = pltpu.get_barrier_semaphore()
    peers = [*torus.neighbours(), device("core", 1), device("x", 1), device("x", -1)]
    for peer in peers:
        pl.semaphore_signal(barrier, inc=1, device_id=peer, device_id_type=MESH)
    loads = [
        pltpu.make_async_copy(source, target, w_sem.at[n])
        for n, (source, target) in enumerate(((w_query, wq), (w_key, wk), (w_value, wv), (w_output, wo)))
    ]
    for load in loads:
        load.start()

    expert_rows = lax.broadcasted_iota(jnp.int32, (EXPERTS, ROWS), 0)
    member = jnp.zeros((EXPERTS, ROWS), jnp.float32)
    for k in range(TOPK):
        member = member + jnp.where(expert_rows == routes_t[pl.ds(k, 1), :], 1.0, 0.0)
    laid = jnp.concatenate([member[8 * q : 8 * q + 8] for q in range(4)], axis=1)
    packed[...] = jnp.concatenate([laid, jnp.zeros_like(laid)], axis=0).astype(jnp.bfloat16)
    first_row = pl.multiple_of(torus.expert * FULL, 16)
    owns = [
        pltpu.make_async_copy(packed, cot_all.at[pl.ds(first_row, EXTRA)], own_sem.at[0]),
        pltpu.make_async_copy(cot, cot_all.at[pl.ds(pl.multiple_of(first_row + EXTRA, 16), ROWS)], own_sem.at[1]),
    ]
    for copy in owns:
        copy.start()
    for copy in owns:
        copy.wait()
    pl.semaphore_wait(barrier, len(peers))

    def gather(number, axis, other, low, first, second):
        return Gather(torus, cot_all, ag_send, ag_recv, number, axis, other, low, first, second, FULL)

    a_first = gather(0, "y", 0, 0, 64, 64)
    b_first = gather(1, "z", 0, 128, 80, 64)
    a_second = {d: gather(2 + d % RING, "z", d, 0, 64, 64) for d in (0, 1, -1, 2)}
    b_second = {d: gather(6 + d % RING, "y", d, 128, 80, 64) for d in (0, 1, -1, 2)}
    gathers = [a_first, b_first, *a_second.values(), *b_second.values()]
    a_first.first()
    b_first.first()
    b_second[0].first()
    a_second[0].first()

    @pl.loop(0, 4)
    def _(n):
        at = pl.ds(pl.multiple_of(n * 64, 64), 64)
        rows = tokens[at].astype(jnp.float32)
        normed[at] = (rows * rms_scale(rows) * attn_gain[...].astype(jnp.float32)).astype(jnp.bfloat16)

    for load in loads:
        load.wait()

    keys = Keys(here, device, kv, kv_send, kv_recv)
    key_raw[...] = dot_nn(normed[...], wk[...])
    scaled = key_raw[...]
    scaled = (scaled * rms_scale(scaled) * key_gain[...].astype(jnp.float32)).T
    for j in range(KV_HEADS):
        head = turned_rows(scaled[j * 64 : j * 64 + 64], cosine[...], sine[...])
        kv[me, pl.ds(j * 64, 64)] = head.astype(jnp.bfloat16)
    kv[me, pl.ds(512, 512)] = dot_nn(normed[...], wv[...]).T.astype(jnp.bfloat16)
    keys.start(0, 1, 2)
    query_raw[...] = dot_nn(normed[...], wq[...])
    scaled = query_raw[...]
    turned[...] = (scaled * rms_scale(scaled) * query_gain[...].astype(jnp.float32)).T

    @pl.loop(0, KV_HEADS)
    def _(j):
        for r in range(2):
            head = turned[pl.ds(pl.multiple_of(j * 128 + r * 64, 64), 64)]
            head = turned_rows(head, cosine[...], sine[...])
            queries[j, :, r * ROWS : (r + 1) * ROWS] = (head * HEAD_DIM**-0.5).astype(jnp.bfloat16)

    a_first.second()
    b_first.second()
    for d in (1, -1):
        b_second[d].first()
        a_second[d].first()

    key_at = lax.broadcasted_iota(jnp.int32, (ROWS, 2 * ROWS), 0)
    query_at = lax.broadcasted_iota(jnp.int32, (ROWS, 2 * ROWS), 1) % ROWS
    valid = (key_at <= query_at) & (key_at + me * ROWS < length[...])

    @pl.loop(0, KV_HEADS)
    def _(j):
        key_head = kv[me, pl.ds(pl.multiple_of(j * 64, 64), 64)]
        value_head = kv[me, pl.ds(pl.multiple_of(512 + j * 64, 64), 64)]
        scores = jnp.where(valid, dot_tn(key_head, queries[j]), -1e30)
        top = jnp.max(scores, axis=0, keepdims=True)
        probs = jnp.exp(scores - top)
        most[j] = top
        total[j] = jnp.sum(probs, axis=0, keepdims=True)
        mixed[j] = dot_nn(value_head, probs.astype(jnp.bfloat16))

    @pl.loop(1, 8)
    def _(step):
        @pl.when(step == 1)
        def _():
            a_first.third()
            b_first.third()
            b_second[2].first()
            a_second[2].first()
            keys.arrive(0)

        @pl.when(step == 2)
        def _():
            keys.arrive(1)
            keys.start(3, 5)
            keys.arrive(2)
            keys.start(4, 6)
            b_second[0].second()
            a_second[0].second()

        @pl.when(step == 3)
        def _():
            keys.arrive(5)
            for d in (1, -1):
                b_second[d].second()
                a_second[d].second()

        @pl.when(step == 5)
        def _():
            keys.arrive(3, 4)
            keys.start(7)
            keys.arrive(6)
            b_second[2].second()
            a_second[2].second()

        @pl.when(step == 7)
        def _():
            keys.arrive(7)

        block = (here["x"] + kv_order(here, step) + RING) % RING * 2 + (here["core"] + step) % 2

        @pl.when(block < me)
        def _():
            @pl.loop(0, KV_HEADS)
            def _(j):
                key_head = kv[block, pl.ds(pl.multiple_of(j * 64, 64), 64)]
                value_head = kv[block, pl.ds(pl.multiple_of(512 + j * 64, 64), 64)]
                scores = dot_tn(key_head, queries[j])
                before = most[j]
                top = jnp.maximum(before, jnp.max(scores, axis=0, keepdims=True))
                probs = jnp.exp(scores - top)
                less = jnp.exp(before - top)
                most[j] = top
                total[j] = total[j] * less + jnp.sum(probs, axis=0, keepdims=True)
                mixed[j] = mixed[j] * less + dot_nn(value_head, probs.astype(jnp.bfloat16))

    save = pltpu.make_async_copy(kv, kv_all, kv_sem)
    save.start()

    @pl.loop(0, KV_HEADS)
    def _(j):
        share = total[j]
        log_total[j] = most[j] + jnp.log(share)
        head = (mixed[j] / share).astype(jnp.bfloat16)
        for r in range(2):
            mixed_t[pl.ds(pl.multiple_of(j * 128 + r * 64, 64), 64), :] = head[:, r * ROWS : (r + 1) * ROWS]

    hidden[...] = dot_tn(mixed_t[...], wo[...])

    @pl.loop(0, 4)
    def _(n):
        at = pl.ds(pl.multiple_of(n * 64, 64), 64)
        rows = hidden[at] + tokens[at].astype(jnp.float32)
        hidden[at] = rows
        ffn_in[at] = (rows * rms_scale(rows) * ffn_gain[...].astype(jnp.float32)).astype(jnp.bfloat16)

    for d in (0, 1, -1, 2):
        a_second[d].third()
        b_second[d].third()
    save.wait()
    keys.drain()
    for one in gathers:
        one.drain()


def forward(tokens, cot, routes_t, length, cosine, sine, gains, weights):
    vmem, hbm = pl.BlockSpec(memory_space=pltpu.VMEM), pl.BlockSpec(memory_space=pl.ANY)
    low, wide = jnp.bfloat16, jnp.float32
    shape = jax.ShapeDtypeStruct
    return pl.pallas_call(
        forward_kernel,
        name="forward",
        out_shape=(
            shape((ROWS, 1024), low),
            shape((ROWS, 1024), wide),
            shape((1024, ROWS), low),
            shape((KV_HEADS, HEAD_DIM, 2 * ROWS), low),
            shape((KV_HEADS, 1, 2 * ROWS), wide),
            shape((ROWS, 1024), low),
            shape((ROWS, 1024), wide),
            shape((ROWS, 512), wide),
            shape((8, 1024, ROWS), low),
            shape((16 * FULL, 1024), low),
        ),
        in_specs=[vmem] * 10 + [hbm] * 4,
        out_specs=(vmem,) * 8 + (hbm, hbm),
        scratch_shapes=[
            pltpu.VMEM((1024, 1024), low),
            pltpu.VMEM((1024, 512), low),
            pltpu.VMEM((1024, 512), low),
            pltpu.VMEM((1024, 1024), low),
            pltpu.VMEM((8, 1024, ROWS), low),
            pltpu.VMEM((1024, ROWS), wide),
            pltpu.VMEM((KV_HEADS, 1, 2 * ROWS), wide),
            pltpu.VMEM((KV_HEADS, 1, 2 * ROWS), wide),
            pltpu.VMEM((KV_HEADS, HEAD_DIM, 2 * ROWS), wide),
            pltpu.VMEM((EXTRA, 1024), low),
            pltpu.SemaphoreType.DMA((10, 4)),
            pltpu.SemaphoreType.DMA((10, 4)),
            pltpu.SemaphoreType.DMA((8,)),
            pltpu.SemaphoreType.DMA((8,)),
            pltpu.SemaphoreType.DMA((4,)),
            pltpu.SemaphoreType.DMA,
            pltpu.SemaphoreType.DMA((2,)),
        ],
        compiler_params=pltpu.CompilerParams(
            collective_id=3, has_side_effects=True, vmem_limit_bytes=56 * 2**20
        ),
    )(tokens, cot, routes_t, length, cosine, sine, *gains, *weights)


ORDERS = (("x", "y", "z"), ("y", "z", "x"), ("z", "x", "y"))


class Total:
    def __init__(self, here, device, buffer, final, landing, work, send, recv, number, half, start, rows, base, order):
        self.here, self.device, self.buffer, self.final = here, device, buffer, final
        self.landing, self.work = landing, work
        self.send, self.recv, self.number, self.order = send, recv, number, order
        self.half, self.start, self.rows, self.base = half, start, rows, base

    def own(self):
        return self.here["core"] * self.half + self.start

    def copy(self, which, source, target, axis, step):
        return pltpu.make_async_remote_copy(
            src_ref=source,
            dst_ref=target,
            send_sem=self.send.at[self.number, which],
            recv_sem=self.recv.at[self.number, which],
            device_id=self.device(axis, step),
            device_id_type=MESH,
        )

    def part(self, ref, at, size):
        return ref.at[pl.ds(pl.multiple_of(at, 16), size)]

    def copies(self, stage):
        r, own = self.rows, self.own()
        a, b, c = self.order
        ia, ib = self.here[a], self.here[b]
        second = own + ia * (r // 4)
        third = second + ib * (r // 16)
        land1, land2, land3 = self.base + r, self.base + r + 3 * (r // 4), self.base + r + 3 * (r // 4) + 3 * (r // 16)
        if stage == 0:
            there = (1 - self.here["core"]) * self.half + self.start
            return [self.copy(0, self.part(self.buffer, there, r), self.part(self.landing, self.base, r), "core", 1)]
        if stage == 6:
            whole = self.part(self.final, own, r)
            return [self.copy(16, whole, whole, "core", 1)]
        found = []
        for d in (1, 2, 3):
            if stage == 1:
                source = self.part(self.buffer, own + (ia + d) % RING * (r // 4), r // 4)
                target, axis = self.part(self.landing, land1 + (d - 1) * (r // 4), r // 4), a
            elif stage == 2:
                source = self.part(self.buffer, second + (ib + d) % RING * (r // 16), r // 16)
                target, axis = self.part(self.landing, land2 + (d - 1) * (r // 16), r // 16), b
            elif stage == 3:
                source = self.work.at[self.number, pl.ds(0, r // 16)]
                target, axis = self.part(self.landing, land3 + (d - 1) * (r // 16), r // 16), c
            elif stage == 4:
                source = self.part(self.final, third, r // 16)
                target, axis = source, b
            else:
                source = self.part(self.final, second, r // 4)
                target, axis = source, a
            found.append(self.copy(1 + (stage - 1) * 3 + d - 1, source, target, axis, d))
        return found

    def begin(self, stage):
        for copy in self.copies(stage):
            copy.start()

    def add(self, target, start, size, lands):
        step = 64 if size % 64 == 0 else 16

        @pl.loop(0, size // step)
        def _(k):
            here = pl.ds(pl.multiple_of(start + k * step, 16), step)
            total = self.buffer[here].astype(jnp.float32)
            for land in lands:
                total = total + self.landing[pl.ds(pl.multiple_of(land + k * step, 16), step)].astype(jnp.float32)
            if target is None:
                self.buffer[here] = total.astype(jnp.bfloat16)
            else:
                target[pl.ds(pl.multiple_of(k * step, 16), step)] = total.astype(jnp.bfloat16)

    def finish(self, stage):
        for copy in self.copies(stage):
            copy.wait_recv()
        r, own = self.rows, self.own()
        a, b, _ = self.order
        second = own + self.here[a] * (r // 4)
        third = second + self.here[b] * (r // 16)
        land1, land2, land3 = self.base + r, self.base + r + 3 * (r // 4), self.base + r + 3 * (r // 4) + 3 * (r // 16)
        if stage == 0:
            self.add(None, own, r, [self.base])
        elif stage == 1:
            self.add(None, second, r // 4, [land1 + d * (r // 4) for d in range(3)])
        elif stage == 2:
            self.add(self.work.at[self.number], third, r // 16, [land2 + d * (r // 16) for d in range(3)])
        elif stage == 3:
            r16 = r // 16

            @pl.loop(0, r16 // 16)
            def _(k):
                total = self.work[self.number, pl.ds(pl.multiple_of(k * 16, 16), 16)].astype(jnp.float32)
                for d in range(3):
                    at = land3 + d * r16 + k * 16
                    total = total + self.landing[pl.ds(pl.multiple_of(at, 16), 16)].astype(jnp.float32)
                self.final[pl.ds(pl.multiple_of(third + k * 16, 16), 16)] = total.astype(jnp.bfloat16)

    def drain(self):
        for stage in range(7):
            for copy in self.copies(stage):
                copy.wait_send()


class Small:
    STAGES = (("core", (1,)), ("x", (1, 2, 3)), ("y", (1, 2, 3)), ("z", (1, 2, 3)))

    def __init__(self, device, value, landing, send, recv):
        self.device, self.value, self.landing, self.send, self.recv = device, value, landing, send, recv

    def copies(self, stage):
        axis, steps = self.STAGES[stage]
        first = sum(len(s) for _, s in self.STAGES[:stage])
        return [
            pltpu.make_async_remote_copy(
                src_ref=self.value.at[stage],
                dst_ref=self.landing.at[first + n],
                send_sem=self.send.at[first + n],
                recv_sem=self.recv.at[first + n],
                device_id=self.device(axis, step),
                device_id_type=MESH,
            )
            for n, step in enumerate(steps)
        ]

    def begin(self, stage):
        for copy in self.copies(stage):
            copy.start()

    def finish(self, stage):
        for copy in self.copies(stage):
            copy.wait_recv()
        first = sum(len(s) for _, s in self.STAGES[:stage])
        total = self.value[stage]
        for n in range(len(self.STAGES[stage][1])):
            total = total + self.landing[first + n]
        self.value[stage + 1] = total

    def drain(self):
        for stage in range(4):
            for copy in self.copies(stage):
                copy.wait_send()


def total_kernel(parts, small, whole, small_whole, held, landing, work, values, small_landing, send, recv, small_send, small_recv, load_sem):
    here, device = everywhere()
    barrier = pltpu.get_barrier_semaphore()
    peers = [device("core", 1)] + [device(axis, d) for axis in "xyz" for d in (1, 2, 3)]
    for peer in peers:
        pl.semaphore_signal(barrier, inc=1, device_id=peer, device_id_type=MESH)
    load = pltpu.make_async_copy(parts, held, load_sem)
    load.start()
    values[0] = small[...]
    load.wait()
    pl.semaphore_wait(barrier, len(peers))
    half, base, streams = whole.shape[0] // 2, 0, []
    for s, (start, rows) in enumerate(EARLY):
        streams.append(
            Total(here, device, held, whole, landing, work, send, recv, s, half, start, rows, base, ORDERS[s])
        )
        base += rows + 3 * (rows // 4) + 6 * (rows // 16)
    few = Small(device, values, small_landing, small_send, small_recv)
    for one in streams:
        one.begin(0)
    few.begin(0)
    for stage in range(7):
        for one in streams:
            one.finish(stage)
            if stage < 6:
                one.begin(stage + 1)
        if stage < 4:
            few.finish(stage)
            if stage < 3:
                few.begin(stage + 1)
    small_whole[...] = values[4]
    for one in streams:
        one.drain()
    few.drain()


def total_everywhere(parts, small):
    vmem, hbm = pl.BlockSpec(memory_space=pltpu.VMEM), pl.BlockSpec(memory_space=pl.ANY)
    low = jnp.bfloat16
    rows, width = parts.shape
    room = sum(count + 3 * (count // 4) + 6 * (count // 16) for _, count in EARLY)
    return pl.pallas_call(
        total_kernel,
        name="total",
        out_shape=(
            jax.ShapeDtypeStruct(parts.shape, low),
            jax.ShapeDtypeStruct(small.shape, jnp.float32),
        ),
        in_specs=[hbm, vmem],
        out_specs=(vmem, vmem),
        scratch_shapes=[
            pltpu.VMEM((rows, width), low),
            pltpu.VMEM((room, width), low),
            pltpu.VMEM((3, 48, width), low),
            pltpu.VMEM((5, *small.shape), jnp.float32),
            pltpu.VMEM((10, *small.shape), jnp.float32),
            pltpu.SemaphoreType.DMA((3, 17)),
            pltpu.SemaphoreType.DMA((3, 17)),
            pltpu.SemaphoreType.DMA((10,)),
            pltpu.SemaphoreType.DMA((10,)),
            pltpu.SemaphoreType.DMA,
        ],
        compiler_params=pltpu.CompilerParams(
            collective_id=2, has_side_effects=True, vmem_limit_bytes=56 * 2**20
        ),
    )(parts, small)


class Line:
    def __init__(self, here, device):
        self.here, self.device = here, device

    def along(self, axis, other, step):
        return (self.here["x"] + step + RING) % RING

    def near(self, axis, step):
        return self.device("x", step)


def rms_back(values, gain, grad):
    scale = rms_scale(values)
    lifted = gain * grad
    inner = jnp.mean(values * lifted, axis=-1, keepdims=True)
    return scale * lifted - values * (scale * scale * scale) * inner, jnp.sum(
        grad * values * scale, axis=0, keepdims=True
    )


def turned_back(grads, cosine, sine):
    front, back = grads[: HEAD_DIM // 2], grads[HEAD_DIM // 2 :]
    return jnp.concatenate([front * cosine + back * sine, back * cosine - front * sine], axis=0)


EARLY = ((0, 768), (768, 768), (1536, 512))


def backward_kernel(
    returned, hidden, ffn_in, cot, tokens, normed, query_raw, key_raw, mixed_t, queries, log_total,
    routes_t, length, cosine, sine, attn_gain, query_gain, key_gain, ffn_gain, router_rows,
    mixed_parts, kv_all, w_query, w_key, w_value, w_output,
    mixed_out, token_grad, late, early_small, late_small, output_sum,
    sums, rows, wq, wk, wv, wo, kv, hidden_grad, result, branch, grads, delta, query_grad, turned,
    for_mate, from_mate, kv_sums, kv_rows, kv_grad, raw_grad, key_low, value_low,
    held, final, landing, work, values, small_rows,
    rs_send, rs_recv, mate_send, mate_recv, kv_send, kv_recv, ar_send, ar_recv, small_send, small_recv, load_sem, stage_sem,
):
    torus = Torus()
    here, device = everywhere()
    me = here["x"] * 2 + here["core"]
    barrier = pltpu.get_barrier_semaphore()
    peers = [device("core", 1)] + [device(axis, d) for axis in "xyz" for d in (1, 2, 3)]
    for peer in peers:
        pl.semaphore_signal(barrier, inc=1, device_id=peer, device_id_type=MESH)
    loads = [
        pltpu.make_async_copy(source, target, load_sem.at[n])
        for n, (source, target) in enumerate(
            ((w_output, wo), (mixed_parts, sums), (kv_all, kv), (w_query, wq), (w_key, wk), (w_value, wv))
        )
    ]
    for load in loads:
        load.start()

    expert_rows = lax.broadcasted_iota(jnp.int32, (EXPERTS, ROWS), 0)
    member = jnp.zeros((EXPERTS, ROWS), jnp.float32)
    for k in range(TOPK):
        member = member + jnp.where(expert_rows == routes_t[pl.ds(k, 1), :], 1.0, 0.0)
    named = member > 0.5
    logits = jnp.where(named, dot_nt(router_rows[...], ffn_in[...]), -1e30)
    weight = jnp.where(named, jnp.exp(logits - jnp.max(logits, axis=0, keepdims=True)), 0.0)
    gates = weight / jnp.sum(weight, axis=0, keepdims=True)
    gate_grad = jnp.concatenate([returned[:8, q * ROWS : (q + 1) * ROWS] for q in range(4)], axis=0)
    logit_grad = (gates * (gate_grad - jnp.sum(gates * gate_grad, axis=0, keepdims=True))).astype(jnp.bfloat16)
    result[...] = dot_tn(logit_grad, router_rows[...])
    values[0, :EXPERTS] = dot_nn(logit_grad, ffn_in[...])

    def ffn_part(n, gain_grad):
        at = pl.ds(pl.multiple_of(n * 64, 64), 64)
        grad = result[at] + returned[pl.ds(pl.multiple_of(n * 64 + EXTRA, 16), 64)]
        part, more = rms_back(hidden[at], ffn_gain[...].astype(jnp.float32), grad)
        part = part + cot[at].astype(jnp.float32)
        hidden_grad[at] = part
        branch[at] = part.astype(jnp.bfloat16)
        return gain_grad + more

    gain_grad = lax.fori_loop(0, 4, ffn_part, jnp.zeros((1, 1024), jnp.float32))
    values[0, EXPERTS:] = jnp.concatenate([gain_grad, jnp.zeros((7, 1024), jnp.float32)], axis=0)

    loads[0].wait()
    turned[...] = dot_nt(wo[...], branch[...])

    @pl.loop(0, KV_HEADS)
    def _(j):
        for r in range(2):
            at = pl.ds(pl.multiple_of(j * 128 + r * 64, 64), 64)
            low = turned[at].astype(jnp.bfloat16)
            grads[j, :, r * ROWS : (r + 1) * ROWS] = low
            delta[j, :, r * ROWS : (r + 1) * ROWS] = jnp.sum(
                low.astype(jnp.float32) * mixed_t[at].astype(jnp.float32), axis=0, keepdims=True
            )
        query_grad[j] = jnp.zeros((HEAD_DIM, 2 * ROWS), jnp.float32)

    @pl.loop(0, 4)
    def _(n):
        at = pl.ds(pl.multiple_of(n * 256, 256), 256)
        part = dot_nn(mixed_t[at], branch[...]).astype(jnp.bfloat16)
        for q in range(4):
            held[pl.ds(pl.multiple_of(q * 1024 + n * 256, 256), 256)] = part[:, q * 256 : (q + 1) * 256]

    for load in loads[1:]:
        load.wait()
    pl.semaphore_wait(barrier, len(peers))

    half, base, early = 2048, 0, []
    for s, (start, count) in enumerate(EARLY):
        early.append(
            Total(here, device, held, final, landing, work, ar_send, ar_recv, s, half, start, count, base, ORDERS[s])
        )
        base += count + 3 * (count // 4) + 6 * (count // 16)
    few = Small(device, values, small_rows, small_send, small_recv)
    order = (2, 1, -1, 0)
    leads = []
    for n, d in enumerate(order):
        leads.append(Scatter(torus, sums, rows, rs_send, rs_recv, n, n * 384, "z", d, 0, 64, 64))
        leads.append(Scatter(torus, sums, rows, rs_send, rs_recv, 4 + n, (5 + n) * 384, "y", d, 128, 64, 64))
    lasts = [
        Scatter(torus, sums, rows, rs_send, rs_recv, 8, 4 * 384, "y", 0, 0, 64, 64),
        Scatter(torus, sums, rows, rs_send, rs_recv, 9, 9 * 384, "z", 0, 128, 64, 64),
    ]
    ring = Scatter(Line(here, device), kv_sums, kv_rows, kv_send, kv_recv, 0, 0, "x", 0, 0, 512, 512)

    for one in early:
        one.begin(0)
    few.begin(0)
    for one in leads:
        one.first()

    def early_step(stage):
        for one in early:
            one.finish(stage)
            if stage < 6:
                one.begin(stage + 1)
        if stage < 4:
            few.finish(stage)
            if stage < 3:
                few.begin(stage + 1)

    def mate_copy(turn, at):
        return pltpu.make_async_remote_copy(
            src_ref=for_mate.at[at],
            dst_ref=from_mate.at[at],
            send_sem=mate_send.at[turn],
            recv_sem=mate_recv.at[turn],
            device_id=device("core", 1),
            device_id_type=MESH,
        )

    key_at = lax.broadcasted_iota(jnp.int32, (ROWS, 2 * ROWS), 0)
    query_at = lax.broadcasted_iota(jnp.int32, (ROWS, 2 * ROWS), 1) % ROWS
    valid = (key_at <= query_at) & (key_at + me * ROWS < length[...])

    def block_grads(block, target, at, masked):
        @pl.loop(0, KV_HEADS)
        def _(j):
            key_lines = pl.ds(pl.multiple_of(j * 64, 64), 64)
            value_lines = pl.ds(pl.multiple_of(512 + j * 64, 64), 64)
            key_head, value_head = kv[block, key_lines], kv[block, value_lines]
            probs = jnp.exp(dot_tn(key_head, queries[j]) - log_total[j])
            if masked:
                probs = jnp.where(valid, probs, 0.0)
            probs_grad = dot_tn(value_head, grads[j])
            score_grad = (probs * (probs_grad - delta[j])).astype(jnp.bfloat16)
            target[at, key_lines] = dot_nt(queries[j], score_grad).astype(jnp.bfloat16)
            target[at, value_lines] = dot_nt(grads[j], probs.astype(jnp.bfloat16)).astype(jnp.bfloat16)
            query_grad[j] += dot_nn(key_head, score_grad)

    def from_other(turn, at):
        mate_copy(turn, at).wait_recv()

        @pl.loop(0, 16)
        def _(n):
            lines = pl.ds(pl.multiple_of(n * 64, 64), 64)
            total = kv_sums[at, lines].astype(jnp.float32) + from_mate[at, lines].astype(jnp.float32)
            kv_sums[at, lines] = total.astype(jnp.bfloat16)

    def turn_x(turn):
        offset = (1 - turn % 2) * (2 + turn // 2) + (turn % 2) * (1 - turn // 2)
        return (here["x"] + offset + RING) % RING

    @pl.loop(0, 4)
    def _(turn):
        @pl.when(turn == 1)
        def _():
            early_step(0)
            for one in leads:
                one.second()

        @pl.when(turn == 2)
        def _():
            early_step(2)

        @pl.when(turn == 3)
        def _():
            early_step(4)
            for one in leads[:2]:
                one.third()
            for one in lasts:
                one.first()

        at = turn_x(turn)
        other = at * 2 + 1 - here["core"]

        @pl.when(other < me)
        def _():
            block_grads(other, for_mate, at, False)

        @pl.when(other >= me)
        def _():
            for_mate[at] = jnp.zeros((1024, ROWS), jnp.bfloat16)

        mate_copy(turn, at).start()

        @pl.when(turn == 1)
        def _():
            early_step(1)

        @pl.when(turn == 2)
        def _():
            early_step(3)

        @pl.when(turn == 3)
        def _():
            early_step(5)
            for one in leads[2:]:
                one.third()
            for one in lasts:
                one.second()

        own = at * 2 + here["core"]

        @pl.when(own < me)
        def _():
            block_grads(own, kv_sums, at, False)

        @pl.when(own > me)
        def _():
            kv_sums[at] = jnp.zeros((1024, ROWS), jnp.bfloat16)

        @pl.when(own == me)
        def _():
            block_grads(own, kv_sums, at, True)

        from_other(turn, at)

        @pl.when(turn == 0)
        def _():
            ring.first()

        @pl.when(turn == 2)
        def _():
            ring.second()

    @pl.loop(0, KV_HEADS)
    def _(j):
        for r in range(2):
            head = query_grad[j, :, r * ROWS : (r + 1) * ROWS] * HEAD_DIM**-0.5
            turned[pl.ds(pl.multiple_of(j * 128 + r * 64, 64), 64)] = turned_back(head, cosine[...], sine[...])

    result[...] = turned[...].T

    def query_part(n, gain_grad):
        at = pl.ds(pl.multiple_of(n * 64, 64), 64)
        part, more = rms_back(query_raw[at], query_gain[...].astype(jnp.float32), result[at])
        raw_grad[at] = part.astype(jnp.bfloat16)
        return gain_grad + more

    query_gain_grad = lax.fori_loop(0, 4, query_part, jnp.zeros((1, 1024), jnp.float32))

    @pl.loop(0, 4)
    def _(n):
        columns = pl.ds(pl.multiple_of(n * 256, 256), 256)
        part = dot_tn(normed[:, columns], raw_grad[...]).astype(jnp.bfloat16)
        for q in range(2):
            late[pl.ds(pl.multiple_of(q * 1024 + n * 256, 256), 256)] = part[:, q * 512 : (q + 1) * 512]

    result[...] = dot_nt(raw_grad[...], wq[...])
    early_step(6)
    ring.third(kv_grad)

    for j in range(KV_HEADS):
        turned[j * 64 : j * 64 + 64] = turned_back(kv_grad[j * 64 : j * 64 + 64], cosine[...], sine[...])
    part, key_gain_grad = rms_back(key_raw[...], key_gain[...].astype(jnp.float32), turned[:512].T)
    key_low[...] = part.astype(jnp.bfloat16)
    value_low[...] = kv_grad[512:].T.astype(jnp.bfloat16)

    @pl.loop(0, 4)
    def _(n):
        columns = pl.ds(pl.multiple_of(n * 256, 256), 256)
        here_rows = normed[:, columns]
        late[pl.ds(pl.multiple_of(2048 + n * 256, 256), 256)] = dot_tn(here_rows, key_low[...]).astype(jnp.bfloat16)
        late[pl.ds(pl.multiple_of(3072 + n * 256, 256), 256)] = dot_tn(here_rows, value_low[...]).astype(jnp.bfloat16)

    result[...] += dot_nt(key_low[...], wk[...]) + dot_nt(value_low[...], wv[...])

    def token_part(n, gain_grad):
        at = pl.ds(pl.multiple_of(n * 64, 64), 64)
        part, more = rms_back(tokens[at].astype(jnp.float32), attn_gain[...].astype(jnp.float32), result[at])
        token_grad[at] = (hidden_grad[at] + part).astype(jnp.bfloat16)
        return gain_grad + more

    attn_gain_grad = lax.fori_loop(0, 4, token_part, jnp.zeros((1, 1024), jnp.float32))
    key_wide = jnp.concatenate([key_gain_grad, jnp.zeros((1, 512), jnp.float32)], axis=1)
    late_small[...] = jnp.concatenate(
        [attn_gain_grad, query_gain_grad, key_wide, jnp.zeros((5, 1024), jnp.float32)], axis=0
    )

    stages = (turned, kv_grad)
    for q in range(4):
        slot = q % 2
        out = pltpu.make_async_copy(stages[slot], output_sum.at[:, pl.ds(q * 256, 256)], stage_sem.at[slot])
        if q >= 2:
            out.wait()
        stages[slot][...] = final[q * 1024 : (q + 1) * 1024].astype(jnp.float32)
        out.start()
    early_small[...] = values[4]

    for one in lasts:
        one.third(result)

    @pl.loop(0, 4)
    def _(n):
        at = pl.ds(pl.multiple_of(n * 64, 64), 64)
        mixed_out[at] = (hidden[at] + result[at]).astype(jnp.bfloat16)

    for slot in range(2):
        pltpu.make_async_copy(stages[slot], output_sum.at[:, pl.ds(0, 256)], stage_sem.at[slot]).wait()
    for one in [*leads, *lasts, ring, *early, few]:
        one.drain()
    for turn in range(4):
        mate_copy(turn, 0).wait_send()


def backward(smalls, larges):
    vmem, hbm = pl.BlockSpec(memory_space=pltpu.VMEM), pl.BlockSpec(memory_space=pl.ANY)
    low, wide = jnp.bfloat16, jnp.float32
    shape = jax.ShapeDtypeStruct
    dma = pltpu.SemaphoreType.DMA
    room = sum(count + 3 * (count // 4) + 6 * (count // 16) for _, count in EARLY)
    return pl.pallas_call(
        backward_kernel,
        name="backward",
        out_shape=(
            shape((ROWS, 1024), low),
            shape((ROWS, 1024), low),
            shape((4096, 512), low),
            shape((40, 1024), wide),
            shape((8, 1024), wide),
            shape((1024, 1024), wide),
        ),
        in_specs=[vmem] * len(smalls) + [hbm] * len(larges),
        out_specs=(vmem,) * 5 + (hbm,),
        scratch_shapes=[
            pltpu.VMEM((16, ROWS, 1024), low),
            pltpu.VMEM((10 * 384, 1024), low),
            pltpu.VMEM((1024, 1024), low),
            pltpu.VMEM((1024, 512), low),
            pltpu.VMEM((1024, 512), low),
            pltpu.VMEM((1024, 1024), low),
            pltpu.VMEM((8, 1024, ROWS), low),
            pltpu.VMEM((ROWS, 1024), wide),
            pltpu.VMEM((ROWS, 1024), wide),
            pltpu.VMEM((ROWS, 1024), low),
            pltpu.VMEM((KV_HEADS, HEAD_DIM, 2 * ROWS), low),
            pltpu.VMEM((KV_HEADS, 1, 2 * ROWS), wide),
            pltpu.VMEM((KV_HEADS, HEAD_DIM, 2 * ROWS), wide),
            pltpu.VMEM((1024, ROWS), wide),
            pltpu.VMEM((4, 1024, ROWS), low),
            pltpu.VMEM((4, 1024, ROWS), low),
            pltpu.VMEM((4, 1024, ROWS), low),
            pltpu.VMEM((3072, ROWS), low),
            pltpu.VMEM((1024, ROWS), wide),
            pltpu.VMEM((ROWS, 1024), low),
            pltpu.VMEM((ROWS, 512), low),
            pltpu.VMEM((ROWS, 512), low),
            pltpu.VMEM((4096, 256), low),
            pltpu.VMEM((4096, 256), low),
            pltpu.VMEM((room, 256), low),
            pltpu.VMEM((3, 48, 256), low),
            pltpu.VMEM((5, 40, 1024), wide),
            pltpu.VMEM((10, 40, 1024), wide),
            dma((10, 4)),
            dma((10, 4)),
            dma((4,)),
            dma((4,)),
            dma((1, 4)),
            dma((1, 4)),
            dma((3, 17)),
            dma((3, 17)),
            dma((10,)),
            dma((10,)),
            dma((6,)),
            dma((2,)),
        ],
        compiler_params=pltpu.CompilerParams(
            collective_id=4, has_side_effects=True, vmem_limit_bytes=63 * 2**20
        ),
        cost_estimate=pl.CostEstimate(flops=100 * 10**9, bytes_accessed=60 * 10**6, transcendentals=8 * 10**6),
    )(*smalls, *larges)


def body(
    tokens,
    cotangent,
    lengths,
    routes,
    attn_gain,
    w_query,
    w_key,
    w_value,
    query_gain,
    key_gain,
    w_output,
    ffn_gain,
    w_router,
    w_gate,
    w_up,
    w_down,
):
    query_pos = lax.axis_index("dp") * ROWS + jnp.arange(ROWS, dtype=jnp.int32)
    cosine, sine_table = rope_tables(query_pos)
    cosine, sine_table = cosine.T, sine_table.T
    routes_t, length = routes[0].T, lengths.reshape(1, 1)
    gains = [gain.reshape(1, -1) for gain in (attn_gain, query_gain, key_gain, ffn_gain)]
    weights = (w_query, w_key, w_value, w_output)
    router_rows = w_router.T
    ffn_in, hidden, mixed_t, queries, log_total, normed, query_raw, key_raw, kv_all, cot_all = forward(
        tokens[0], cotangent[0], routes_t, length, cosine, sine_table, gains, weights
    )
    returned, mixed_parts, gate_up_w_grad, down_grad = moe(ffn_in, cot_all, router_rows, w_gate, w_up, w_down)
    gate_up_sum, down_w_sum = lax.psum((gate_up_w_grad, down_grad), "dp")
    mixed_out, token_grad, late, early_small, late_small, output_w_sum = backward(
        (
            returned, hidden, ffn_in, cotangent[0], tokens[0], normed, query_raw, key_raw, mixed_t, queries,
            log_total, routes_t, length, cosine, sine_table, *gains, router_rows,
        ),
        (mixed_parts, kv_all, *weights),
    )
    weight_sums, small_sums = total_everywhere(late, late_small)
    weight_sums = weight_sums.astype(jnp.float32)
    query_w_sum = jnp.concatenate([weight_sums[:1024], weight_sums[1024:2048]], axis=1)
    key_w_sum, value_w_sum = weight_sums[2048:3072], weight_sums[3072:4096]
    router_sum = early_small[:EXPERTS].T
    ffn_gain_sum, attn_gain_sum, query_gain_sum = early_small[EXPERTS], small_sums[0], small_sums[1]
    key_gain_sum = small_sums[2, :512]
    gate_w_sum = gate_up_sum[:, :, :512].astype(jnp.float32)
    up_w_sum = gate_up_sum[:, :, 512:].astype(jnp.float32)
    down_w_sum = down_w_sum.astype(jnp.float32)
    return (
        mixed_out[None],
        token_grad[None],
        attn_gain_sum,
        query_w_sum,
        key_w_sum,
        value_w_sum,
        query_gain_sum,
        key_gain_sum,
        output_w_sum,
        ffn_gain_sum,
        router_sum,
        gate_w_sum,
        up_w_sum,
        down_w_sum,
    )


def solution(mesh):
    return jax.shard_map(
        body,
        mesh=mesh,
        in_specs=(
            P("expert", "dp", None),
            P("expert", "dp", None),
            P("expert"),
            P("expert", "dp", None),
            P(),
            P(),
            P(),
            P(),
            P(),
            P(),
            P(),
            P(),
            P(),
            P("expert", None, None),
            P("expert", None, None),
            P("expert", None, None),
        ),
        out_specs=(
            P("expert", "dp", None),
            P("expert", "dp", None),
            P(),
            P(),
            P(),
            P(),
            P(),
            P(),
            P(),
            P(),
            P(),
            P("expert", None, None),
            P("expert", None, None),
            P("expert", None, None),
        ),
        check_vma=False,
    )
```

```python
import math

import jax
import jax.numpy as jnp
from jax import lax
from jax.experimental import pallas as pl
from jax.experimental.pallas import tpu as pltpu
from jax.sharding import PartitionSpec as P

HEADS = 16
KV_HEADS = 8
HEAD_DIM = 64
EXPERTS = 32
TOPK = 8
CAP = 80


epsilon = 1e-06


def rope_tables(positions):
    steps_half = jnp.arange(HEAD_DIM // 2).astype(jnp.float32)
    inverse = jnp.exp(steps_half * (-2.0 * math.log(10000.0) / HEAD_DIM))
    angles = positions.astype(jnp.float32)[:, None] * inverse[None, :]
    return (jnp.cos(angles), jnp.sin(angles))


RING = 4
ROWS = 256
EXTRA = 16
FULL = ROWS + EXTRA
GROUP = 4 * CAP
MESH = pl.DeviceIdType.MESH


def dot_nn(a, b):
    return jnp.dot(a, b, preferred_element_type=jnp.float32)


def dot_nt(a, b):
    return lax.dot_general(a, b, (((1,), (1,)), ((), ())), preferred_element_type=jnp.float32)


def dot_tn(a, b):
    return lax.dot_general(a, b, (((0,), (0,)), ((), ())), preferred_element_type=jnp.float32)


class Torus:
    def __init__(self):
        self.dp = lax.axis_index("dp")
        expert = lax.axis_index("expert")
        self.expert = expert
        self.z, self.y = expert // RING, expert % RING

    def block(self, dz, dy):
        return ((self.z + dz + RING) % RING) * RING + (self.y + dy + RING) % RING

    def near(self, axis, step):
        return (self.dp, self.block(step, 0) if axis == "z" else self.block(0, step))

    def along(self, axis, other, step):
        return self.block(step, other) if axis == "z" else self.block(other, step)

    def neighbours(self):
        return [self.near(axis, step) for axis in "yz" for step in (1, -1)]


class Gather:
    def __init__(self, torus, buffer, send, recv, number, axis, other, low, first, second, stride):
        self.torus, self.buffer, self.send, self.recv = torus, buffer, send, recv
        self.number, self.axis, self.other, self.stride = number, axis, other, stride
        self.whole, self.front, self.rear = (low, first + second), (low, first), (low + first, second)

    def copy(self, which, offset, part, step):
        at = self.torus.along(self.axis, self.other, offset) * self.stride + part[0]
        rows = self.buffer.at[pl.ds(pl.multiple_of(at, 16), part[1])]
        return pltpu.make_async_remote_copy(
            src_ref=rows,
            dst_ref=rows,
            send_sem=self.send.at[self.number, which],
            recv_sem=self.recv.at[self.number, which],
            device_id=self.torus.near(self.axis, step),
            device_id_type=MESH,
        )

    def first(self):
        self.copy(0, 0, self.whole, 1).start()
        self.copy(1, 0, self.whole, -1).start()

    def second(self):
        self.copy(0, -1, self.whole, 1).wait_recv()
        self.copy(2, -1, self.front, 1).start()
        self.copy(1, 1, self.whole, -1).wait_recv()
        self.copy(3, 1, self.rear, -1).start()

    def third(self):
        self.copy(2, 2, self.front, 1).wait_recv()
        self.copy(3, 2, self.rear, -1).wait_recv()

    def drain(self):
        self.copy(0, 0, self.whole, 1).wait_send()
        self.copy(1, 0, self.whole, -1).wait_send()
        self.copy(2, -1, self.front, 1).wait_send()
        self.copy(3, 1, self.rear, -1).wait_send()


class Scatter:
    def __init__(self, torus, sums, landing, send, recv, number, base, axis, other, low, first, second):
        self.torus, self.sums, self.landing, self.send, self.recv = torus, sums, landing, send, recv
        self.number, self.axis, self.other = number, axis, other
        self.low, self.parts = low, (first, second)
        self.size = first + second
        self.slots = (base, base + first, base + self.size, base + 2 * self.size)

    def rows(self, which):
        if which == 0:
            return self.low, self.parts[0]
        if which == 1:
            return self.low + self.parts[0], self.parts[1]
        return self.low, self.size

    def at(self, offset):
        return self.torus.along(self.axis, self.other, offset)

    def copy(self, which):
        start, size = self.rows(which)
        offset = (2, 2, 1, -1)[which]
        return pltpu.make_async_remote_copy(
            src_ref=self.sums.at[self.at(offset), pl.ds(start, size)],
            dst_ref=self.landing.at[pl.ds(self.slots[which], size)],
            send_sem=self.send.at[self.number, which],
            recv_sem=self.recv.at[self.number, which],
            device_id=self.torus.near(self.axis, (1, -1, 1, -1)[which]),
            device_id_type=MESH,
        )

    def add(self, which, offset):
        start, size = self.rows(which)
        block = self.at(offset)

        @pl.loop(0, size // 16)
        def _(k):
            here = pl.ds(pl.multiple_of(start + k * 16, 16), 16)
            there = pl.ds(pl.multiple_of(self.slots[which] + k * 16, 16), 16)
            total = self.sums[block, here].astype(jnp.float32) + self.landing[there].astype(jnp.float32)
            self.sums[block, here] = total.astype(jnp.bfloat16)

    def first(self):
        self.copy(0).start()
        self.copy(1).start()

    def second(self):
        self.copy(0).wait_recv()
        self.add(0, 1)
        self.copy(2).start()
        self.copy(1).wait_recv()
        self.add(1, -1)
        self.copy(3).start()

    def third(self, put=None):
        self.copy(2).wait_recv()
        self.copy(3).wait_recv()
        block = self.at(0)

        @pl.loop(0, self.size // 16)
        def _(k):
            here = pl.ds(pl.multiple_of(self.low + k * 16, 16), 16)
            left = pl.ds(pl.multiple_of(self.slots[2] + k * 16, 16), 16)
            right = pl.ds(pl.multiple_of(self.slots[3] + k * 16, 16), 16)
            total = (
                self.sums[block, here].astype(jnp.float32)
                + self.landing[left].astype(jnp.float32)
                + self.landing[right].astype(jnp.float32)
            )
            if put is None:
                self.sums[block, here] = total.astype(jnp.bfloat16)
            else:
                put(here, total)

    def drain(self):
        for which in range(4):
            self.copy(which).wait_send()


def moe_kernel(
    ffn, cot, wr, w_gate, w_up, w_down,
    ret, mixed, grad_g, grad_u, grad_d,
    rows, sums, wgu, wd, held, pair, inner, dgu, mixing, back, cotv, before, chosen, gate_rows, grad_rows, stage,
    ag_send, ag_recv, rs_send, rs_recv, w_sem, cot_sem, stage_sem, half_sem, credit,
):
    torus = Torus()
    barrier = pltpu.get_barrier_semaphore()
    for device in torus.neighbours():
        pl.semaphore_signal(barrier, inc=1, device_id=device, device_id_type=MESH)

    weights = [
        pltpu.make_async_copy(w_gate, wgu.at[:, :, pl.ds(0, 512)], w_sem.at[0]),
        pltpu.make_async_copy(w_up, wgu.at[:, :, pl.ds(512, 512)], w_sem.at[1]),
        pltpu.make_async_copy(w_down, wd, w_sem.at[2]),
    ]
    for copy in weights:
        copy.start()

    def group_z(g):
        return (torus.z + g + (g // 2) * (1 - 2 * (g % 2))) % RING

    def cot_copy(g):
        return pltpu.make_async_copy(cot.at[pl.ds(pl.multiple_of(group_z(g) * RING * FULL, 16), RING * FULL)], cotv, cot_sem)

    cot_copy(0).start()
    rows[pl.ds(pl.multiple_of(torus.expert * ROWS, ROWS), ROWS)] = ffn[...]
    pl.semaphore_wait(barrier, 4)

    def gather(number, axis, other, low):
        return Gather(torus, rows, ag_send, ag_recv, number, axis, other, low, ROWS // 4, ROWS // 4, ROWS)

    a_first = gather(0, "y", 0, 0)
    b_first = gather(1, "z", 0, ROWS // 2)
    a_second = {d: gather(2 + d % RING, "z", d, 0) for d in (0, 1, -1, 2)}
    b_second = {d: gather(6 + d % RING, "y", d, ROWS // 2) for d in (0, 1, -1, 2)}
    gathers = [a_first, b_first, *a_second.values(), *b_second.values()]

    a_first.first()
    b_first.first()
    b_second[0].first()
    a_second[0].first()
    a_first.second()
    b_first.second()
    for d in (1, -1):
        b_second[d].first()
        a_second[d].first()
    a_first.third()
    b_first.third()
    b_second[2].first()
    a_second[2].first()
    for copy in weights:
        copy.wait()

    earlier = lax.broadcasted_iota(jnp.int32, (ROWS, ROWS), 0) < lax.broadcasted_iota(jnp.int32, (ROWS, ROWS), 1)
    before[...] = jnp.where(earlier, 1.0, 0.0).astype(jnp.bfloat16)
    slot_at = lax.broadcasted_iota(jnp.int32, (CAP, ROWS), 0).astype(jnp.float32)

    def stage_copy(slot, target):
        return pltpu.make_async_copy(stage.at[slot], target, stage_sem.at[slot])

    def half_copy(slot, half, target):
        return pltpu.make_async_copy(stage.at[slot, :, pl.ds(half * 512, 512)], target, half_sem.at[slot, half])

    expert_rows = lax.broadcasted_iota(jnp.int32, (EXPERTS, ROWS), 0)

    @pl.loop(0, 4)
    def _(g):
        @pl.when(g == 0)
        def _():
            b_second[0].second()
            a_second[0].second()
            b_second[0].third()

        @pl.when(g == 1)
        def _():
            for d in (1, -1):
                b_second[d].second()
                a_second[d].second()
            a_second[2].second()
            b_second[1].third()

        @pl.when(g == 2)
        def _():
            b_second[2].second()
            b_second[-1].third()

        @pl.when(g == 3)
        def _():
            for d in (0, 1, -1, 2):
                a_second[d].third()
            b_second[2].third()

        cot_copy(g).wait()
        first_source = group_z(g) * RING

        @pl.loop(0, 4)
        def _(j):
            source = first_source + j
            block = rows[pl.ds(pl.multiple_of(source * ROWS, ROWS), ROWS)]
            laid = cotv[pl.ds(pl.multiple_of(j * FULL, 16), EXTRA)].astype(jnp.float32)
            member = jnp.concatenate([laid[:8, q * ROWS : (q + 1) * ROWS] for q in range(4)], axis=0)
            named = member > 0.5
            slots = dot_nn(member.astype(jnp.bfloat16), before[...])
            slots = jnp.where(named, slots, -1.0)
            logits = jnp.where(named, dot_nt(wr[...], block), -1e30)
            weight = jnp.where(named, jnp.exp(logits - jnp.max(logits, axis=0, keepdims=True)), 0.0)
            gates = weight / jnp.sum(weight, axis=0, keepdims=True)
            picked = []
            for e in range(2):
                own = jnp.sum(
                    jnp.where(expert_rows == torus.expert * 2 + e, slots, 0.0), axis=0, keepdims=True
                )
                picked.append(jnp.where(slot_at == own, 1.0, 0.0))
            both = jnp.concatenate(picked, axis=0).astype(jnp.bfloat16)
            chosen[j] = both
            grad_block = cotv[pl.ds(pl.multiple_of(j * FULL + EXTRA, 16), ROWS)]
            took = dot_nn(both, jnp.concatenate([block, grad_block], axis=1)).astype(jnp.bfloat16)
            here = pl.ds(pl.multiple_of(j * CAP, 16), CAP)
            there = pl.ds(pl.multiple_of(g * GROUP + j * CAP, 16), CAP)
            for e in range(2):
                own = jnp.sum(
                    jnp.where(expert_rows == torus.expert * 2 + e, gates, 0.0), axis=0, keepdims=True
                )
                of_rows = jnp.sum(picked[e] * own, axis=1, keepdims=True)
                gate_rows[e, here] = jnp.broadcast_to(of_rows, (CAP, 128))
                held[e, there] = took[e * CAP : (e + 1) * CAP, :1024]
                mixing[e, here] = took[e * CAP : (e + 1) * CAP, 1024:]

        @pl.when(g < 3)
        def _():
            cot_copy(g + 1).start()

        @pl.when(g == 3)
        def _():
            for one in gathers:
                one.drain()
            for device in torus.neighbours():
                pl.semaphore_signal(credit, inc=1, device_id=device, device_id_type=MESH)

        @pl.loop(0, 2)
        def _(e):
            there = pl.ds(pl.multiple_of(g * GROUP, 16), GROUP)
            both = dot_nn(held[e, there], wgu[e])
            gate, up = both[:, :512], both[:, 512:]
            sig = jax.nn.sigmoid(gate)
            silu = gate * sig
            act = (silu * up).astype(jnp.bfloat16)
            inner[e, there] = act
            out = dot_nn(act, wd[e]).astype(jnp.bfloat16).astype(jnp.float32)
            grad = mixing[e].astype(jnp.float32)
            weight = gate_rows[e][:, :1]
            grad_rows[e] = jnp.broadcast_to(jnp.sum(grad * out, axis=1, keepdims=True), (GROUP, 128))
            pair[e, there] = (weight * grad).astype(jnp.bfloat16)
            mixing[e] = (weight * out).astype(jnp.bfloat16)
            inner_grad = dot_nt(pair[e, there], wd[e])
            dgu[e, there, :512] = (inner_grad * up * sig * (1.0 + gate * (1.0 - sig))).astype(jnp.bfloat16)
            dgu[e, there, 512:] = (inner_grad * silu).astype(jnp.bfloat16)
            back[e] = dot_nt(dgu[e, there], wgu[e]).astype(jnp.bfloat16)

        @pl.loop(0, 4)
        def _(j):
            source = first_source + j
            both = chosen[j]
            picked = both.astype(jnp.float32)
            here = pl.ds(pl.multiple_of(j * CAP, 16), CAP)
            compact = jnp.concatenate(
                [jnp.concatenate([back[e, here], mixing[e, here]], axis=1) for e in range(2)], axis=0
            )
            spread = dot_tn(both, compact).astype(jnp.bfloat16)
            sums[source, pl.ds(EXTRA, ROWS)] = spread[:, :1024]
            grads = jnp.zeros((EXPERTS, ROWS), jnp.float32)
            for e in range(2):
                own = jnp.sum(
                    picked[e * CAP : (e + 1) * CAP] * grad_rows[e, here][:, :1], axis=0, keepdims=True
                )
                grads = grads + jnp.where(expert_rows == torus.expert * 2 + e, own, 0.0)
            laid = jnp.concatenate([grads[8 * q : 8 * q + 8] for q in range(4)], axis=1)
            sums[source, pl.ds(0, EXTRA)] = jnp.concatenate([laid, jnp.zeros_like(laid)], axis=0).astype(
                jnp.bfloat16
            )
            slot = j % 2

            @pl.when((g > 0) | (j > 1))
            def _():
                stage_copy(slot, mixed.at[source]).wait()

            stage[slot] = spread[:, 1024:]
            stage_copy(slot, mixed.at[source]).start()

    pl.semaphore_wait(credit, 4)

    order = (2, 1, -1, 0)
    a_lead = {}
    b_lead = {}
    for n, d in enumerate(order):
        a_lead[d] = Scatter(
            torus, sums, rows, rs_send, rs_recv, n, n * 384, "z", d, 0, 64, 64
        )
        b_lead[d] = Scatter(
            torus, sums, rows, rs_send, rs_recv, 4 + n, 1920 + n * 432, "y", d, 128, 80, 64
        )
    a_last = Scatter(torus, sums, rows, rs_send, rs_recv, 8, 4 * 384, "y", 0, 0, 64, 64)
    b_last = Scatter(torus, sums, rows, rs_send, rs_recv, 9, 1920 + 4 * 432, "z", 0, 128, 80, 64)

    def write_pair(low, high):
        @pl.loop(low, high)
        def _(k):
            slot = k % 2
            e, c = k // 4, k % 4

            @pl.when(k < 2)
            def _():
                stage_copy(slot, grad_d.at[0, pl.ds(0, 256)]).wait()

            @pl.when(k >= 2)
            def _():
                half_copy(slot, 0, grad_g.at[0, pl.ds(0, 256)]).wait()
                half_copy(slot, 1, grad_u.at[0, pl.ds(0, 256)]).wait()

            columns = pl.ds(pl.multiple_of(c * 256, 256), 256)
            stage[slot] = dot_tn(held[e, :, columns], dgu[e]).astype(jnp.bfloat16)
            half_copy(slot, 0, grad_g.at[e, columns]).start()
            half_copy(slot, 1, grad_u.at[e, columns]).start()

    def write_down():
        @pl.loop(0, 4)
        def _(k):
            slot = k % 2
            e, c = k // 2, k % 2

            @pl.when(k < 2)
            def _():
                half_copy(slot, 0, grad_g.at[0, pl.ds(0, 256)]).wait()
                half_copy(slot, 1, grad_u.at[0, pl.ds(0, 256)]).wait()

            @pl.when(k >= 2)
            def _():
                stage_copy(slot, grad_d.at[0, pl.ds(0, 256)]).wait()

            columns = pl.ds(pl.multiple_of(c * 256, 256), 256)
            stage[slot] = dot_tn(inner[e, :, columns], pair[e]).astype(jnp.bfloat16)
            stage_copy(slot, grad_d.at[e, columns]).start()

    for d in order:
        b_lead[d].first()
        a_lead[d].first()
    write_pair(0, 4)
    for d in order:
        b_lead[d].second()
        a_lead[d].second()
    write_pair(4, 8)
    write_down()
    for slot in range(2):
        stage_copy(slot, grad_d.at[0, pl.ds(0, 256)]).wait()
    for d in order:
        b_lead[d].third()
        a_lead[d].third()
        if d == 2:
            b_last.first()
            a_last.first()
    b_last.second()
    a_last.second()

    def put(at, total):
        ret[at] = total

    b_last.third(put)
    a_last.third(put)
    for one in [*a_lead.values(), *b_lead.values(), a_last, b_last]:
        one.drain()


def moe(ffn_in, cot_all, router_rows, w_gate, w_up, w_down):
    vmem, hbm = pl.BlockSpec(memory_space=pltpu.VMEM), pl.BlockSpec(memory_space=pl.ANY)
    low, total = jnp.bfloat16, 4 * GROUP
    return pl.pallas_call(
        moe_kernel,
        name="moe",
        out_shape=(
            jax.ShapeDtypeStruct((FULL, 1024), jnp.float32),
            jax.ShapeDtypeStruct((16, ROWS, 1024), low),
            jax.ShapeDtypeStruct((2, 1024, 512), low),
            jax.ShapeDtypeStruct((2, 1024, 512), low),
            jax.ShapeDtypeStruct((2, 512, 1024), low),
        ),
        in_specs=[vmem, hbm, vmem, hbm, hbm, hbm],
        out_specs=(vmem, hbm, hbm, hbm, hbm),
        scratch_shapes=[
            pltpu.VMEM((16 * ROWS, 1024), low),
            pltpu.VMEM((16, FULL, 1024), low),
            pltpu.VMEM((2, 1024, 1024), low),
            pltpu.VMEM((2, 512, 1024), low),
            pltpu.VMEM((2, total, 1024), low),
            pltpu.VMEM((2, total, 1024), low),
            pltpu.VMEM((2, total, 512), low),
            pltpu.VMEM((2, total, 1024), low),
            pltpu.VMEM((2, GROUP, 1024), low),
            pltpu.VMEM((2, GROUP, 1024), low),
            pltpu.VMEM((4 * FULL, 1024), low),
            pltpu.VMEM((ROWS, ROWS), low),
            pltpu.VMEM((4, 2 * CAP, ROWS), low),
            pltpu.VMEM((2, GROUP, 128), jnp.float32),
            pltpu.VMEM((2, GROUP, 128), jnp.float32),
            pltpu.VMEM((2, ROWS, 1024), low),
            pltpu.SemaphoreType.DMA((10, 4)),
            pltpu.SemaphoreType.DMA((10, 4)),
            pltpu.SemaphoreType.DMA((10, 4)),
            pltpu.SemaphoreType.DMA((10, 4)),
            pltpu.SemaphoreType.DMA((3,)),
            pltpu.SemaphoreType.DMA,
            pltpu.SemaphoreType.DMA((2,)),
            pltpu.SemaphoreType.DMA((2, 2)),
            pltpu.SemaphoreType.REGULAR,
        ],
        compiler_params=pltpu.CompilerParams(
            collective_id=1, has_side_effects=True, vmem_limit_bytes=63 * 2**20
        ),
        cost_estimate=pl.CostEstimate(flops=50 * 10**9, bytes_accessed=40 * 10**6, transcendentals=2 * 10**6),
    )(ffn_in, cot_all, router_rows, w_gate, w_up, w_down)


def everywhere():
    dp, expert = lax.axis_index("dp"), lax.axis_index("expert")
    here = {"x": dp // 2, "core": dp % 2, "z": expert // RING, "y": expert % RING}

    def device(axis, step):
        there = dict(here)
        size = 2 if axis == "core" else RING
        there[axis] = (here[axis] + step + size) % size
        return (there["x"] * 2 + there["core"], there["z"] * RING + there["y"])

    return here, device


def rms_scale(values):
    return lax.rsqrt(jnp.mean(values * values, axis=-1, keepdims=True) + epsilon)


def as_row(gain):
    return gain[...].astype(jnp.float32).reshape(1, -1)


def turned_rows(values, cosine, sine):
    front, back = values[: HEAD_DIM // 2], values[HEAD_DIM // 2 :]
    return jnp.concatenate([front * cosine - back * sine, back * cosine + front * sine], axis=0)


def kv_order(here, step):
    turn = step // 2
    return (turn % 2) * (3 - turn // 2) + (1 - turn % 2) * (turn // 2)


class Keys:
    def __init__(self, here, device, blocks, send, recv):
        self.here, self.device, self.blocks, self.send, self.recv = here, device, blocks, send, recv
        self.lines = blocks.shape[1]

    def copy(self, which):
        half = self.lines // 2
        offset, start, size, axis, step = (
            (0, 0, self.lines, "core", 1),
            (0, 0, self.lines, "x", 1),
            (0, 0, self.lines, "x", -1),
            (-1, 0, half, "x", 1),
            (1, half, half, "x", -1),
            (-1, 0, self.lines, "core", 1),
            (1, 0, self.lines, "core", 1),
            (2, 0, self.lines, "core", 1),
        )[which]
        block = (self.here["x"] + offset + RING) % RING * 2 + self.here["core"]
        part = self.blocks.at[block, pl.ds(start, size)]
        return pltpu.make_async_remote_copy(
            src_ref=part,
            dst_ref=part,
            send_sem=self.send.at[which],
            recv_sem=self.recv.at[which],
            device_id=self.device(axis, step),
            device_id_type=MESH,
        )

    def start(self, *which):
        for one in which:
            self.copy(one).start()

    def arrive(self, *which):
        for one in which:
            self.copy(one).wait_recv()

    def drain(self):
        for one in range(8):
            self.copy(one).wait_send()


def forward_kernel(
    tokens, cot, routes_t, length, cosine, sine, attn_gain, query_gain, key_gain, ffn_gain,
    w_query, w_key, w_value, w_output,
    ffn_in, hidden, mixed_t, queries, log_total, normed, query_raw, key_raw, kv_all, cot_all,
    wq, wk, wv, wo, kv, turned, most, total, mixed, packed,
    ag_send, ag_recv, kv_send, kv_recv, w_sem, kv_sem, own_sem,
):
    torus = Torus()
    here, device = everywhere()
    me = here["x"] * 2 + here["core"]
    barrier = pltpu.get_barrier_semaphore()
    peers = [*torus.neighbours(), device("core", 1), device("x", 1), device("x", -1)]
    for peer in peers:
        pl.semaphore_signal(barrier, inc=1, device_id=peer, device_id_type=MESH)
    loads = [
        pltpu.make_async_copy(source, target, w_sem.at[n])
        for n, (source, target) in enumerate(((w_query, wq), (w_key, wk), (w_value, wv), (w_output, wo)))
    ]
    for load in loads:
        load.start()

    expert_rows = lax.broadcasted_iota(jnp.int32, (EXPERTS, ROWS), 0)
    member = jnp.zeros((EXPERTS, ROWS), jnp.float32)
    for k in range(TOPK):
        member = member + jnp.where(expert_rows == routes_t[pl.ds(k, 1), :], 1.0, 0.0)
    laid = jnp.concatenate([member[8 * q : 8 * q + 8] for q in range(4)], axis=1)
    packed[...] = jnp.concatenate([laid, jnp.zeros_like(laid)], axis=0).astype(jnp.bfloat16)
    first_row = pl.multiple_of(torus.expert * FULL, 16)
    owns = [
        pltpu.make_async_copy(packed, cot_all.at[pl.ds(first_row, EXTRA)], own_sem.at[0]),
        pltpu.make_async_copy(cot, cot_all.at[pl.ds(pl.multiple_of(first_row + EXTRA, 16), ROWS)], own_sem.at[1]),
    ]
    for copy in owns:
        copy.start()
    for copy in owns:
        copy.wait()
    pl.semaphore_wait(barrier, len(peers))

    def gather(number, axis, other, low, first, second):
        return Gather(torus, cot_all, ag_send, ag_recv, number, axis, other, low, first, second, FULL)

    a_first = gather(0, "y", 0, 0, 64, 64)
    b_first = gather(1, "z", 0, 128, 80, 64)
    a_second = {d: gather(2 + d % RING, "z", d, 0, 64, 64) for d in (0, 1, -1, 2)}
    b_second = {d: gather(6 + d % RING, "y", d, 128, 80, 64) for d in (0, 1, -1, 2)}
    gathers = [a_first, b_first, *a_second.values(), *b_second.values()]
    a_first.first()
    b_first.first()
    b_second[0].first()
    a_second[0].first()

    @pl.loop(0, 4)
    def _(n):
        at = pl.ds(pl.multiple_of(n * 64, 64), 64)
        rows = tokens[at].astype(jnp.float32)
        normed[at] = (rows * rms_scale(rows) * as_row(attn_gain)).astype(jnp.bfloat16)

    for load in loads:
        load.wait()

    keys = Keys(here, device, kv, kv_send, kv_recv)
    key_raw[...] = dot_nn(normed[...], wk[...])
    scaled = key_raw[...]
    scaled = (scaled * rms_scale(scaled) * as_row(key_gain)).T
    for j in range(KV_HEADS):
        head = turned_rows(scaled[j * 64 : j * 64 + 64], cosine[...], sine[...])
        kv[me, pl.ds(j * 64, 64)] = head.astype(jnp.bfloat16)
    kv[me, pl.ds(512, 512)] = dot_nn(normed[...], wv[...]).T.astype(jnp.bfloat16)
    keys.start(0, 1, 2)
    query_raw[...] = dot_nn(normed[...], wq[...])
    scaled = query_raw[...]
    turned[...] = (scaled * rms_scale(scaled) * as_row(query_gain)).T

    for j in range(KV_HEADS):
        for r in range(2):
            head = turned[j * 128 + r * 64 : j * 128 + r * 64 + 64]
            head = turned_rows(head, cosine[...], sine[...])
            queries[j, :, r * ROWS : (r + 1) * ROWS] = (head * HEAD_DIM**-0.5).astype(jnp.bfloat16)

    a_first.second()
    b_first.second()
    for d in (1, -1):
        b_second[d].first()
        a_second[d].first()

    key_at = lax.broadcasted_iota(jnp.int32, (ROWS, 2 * ROWS), 0)
    query_at = lax.broadcasted_iota(jnp.int32, (ROWS, 2 * ROWS), 1) % ROWS
    valid = (key_at <= query_at) & (key_at + me * ROWS < length[...])

    def heads_of(block):
        keys_here = [kv[block, j * 64 : j * 64 + 64] for j in range(KV_HEADS)]
        values_here = [kv[block, 512 + j * 64 : 576 + j * 64] for j in range(KV_HEADS)]
        return keys_here, values_here

    keys_here, values_here = heads_of(me)
    scores = [jnp.where(valid, dot_tn(keys_here[j], queries[j]), -1e30) for j in range(KV_HEADS)]
    tops = [jnp.max(one, axis=0, keepdims=True) for one in scores]
    probs = [jnp.exp(one - top) for one, top in zip(scores, tops)]
    parts = [dot_nn(one, prob.astype(jnp.bfloat16)) for one, prob in zip(values_here, probs)]
    for j in range(KV_HEADS):
        most[j] = tops[j]
        total[j] = jnp.sum(probs[j], axis=0, keepdims=True)
        mixed[j] = parts[j]

    @pl.loop(1, 8)
    def _(step):
        @pl.when(step == 1)
        def _():
            a_first.third()
            b_first.third()
            b_second[2].first()
            a_second[2].first()
            keys.arrive(0)

        @pl.when(step == 2)
        def _():
            keys.arrive(1)
            keys.start(3, 5)
            keys.arrive(2)
            keys.start(4, 6)
            b_second[0].second()
            a_second[0].second()

        @pl.when(step == 3)
        def _():
            keys.arrive(5)
            for d in (1, -1):
                b_second[d].second()
                a_second[d].second()

        @pl.when(step == 5)
        def _():
            keys.arrive(3, 4)
            keys.start(7)
            keys.arrive(6)
            b_second[2].second()
            a_second[2].second()

        @pl.when(step == 7)
        def _():
            keys.arrive(7)

        block = (here["x"] + kv_order(here, step) + RING) % RING * 2 + (here["core"] + step) % 2

        @pl.when(block < me)
        def _():
            keys_here, values_here = heads_of(block)
            before = [most[j] for j in range(KV_HEADS)]
            shares = [total[j] for j in range(KV_HEADS)]
            sums = [mixed[j] for j in range(KV_HEADS)]
            scores = [dot_tn(keys_here[j], queries[j]) for j in range(KV_HEADS)]
            tops = [jnp.maximum(old, jnp.max(one, axis=0, keepdims=True)) for old, one in zip(before, scores)]
            probs = [jnp.exp(one - top) for one, top in zip(scores, tops)]
            less = [jnp.exp(old - top) for old, top in zip(before, tops)]
            parts = [dot_nn(one, prob.astype(jnp.bfloat16)) for one, prob in zip(values_here, probs)]
            for j in range(KV_HEADS):
                most[j] = tops[j]
                total[j] = shares[j] * less[j] + jnp.sum(probs[j], axis=0, keepdims=True)
                mixed[j] = sums[j] * less[j] + parts[j]

    save = pltpu.make_async_copy(kv, kv_all, kv_sem)
    save.start()

    for j in range(KV_HEADS):
        share = total[j]
        log_total[j] = most[j] + jnp.log(share)
        head = (mixed[j] * (1.0 / share)).astype(jnp.bfloat16)
        for r in range(2):
            mixed_t[j * 128 + r * 64 : j * 128 + r * 64 + 64, :] = head[:, r * ROWS : (r + 1) * ROWS]

    hidden[...] = dot_tn(mixed_t[...], wo[...])

    @pl.loop(0, 4)
    def _(n):
        at = pl.ds(pl.multiple_of(n * 64, 64), 64)
        rows = hidden[at] + tokens[at].astype(jnp.float32)
        hidden[at] = rows
        ffn_in[at] = (rows * rms_scale(rows) * as_row(ffn_gain)).astype(jnp.bfloat16)

    for d in (0, 1, -1, 2):
        a_second[d].third()
        b_second[d].third()
    save.wait()
    keys.drain()
    for one in gathers:
        one.drain()


def forward(tokens, cot, routes_t, length, cosine, sine, gains, weights):
    vmem, hbm = pl.BlockSpec(memory_space=pltpu.VMEM), pl.BlockSpec(memory_space=pl.ANY)
    low, wide = jnp.bfloat16, jnp.float32
    shape = jax.ShapeDtypeStruct
    return pl.pallas_call(
        forward_kernel,
        name="forward",
        out_shape=(
            shape((ROWS, 1024), low),
            shape((ROWS, 1024), wide),
            shape((1024, ROWS), low),
            shape((KV_HEADS, HEAD_DIM, 2 * ROWS), low),
            shape((KV_HEADS, 1, 2 * ROWS), wide),
            shape((ROWS, 1024), low),
            shape((ROWS, 1024), wide),
            shape((ROWS, 512), wide),
            shape((8, 1024, ROWS), low),
            shape((16 * FULL, 1024), low),
        ),
        in_specs=[vmem] * 10 + [hbm] * 4,
        out_specs=(vmem,) * 8 + (hbm, hbm),
        scratch_shapes=[
            pltpu.VMEM((1024, 1024), low),
            pltpu.VMEM((1024, 512), low),
            pltpu.VMEM((1024, 512), low),
            pltpu.VMEM((1024, 1024), low),
            pltpu.VMEM((8, 1024, ROWS), low),
            pltpu.VMEM((1024, ROWS), wide),
            pltpu.VMEM((KV_HEADS, 1, 2 * ROWS), wide),
            pltpu.VMEM((KV_HEADS, 1, 2 * ROWS), wide),
            pltpu.VMEM((KV_HEADS, HEAD_DIM, 2 * ROWS), wide),
            pltpu.VMEM((EXTRA, 1024), low),
            pltpu.SemaphoreType.DMA((10, 4)),
            pltpu.SemaphoreType.DMA((10, 4)),
            pltpu.SemaphoreType.DMA((8,)),
            pltpu.SemaphoreType.DMA((8,)),
            pltpu.SemaphoreType.DMA((4,)),
            pltpu.SemaphoreType.DMA,
            pltpu.SemaphoreType.DMA((2,)),
        ],
        compiler_params=pltpu.CompilerParams(
            collective_id=3, has_side_effects=True, vmem_limit_bytes=56 * 2**20
        ),
    )(tokens, cot, routes_t, length, cosine, sine, *gains, *weights)


ORDERS = (("x", "y", "z"), ("y", "z", "x"), ("z", "x", "y"))
STREAMS = ((0, 768), (768, 768), (1536, 512))


class Total:
    def __init__(self, here, device, buffer, shift, final, landing, work, send, recv, number, stream):
        self.here, self.device, self.buffer, self.shift, self.final = here, device, buffer, shift, final
        self.landing, self.work = landing, work
        self.send, self.recv, self.number, self.order = send, recv, number, ORDERS[(stream + number // 3) % 3]
        self.start, self.rows = STREAMS[stream]
        first = self.start + self.start * 9 // 8
        r = self.rows
        self.lands = (first, first + r, first + r + 3 * (r // 4), first + r + 3 * (r // 4) + 3 * (r // 16))

    def own(self):
        return self.here["core"] * 2048 + self.start

    def copy(self, which, source, target, axis, step):
        return pltpu.make_async_remote_copy(
            src_ref=source,
            dst_ref=target,
            send_sem=self.send.at[self.number, which],
            recv_sem=self.recv.at[self.number, which],
            device_id=self.device(axis, step),
            device_id_type=MESH,
        )

    def held(self, at, size):
        return self.buffer.at[pl.ds(pl.multiple_of(at + self.shift, 16), size)]

    def ready(self, at, size):
        return self.final.at[pl.ds(pl.multiple_of(at, 16), size)]

    def land(self, stage, n, size):
        return self.landing.at[pl.ds(self.lands[stage] + n * size, size)]

    def copies(self, stage):
        r, own = self.rows, self.own()
        a, b, c = self.order
        ia, ib = self.here[a], self.here[b]
        second = own + ia * (r // 4)
        third = second + ib * (r // 16)
        if stage == 0:
            there = (1 - self.here["core"]) * 2048 + self.start
            return [self.copy(0, self.held(there, r), self.land(0, 0, r), "core", 1)]
        if stage == 6:
            return [self.copy(16, self.ready(own, r), self.ready(own, r), "core", 1)]
        found = []
        for d in (1, 2, 3):
            if stage == 1:
                source, target, axis = self.held(own + (ia + d) % RING * (r // 4), r // 4), self.land(1, d - 1, r // 4), a
            elif stage == 2:
                source = self.held(second + (ib + d) % RING * (r // 16), r // 16)
                target, axis = self.land(2, d - 1, r // 16), b
            elif stage == 3:
                source = self.work.at[self.number, pl.ds(0, r // 16)]
                target, axis = self.land(3, d - 1, r // 16), c
            elif stage == 4:
                source, target, axis = self.ready(third, r // 16), self.ready(third, r // 16), b
            else:
                source, target, axis = self.ready(second, r // 4), self.ready(second, r // 4), a
            found.append(self.copy(1 + (stage - 1) * 3 + d - 1, source, target, axis, d))
        return found

    def begin(self, stage):
        for copy in self.copies(stage):
            copy.start()

    def add(self, stage, load, store, size, count):
        step = 64 if size % 64 == 0 else 16

        @pl.loop(0, size // step)
        def _(k):
            at = k * step
            total = load(at, step).astype(jnp.float32)
            for n in range(count):
                land = pl.ds(pl.multiple_of(self.lands[stage] + n * size + at, 16), step)
                total = total + self.landing[land].astype(jnp.float32)
            store(at, step, total.astype(jnp.bfloat16))

    def finish(self, stage):
        for copy in self.copies(stage):
            copy.wait_recv()
        if stage > 3:
            return
        r, own = self.rows, self.own()
        a, b, _ = self.order
        second = own + self.here[a] * (r // 4)
        third = second + self.here[b] * (r // 16)
        first = (own, second, third, third)[stage] + self.shift

        def in_place(at, step, *value):
            lines = pl.ds(pl.multiple_of(first + at, 16), step)
            if not value:
                return self.buffer[lines]
            self.buffer[lines] = value[0]

        def in_work(at, step, *value):
            lines = pl.ds(pl.multiple_of(at, 16), step)
            if not value:
                return self.work[self.number, lines]
            self.work[self.number, lines] = value[0]

        def in_final(at, step, value):
            self.final[pl.ds(pl.multiple_of(third + at, 16), step)] = value

        if stage == 0:
            self.add(0, in_place, in_place, r, 1)
        elif stage == 1:
            self.add(1, in_place, in_place, r // 4, 3)
        elif stage == 2:
            self.add(2, in_place, in_work, r // 16, 3)
        else:
            self.add(3, in_work, in_final, r // 16, 3)

    def drain(self):
        for stage in range(7):
            for copy in self.copies(stage):
                copy.wait_send()


class Small:
    STAGES = (("core", (1,)), ("x", (1, 2, 3)), ("y", (1, 2, 3)), ("z", (1, 2, 3)))

    def __init__(self, device, value, landing, send, recv):
        self.device, self.value, self.landing, self.send, self.recv = device, value, landing, send, recv

    def copies(self, stage):
        axis, steps = self.STAGES[stage]
        first = sum(len(s) for _, s in self.STAGES[:stage])
        return [
            pltpu.make_async_remote_copy(
                src_ref=self.value.at[stage],
                dst_ref=self.landing.at[first + n],
                send_sem=self.send.at[first + n],
                recv_sem=self.recv.at[first + n],
                device_id=self.device(axis, step),
                device_id_type=MESH,
            )
            for n, step in enumerate(steps)
        ]

    def begin(self, stage):
        for copy in self.copies(stage):
            copy.start()

    def finish(self, stage):
        for copy in self.copies(stage):
            copy.wait_recv()
        first = sum(len(s) for _, s in self.STAGES[:stage])
        total = self.value[stage]
        for n in range(len(self.STAGES[stage][1])):
            total = total + self.landing[first + n]
        self.value[stage + 1] = total

    def drain(self):
        for stage in range(4):
            for copy in self.copies(stage):
                copy.wait_send()


class Line:
    def __init__(self, here, device):
        self.here, self.device = here, device

    def along(self, axis, other, step):
        return (self.here["x"] + step + RING) % RING

    def near(self, axis, step):
        return self.device("x", step)


def rms_back(values, gain, grad):
    scale = rms_scale(values)
    lifted = gain * grad
    inner = jnp.mean(values * lifted, axis=-1, keepdims=True)
    return scale * lifted - values * (scale * scale * scale) * inner, jnp.sum(
        grad * values * scale, axis=0, keepdims=True
    )


def turned_back(grads, cosine, sine):
    front, back = grads[: HEAD_DIM // 2], grads[HEAD_DIM // 2 :]
    return jnp.concatenate([front * cosine + back * sine, back * cosine - front * sine], axis=0)


def backward_kernel(
    hidden, ffn_in, cot, tokens, normed, key_raw, mixed_t, queries, log_total,
    routes_t, length, cosine, sine, attn_gain, query_gain, key_gain, ffn_gain, router_rows,
    returned_all, query_raw_all, mixed_parts, kv_all, w_query, w_key, w_value, w_output,
    mixed_out, token_grad, early_small, late_small, query_sum, key_sum, value_sum, output_sum,
    sums, rows, returned, square, kv, hidden_grad, result, branch, grads, delta, query_grad, turned,
    for_mate, from_mate, kv_sums, kv_rows, key_low, value_low,
    held, finals, landing, work, values, small_rows, late_values, late_rows,
    rs_send, rs_recv, mate_send, mate_recv, kv_send, kv_recv, ar_send, ar_recv, small_send, small_recv, load_sem, out_sem,
):
    torus = Torus()
    here, device = everywhere()
    me = here["x"] * 2 + here["core"]
    barrier = pltpu.get_barrier_semaphore()
    peers = [device("core", 1)] + [device(axis, d) for axis in "xyz" for d in (1, 2, 3)]
    for peer in peers:
        pl.semaphore_signal(barrier, inc=1, device_id=peer, device_id_type=MESH)
    loads = [
        pltpu.make_async_copy(source, target, load_sem.at[n])
        for n, (source, target) in enumerate(
            ((returned_all, returned), (w_output, square), (mixed_parts, sums), (kv_all, kv))
        )
    ]
    for load in loads:
        load.start()

    expert_rows = lax.broadcasted_iota(jnp.int32, (EXPERTS, ROWS), 0)
    member = jnp.zeros((EXPERTS, ROWS), jnp.float32)
    for k in range(TOPK):
        member = member + jnp.where(expert_rows == routes_t[pl.ds(k, 1), :], 1.0, 0.0)
    named = member > 0.5
    logits = jnp.where(named, dot_nt(router_rows[...], ffn_in[...]), -1e30)
    weight = jnp.where(named, jnp.exp(logits - jnp.max(logits, axis=0, keepdims=True)), 0.0)
    gates = weight / jnp.sum(weight, axis=0, keepdims=True)
    loads[0].wait()
    gate_grad = jnp.concatenate([returned[:8, q * ROWS : (q + 1) * ROWS] for q in range(4)], axis=0)
    logit_grad = (gates * (gate_grad - jnp.sum(gates * gate_grad, axis=0, keepdims=True))).astype(jnp.bfloat16)
    result[...] = dot_tn(logit_grad, router_rows[...])
    values[0, :EXPERTS] = dot_nn(logit_grad, ffn_in[...])

    def ffn_part(n, gain_grad):
        at = pl.ds(pl.multiple_of(n * 64, 64), 64)
        grad = result[at] + returned[pl.ds(pl.multiple_of(n * 64 + EXTRA, 16), 64)]
        part, more = rms_back(hidden[at], as_row(ffn_gain), grad)
        part = part + cot[at].astype(jnp.float32)
        hidden_grad[at] = part
        branch[at] = part.astype(jnp.bfloat16)
        return gain_grad + more

    gain_grad = lax.fori_loop(0, 4, ffn_part, jnp.zeros((1, 1024), jnp.float32))
    values[0, EXPERTS:] = jnp.concatenate([gain_grad, jnp.zeros((7, 1024), jnp.float32)], axis=0)

    loads[1].wait()
    turned[...] = dot_nt(square[...], branch[...])
    next_load = pltpu.make_async_copy(w_query, square, load_sem.at[6])
    next_load.start()
    query_raw = returned.at[pl.ds(0, ROWS)]
    raw_load = pltpu.make_async_copy(query_raw_all, query_raw, load_sem.at[7])
    raw_load.start()

    for j in range(KV_HEADS):
        for r in range(2):
            at = slice(j * 128 + r * 64, j * 128 + r * 64 + 64)
            low = turned[at].astype(jnp.bfloat16)
            grads[j, :, r * ROWS : (r + 1) * ROWS] = low
            delta[j, :, r * ROWS : (r + 1) * ROWS] = jnp.sum(
                low.astype(jnp.float32) * mixed_t[at].astype(jnp.float32), axis=0, keepdims=True
            )
        query_grad[j] = jnp.zeros((HEAD_DIM, 2 * ROWS), jnp.float32)

    @pl.loop(0, 4)
    def _(n):
        at = pl.ds(pl.multiple_of(n * 256, 256), 256)
        part = dot_nn(mixed_t[at], branch[...]).astype(jnp.bfloat16)
        for q in range(4):
            held[pl.ds(pl.multiple_of(q * 1024 + n * 256, 256), 256)] = part[:, q * 256 : (q + 1) * 256]

    for load in loads[2:]:
        load.wait()
    pl.semaphore_wait(barrier, len(peers))

    def reduction(number, buffer, shift):
        return [
            Total(
                here, device, buffer, shift, finals.at[number], landing.at[number], work,
                ar_send, ar_recv, 3 * number + s, s,
            )
            for s in range(3)
        ]

    early, of_query, of_keys = reduction(0, held, 0), reduction(1, kv, 0), reduction(2, kv, 4096)
    few = Small(device, values, small_rows, small_send.at[0], small_recv.at[0])
    late_few = Small(device, late_values, late_rows, small_send.at[1], small_recv.at[1])
    order = (2, 1, -1, 0)
    leads = []
    for n, d in enumerate(order):
        leads.append(Scatter(torus, sums, rows, rs_send, rs_recv, n, n * 384, "z", d, 0, 64, 64))
        leads.append(Scatter(torus, sums, rows, rs_send, rs_recv, 4 + n, (5 + n) * 384, "y", d, 128, 64, 64))
    lasts = [
        Scatter(torus, sums, rows, rs_send, rs_recv, 8, 4 * 384, "y", 0, 0, 64, 64),
        Scatter(torus, sums, rows, rs_send, rs_recv, 9, 9 * 384, "z", 0, 128, 64, 64),
    ]
    ring = Scatter(Line(here, device), kv_sums, kv_rows, kv_send, kv_recv, 0, 0, "x", 0, 0, 512, 512)

    for one in early:
        one.begin(0)
    few.begin(0)
    for one in leads:
        one.first()

    def onward(streams, stage, small=None):
        for one in streams:
            one.finish(stage)
            if stage < 6:
                one.begin(stage + 1)
        if small is not None and stage < 4:
            small.finish(stage)
            if stage < 3:
                small.begin(stage + 1)

    def early_step(stage):
        onward(early, stage, few)

    def write_out(number, column, target, at):
        block = finals.at[number, pl.ds(column * 1024, 1024)]
        return pltpu.make_async_copy(block, target.at[:, pl.ds(at * 256, 256)], out_sem.at[number, column])

    outs = [write_out(0, q, output_sum, q) for q in range(4)]
    outs += [write_out(1, q, query_sum, q) for q in range(4)]
    outs += [write_out(2, q, key_sum, q) for q in range(2)]
    outs += [write_out(2, 2 + q, value_sum, q) for q in range(2)]

    def mate_copy(turn, at):
        return pltpu.make_async_remote_copy(
            src_ref=for_mate.at[turn % 2],
            dst_ref=from_mate.at[at],
            send_sem=mate_send.at[turn],
            recv_sem=mate_recv.at[turn],
            device_id=device("core", 1),
            device_id_type=MESH,
        )

    key_at = lax.broadcasted_iota(jnp.int32, (ROWS, 2 * ROWS), 0)
    query_at = lax.broadcasted_iota(jnp.int32, (ROWS, 2 * ROWS), 1) % ROWS
    valid = (key_at <= query_at) & (key_at + me * ROWS < length[...])

    def block_grads(block, target, at, masked):
        for group in range(2):
            heads = range(4 * group, 4 * group + 4)
            key_heads = [kv[pl.ds(pl.multiple_of(block * 1024 + j * 64, 64), 64)] for j in heads]
            value_heads = [kv[pl.ds(pl.multiple_of(block * 1024 + 512 + j * 64, 64), 64)] for j in heads]
            probs = [jnp.exp(dot_tn(one, queries[j]) - log_total[j]) for one, j in zip(key_heads, heads)]
            if masked:
                probs = [jnp.where(valid, one, 0.0) for one in probs]
            probs_grads = [dot_tn(one, grads[j]) for one, j in zip(value_heads, heads)]
            lows = [
                (one * (grad - delta[j])).astype(jnp.bfloat16) for one, grad, j in zip(probs, probs_grads, heads)
            ]
            key_parts = [dot_nt(queries[j], low).astype(jnp.bfloat16) for low, j in zip(lows, heads)]
            value_parts = [
                dot_nt(grads[j], one.astype(jnp.bfloat16)).astype(jnp.bfloat16) for one, j in zip(probs, heads)
            ]
            query_parts = [dot_nn(one, low) for one, low in zip(key_heads, lows)]
            for n, j in enumerate(heads):
                target[at, j * 64 : j * 64 + 64] = key_parts[n]
                target[at, 512 + j * 64 : 576 + j * 64] = value_parts[n]
                query_grad[j] += query_parts[n]

    def from_other(turn, at):
        mate_copy(turn, at).wait_recv()

        @pl.loop(0, 16)
        def _(n):
            lines = pl.ds(pl.multiple_of(n * 64, 64), 64)
            total = kv_sums[at, lines].astype(jnp.float32) + from_mate[at, lines].astype(jnp.float32)
            kv_sums[at, lines] = total.astype(jnp.bfloat16)

    def turn_x(turn):
        offset = (1 - turn % 2) * (2 + turn // 2) + (turn % 2) * (1 - turn // 2)
        return (here["x"] + offset + RING) % RING

    @pl.loop(0, 4)
    def _(turn):
        @pl.when(turn == 1)
        def _():
            early_step(0)
            for one in leads:
                one.second()

        @pl.when(turn == 2)
        def _():
            early_step(2)

        @pl.when(turn == 3)
        def _():
            early_step(4)
            for one in leads[:2]:
                one.third()
            for one in lasts:
                one.first()

        at = turn_x(turn)
        other = at * 2 + 1 - here["core"]

        @pl.when(turn >= 2)
        def _():
            mate_copy(turn - 2, at).wait_send()

        @pl.when(other < me)
        def _():
            block_grads(other, for_mate, turn % 2, False)

        @pl.when(other >= me)
        def _():
            for_mate[turn % 2] = jnp.zeros((1024, ROWS), jnp.bfloat16)

        mate_copy(turn, at).start()

        @pl.when(turn == 1)
        def _():
            early_step(1)

        @pl.when(turn == 2)
        def _():
            early_step(3)

        @pl.when(turn == 3)
        def _():
            early_step(5)
            for one in leads[2:]:
                one.third()
            for one in lasts:
                one.second()

        own = at * 2 + here["core"]

        @pl.when(own < me)
        def _():
            block_grads(own, kv_sums, at, False)

        @pl.when(own > me)
        def _():
            kv_sums[at] = jnp.zeros((1024, ROWS), jnp.bfloat16)

        @pl.when(own == me)
        def _():
            block_grads(own, kv_sums, at, True)

        from_other(turn, at)

        @pl.when(turn == 0)
        def _():
            ring.first()

        @pl.when(turn == 2)
        def _():
            ring.second()

    for j in range(KV_HEADS):
        for r in range(2):
            head = query_grad[j, :, r * ROWS : (r + 1) * ROWS] * HEAD_DIM**-0.5
            turned[j * 128 + r * 64 : j * 128 + r * 64 + 64] = turned_back(head, cosine[...], sine[...])

    raw_load.wait()
    result[...] = turned[...].T

    def query_part(n, gain_grad):
        at = pl.ds(pl.multiple_of(n * 64, 64), 64)
        part, more = rms_back(query_raw[at], as_row(query_gain), result[at])
        branch[at] = part.astype(jnp.bfloat16)
        return gain_grad + more

    query_gain_grad = lax.fori_loop(0, 4, query_part, jnp.zeros((1, 1024), jnp.float32))

    @pl.loop(0, 4)
    def _(n):
        columns = pl.ds(pl.multiple_of(n * 256, 256), 256)
        part = dot_tn(normed[:, columns], branch[...]).astype(jnp.bfloat16)
        for q in range(4):
            kv[pl.ds(pl.multiple_of(q * 1024 + n * 256, 256), 256)] = part[:, q * 256 : (q + 1) * 256]

    for one in of_query:
        one.begin(0)
    early_step(6)
    for q in range(4):
        outs[q].start()
    early_small[...] = values[4]

    def put(at, total):
        turned[at] = total

    ring.third(put)
    for j in range(KV_HEADS):
        turned[j * 64 : j * 64 + 64] = turned_back(turned[j * 64 : j * 64 + 64], cosine[...], sine[...])
    part, key_gain_grad = rms_back(key_raw[...], as_row(key_gain), turned[:512].T)
    key_low[...] = part.astype(jnp.bfloat16)
    value_low[...] = turned[512:].T.astype(jnp.bfloat16)

    @pl.loop(0, 4)
    def _(n):
        columns = pl.ds(pl.multiple_of(n * 256, 256), 256)
        part = dot_tn(normed[:, columns], jnp.concatenate([key_low[...], value_low[...]], axis=1)).astype(jnp.bfloat16)
        for q in range(4):
            kv[pl.ds(pl.multiple_of(4096 + q * 1024 + n * 256, 256), 256)] = part[:, q * 256 : (q + 1) * 256]

    for one in of_keys:
        one.begin(0)
    onward(of_query, 0)
    next_load.wait()
    result[...] = dot_nt(branch[...], square[...])
    last_loads = [
        pltpu.make_async_copy(w_key, square.at[:, pl.ds(0, 512)], load_sem.at[4]),
        pltpu.make_async_copy(w_value, square.at[:, pl.ds(512, 512)], load_sem.at[5]),
    ]
    for load in last_loads:
        load.start()
    onward(of_keys, 0)
    onward(of_query, 1)
    for load in last_loads:
        load.wait()
    result[...] += dot_nt(jnp.concatenate([key_low[...], value_low[...]], axis=1), square[...])
    onward(of_keys, 1)
    onward(of_query, 2)

    def token_part(n, gain_grad):
        at = pl.ds(pl.multiple_of(n * 64, 64), 64)
        part, more = rms_back(tokens[at].astype(jnp.float32), as_row(attn_gain), result[at])
        token_grad[at] = (hidden_grad[at] + part).astype(jnp.bfloat16)
        return gain_grad + more

    attn_gain_grad = lax.fori_loop(0, 4, token_part, jnp.zeros((1, 1024), jnp.float32))
    key_wide = jnp.concatenate([key_gain_grad, jnp.zeros((1, 512), jnp.float32)], axis=1)
    late_values[0] = jnp.concatenate(
        [attn_gain_grad, query_gain_grad, key_wide, jnp.zeros((5, 1024), jnp.float32)], axis=0
    )
    late_few.begin(0)
    onward(of_keys, 2)
    onward(of_query, 3, None)
    late_few.finish(0)
    late_few.begin(1)

    def put_mixed(at, total):
        mixed_out[at] = (hidden[at] + total).astype(jnp.bfloat16)

    for one in lasts:
        one.third(put_mixed)
    onward(of_keys, 3)
    onward(of_query, 4)
    late_few.finish(1)
    late_few.begin(2)
    onward(of_keys, 4)
    onward(of_query, 5)
    late_few.finish(2)
    late_few.begin(3)
    onward(of_keys, 5)
    onward(of_query, 6)
    for q in range(4, 8):
        outs[q].start()
    late_few.finish(3)
    late_small[...] = late_values[4]
    onward(of_keys, 6)
    for q in range(8, 12):
        outs[q].start()
    for one in [*leads, *lasts, ring, *early, *of_query, *of_keys, few, late_few]:
        one.drain()
    for turn in (2, 3):
        mate_copy(turn, 0).wait_send()
    for out in outs:
        out.wait()


def backward(smalls, larges):
    vmem, hbm = pl.BlockSpec(memory_space=pltpu.VMEM), pl.BlockSpec(memory_space=pl.ANY)
    low, wide = jnp.bfloat16, jnp.float32
    shape = jax.ShapeDtypeStruct
    dma = pltpu.SemaphoreType.DMA
    return pl.pallas_call(
        backward_kernel,
        name="backward",
        out_shape=(
            shape((ROWS, 1024), low),
            shape((ROWS, 1024), low),
            shape((40, 1024), wide),
            shape((8, 1024), wide),
            shape((1024, 1024), low),
            shape((1024, 512), low),
            shape((1024, 512), low),
            shape((1024, 1024), low),
        ),
        in_specs=[vmem] * len(smalls) + [hbm] * len(larges),
        out_specs=(vmem,) * 4 + (hbm,) * 4,
        scratch_shapes=[
            pltpu.VMEM((16, ROWS, 1024), low),
            pltpu.VMEM((10 * 384, 1024), low),
            pltpu.VMEM((FULL, 1024), wide),
            pltpu.VMEM((1024, 1024), low),
            pltpu.VMEM((8 * 1024, ROWS), low),
            pltpu.VMEM((ROWS, 1024), wide),
            pltpu.VMEM((ROWS, 1024), wide),
            pltpu.VMEM((ROWS, 1024), low),
            pltpu.VMEM((KV_HEADS, HEAD_DIM, 2 * ROWS), low),
            pltpu.VMEM((KV_HEADS, 1, 2 * ROWS), wide),
            pltpu.VMEM((KV_HEADS, HEAD_DIM, 2 * ROWS), wide),
            pltpu.VMEM((1024, ROWS), wide),
            pltpu.VMEM((2, 1024, ROWS), low),
            pltpu.VMEM((4, 1024, ROWS), low),
            pltpu.VMEM((4, 1024, ROWS), low),
            pltpu.VMEM((3072, ROWS), low),
            pltpu.VMEM((ROWS, 512), low),
            pltpu.VMEM((ROWS, 512), low),
            pltpu.VMEM((4096, 256), low),
            pltpu.VMEM((3, 4096, 256), low),
            pltpu.VMEM((3, 4352, 256), low),
            pltpu.VMEM((9, 48, 256), low),
            pltpu.VMEM((5, 40, 1024), wide),
            pltpu.VMEM((10, 40, 1024), wide),
            pltpu.VMEM((5, 8, 1024), wide),
            pltpu.VMEM((10, 8, 1024), wide),
            dma((10, 4)),
            dma((10, 4)),
            dma((4,)),
            dma((4,)),
            dma((1, 4)),
            dma((1, 4)),
            dma((9, 17)),
            dma((9, 17)),
            dma((2, 10)),
            dma((2, 10)),
            dma((8,)),
            dma((3, 4)),
        ],
        compiler_params=pltpu.CompilerParams(
            collective_id=4, has_side_effects=True, vmem_limit_bytes=66000000
        ),
        cost_estimate=pl.CostEstimate(flops=100 * 10**9, bytes_accessed=60 * 10**6, transcendentals=8 * 10**6),
    )(*smalls, *larges)


def body(
    tokens,
    cotangent,
    lengths,
    routes,
    attn_gain,
    w_query,
    w_key,
    w_value,
    query_gain,
    key_gain,
    w_output,
    ffn_gain,
    w_router,
    w_gate,
    w_up,
    w_down,
):
    query_pos = lax.axis_index("dp") * ROWS + jnp.arange(ROWS, dtype=jnp.int32)
    cosine, sine_table = rope_tables(query_pos)
    cosine, sine_table = cosine.T, sine_table.T
    routes_t, length = routes[0].T, lengths.reshape(1, 1)
    gains = [attn_gain, query_gain, key_gain, ffn_gain]
    weights = (w_query, w_key, w_value, w_output)
    router_rows = w_router.T
    ffn_in, hidden, mixed_t, queries, log_total, normed, query_raw, key_raw, kv_all, cot_all = forward(
        tokens[0], cotangent[0], routes_t, length, cosine, sine_table, gains, weights
    )
    returned, mixed_parts, *expert_grads = moe(ffn_in, cot_all, router_rows, w_gate, w_up, w_down)
    expert_sums = lax.psum(tuple(expert_grads), "dp")
    mixed_out, token_grad, early_small, late_small, *weight_sums = backward(
        (
            hidden, ffn_in, cotangent[0], tokens[0], normed, key_raw, mixed_t, queries, log_total, routes_t,
            length, cosine, sine_table, *gains, router_rows,
        ),
        (returned, query_raw, mixed_parts, kv_all.reshape(8 * 1024, ROWS), *weights),
    )
    query_w_sum, key_w_sum, value_w_sum, output_w_sum = [part.astype(jnp.float32) for part in weight_sums]
    gate_w_sum, up_w_sum, down_w_sum = [part.astype(jnp.float32) for part in expert_sums]
    router_sum = early_small[:EXPERTS].T
    ffn_gain_sum, attn_gain_sum, query_gain_sum = early_small[EXPERTS], late_small[0], late_small[1]
    key_gain_sum = late_small[2, :512]
    return (
        mixed_out[None],
        token_grad[None],
        attn_gain_sum,
        query_w_sum,
        key_w_sum,
        value_w_sum,
        query_gain_sum,
        key_gain_sum,
        output_w_sum,
        ffn_gain_sum,
        router_sum,
        gate_w_sum,
        up_w_sum,
        down_w_sum,
    )


def solution(mesh):
    return jax.shard_map(
        body,
        mesh=mesh,
        in_specs=(
            P("expert", "dp", None),
            P("expert", "dp", None),
            P("expert"),
            P("expert", "dp", None),
            P(),
            P(),
            P(),
            P(),
            P(),
            P(),
            P(),
            P(),
            P(),
            P("expert", None, None),
            P("expert", None, None),
            P("expert", None, None),
        ),
        out_specs=(
            P("expert", "dp", None),
            P("expert", "dp", None),
            P(),
            P(),
            P(),
            P(),
            P(),
            P(),
            P(),
            P(),
            P(),
            P("expert", None, None),
            P("expert", None, None),
            P("expert", None, None),
        ),
        check_vma=False,
    )
```

```python
import math

import jax
import jax.numpy as jnp
from jax import lax
from jax.experimental import pallas as pl
from jax.experimental.pallas import tpu as pltpu
from jax.sharding import PartitionSpec as P

HEADS = 16
KV_HEADS = 8
HEAD_DIM = 64
EXPERTS = 32
TOPK = 8
CAP = 80


epsilon = 1e-06


def rope_tables(positions):
    steps_half = jnp.arange(HEAD_DIM // 2).astype(jnp.float32)
    inverse = jnp.exp(steps_half * (-2.0 * math.log(10000.0) / HEAD_DIM))
    angles = positions.astype(jnp.float32)[:, None] * inverse[None, :]
    return (jnp.cos(angles), jnp.sin(angles))


RING = 4
ROWS = 256
EXTRA = 16
FULL = ROWS + EXTRA
GROUP = 4 * CAP
MESH = pl.DeviceIdType.MESH


def dot_nn(a, b):
    return jnp.dot(a, b, preferred_element_type=jnp.float32)


def dot_nt(a, b):
    return lax.dot_general(a, b, (((1,), (1,)), ((), ())), preferred_element_type=jnp.float32)


def dot_tn(a, b):
    return lax.dot_general(a, b, (((0,), (0,)), ((), ())), preferred_element_type=jnp.float32)


class Torus:
    def __init__(self):
        self.dp = lax.axis_index("dp")
        expert = lax.axis_index("expert")
        self.expert = expert
        self.z, self.y = expert // RING, expert % RING

    def block(self, dz, dy):
        return ((self.z + dz + RING) % RING) * RING + (self.y + dy + RING) % RING

    def near(self, axis, step):
        return (self.dp, self.block(step, 0) if axis == "z" else self.block(0, step))

    def along(self, axis, other, step):
        return self.block(step, other) if axis == "z" else self.block(other, step)

    def neighbours(self):
        return [self.near(axis, step) for axis in "yz" for step in (1, -1)]


class Gather:
    def __init__(self, torus, buffer, send, recv, number, axis, other, low, first, second, stride):
        self.torus, self.buffer, self.send, self.recv = torus, buffer, send, recv
        self.number, self.axis, self.other, self.stride = number, axis, other, stride
        self.whole, self.front, self.rear = (low, first + second), (low, first), (low + first, second)

    def copy(self, which, offset, part, step):
        at = self.torus.along(self.axis, self.other, offset) * self.stride + part[0]
        rows = self.buffer.at[pl.ds(pl.multiple_of(at, 16), part[1])]
        return pltpu.make_async_remote_copy(
            src_ref=rows,
            dst_ref=rows,
            send_sem=self.send.at[self.number, which],
            recv_sem=self.recv.at[self.number, which],
            device_id=self.torus.near(self.axis, step),
            device_id_type=MESH,
        )

    def first(self):
        self.copy(0, 0, self.whole, 1).start()
        self.copy(1, 0, self.whole, -1).start()

    def second(self):
        self.copy(0, -1, self.whole, 1).wait_recv()
        self.copy(2, -1, self.front, 1).start()
        self.copy(1, 1, self.whole, -1).wait_recv()
        self.copy(3, 1, self.rear, -1).start()

    def third(self):
        self.copy(2, 2, self.front, 1).wait_recv()
        self.copy(3, 2, self.rear, -1).wait_recv()

    def drain(self):
        self.copy(0, 0, self.whole, 1).wait_send()
        self.copy(1, 0, self.whole, -1).wait_send()
        self.copy(2, -1, self.front, 1).wait_send()
        self.copy(3, 1, self.rear, -1).wait_send()


class Scatter:
    def __init__(self, torus, sums, landing, send, recv, number, base, axis, other, low, first, second):
        self.torus, self.sums, self.landing, self.send, self.recv = torus, sums, landing, send, recv
        self.number, self.axis, self.other = number, axis, other
        self.low, self.parts = low, (first, second)
        self.size = first + second
        self.slots = (base, base + first, base + self.size, base + 2 * self.size)

    def rows(self, which):
        if which == 0:
            return self.low, self.parts[0]
        if which == 1:
            return self.low + self.parts[0], self.parts[1]
        return self.low, self.size

    def at(self, offset):
        return self.torus.along(self.axis, self.other, offset)

    def copy(self, which):
        start, size = self.rows(which)
        offset = (2, 2, 1, -1)[which]
        return pltpu.make_async_remote_copy(
            src_ref=self.sums.at[self.at(offset), pl.ds(start, size)],
            dst_ref=self.landing.at[pl.ds(self.slots[which], size)],
            send_sem=self.send.at[self.number, which],
            recv_sem=self.recv.at[self.number, which],
            device_id=self.torus.near(self.axis, (1, -1, 1, -1)[which]),
            device_id_type=MESH,
        )

    def add(self, which, offset):
        start, size = self.rows(which)
        block = self.at(offset)

        @pl.loop(0, size // 16)
        def _(k):
            here = pl.ds(pl.multiple_of(start + k * 16, 16), 16)
            there = pl.ds(pl.multiple_of(self.slots[which] + k * 16, 16), 16)
            total = self.sums[block, here].astype(jnp.float32) + self.landing[there].astype(jnp.float32)
            self.sums[block, here] = total.astype(jnp.bfloat16)

    def first(self):
        self.copy(0).start()
        self.copy(1).start()

    def second(self):
        self.copy(0).wait_recv()
        self.add(0, 1)
        self.copy(2).start()
        self.copy(1).wait_recv()
        self.add(1, -1)
        self.copy(3).start()

    def third(self, put=None):
        self.copy(2).wait_recv()
        self.copy(3).wait_recv()
        block = self.at(0)

        @pl.loop(0, self.size // 16)
        def _(k):
            here = pl.ds(pl.multiple_of(self.low + k * 16, 16), 16)
            left = pl.ds(pl.multiple_of(self.slots[2] + k * 16, 16), 16)
            right = pl.ds(pl.multiple_of(self.slots[3] + k * 16, 16), 16)
            total = (
                self.sums[block, here].astype(jnp.float32)
                + self.landing[left].astype(jnp.float32)
                + self.landing[right].astype(jnp.float32)
            )
            if put is None:
                self.sums[block, here] = total.astype(jnp.bfloat16)
            else:
                put(here, total)

    def drain(self):
        for which in range(4):
            self.copy(which).wait_send()


def moe_kernel(
    ffn, cot, wr, w_gate, w_up, w_down,
    ret, mixed, own_gu, own_down,
    rows, sums, wgu, wd, held, pair, inner, dgu, mixing, back, cotv, before, chosen, gate_rows, grad_rows, stage,
    mate_rows, gu_sums, down_sums, ring_rows,
    ag_send, ag_recv, rs_send, rs_recv, w_sem, cot_sem, stage_sem, mate_send, mate_recv, x_send, x_recv, credit,
):
    torus = Torus()
    place, place_of = everywhere()
    barrier = pltpu.get_barrier_semaphore()
    peers = [*torus.neighbours(), place_of("core", 1), place_of("x", 1), place_of("x", -1)]
    for device in peers:
        pl.semaphore_signal(barrier, inc=1, device_id=device, device_id_type=MESH)

    weights = [
        pltpu.make_async_copy(w_gate, wgu.at[:, :, pl.ds(0, 512)], w_sem.at[0]),
        pltpu.make_async_copy(w_up, wgu.at[:, :, pl.ds(512, 512)], w_sem.at[1]),
        pltpu.make_async_copy(w_down, wd, w_sem.at[2]),
    ]
    for copy in weights:
        copy.start()

    def group_z(g):
        return (torus.z + g + (g // 2) * (1 - 2 * (g % 2))) % RING

    def cot_copy(g):
        return pltpu.make_async_copy(cot.at[pl.ds(pl.multiple_of(group_z(g) * RING * FULL, 16), RING * FULL)], cotv, cot_sem)

    cot_copy(0).start()
    rows[pl.ds(pl.multiple_of(torus.expert * ROWS, ROWS), ROWS)] = ffn[...]
    pl.semaphore_wait(barrier, len(peers))

    def gather(number, axis, other, low):
        return Gather(torus, rows, ag_send, ag_recv, number, axis, other, low, ROWS // 4, ROWS // 4, ROWS)

    a_first = gather(0, "y", 0, 0)
    b_first = gather(1, "z", 0, ROWS // 2)
    a_second = {d: gather(2 + d % RING, "z", d, 0) for d in (0, 1, -1, 2)}
    b_second = {d: gather(6 + d % RING, "y", d, ROWS // 2) for d in (0, 1, -1, 2)}
    gathers = [a_first, b_first, *a_second.values(), *b_second.values()]

    a_first.first()
    b_first.first()
    b_second[0].first()
    a_second[0].first()
    a_first.second()
    b_first.second()
    for d in (1, -1):
        b_second[d].first()
        a_second[d].first()
    a_first.third()
    b_first.third()
    b_second[2].first()
    a_second[2].first()
    for copy in weights:
        copy.wait()

    earlier = lax.broadcasted_iota(jnp.int32, (ROWS, ROWS), 0) < lax.broadcasted_iota(jnp.int32, (ROWS, ROWS), 1)
    before[...] = jnp.where(earlier, 1.0, 0.0).astype(jnp.bfloat16)
    slot_at = lax.broadcasted_iota(jnp.int32, (CAP, ROWS), 0).astype(jnp.float32)

    def stage_copy(slot, target):
        return pltpu.make_async_copy(stage.at[slot], target, stage_sem.at[slot])

    expert_rows = lax.broadcasted_iota(jnp.int32, (EXPERTS, ROWS), 0)

    @pl.loop(0, 4)
    def _(g):
        @pl.when(g == 0)
        def _():
            b_second[0].second()
            a_second[0].second()
            b_second[0].third()

        @pl.when(g == 1)
        def _():
            for d in (1, -1):
                b_second[d].second()
                a_second[d].second()
            a_second[2].second()
            b_second[1].third()

        @pl.when(g == 2)
        def _():
            b_second[2].second()
            b_second[-1].third()

        @pl.when(g == 3)
        def _():
            for d in (0, 1, -1, 2):
                a_second[d].third()
            b_second[2].third()

        cot_copy(g).wait()
        first_source = group_z(g) * RING

        @pl.loop(0, 4)
        def _(j):
            source = first_source + j
            block = rows[pl.ds(pl.multiple_of(source * ROWS, ROWS), ROWS)]
            laid = cotv[pl.ds(pl.multiple_of(j * FULL, 16), EXTRA)].astype(jnp.float32)
            member = jnp.concatenate([laid[:8, q * ROWS : (q + 1) * ROWS] for q in range(4)], axis=0)
            named = member > 0.5
            slots = dot_nn(member.astype(jnp.bfloat16), before[...])
            slots = jnp.where(named, slots, -1.0)
            logits = jnp.where(named, dot_nt(wr[...], block), -1e30)
            weight = jnp.where(named, jnp.exp(logits - jnp.max(logits, axis=0, keepdims=True)), 0.0)
            gates = weight / jnp.sum(weight, axis=0, keepdims=True)
            picked = []
            for e in range(2):
                own = jnp.sum(
                    jnp.where(expert_rows == torus.expert * 2 + e, slots, 0.0), axis=0, keepdims=True
                )
                picked.append(jnp.where(slot_at == own, 1.0, 0.0))
            both = jnp.concatenate(picked, axis=0).astype(jnp.bfloat16)
            chosen[j] = both
            grad_block = cotv[pl.ds(pl.multiple_of(j * FULL + EXTRA, 16), ROWS)]
            took = dot_nn(both, jnp.concatenate([block, grad_block], axis=1)).astype(jnp.bfloat16)
            here = pl.ds(pl.multiple_of(j * CAP, 16), CAP)
            there = pl.ds(pl.multiple_of(g * GROUP + j * CAP, 16), CAP)
            for e in range(2):
                own = jnp.sum(
                    jnp.where(expert_rows == torus.expert * 2 + e, gates, 0.0), axis=0, keepdims=True
                )
                of_rows = jnp.sum(picked[e] * own, axis=1, keepdims=True)
                gate_rows[e, here] = jnp.broadcast_to(of_rows, (CAP, 128))
                held[e, there] = took[e * CAP : (e + 1) * CAP, :1024]
                mixing[e, here] = took[e * CAP : (e + 1) * CAP, 1024:]

        @pl.when(g < 3)
        def _():
            cot_copy(g + 1).start()

        @pl.when(g == 3)
        def _():
            for one in gathers:
                one.drain()
            for device in torus.neighbours():
                pl.semaphore_signal(credit, inc=1, device_id=device, device_id_type=MESH)

        @pl.loop(0, 2)
        def _(e):
            there = pl.ds(pl.multiple_of(g * GROUP, 16), GROUP)
            both = dot_nn(held[e, there], wgu[e])
            gate, up = both[:, :512], both[:, 512:]
            sig = jax.nn.sigmoid(gate)
            silu = gate * sig
            act = (silu * up).astype(jnp.bfloat16)
            inner[e, there] = act
            out = dot_nn(act, wd[e]).astype(jnp.bfloat16).astype(jnp.float32)
            grad = mixing[e].astype(jnp.float32)
            weight = gate_rows[e][:, :1]
            grad_rows[e] = jnp.broadcast_to(jnp.sum(grad * out, axis=1, keepdims=True), (GROUP, 128))
            pair[e, there] = (weight * grad).astype(jnp.bfloat16)
            mixing[e] = (weight * out).astype(jnp.bfloat16)
            inner_grad = dot_nt(pair[e, there], wd[e])
            dgu[e, there, :512] = (inner_grad * up * sig * (1.0 + gate * (1.0 - sig))).astype(jnp.bfloat16)
            dgu[e, there, 512:] = (inner_grad * silu).astype(jnp.bfloat16)
            back[e] = dot_nt(dgu[e, there], wgu[e]).astype(jnp.bfloat16)

        @pl.loop(0, 4)
        def _(j):
            source = first_source + j
            both = chosen[j]
            picked = both.astype(jnp.float32)
            here = pl.ds(pl.multiple_of(j * CAP, 16), CAP)
            compact = jnp.concatenate(
                [jnp.concatenate([back[e, here], mixing[e, here]], axis=1) for e in range(2)], axis=0
            )
            spread = dot_tn(both, compact).astype(jnp.bfloat16)
            sums[source, pl.ds(EXTRA, ROWS)] = spread[:, :1024]
            grads = jnp.zeros((EXPERTS, ROWS), jnp.float32)
            for e in range(2):
                own = jnp.sum(
                    picked[e * CAP : (e + 1) * CAP] * grad_rows[e, here][:, :1], axis=0, keepdims=True
                )
                grads = grads + jnp.where(expert_rows == torus.expert * 2 + e, own, 0.0)
            laid = jnp.concatenate([grads[8 * q : 8 * q + 8] for q in range(4)], axis=1)
            sums[source, pl.ds(0, EXTRA)] = jnp.concatenate([laid, jnp.zeros_like(laid)], axis=0).astype(
                jnp.bfloat16
            )
            slot = j % 2

            @pl.when((g > 0) | (j > 1))
            def _():
                stage_copy(slot, mixed.at[source]).wait()

            stage[slot] = spread[:, 1024:]
            stage_copy(slot, mixed.at[source]).start()

    pl.semaphore_wait(credit, 4)

    order = (2, 1, -1, 0)
    a_lead = {}
    b_lead = {}
    for n, d in enumerate(order):
        a_lead[d] = Scatter(
            torus, sums, rows, rs_send, rs_recv, n, n * 384, "z", d, 0, 64, 64
        )
        b_lead[d] = Scatter(
            torus, sums, rows, rs_send, rs_recv, 4 + n, 1920 + n * 432, "y", d, 128, 80, 64
        )
    a_last = Scatter(torus, sums, rows, rs_send, rs_recv, 8, 4 * 384, "y", 0, 0, 64, 64)
    b_last = Scatter(torus, sums, rows, rs_send, rs_recv, 9, 1920 + 4 * 432, "z", 0, 128, 80, 64)

    def chunk(e, k):
        if k < 4:
            return dot_tn(held[e, :, k * 256 : (k + 1) * 256], dgu[e]).astype(jnp.bfloat16)
        return dot_tn(inner[e, :, (k - 4) * 256 : (k - 3) * 256], pair[e]).astype(jnp.bfloat16)

    def mate_copy(k):
        return pltpu.make_async_remote_copy(
            src_ref=stage.at[k % 2],
            dst_ref=mate_rows.at[pl.ds(k * 256, 256)],
            send_sem=mate_send.at[k],
            recv_sem=mate_recv.at[k],
            device_id=place_of("core", 1),
            device_id_type=MESH,
        )

    line = Line(place, place_of)
    rings = [
        Scatter(line, gu_sums, ring_rows, x_send, x_recv, 0, 0, "x", 0, 0, 128, 128),
        Scatter(line, down_sums, ring_rows, x_send, x_recv, 1, 768, "x", 0, 0, 64, 64),
    ]

    for d in order:
        b_lead[d].first()
        a_lead[d].first()
    for k in range(6):
        if k < 2:
            stage_copy(k, mixed.at[0]).wait()
        else:
            mate_copy(k - 2).wait_send()
        stage[k % 2] = chunk(1 - place["core"], k)
        mate_copy(k).start()
        own = chunk(place["core"], k)
        if k < 4:
            gu_sums[k] = own
        else:
            down_sums[2 * k - 8] = own[:128]
            down_sums[2 * k - 7] = own[128:]
    for d in order:
        b_lead[d].second()
        a_lead[d].second()
    for k in range(6):
        mate_copy(k).wait_recv()

        @pl.loop(0, 4)
        def _(n):
            other = mate_rows[pl.ds(pl.multiple_of(k * 256 + n * 64, 64), 64)].astype(jnp.float32)
            if k < 4:
                at = (k, pl.ds(pl.multiple_of(n * 64, 64), 64))
                gu_sums[at] = (gu_sums[at].astype(jnp.float32) + other).astype(jnp.bfloat16)
            else:
                at = (2 * k - 8 + n // 2, pl.ds(pl.multiple_of(n % 2 * 64, 64), 64))
                down_sums[at] = (down_sums[at].astype(jnp.float32) + other).astype(jnp.bfloat16)

    for one in rings:
        one.first()
    for one in rings:
        one.second()
    for d in order:
        b_lead[d].third()
        a_lead[d].third()
        if d == 2:
            b_last.first()
            a_last.first()
    b_last.second()
    a_last.second()

    def put(at, total):
        ret[at] = total

    b_last.third(put)
    a_last.third(put)

    def put_gu(at, total):
        own_gu[at] = total.astype(jnp.bfloat16)

    def put_down(at, total):
        own_down[at] = total.astype(jnp.bfloat16)

    rings[0].third(put_gu)
    rings[1].third(put_down)
    for one in [*a_lead.values(), *b_lead.values(), a_last, b_last, *rings]:
        one.drain()
    for k in (4, 5):
        mate_copy(k).wait_send()


def moe(ffn_in, cot_all, router_rows, w_gate, w_up, w_down):
    vmem, hbm = pl.BlockSpec(memory_space=pltpu.VMEM), pl.BlockSpec(memory_space=pl.ANY)
    low, total = jnp.bfloat16, 4 * GROUP
    return pl.pallas_call(
        moe_kernel,
        name="moe",
        out_shape=(
            jax.ShapeDtypeStruct((FULL, 1024), jnp.float32),
            jax.ShapeDtypeStruct((16, ROWS, 1024), low),
            jax.ShapeDtypeStruct((256, 1024), low),
            jax.ShapeDtypeStruct((128, 1024), low),
        ),
        in_specs=[vmem, hbm, vmem, hbm, hbm, hbm],
        out_specs=(vmem, hbm, vmem, vmem),
        scratch_shapes=[
            pltpu.VMEM((16 * ROWS, 1024), low),
            pltpu.VMEM((16, FULL, 1024), low),
            pltpu.VMEM((2, 1024, 1024), low),
            pltpu.VMEM((2, 512, 1024), low),
            pltpu.VMEM((2, total, 1024), low),
            pltpu.VMEM((2, total, 1024), low),
            pltpu.VMEM((2, total, 512), low),
            pltpu.VMEM((2, total, 1024), low),
            pltpu.VMEM((2, GROUP, 1024), low),
            pltpu.VMEM((2, GROUP, 1024), low),
            pltpu.VMEM((4 * FULL, 1024), low),
            pltpu.VMEM((ROWS, ROWS), low),
            pltpu.VMEM((4, 2 * CAP, ROWS), low),
            pltpu.VMEM((2, GROUP, 128), jnp.float32),
            pltpu.VMEM((2, GROUP, 128), jnp.float32),
            pltpu.VMEM((2, ROWS, 1024), low),
            pltpu.VMEM((6 * 256, 1024), low),
            pltpu.VMEM((4, 256, 1024), low),
            pltpu.VMEM((4, 128, 1024), low),
            pltpu.VMEM((1152, 1024), low),
            pltpu.SemaphoreType.DMA((10, 4)),
            pltpu.SemaphoreType.DMA((10, 4)),
            pltpu.SemaphoreType.DMA((10, 4)),
            pltpu.SemaphoreType.DMA((10, 4)),
            pltpu.SemaphoreType.DMA((3,)),
            pltpu.SemaphoreType.DMA,
            pltpu.SemaphoreType.DMA((2,)),
            pltpu.SemaphoreType.DMA((6,)),
            pltpu.SemaphoreType.DMA((6,)),
            pltpu.SemaphoreType.DMA((2, 4)),
            pltpu.SemaphoreType.DMA((2, 4)),
            pltpu.SemaphoreType.REGULAR,
        ],
        compiler_params=pltpu.CompilerParams(
            collective_id=1, has_side_effects=True, vmem_limit_bytes=63 * 2**20
        ),
        cost_estimate=pl.CostEstimate(flops=50 * 10**9, bytes_accessed=40 * 10**6, transcendentals=2 * 10**6),
    )(ffn_in, cot_all, router_rows, w_gate, w_up, w_down)


def everywhere():
    dp, expert = lax.axis_index("dp"), lax.axis_index("expert")
    here = {"x": dp // 2, "core": dp % 2, "z": expert // RING, "y": expert % RING}

    def device(axis, step):
        there = dict(here)
        size = 2 if axis == "core" else RING
        there[axis] = (here[axis] + step + size) % size
        return (there["x"] * 2 + there["core"], there["z"] * RING + there["y"])

    return here, device


def rms_scale(values):
    return lax.rsqrt(jnp.mean(values * values, axis=-1, keepdims=True) + epsilon)


def as_row(gain):
    return gain[...].astype(jnp.float32).reshape(1, -1)


def turned_rows(values, cosine, sine):
    front, back = values[: HEAD_DIM // 2], values[HEAD_DIM // 2 :]
    return jnp.concatenate([front * cosine - back * sine, back * cosine + front * sine], axis=0)


def kv_order(here, step):
    turn = step // 2
    return (turn % 2) * (3 - turn // 2) + (1 - turn % 2) * (turn // 2)


class Keys:
    def __init__(self, here, device, blocks, send, recv):
        self.here, self.device, self.blocks, self.send, self.recv = here, device, blocks, send, recv
        self.lines = blocks.shape[1]

    def copy(self, which):
        half = self.lines // 2
        offset, start, size, axis, step = (
            (0, 0, self.lines, "core", 1),
            (0, 0, self.lines, "x", 1),
            (0, 0, self.lines, "x", -1),
            (-1, 0, half, "x", 1),
            (1, half, half, "x", -1),
            (-1, 0, self.lines, "core", 1),
            (1, 0, self.lines, "core", 1),
            (2, 0, self.lines, "core", 1),
        )[which]
        block = (self.here["x"] + offset + RING) % RING * 2 + self.here["core"]
        part = self.blocks.at[block, pl.ds(start, size)]
        return pltpu.make_async_remote_copy(
            src_ref=part,
            dst_ref=part,
            send_sem=self.send.at[which],
            recv_sem=self.recv.at[which],
            device_id=self.device(axis, step),
            device_id_type=MESH,
        )

    def start(self, *which):
        for one in which:
            self.copy(one).start()

    def arrive(self, *which):
        for one in which:
            self.copy(one).wait_recv()

    def drain(self):
        for one in range(8):
            self.copy(one).wait_send()


def forward_kernel(
    tokens, cot, routes_t, length, cosine, sine, attn_gain, query_gain, key_gain, ffn_gain,
    w_query, w_key, w_value, w_output,
    ffn_in, hidden, mixed_t, queries, log_total, normed, query_raw, key_raw, kv_all, cot_all,
    wq, wk, wv, wo, kv, turned, most, total, mixed, packed,
    ag_send, ag_recv, kv_send, kv_recv, w_sem, kv_sem, own_sem,
):
    torus = Torus()
    here, device = everywhere()
    me = here["x"] * 2 + here["core"]
    barrier = pltpu.get_barrier_semaphore()
    peers = [*torus.neighbours(), device("core", 1), device("x", 1), device("x", -1)]
    for peer in peers:
        pl.semaphore_signal(barrier, inc=1, device_id=peer, device_id_type=MESH)
    loads = [
        pltpu.make_async_copy(source, target, w_sem.at[n])
        for n, (source, target) in enumerate(((w_query, wq), (w_key, wk), (w_value, wv), (w_output, wo)))
    ]
    for load in loads:
        load.start()

    expert_rows = lax.broadcasted_iota(jnp.int32, (EXPERTS, ROWS), 0)
    member = jnp.zeros((EXPERTS, ROWS), jnp.float32)
    for k in range(TOPK):
        member = member + jnp.where(expert_rows == routes_t[pl.ds(k, 1), :], 1.0, 0.0)
    laid = jnp.concatenate([member[8 * q : 8 * q + 8] for q in range(4)], axis=1)
    packed[...] = jnp.concatenate([laid, jnp.zeros_like(laid)], axis=0).astype(jnp.bfloat16)
    first_row = pl.multiple_of(torus.expert * FULL, 16)
    owns = [
        pltpu.make_async_copy(packed, cot_all.at[pl.ds(first_row, EXTRA)], own_sem.at[0]),
        pltpu.make_async_copy(cot, cot_all.at[pl.ds(pl.multiple_of(first_row + EXTRA, 16), ROWS)], own_sem.at[1]),
    ]
    for copy in owns:
        copy.start()
    for copy in owns:
        copy.wait()
    pl.semaphore_wait(barrier, len(peers))

    def gather(number, axis, other, low, first, second):
        return Gather(torus, cot_all, ag_send, ag_recv, number, axis, other, low, first, second, FULL)

    a_first = gather(0, "y", 0, 0, 64, 64)
    b_first = gather(1, "z", 0, 128, 80, 64)
    a_second = {d: gather(2 + d % RING, "z", d, 0, 64, 64) for d in (0, 1, -1, 2)}
    b_second = {d: gather(6 + d % RING, "y", d, 128, 80, 64) for d in (0, 1, -1, 2)}
    gathers = [a_first, b_first, *a_second.values(), *b_second.values()]
    a_first.first()
    b_first.first()
    b_second[0].first()
    a_second[0].first()

    @pl.loop(0, 4)
    def _(n):
        at = pl.ds(pl.multiple_of(n * 64, 64), 64)
        rows = tokens[at].astype(jnp.float32)
        normed[at] = (rows * rms_scale(rows) * as_row(attn_gain)).astype(jnp.bfloat16)

    for load in loads:
        load.wait()

    keys = Keys(here, device, kv, kv_send, kv_recv)
    key_raw[...] = dot_nn(normed[...], wk[...])
    scaled = key_raw[...]
    scaled = (scaled * rms_scale(scaled) * as_row(key_gain)).T
    for j in range(KV_HEADS):
        head = turned_rows(scaled[j * 64 : j * 64 + 64], cosine[...], sine[...])
        kv[me, pl.ds(j * 64, 64)] = head.astype(jnp.bfloat16)
    kv[me, pl.ds(512, 512)] = dot_nn(normed[...], wv[...]).T.astype(jnp.bfloat16)
    keys.start(0, 1, 2)
    query_raw[...] = dot_nn(normed[...], wq[...])
    scaled = query_raw[...]
    turned[...] = (scaled * rms_scale(scaled) * as_row(query_gain)).T

    for j in range(KV_HEADS):
        for r in range(2):
            head = turned[j * 128 + r * 64 : j * 128 + r * 64 + 64]
            head = turned_rows(head, cosine[...], sine[...])
            queries[j, :, r * ROWS : (r + 1) * ROWS] = (head * HEAD_DIM**-0.5).astype(jnp.bfloat16)

    a_first.second()
    b_first.second()
    for d in (1, -1):
        b_second[d].first()
        a_second[d].first()

    key_at = lax.broadcasted_iota(jnp.int32, (ROWS, 2 * ROWS), 0)
    query_at = lax.broadcasted_iota(jnp.int32, (ROWS, 2 * ROWS), 1) % ROWS
    valid = (key_at <= query_at) & (key_at + me * ROWS < length[...])

    def heads_of(block):
        keys_here = [kv[block, j * 64 : j * 64 + 64] for j in range(KV_HEADS)]
        values_here = [kv[block, 512 + j * 64 : 576 + j * 64] for j in range(KV_HEADS)]
        return keys_here, values_here

    keys_here, values_here = heads_of(me)
    scores = [jnp.where(valid, dot_tn(keys_here[j], queries[j]), -1e30) for j in range(KV_HEADS)]
    tops = [jnp.max(one, axis=0, keepdims=True) for one in scores]
    probs = [jnp.exp(one - top) for one, top in zip(scores, tops)]
    parts = [dot_nn(one, prob.astype(jnp.bfloat16)) for one, prob in zip(values_here, probs)]
    for j in range(KV_HEADS):
        most[j] = tops[j]
        total[j] = jnp.sum(probs[j], axis=0, keepdims=True)
        mixed[j] = parts[j]

    @pl.loop(1, 8)
    def _(step):
        @pl.when(step == 1)
        def _():
            a_first.third()
            b_first.third()
            b_second[2].first()
            a_second[2].first()
            keys.arrive(0)

        @pl.when(step == 2)
        def _():
            keys.arrive(1)
            keys.start(3, 5)
            keys.arrive(2)
            keys.start(4, 6)
            b_second[0].second()
            a_second[0].second()

        @pl.when(step == 3)
        def _():
            keys.arrive(5)
            for d in (1, -1):
                b_second[d].second()
                a_second[d].second()

        @pl.when(step == 5)
        def _():
            keys.arrive(3, 4)
            keys.start(7)
            keys.arrive(6)
            b_second[2].second()
            a_second[2].second()

        @pl.when(step == 7)
        def _():
            keys.arrive(7)

        block = (here["x"] + kv_order(here, step) + RING) % RING * 2 + (here["core"] + step) % 2

        @pl.when(block < me)
        def _():
            keys_here, values_here = heads_of(block)
            before = [most[j] for j in range(KV_HEADS)]
            shares = [total[j] for j in range(KV_HEADS)]
            sums = [mixed[j] for j in range(KV_HEADS)]
            scores = [dot_tn(keys_here[j], queries[j]) for j in range(KV_HEADS)]
            tops = [jnp.maximum(old, jnp.max(one, axis=0, keepdims=True)) for old, one in zip(before, scores)]
            probs = [jnp.exp(one - top) for one, top in zip(scores, tops)]
            less = [jnp.exp(old - top) for old, top in zip(before, tops)]
            parts = [dot_nn(one, prob.astype(jnp.bfloat16)) for one, prob in zip(values_here, probs)]
            for j in range(KV_HEADS):
                most[j] = tops[j]
                total[j] = shares[j] * less[j] + jnp.sum(probs[j], axis=0, keepdims=True)
                mixed[j] = sums[j] * less[j] + parts[j]

    save = pltpu.make_async_copy(kv, kv_all, kv_sem)
    save.start()

    for j in range(KV_HEADS):
        share = total[j]
        log_total[j] = most[j] + jnp.log(share)
        head = (mixed[j] * (1.0 / share)).astype(jnp.bfloat16)
        for r in range(2):
            mixed_t[j * 128 + r * 64 : j * 128 + r * 64 + 64, :] = head[:, r * ROWS : (r + 1) * ROWS]

    hidden[...] = dot_tn(mixed_t[...], wo[...])

    @pl.loop(0, 4)
    def _(n):
        at = pl.ds(pl.multiple_of(n * 64, 64), 64)
        rows = hidden[at] + tokens[at].astype(jnp.float32)
        hidden[at] = rows
        ffn_in[at] = (rows * rms_scale(rows) * as_row(ffn_gain)).astype(jnp.bfloat16)

    for d in (0, 1, -1, 2):
        a_second[d].third()
        b_second[d].third()
    save.wait()
    keys.drain()
    for one in gathers:
        one.drain()


def forward(tokens, cot, routes_t, length, cosine, sine, gains, weights):
    vmem, hbm = pl.BlockSpec(memory_space=pltpu.VMEM), pl.BlockSpec(memory_space=pl.ANY)
    low, wide = jnp.bfloat16, jnp.float32
    shape = jax.ShapeDtypeStruct
    return pl.pallas_call(
        forward_kernel,
        name="forward",
        out_shape=(
            shape((ROWS, 1024), low),
            shape((ROWS, 1024), wide),
            shape((1024, ROWS), low),
            shape((KV_HEADS, HEAD_DIM, 2 * ROWS), low),
            shape((KV_HEADS, 1, 2 * ROWS), wide),
            shape((ROWS, 1024), low),
            shape((ROWS, 1024), wide),
            shape((ROWS, 512), wide),
            shape((8, 1024, ROWS), low),
            shape((16 * FULL, 1024), low),
        ),
        in_specs=[vmem] * 10 + [hbm] * 4,
        out_specs=(vmem,) * 8 + (hbm, hbm),
        scratch_shapes=[
            pltpu.VMEM((1024, 1024), low),
            pltpu.VMEM((1024, 512), low),
            pltpu.VMEM((1024, 512), low),
            pltpu.VMEM((1024, 1024), low),
            pltpu.VMEM((8, 1024, ROWS), low),
            pltpu.VMEM((1024, ROWS), wide),
            pltpu.VMEM((KV_HEADS, 1, 2 * ROWS), wide),
            pltpu.VMEM((KV_HEADS, 1, 2 * ROWS), wide),
            pltpu.VMEM((KV_HEADS, HEAD_DIM, 2 * ROWS), wide),
            pltpu.VMEM((EXTRA, 1024), low),
            pltpu.SemaphoreType.DMA((10, 4)),
            pltpu.SemaphoreType.DMA((10, 4)),
            pltpu.SemaphoreType.DMA((8,)),
            pltpu.SemaphoreType.DMA((8,)),
            pltpu.SemaphoreType.DMA((4,)),
            pltpu.SemaphoreType.DMA,
            pltpu.SemaphoreType.DMA((2,)),
        ],
        compiler_params=pltpu.CompilerParams(
            collective_id=3, has_side_effects=True, vmem_limit_bytes=56 * 2**20
        ),
    )(tokens, cot, routes_t, length, cosine, sine, *gains, *weights)


ORDERS = (("x", "y", "z"), ("y", "z", "x"), ("z", "x", "y"))
STREAMS = ((0, 768), (768, 768), (1536, 512))


class Total:
    def __init__(self, here, device, buffer, shift, final, landing, work, send, recv, number, stream):
        self.here, self.device, self.buffer, self.shift, self.final = here, device, buffer, shift, final
        self.landing, self.work = landing, work
        self.send, self.recv, self.number, self.order = send, recv, number, ORDERS[(stream + number // 3) % 3]
        self.start, self.rows = STREAMS[stream]
        first = self.start + self.start * 9 // 8
        r = self.rows
        self.lands = (first, first + r, first + r + 3 * (r // 4), first + r + 3 * (r // 4) + 3 * (r // 16))

    def own(self):
        return self.here["core"] * 2048 + self.start

    def copy(self, which, source, target, axis, step):
        return pltpu.make_async_remote_copy(
            src_ref=source,
            dst_ref=target,
            send_sem=self.send.at[self.number, which],
            recv_sem=self.recv.at[self.number, which],
            device_id=self.device(axis, step),
            device_id_type=MESH,
        )

    def held(self, at, size):
        return self.buffer.at[pl.ds(pl.multiple_of(at + self.shift, 16), size)]

    def ready(self, at, size):
        return self.final.at[pl.ds(pl.multiple_of(at, 16), size)]

    def land(self, stage, n, size):
        return self.landing.at[pl.ds(self.lands[stage] + n * size, size)]

    def copies(self, stage):
        r, own = self.rows, self.own()
        a, b, c = self.order
        ia, ib = self.here[a], self.here[b]
        second = own + ia * (r // 4)
        third = second + ib * (r // 16)
        if stage == 0:
            there = (1 - self.here["core"]) * 2048 + self.start
            return [self.copy(0, self.held(there, r), self.land(0, 0, r), "core", 1)]
        if stage == 6:
            return [self.copy(16, self.ready(own, r), self.ready(own, r), "core", 1)]
        found = []
        for d in (1, 2, 3):
            if stage == 1:
                source, target, axis = self.held(own + (ia + d) % RING * (r // 4), r // 4), self.land(1, d - 1, r // 4), a
            elif stage == 2:
                source = self.held(second + (ib + d) % RING * (r // 16), r // 16)
                target, axis = self.land(2, d - 1, r // 16), b
            elif stage == 3:
                source = self.work.at[self.number, pl.ds(0, r // 16)]
                target, axis = self.land(3, d - 1, r // 16), c
            elif stage == 4:
                source, target, axis = self.ready(third, r // 16), self.ready(third, r // 16), b
            else:
                source, target, axis = self.ready(second, r // 4), self.ready(second, r // 4), a
            found.append(self.copy(1 + (stage - 1) * 3 + d - 1, source, target, axis, d))
        return found

    def begin(self, stage):
        for copy in self.copies(stage):
            copy.start()

    def add(self, stage, load, store, size, count):
        step = 64 if size % 64 == 0 else 16

        @pl.loop(0, size // step)
        def _(k):
            at = k * step
            total = load(at, step).astype(jnp.float32)
            for n in range(count):
                land = pl.ds(pl.multiple_of(self.lands[stage] + n * size + at, 16), step)
                total = total + self.landing[land].astype(jnp.float32)
            store(at, step, total.astype(jnp.bfloat16))

    def finish(self, stage):
        for copy in self.copies(stage):
            copy.wait_recv()
        if stage > 3:
            return
        r, own = self.rows, self.own()
        a, b, _ = self.order
        second = own + self.here[a] * (r // 4)
        third = second + self.here[b] * (r // 16)
        first = (own, second, third, third)[stage] + self.shift

        def in_place(at, step, *value):
            lines = pl.ds(pl.multiple_of(first + at, 16), step)
            if not value:
                return self.buffer[lines]
            self.buffer[lines] = value[0]

        def in_work(at, step, *value):
            lines = pl.ds(pl.multiple_of(at, 16), step)
            if not value:
                return self.work[self.number, lines]
            self.work[self.number, lines] = value[0]

        def in_final(at, step, value):
            self.final[pl.ds(pl.multiple_of(third + at, 16), step)] = value

        if stage == 0:
            self.add(0, in_place, in_place, r, 1)
        elif stage == 1:
            self.add(1, in_place, in_place, r // 4, 3)
        elif stage == 2:
            self.add(2, in_place, in_work, r // 16, 3)
        else:
            self.add(3, in_work, in_final, r // 16, 3)

    def drain(self):
        for stage in range(7):
            for copy in self.copies(stage):
                copy.wait_send()


class Small:
    STAGES = (("core", (1,)), ("x", (1, 2, 3)), ("y", (1, 2, 3)), ("z", (1, 2, 3)))

    def __init__(self, device, value, landing, send, recv):
        self.device, self.value, self.landing, self.send, self.recv = device, value, landing, send, recv

    def copies(self, stage):
        axis, steps = self.STAGES[stage]
        first = sum(len(s) for _, s in self.STAGES[:stage])
        return [
            pltpu.make_async_remote_copy(
                src_ref=self.value.at[stage],
                dst_ref=self.landing.at[first + n],
                send_sem=self.send.at[first + n],
                recv_sem=self.recv.at[first + n],
                device_id=self.device(axis, step),
                device_id_type=MESH,
            )
            for n, step in enumerate(steps)
        ]

    def begin(self, stage):
        for copy in self.copies(stage):
            copy.start()

    def finish(self, stage):
        for copy in self.copies(stage):
            copy.wait_recv()
        first = sum(len(s) for _, s in self.STAGES[:stage])
        total = self.value[stage]
        for n in range(len(self.STAGES[stage][1])):
            total = total + self.landing[first + n]
        self.value[stage + 1] = total

    def drain(self):
        for stage in range(4):
            for copy in self.copies(stage):
                copy.wait_send()


class Line:
    def __init__(self, here, device):
        self.here, self.device = here, device

    def along(self, axis, other, step):
        return (self.here["x"] + step + RING) % RING

    def near(self, axis, step):
        return self.device("x", step)


def rms_back(values, gain, grad):
    scale = rms_scale(values)
    lifted = gain * grad
    inner = jnp.mean(values * lifted, axis=-1, keepdims=True)
    return scale * lifted - values * (scale * scale * scale) * inner, jnp.sum(
        grad * values * scale, axis=0, keepdims=True
    )


def turned_back(grads, cosine, sine):
    front, back = grads[: HEAD_DIM // 2], grads[HEAD_DIM // 2 :]
    return jnp.concatenate([front * cosine + back * sine, back * cosine - front * sine], axis=0)


def backward_kernel(
    hidden, ffn_in, cot, tokens, normed, key_raw, mixed_t, queries, log_total,
    routes_t, length, cosine, sine, attn_gain, query_gain, key_gain, ffn_gain, router_rows,
    returned_all, query_raw_all, mixed_parts, kv_all, w_query, w_key, w_value, w_output, own_gu, own_down,
    mixed_out, token_grad, early_small, late_small, query_sum, key_sum, value_sum, output_sum, all_gu, all_down,
    sums, rows, returned, square, kv, hidden_grad, result, branch, grads, delta, query_grad, turned,
    for_mate, from_mate, kv_sums, kv_rows, key_low, value_low,
    held, finals, landing, work, values, small_rows, late_values, late_rows,
    rs_send, rs_recv, mate_send, mate_recv, kv_send, kv_recv, ar_send, ar_recv, small_send, small_recv, load_sem, out_sem, ex_send, ex_recv,
):
    torus = Torus()
    here, device = everywhere()
    me = here["x"] * 2 + here["core"]
    barrier = pltpu.get_barrier_semaphore()
    peers = [device("core", 1)] + [device(axis, d) for axis in "xyz" for d in (1, 2, 3)]
    for peer in peers:
        pl.semaphore_signal(barrier, inc=1, device_id=peer, device_id_type=MESH)
    loads = [
        pltpu.make_async_copy(source, target, load_sem.at[n])
        for n, (source, target) in enumerate(
            ((returned_all, returned), (w_output, square), (mixed_parts, sums), (kv_all, kv))
        )
    ]
    for load in loads:
        load.start()
    owns = [
        pltpu.make_async_copy(own_gu, all_gu.at[me], load_sem.at[8]),
        pltpu.make_async_copy(own_down, all_down.at[me], load_sem.at[9]),
    ]
    for copy in owns:
        copy.start()

    expert_rows = lax.broadcasted_iota(jnp.int32, (EXPERTS, ROWS), 0)
    member = jnp.zeros((EXPERTS, ROWS), jnp.float32)
    for k in range(TOPK):
        member = member + jnp.where(expert_rows == routes_t[pl.ds(k, 1), :], 1.0, 0.0)
    named = member > 0.5
    logits = jnp.where(named, dot_nt(router_rows[...], ffn_in[...]), -1e30)
    weight = jnp.where(named, jnp.exp(logits - jnp.max(logits, axis=0, keepdims=True)), 0.0)
    gates = weight / jnp.sum(weight, axis=0, keepdims=True)
    loads[0].wait()
    gate_grad = jnp.concatenate([returned[:8, q * ROWS : (q + 1) * ROWS] for q in range(4)], axis=0)
    logit_grad = (gates * (gate_grad - jnp.sum(gates * gate_grad, axis=0, keepdims=True))).astype(jnp.bfloat16)
    result[...] = dot_tn(logit_grad, router_rows[...])
    values[0, :EXPERTS] = dot_nn(logit_grad, ffn_in[...])

    def ffn_part(n, gain_grad):
        at = pl.ds(pl.multiple_of(n * 64, 64), 64)
        grad = result[at] + returned[pl.ds(pl.multiple_of(n * 64 + EXTRA, 16), 64)]
        part, more = rms_back(hidden[at], as_row(ffn_gain), grad)
        part = part + cot[at].astype(jnp.float32)
        hidden_grad[at] = part
        branch[at] = part.astype(jnp.bfloat16)
        return gain_grad + more

    gain_grad = lax.fori_loop(0, 4, ffn_part, jnp.zeros((1, 1024), jnp.float32))
    values[0, EXPERTS:] = jnp.concatenate([gain_grad, jnp.zeros((7, 1024), jnp.float32)], axis=0)

    loads[1].wait()
    turned[...] = dot_nt(square[...], branch[...])
    next_load = pltpu.make_async_copy(w_query, square, load_sem.at[6])
    next_load.start()
    query_raw = returned.at[pl.ds(0, ROWS)]
    raw_load = pltpu.make_async_copy(query_raw_all, query_raw, load_sem.at[7])
    raw_load.start()

    for j in range(KV_HEADS):
        for r in range(2):
            at = slice(j * 128 + r * 64, j * 128 + r * 64 + 64)
            low = turned[at].astype(jnp.bfloat16)
            grads[j, :, r * ROWS : (r + 1) * ROWS] = low
            delta[j, :, r * ROWS : (r + 1) * ROWS] = jnp.sum(
                low.astype(jnp.float32) * mixed_t[at].astype(jnp.float32), axis=0, keepdims=True
            )
        query_grad[j] = jnp.zeros((HEAD_DIM, 2 * ROWS), jnp.float32)

    @pl.loop(0, 4)
    def _(n):
        at = pl.ds(pl.multiple_of(n * 256, 256), 256)
        part = dot_nn(mixed_t[at], branch[...]).astype(jnp.bfloat16)
        for q in range(4):
            held[pl.ds(pl.multiple_of(q * 1024 + n * 256, 256), 256)] = part[:, q * 256 : (q + 1) * 256]

    for load in [*loads[2:], *owns]:
        load.wait()
    pl.semaphore_wait(barrier, len(peers))

    def reduction(number, buffer, shift):
        return [
            Total(
                here, device, buffer, shift, finals.at[number], landing.at[number], work,
                ar_send, ar_recv, 3 * number + s, s,
            )
            for s in range(3)
        ]

    early, of_query, of_keys = reduction(0, held, 0), reduction(1, kv, 0), reduction(2, kv, 4096)
    few = Small(device, values, small_rows, small_send.at[0], small_recv.at[0])
    late_few = Small(device, late_values, late_rows, small_send.at[1], small_recv.at[1])
    order = (2, 1, -1, 0)
    leads = []
    for n, d in enumerate(order):
        leads.append(Scatter(torus, sums, rows, rs_send, rs_recv, n, n * 384, "z", d, 0, 64, 64))
        leads.append(Scatter(torus, sums, rows, rs_send, rs_recv, 4 + n, (5 + n) * 384, "y", d, 128, 64, 64))
    lasts = [
        Scatter(torus, sums, rows, rs_send, rs_recv, 8, 4 * 384, "y", 0, 0, 64, 64),
        Scatter(torus, sums, rows, rs_send, rs_recv, 9, 9 * 384, "z", 0, 128, 64, 64),
    ]
    ring = Scatter(Line(here, device), kv_sums, kv_rows, kv_send, kv_recv, 0, 0, "x", 0, 0, 512, 512)

    experts = [
        Keys(here, device, blocks, ex_send.at[n], ex_recv.at[n]) for n, blocks in enumerate((all_gu, all_down))
    ]
    for one in experts:
        one.start(0, 1, 2)
    for one in early:
        one.begin(0)
    few.begin(0)
    for one in leads:
        one.first()

    def onward(streams, stage, small=None):
        for one in streams:
            one.finish(stage)
            if stage < 6:
                one.begin(stage + 1)
        if small is not None and stage < 4:
            small.finish(stage)
            if stage < 3:
                small.begin(stage + 1)

    def early_step(stage):
        onward(early, stage, few)

    def write_out(number, column, target, at):
        block = finals.at[number, pl.ds(column * 1024, 1024)]
        return pltpu.make_async_copy(block, target.at[:, pl.ds(at * 256, 256)], out_sem.at[number, column])

    outs = [write_out(0, q, output_sum, q) for q in range(4)]
    outs += [write_out(1, q, query_sum, q) for q in range(4)]
    outs += [write_out(2, q, key_sum, q) for q in range(2)]
    outs += [write_out(2, 2 + q, value_sum, q) for q in range(2)]

    def mate_copy(turn, at):
        return pltpu.make_async_remote_copy(
            src_ref=for_mate.at[turn % 2],
            dst_ref=from_mate.at[at],
            send_sem=mate_send.at[turn],
            recv_sem=mate_recv.at[turn],
            device_id=device("core", 1),
            device_id_type=MESH,
        )

    key_at = lax.broadcasted_iota(jnp.int32, (ROWS, 2 * ROWS), 0)
    query_at = lax.broadcasted_iota(jnp.int32, (ROWS, 2 * ROWS), 1) % ROWS
    valid = (key_at <= query_at) & (key_at + me * ROWS < length[...])

    def block_grads(block, target, at, masked):
        for group in range(2):
            heads = range(4 * group, 4 * group + 4)
            key_heads = [kv[pl.ds(pl.multiple_of(block * 1024 + j * 64, 64), 64)] for j in heads]
            value_heads = [kv[pl.ds(pl.multiple_of(block * 1024 + 512 + j * 64, 64), 64)] for j in heads]
            probs = [jnp.exp(dot_tn(one, queries[j]) - log_total[j]) for one, j in zip(key_heads, heads)]
            if masked:
                probs = [jnp.where(valid, one, 0.0) for one in probs]
            probs_grads = [dot_tn(one, grads[j]) for one, j in zip(value_heads, heads)]
            lows = [
                (one * (grad - delta[j])).astype(jnp.bfloat16) for one, grad, j in zip(probs, probs_grads, heads)
            ]
            key_parts = [dot_nt(queries[j], low).astype(jnp.bfloat16) for low, j in zip(lows, heads)]
            value_parts = [
                dot_nt(grads[j], one.astype(jnp.bfloat16)).astype(jnp.bfloat16) for one, j in zip(probs, heads)
            ]
            query_parts = [dot_nn(one, low) for one, low in zip(key_heads, lows)]
            for n, j in enumerate(heads):
                target[at, j * 64 : j * 64 + 64] = key_parts[n]
                target[at, 512 + j * 64 : 576 + j * 64] = value_parts[n]
                query_grad[j] += query_parts[n]

    def from_other(turn, at):
        mate_copy(turn, at).wait_recv()

        @pl.loop(0, 16)
        def _(n):
            lines = pl.ds(pl.multiple_of(n * 64, 64), 64)
            total = kv_sums[at, lines].astype(jnp.float32) + from_mate[at, lines].astype(jnp.float32)
            kv_sums[at, lines] = total.astype(jnp.bfloat16)

    def turn_x(turn):
        offset = (1 - turn % 2) * (2 + turn // 2) + (turn % 2) * (1 - turn // 2)
        return (here["x"] + offset + RING) % RING

    @pl.loop(0, 4)
    def _(turn):
        @pl.when(turn == 1)
        def _():
            early_step(0)
            for one in leads:
                one.second()

        @pl.when(turn == 2)
        def _():
            early_step(2)
            for one in experts:
                one.arrive(1)
                one.start(3, 5)
                one.arrive(2)
                one.start(4, 6)

        @pl.when(turn == 3)
        def _():
            early_step(4)
            for one in leads[:2]:
                one.third()
            for one in lasts:
                one.first()

        at = turn_x(turn)
        other = at * 2 + 1 - here["core"]

        @pl.when(turn >= 2)
        def _():
            mate_copy(turn - 2, at).wait_send()

        @pl.when(other < me)
        def _():
            block_grads(other, for_mate, turn % 2, False)

        @pl.when(other >= me)
        def _():
            for_mate[turn % 2] = jnp.zeros((1024, ROWS), jnp.bfloat16)

        mate_copy(turn, at).start()

        @pl.when(turn == 1)
        def _():
            early_step(1)

        @pl.when(turn == 2)
        def _():
            early_step(3)

        @pl.when(turn == 3)
        def _():
            early_step(5)
            for one in leads[2:]:
                one.third()
            for one in lasts:
                one.second()

        own = at * 2 + here["core"]

        @pl.when(own < me)
        def _():
            block_grads(own, kv_sums, at, False)

        @pl.when(own > me)
        def _():
            kv_sums[at] = jnp.zeros((1024, ROWS), jnp.bfloat16)

        @pl.when(own == me)
        def _():
            block_grads(own, kv_sums, at, True)

        from_other(turn, at)

        @pl.when(turn == 0)
        def _():
            ring.first()

        @pl.when(turn == 2)
        def _():
            ring.second()

    for j in range(KV_HEADS):
        for r in range(2):
            head = query_grad[j, :, r * ROWS : (r + 1) * ROWS] * HEAD_DIM**-0.5
            turned[j * 128 + r * 64 : j * 128 + r * 64 + 64] = turned_back(head, cosine[...], sine[...])

    raw_load.wait()
    result[...] = turned[...].T

    def query_part(n, gain_grad):
        at = pl.ds(pl.multiple_of(n * 64, 64), 64)
        part, more = rms_back(query_raw[at], as_row(query_gain), result[at])
        branch[at] = part.astype(jnp.bfloat16)
        return gain_grad + more

    query_gain_grad = lax.fori_loop(0, 4, query_part, jnp.zeros((1, 1024), jnp.float32))

    @pl.loop(0, 4)
    def _(n):
        columns = pl.ds(pl.multiple_of(n * 256, 256), 256)
        part = dot_tn(normed[:, columns], branch[...]).astype(jnp.bfloat16)
        for q in range(4):
            kv[pl.ds(pl.multiple_of(q * 1024 + n * 256, 256), 256)] = part[:, q * 256 : (q + 1) * 256]

    for one in of_query:
        one.begin(0)
    early_step(6)
    for one in experts:
        one.arrive(3, 4)
        one.start(7)
    for q in range(4):
        outs[q].start()
    early_small[...] = values[4]

    def put(at, total):
        turned[at] = total

    ring.third(put)
    for j in range(KV_HEADS):
        turned[j * 64 : j * 64 + 64] = turned_back(turned[j * 64 : j * 64 + 64], cosine[...], sine[...])
    part, key_gain_grad = rms_back(key_raw[...], as_row(key_gain), turned[:512].T)
    key_low[...] = part.astype(jnp.bfloat16)
    value_low[...] = turned[512:].T.astype(jnp.bfloat16)

    @pl.loop(0, 4)
    def _(n):
        columns = pl.ds(pl.multiple_of(n * 256, 256), 256)
        part = dot_tn(normed[:, columns], jnp.concatenate([key_low[...], value_low[...]], axis=1)).astype(jnp.bfloat16)
        for q in range(4):
            kv[pl.ds(pl.multiple_of(4096 + q * 1024 + n * 256, 256), 256)] = part[:, q * 256 : (q + 1) * 256]

    for one in of_keys:
        one.begin(0)
    onward(of_query, 0)
    next_load.wait()
    result[...] = dot_nt(branch[...], square[...])
    last_loads = [
        pltpu.make_async_copy(w_key, square.at[:, pl.ds(0, 512)], load_sem.at[4]),
        pltpu.make_async_copy(w_value, square.at[:, pl.ds(512, 512)], load_sem.at[5]),
    ]
    for load in last_loads:
        load.start()
    onward(of_keys, 0)
    onward(of_query, 1)
    for load in last_loads:
        load.wait()
    result[...] += dot_nt(jnp.concatenate([key_low[...], value_low[...]], axis=1), square[...])
    onward(of_keys, 1)
    onward(of_query, 2)

    def token_part(n, gain_grad):
        at = pl.ds(pl.multiple_of(n * 64, 64), 64)
        part, more = rms_back(tokens[at].astype(jnp.float32), as_row(attn_gain), result[at])
        token_grad[at] = (hidden_grad[at] + part).astype(jnp.bfloat16)
        return gain_grad + more

    attn_gain_grad = lax.fori_loop(0, 4, token_part, jnp.zeros((1, 1024), jnp.float32))
    key_wide = jnp.concatenate([key_gain_grad, jnp.zeros((1, 512), jnp.float32)], axis=1)
    late_values[0] = jnp.concatenate(
        [attn_gain_grad, query_gain_grad, key_wide, jnp.zeros((5, 1024), jnp.float32)], axis=0
    )
    late_few.begin(0)
    onward(of_keys, 2)
    onward(of_query, 3, None)
    late_few.finish(0)
    late_few.begin(1)

    def put_mixed(at, total):
        mixed_out[at] = (hidden[at] + total).astype(jnp.bfloat16)

    for one in lasts:
        one.third(put_mixed)
    onward(of_keys, 3)
    onward(of_query, 4)
    late_few.finish(1)
    late_few.begin(2)
    onward(of_keys, 4)
    onward(of_query, 5)
    late_few.finish(2)
    late_few.begin(3)
    onward(of_keys, 5)
    onward(of_query, 6)
    for q in range(4, 8):
        outs[q].start()
    late_few.finish(3)
    late_small[...] = late_values[4]
    onward(of_keys, 6)
    for q in range(8, 12):
        outs[q].start()
    for one in experts:
        one.arrive(0, 5, 6, 7)
    for one in [*experts, *leads, *lasts, ring, *early, *of_query, *of_keys, few, late_few]:
        one.drain()
    for turn in (2, 3):
        mate_copy(turn, 0).wait_send()
    for out in outs:
        out.wait()


def backward(smalls, larges):
    vmem, hbm = pl.BlockSpec(memory_space=pltpu.VMEM), pl.BlockSpec(memory_space=pl.ANY)
    low, wide = jnp.bfloat16, jnp.float32
    shape = jax.ShapeDtypeStruct
    dma = pltpu.SemaphoreType.DMA
    return pl.pallas_call(
        backward_kernel,
        name="backward",
        out_shape=(
            shape((ROWS, 1024), low),
            shape((ROWS, 1024), low),
            shape((40, 1024), wide),
            shape((8, 1024), wide),
            shape((1024, 1024), low),
            shape((1024, 512), low),
            shape((1024, 512), low),
            shape((1024, 1024), low),
            shape((8, 256, 1024), low),
            shape((8, 128, 1024), low),
        ),
        in_specs=[vmem] * len(smalls) + [hbm] * len(larges),
        out_specs=(vmem,) * 4 + (hbm,) * 6,
        scratch_shapes=[
            pltpu.VMEM((16, ROWS, 1024), low),
            pltpu.VMEM((10 * 384, 1024), low),
            pltpu.VMEM((FULL, 1024), wide),
            pltpu.VMEM((1024, 1024), low),
            pltpu.VMEM((8 * 1024, ROWS), low),
            pltpu.VMEM((ROWS, 1024), wide),
            pltpu.VMEM((ROWS, 1024), wide),
            pltpu.VMEM((ROWS, 1024), low),
            pltpu.VMEM((KV_HEADS, HEAD_DIM, 2 * ROWS), low),
            pltpu.VMEM((KV_HEADS, 1, 2 * ROWS), wide),
            pltpu.VMEM((KV_HEADS, HEAD_DIM, 2 * ROWS), wide),
            pltpu.VMEM((1024, ROWS), wide),
            pltpu.VMEM((2, 1024, ROWS), low),
            pltpu.VMEM((4, 1024, ROWS), low),
            pltpu.VMEM((4, 1024, ROWS), low),
            pltpu.VMEM((3072, ROWS), low),
            pltpu.VMEM((ROWS, 512), low),
            pltpu.VMEM((ROWS, 512), low),
            pltpu.VMEM((4096, 256), low),
            pltpu.VMEM((3, 4096, 256), low),
            pltpu.VMEM((3, 4352, 256), low),
            pltpu.VMEM((9, 48, 256), low),
            pltpu.VMEM((5, 40, 1024), wide),
            pltpu.VMEM((10, 40, 1024), wide),
            pltpu.VMEM((5, 8, 1024), wide),
            pltpu.VMEM((10, 8, 1024), wide),
            dma((10, 4)),
            dma((10, 4)),
            dma((4,)),
            dma((4,)),
            dma((1, 4)),
            dma((1, 4)),
            dma((9, 17)),
            dma((9, 17)),
            dma((2, 10)),
            dma((2, 10)),
            dma((10,)),
            dma((3, 4)),
            dma((2, 8)),
            dma((2, 8)),
        ],
        compiler_params=pltpu.CompilerParams(
            collective_id=4, has_side_effects=True, vmem_limit_bytes=66000000
        ),
        cost_estimate=pl.CostEstimate(flops=100 * 10**9, bytes_accessed=60 * 10**6, transcendentals=8 * 10**6),
    )(*smalls, *larges)


def widen_kernel(
    early, late, mixed, tokens, query, key, value, output, gate_up, down,
    ffn_gain, attn_gain, query_gain, key_gain, router,
    mixed_out, token_out, query_out, key_out, value_out, output_out, gate_out, up_out, down_out,
    query_in, key_in, value_in, output_in, gate_up_in, down_in,
    query_wide, key_wide, value_wide, output_wide, gate_up_wide, down_wide,
    in_sem, out_sem,
):
    through = [
        pltpu.make_async_copy(mixed, mixed_out, out_sem.at[0]),
        pltpu.make_async_copy(tokens, token_out, out_sem.at[1]),
    ]
    for copy in through:
        copy.start()
    arrays = (
        (query, query_in, query_wide, query_out),
        (output, output_in, output_wide, output_out),
        (key, key_in, key_wide, key_out),
        (value, value_in, value_wide, value_out),
    )
    parts = []
    for source, low, wide, target in arrays:
        for n in range(0, 1024, 512):
            at = pl.ds(n, 512)
            parts.append((source.at[at], low.at[at], wide.at[at], [(wide.at[at], target.at[at])]))
    for block in range(8):
        rows, e = pl.ds(block // 2 * 256, 256), block % 2
        wide = gate_up_wide.at[block]
        targets = [
            (wide.at[:, pl.ds(0, 512)], gate_out.at[e, rows]),
            (wide.at[:, pl.ds(512, 512)], up_out.at[e, rows]),
        ]
        parts.append((gate_up.at[block], gate_up_in.at[block], wide, targets))
    for block in range(8):
        wide = down_wide.at[block]
        target = down_out.at[block % 2, pl.ds(block // 2 * 128, 128)]
        parts.append((down.at[block], down_in.at[block], wide, [(wide, target)]))
    loads = [pltpu.make_async_copy(source, low, in_sem.at[n]) for n, (source, low, _, _) in enumerate(parts)]
    for load in loads:
        load.start()
    ffn_gain[...] = early[EXPERTS]
    attn_gain[...] = late[0]
    query_gain[...] = late[1]
    key_gain[...] = late[2, :512]
    router[...] = early[:EXPERTS].T
    stores = []
    for load, (_, low, wide, targets) in zip(loads, parts):
        load.wait()
        wide[...] = low[...].astype(jnp.float32)
        for source, target in targets:
            stores.append(pltpu.make_async_copy(source, target, out_sem.at[2 + len(stores)]))
            stores[-1].start()
    for copy in [*through, *stores]:
        copy.wait()


def widen(arrays):
    vmem, hbm = pl.BlockSpec(memory_space=pltpu.VMEM), pl.BlockSpec(memory_space=pl.ANY)
    low, wide = jnp.bfloat16, jnp.float32
    shape = jax.ShapeDtypeStruct
    held = ((1024, 1024), (1024, 512), (1024, 512), (1024, 1024), (8, 256, 1024), (8, 128, 1024))
    return pl.pallas_call(
        widen_kernel,
        name="widen",
        out_shape=(
            shape((1024,), wide),
            shape((1024,), wide),
            shape((1024,), wide),
            shape((512,), wide),
            shape((1024, EXPERTS), wide),
            shape((ROWS, 1024), low),
            shape((ROWS, 1024), low),
            shape((1024, 1024), wide),
            shape((1024, 512), wide),
            shape((1024, 512), wide),
            shape((1024, 1024), wide),
            shape((2, 1024, 512), wide),
            shape((2, 1024, 512), wide),
            shape((2, 512, 1024), wide),
        ),
        in_specs=[vmem] * 2 + [hbm] * 8,
        out_specs=(vmem,) * 5 + (hbm,) * 9,
        scratch_shapes=[
            *[pltpu.VMEM(size, low) for size in held],
            *[pltpu.VMEM(size, wide) for size in held],
            pltpu.SemaphoreType.DMA((24,)),
            pltpu.SemaphoreType.DMA((34,)),
        ],
        compiler_params=pltpu.CompilerParams(vmem_limit_bytes=56 * 2**20),
    )(*arrays)


def body(
    tokens,
    cotangent,
    lengths,
    routes,
    attn_gain,
    w_query,
    w_key,
    w_value,
    query_gain,
    key_gain,
    w_output,
    ffn_gain,
    w_router,
    w_gate,
    w_up,
    w_down,
):
    query_pos = lax.axis_index("dp") * ROWS + jnp.arange(ROWS, dtype=jnp.int32)
    cosine, sine_table = rope_tables(query_pos)
    cosine, sine_table = cosine.T, sine_table.T
    routes_t, length = routes[0].T, lengths.reshape(1, 1)
    gains = [attn_gain, query_gain, key_gain, ffn_gain]
    weights = (w_query, w_key, w_value, w_output)
    router_rows = w_router.T
    ffn_in, hidden, mixed_t, queries, log_total, normed, query_raw, key_raw, kv_all, cot_all = forward(
        tokens[0], cotangent[0], routes_t, length, cosine, sine_table, gains, weights
    )
    returned, mixed_parts, own_gu, own_down = moe(ffn_in, cot_all, router_rows, w_gate, w_up, w_down)
    mixed_low, token_low, early_small, late_small, *sums = backward(
        (
            hidden, ffn_in, cotangent[0], tokens[0], normed, key_raw, mixed_t, queries, log_total, routes_t,
            length, cosine, sine_table, *gains, router_rows,
        ),
        (returned, query_raw, mixed_parts, kv_all.reshape(8 * 1024, ROWS), *weights, own_gu, own_down),
    )
    (
        ffn_gain_sum, attn_gain_sum, query_gain_sum, key_gain_sum, router_sum, mixed_out, token_grad,
        query_w_sum, key_w_sum, value_w_sum, output_w_sum, gate_w_sum, up_w_sum, down_w_sum,
    ) = widen((early_small, late_small, mixed_low, token_low, *sums))
    return (
        mixed_out[None],
        token_grad[None],
        attn_gain_sum,
        query_w_sum,
        key_w_sum,
        value_w_sum,
        query_gain_sum,
        key_gain_sum,
        output_w_sum,
        ffn_gain_sum,
        router_sum,
        gate_w_sum,
        up_w_sum,
        down_w_sum,
    )


def solution(mesh):
    return jax.shard_map(
        body,
        mesh=mesh,
        in_specs=(
            P("expert", "dp", None),
            P("expert", "dp", None),
            P("expert"),
            P("expert", "dp", None),
            P(),
            P(),
            P(),
            P(),
            P(),
            P(),
            P(),
            P(),
            P(),
            P("expert", None, None),
            P("expert", None, None),
            P("expert", None, None),
        ),
        out_specs=(
            P("expert", "dp", None),
            P("expert", "dp", None),
            P(),
            P(),
            P(),
            P(),
            P(),
            P(),
            P(),
            P(),
            P(),
            P("expert", None, None),
            P("expert", None, None),
            P("expert", None, None),
        ),
        check_vma=False,
    )
```

```python
import math

import jax
import jax.numpy as jnp
from jax import lax
from jax.experimental import pallas as pl
from jax.experimental.pallas import tpu as pltpu
from jax.sharding import PartitionSpec as P

HEADS = 16
KV_HEADS = 8
HEAD_DIM = 64
EXPERTS = 32
TOPK = 8
CAP = 80


epsilon = 1e-06


def rope_tables(positions):
    steps_half = jnp.arange(HEAD_DIM // 2).astype(jnp.float32)
    inverse = jnp.exp(steps_half * (-2.0 * math.log(10000.0) / HEAD_DIM))
    angles = positions.astype(jnp.float32)[:, None] * inverse[None, :]
    return (jnp.cos(angles), jnp.sin(angles))


RING = 4
ROWS = 256
EXTRA = 16
FULL = ROWS + EXTRA
SENT = 160
LEFT = FULL - SENT
BOTH = ROWS + LEFT
GROUP = 4 * CAP
MESH = pl.DeviceIdType.MESH


def dot_nn(a, b):
    return jnp.dot(a, b, preferred_element_type=jnp.float32)


def dot_nt(a, b):
    return lax.dot_general(a, b, (((1,), (1,)), ((), ())), preferred_element_type=jnp.float32)


def dot_tn(a, b):
    return lax.dot_general(a, b, (((0,), (0,)), ((), ())), preferred_element_type=jnp.float32)


def step_of(size):
    return next(step for step in (64, 48, 32, 16) if size % step == 0)


class Torus:
    def __init__(self):
        self.dp = lax.axis_index("dp")
        expert = lax.axis_index("expert")
        self.expert = expert
        self.z, self.y = expert // RING, expert % RING

    def block(self, dz, dy):
        return ((self.z + dz + RING) % RING) * RING + (self.y + dy + RING) % RING

    def near(self, axis, step):
        return (self.dp, self.block(step, 0) if axis == "z" else self.block(0, step))

    def along(self, axis, other, step):
        return self.block(step, other) if axis == "z" else self.block(other, step)

    def neighbours(self):
        return [self.near(axis, step) for axis in "yz" for step in (1, -1)]


class Gather:
    def __init__(self, torus, buffer, send, recv, number, axis, other, low, first, second, stride):
        self.torus, self.buffer, self.send, self.recv = torus, buffer, send, recv
        self.number, self.axis, self.other, self.stride = number, axis, other, stride
        self.whole, self.front, self.rear = (low, first + second), (low, first), (low + first, second)

    def copy(self, which, offset, part, step):
        at = self.torus.along(self.axis, self.other, offset) * self.stride + part[0]
        rows = self.buffer.at[pl.ds(pl.multiple_of(at, 16), part[1])]
        return pltpu.make_async_remote_copy(
            src_ref=rows,
            dst_ref=rows,
            send_sem=self.send.at[self.number, which],
            recv_sem=self.recv.at[self.number, which],
            device_id=self.torus.near(self.axis, step),
            device_id_type=MESH,
        )

    def first(self):
        self.copy(0, 0, self.whole, 1).start()
        self.copy(1, 0, self.whole, -1).start()

    def second(self):
        self.copy(0, -1, self.whole, 1).wait_recv()
        self.copy(2, -1, self.front, 1).start()
        self.copy(1, 1, self.whole, -1).wait_recv()
        self.copy(3, 1, self.rear, -1).start()

    def third(self):
        self.copy(2, 2, self.front, 1).wait_recv()
        self.copy(3, 2, self.rear, -1).wait_recv()

    def drain(self):
        self.copy(0, 0, self.whole, 1).wait_send()
        self.copy(1, 0, self.whole, -1).wait_send()
        self.copy(2, -1, self.front, 1).wait_send()
        self.copy(3, 1, self.rear, -1).wait_send()


class Scatter:
    def __init__(self, torus, sums, landing, send, recv, number, base, axis, other, low, first, second):
        self.torus, self.sums, self.landing, self.send, self.recv = torus, sums, landing, send, recv
        self.number, self.axis, self.other = number, axis, other
        self.low, self.parts = low, (first, second)
        self.size = first + second
        self.slots = (base, base + first, base + self.size, base + 2 * self.size)

    def rows(self, which):
        if which == 0:
            return self.low, self.parts[0]
        if which == 1:
            return self.low + self.parts[0], self.parts[1]
        return self.low, self.size

    def at(self, offset):
        return self.torus.along(self.axis, self.other, offset)

    def copy(self, which):
        start, size = self.rows(which)
        offset = (2, 2, 1, -1)[which]
        return pltpu.make_async_remote_copy(
            src_ref=self.sums.at[self.at(offset), pl.ds(start, size)],
            dst_ref=self.landing.at[pl.ds(self.slots[which], size)],
            send_sem=self.send.at[self.number, which],
            recv_sem=self.recv.at[self.number, which],
            device_id=self.torus.near(self.axis, (1, -1, 1, -1)[which]),
            device_id_type=MESH,
        )

    def add(self, which, offset):
        start, size = self.rows(which)
        block = self.at(offset)

        many = step_of(size)

        @pl.loop(0, size // many)
        def _(k):
            here = pl.ds(pl.multiple_of(start + k * many, 16), many)
            there = pl.ds(pl.multiple_of(self.slots[which] + k * many, 16), many)
            total = self.sums[block, here].astype(jnp.float32) + self.landing[there].astype(jnp.float32)
            self.sums[block, here] = total.astype(jnp.bfloat16)

    def first(self):
        self.copy(0).start()
        self.copy(1).start()

    def second(self):
        self.copy(0).wait_recv()
        self.add(0, 1)
        self.copy(2).start()
        self.copy(1).wait_recv()
        self.add(1, -1)
        self.copy(3).start()

    def third(self, put=None):
        self.copy(2).wait_recv()
        self.copy(3).wait_recv()
        block = self.at(0)

        many = step_of(self.size)

        @pl.loop(0, self.size // many)
        def _(k):
            here = pl.ds(pl.multiple_of(self.low + k * many, 16), many)
            left = pl.ds(pl.multiple_of(self.slots[2] + k * many, 16), many)
            right = pl.ds(pl.multiple_of(self.slots[3] + k * many, 16), many)
            total = (
                self.sums[block, here].astype(jnp.float32)
                + self.landing[left].astype(jnp.float32)
                + self.landing[right].astype(jnp.float32)
            )
            if put is None:
                self.sums[block, here] = total.astype(jnp.bfloat16)
            else:
                put(here, total)

    def drain(self):
        for which in range(4):
            self.copy(which).wait_send()


def moe_kernel(
    ffn, cot, own_cot, wr, w_gate, w_up, w_down,
    ret, mixed, own_gu, own_down,
    rows, sums, wgu, wd, held, pair, inner, dgu, mixing, back, cotv, before, chosen, gate_rows, grad_rows, stage,
    mate_rows, gu_sums, down_sums,
    ag_send, ag_recv, rs_send, rs_recv, w_sem, cot_sem, own_sem, stage_sem, mate_send, mate_recv, x_send, x_recv, credit,
):
    torus = Torus()
    place, place_of = everywhere()
    barrier = pltpu.get_barrier_semaphore()
    peers = [*torus.neighbours(), place_of("core", 1), place_of("x", 1), place_of("x", -1)]
    for device in peers:
        pl.semaphore_signal(barrier, inc=1, device_id=device, device_id_type=MESH)

    weights = [
        pltpu.make_async_copy(w_gate, wgu.at[:, :, pl.ds(0, 512)], w_sem.at[0]),
        pltpu.make_async_copy(w_up, wgu.at[:, :, pl.ds(512, 512)], w_sem.at[1]),
        pltpu.make_async_copy(w_down, wd, w_sem.at[2]),
    ]
    for copy in weights:
        copy.start()

    def group_z(g):
        return (torus.z + g + (g // 2) * (1 - 2 * (g % 2))) % RING

    def cot_copy(g):
        return pltpu.make_async_copy(cot.at[pl.ds(pl.multiple_of(group_z(g) * RING * SENT, 16), RING * SENT)], cotv, cot_sem)

    cot_copy(0).start()
    first_row = torus.expert * BOTH
    own_copy = pltpu.make_async_copy(
        own_cot.at[pl.ds(ROWS - LEFT, LEFT)], rows.at[pl.ds(pl.multiple_of(first_row + ROWS, 16), LEFT)], own_sem
    )
    own_copy.start()
    rows[pl.ds(pl.multiple_of(first_row, 16), ROWS)] = ffn[...]
    own_copy.wait()
    pl.semaphore_wait(barrier, len(peers))

    def gather(number, axis, other, low, first, second):
        return Gather(torus, rows, ag_send, ag_recv, number, axis, other, low, first, second, BOTH)

    a_first = gather(0, "y", 0, 0, 96, 96)
    b_first = gather(1, "z", 0, 192, 96, 80)
    a_second = {d: gather(2 + d % RING, "z", d, 0, 96, 96) for d in (0, 1, -1, 2)}
    b_second = {d: gather(6 + d % RING, "y", d, 192, 96, 80) for d in (0, 1, -1, 2)}
    gathers = [a_first, b_first, *a_second.values(), *b_second.values()]

    a_first.first()
    b_first.first()
    b_second[0].first()
    a_second[0].first()
    a_first.second()
    b_first.second()
    for d in (1, -1):
        b_second[d].first()
        a_second[d].first()
    a_first.third()
    b_first.third()
    b_second[2].first()
    a_second[2].first()
    for copy in weights:
        copy.wait()

    earlier = lax.broadcasted_iota(jnp.int32, (ROWS, ROWS), 0) < lax.broadcasted_iota(jnp.int32, (ROWS, ROWS), 1)
    before[...] = jnp.where(earlier, 1.0, 0.0).astype(jnp.bfloat16)
    slot_at = lax.broadcasted_iota(jnp.int32, (CAP, ROWS), 0).astype(jnp.float32)

    def stage_copy(slot, target):
        return pltpu.make_async_copy(stage.at[slot], target, stage_sem.at[slot])

    expert_rows = lax.broadcasted_iota(jnp.int32, (EXPERTS, ROWS), 0)
    order = (2, 1, -1, 0)
    a_lead = {
        d: Scatter(torus, sums, rows, rs_send, rs_recv, n, n * 336, "z", d, 0, 64, 48) for n, d in enumerate(order)
    }
    b_lead = {
        d: Scatter(torus, sums, rows, rs_send, rs_recv, 4 + n, 1680 + n * 480, "y", d, 112, 80, 80)
        for n, d in enumerate(order)
    }
    a_last = Scatter(torus, sums, rows, rs_send, rs_recv, 8, 4 * 336, "y", 0, 0, 64, 48)
    b_last = Scatter(torus, sums, rows, rs_send, rs_recv, 9, 1680 + 4 * 480, "z", 0, 112, 80, 80)

    @pl.loop(0, 4)
    def _(g):
        @pl.when(g == 0)
        def _():
            b_second[0].second()
            a_second[0].second()
            b_second[0].third()

        @pl.when(g == 1)
        def _():
            for d in (1, -1, 2):
                b_second[d].second()
                a_second[d].second()
            b_second[1].third()

        @pl.when(g == 2)
        def _():
            b_second[-1].third()

        @pl.when(g == 3)
        def _():
            for d in (0, 1, -1, 2):
                a_second[d].third()
            b_second[2].third()

        cot_copy(g).wait()
        first_source = group_z(g) * RING

        @pl.loop(0, 4)
        def _(j):
            source = first_source + j
            block = rows[pl.ds(pl.multiple_of(source * BOTH, 16), ROWS)]
            laid = cotv[pl.ds(pl.multiple_of(j * SENT, 16), EXTRA)].astype(jnp.float32)
            member = jnp.concatenate([laid[:8, q * ROWS : (q + 1) * ROWS] for q in range(4)], axis=0)
            named = member > 0.5
            slots = dot_nn(member.astype(jnp.bfloat16), before[...])
            slots = jnp.where(named, slots, -1.0)
            logits = jnp.where(named, dot_nt(wr[...], block), -1e30)
            weight = jnp.where(named, jnp.exp(logits - jnp.max(logits, axis=0, keepdims=True)), 0.0)
            gates = weight / jnp.sum(weight, axis=0, keepdims=True)
            picked = []
            for e in range(2):
                own = jnp.sum(
                    jnp.where(expert_rows == torus.expert * 2 + e, slots, 0.0), axis=0, keepdims=True
                )
                picked.append(jnp.where(slot_at == own, 1.0, 0.0))
            both = jnp.concatenate(picked, axis=0).astype(jnp.bfloat16)
            chosen[j] = both
            grad_block = jnp.concatenate(
                [
                    cotv[pl.ds(pl.multiple_of(j * SENT + EXTRA, 16), SENT - EXTRA)],
                    rows[pl.ds(pl.multiple_of(source * BOTH + ROWS, 16), LEFT)],
                ],
                axis=0,
            )
            took = dot_nn(both, jnp.concatenate([block, grad_block], axis=1)).astype(jnp.bfloat16)
            here = pl.ds(pl.multiple_of(j * CAP, 16), CAP)
            there = pl.ds(pl.multiple_of(g * GROUP + j * CAP, 16), CAP)
            for e in range(2):
                own = jnp.sum(
                    jnp.where(expert_rows == torus.expert * 2 + e, gates, 0.0), axis=0, keepdims=True
                )
                of_rows = jnp.sum(picked[e] * own, axis=1, keepdims=True)
                gate_rows[e, here] = jnp.broadcast_to(of_rows, (CAP, 128))
                held[e, there] = took[e * CAP : (e + 1) * CAP, :1024]
                mixing[e, here] = took[e * CAP : (e + 1) * CAP, 1024:]

        @pl.when(g < 3)
        def _():
            cot_copy(g + 1).start()

        @pl.when(g == 3)
        def _():
            for one in gathers:
                one.drain()
            for device in peers:
                pl.semaphore_signal(credit, inc=1, device_id=device, device_id_type=MESH)
            pl.semaphore_wait(credit, len(peers))
            for d in (0, 1, -1):
                b_lead[d].first()

        @pl.loop(0, 2)
        def _(e):
            there = pl.ds(pl.multiple_of(g * GROUP, 16), GROUP)
            both = dot_nn(held[e, there], wgu[e])
            gate, up = both[:, :512], both[:, 512:]
            sig = jax.nn.sigmoid(gate)
            silu = gate * sig
            act = (silu * up).astype(jnp.bfloat16)
            inner[e, there] = act
            out = dot_nn(act, wd[e]).astype(jnp.bfloat16).astype(jnp.float32)
            grad = mixing[e].astype(jnp.float32)
            weight = gate_rows[e][:, :1]
            grad_rows[e] = jnp.broadcast_to(jnp.sum(grad * out, axis=1, keepdims=True), (GROUP, 128))
            pair[e, there] = (weight * grad).astype(jnp.bfloat16)
            mixing[e] = (weight * out).astype(jnp.bfloat16)
            inner_grad = dot_nt(pair[e, there], wd[e])
            dgu[e, there, :512] = (inner_grad * up * sig * (1.0 + gate * (1.0 - sig))).astype(jnp.bfloat16)
            dgu[e, there, 512:] = (inner_grad * silu).astype(jnp.bfloat16)
            back[e] = dot_nt(dgu[e, there], wgu[e]).astype(jnp.bfloat16)

        @pl.loop(0, 4)
        def _(j):
            source = first_source + j
            both = chosen[j]
            picked = both.astype(jnp.float32)
            here = pl.ds(pl.multiple_of(j * CAP, 16), CAP)
            compact = jnp.concatenate(
                [jnp.concatenate([back[e, here], mixing[e, here]], axis=1) for e in range(2)], axis=0
            )
            spread = dot_tn(both, compact).astype(jnp.bfloat16)
            sums[source, pl.ds(EXTRA, ROWS)] = spread[:, :1024]
            grads = jnp.zeros((EXPERTS, ROWS), jnp.float32)
            for e in range(2):
                own = jnp.sum(
                    picked[e * CAP : (e + 1) * CAP] * grad_rows[e, here][:, :1], axis=0, keepdims=True
                )
                grads = grads + jnp.where(expert_rows == torus.expert * 2 + e, own, 0.0)
            laid = jnp.concatenate([grads[8 * q : 8 * q + 8] for q in range(4)], axis=1)
            sums[source, pl.ds(0, EXTRA)] = jnp.concatenate([laid, jnp.zeros_like(laid)], axis=0).astype(
                jnp.bfloat16
            )
            slot = j % 2

            @pl.when((g > 0) | (j > 1))
            def _():
                stage_copy(slot, mixed.at[source]).wait()

            stage[slot] = spread[:, 1024:]
            stage_copy(slot, mixed.at[source]).start()

    def chunk(e, k):
        if k < 4:
            return dot_tn(held[e, :, k * 256 : (k + 1) * 256], dgu[e]).astype(jnp.bfloat16)
        return dot_tn(inner[e, :, (k - 4) * 256 : (k - 3) * 256], pair[e]).astype(jnp.bfloat16)

    def mate_copy(k):
        return pltpu.make_async_remote_copy(
            src_ref=stage.at[k % 2],
            dst_ref=mate_rows.at[pl.ds(k * 256, 256)],
            send_sem=mate_send.at[k],
            recv_sem=mate_recv.at[k],
            device_id=place_of("core", 1),
            device_id_type=MESH,
        )

    line = Line(place, place_of)
    rings = [
        Scatter(line, gu_sums, rows, x_send, x_recv, 0, 4080, "x", 0, 0, 128, 128),
        Scatter(line, down_sums, rows, x_send, x_recv, 1, 4848, "x", 0, 0, 64, 64),
    ]

    b_lead[2].first()
    for d in order:
        a_lead[d].first()
    for d in (0, 1, -1):
        b_lead[d].second()
    for k in range(6):
        if k < 2:
            stage_copy(k, mixed.at[0]).wait()
        else:
            mate_copy(k - 2).wait_send()
        stage[k % 2] = chunk(1 - place["core"], k)
        mate_copy(k).start()
        own = chunk(place["core"], k)
        if k < 4:
            gu_sums[k] = own
        else:
            down_sums[2 * k - 8] = own[:128]
            down_sums[2 * k - 7] = own[128:]
    b_lead[2].second()
    for d in order:
        a_lead[d].second()
    for k in range(6):
        mate_copy(k).wait_recv()

        @pl.loop(0, 4)
        def _(n):
            other = mate_rows[pl.ds(pl.multiple_of(k * 256 + n * 64, 64), 64)].astype(jnp.float32)
            if k < 4:
                at = (k, pl.ds(pl.multiple_of(n * 64, 64), 64))
                gu_sums[at] = (gu_sums[at].astype(jnp.float32) + other).astype(jnp.bfloat16)
            else:
                at = (2 * k - 8 + n // 2, pl.ds(pl.multiple_of(n % 2 * 64, 64), 64))
                down_sums[at] = (down_sums[at].astype(jnp.float32) + other).astype(jnp.bfloat16)

    for one in rings:
        one.first()
    for one in rings:
        one.second()
    for d in order:
        b_lead[d].third()
        a_lead[d].third()
        if d == 2:
            b_last.first()
            a_last.first()
    b_last.second()
    a_last.second()

    def put(at, total):
        ret[at] = total

    b_last.third(put)
    a_last.third(put)

    def put_gu(at, total):
        own_gu[at] = total.astype(jnp.bfloat16)

    def put_down(at, total):
        own_down[at] = total.astype(jnp.bfloat16)

    rings[0].third(put_gu)
    rings[1].third(put_down)
    for one in [*a_lead.values(), *b_lead.values(), a_last, b_last, *rings]:
        one.drain()
    for k in (4, 5):
        mate_copy(k).wait_send()


def moe(ffn_in, cot_all, own_cot, router_rows, w_gate, w_up, w_down):
    vmem, hbm = pl.BlockSpec(memory_space=pltpu.VMEM), pl.BlockSpec(memory_space=pl.ANY)
    low, total = jnp.bfloat16, 4 * GROUP
    return pl.pallas_call(
        moe_kernel,
        name="moe",
        out_shape=(
            jax.ShapeDtypeStruct((FULL, 1024), jnp.float32),
            jax.ShapeDtypeStruct((16, ROWS, 1024), low),
            jax.ShapeDtypeStruct((256, 1024), low),
            jax.ShapeDtypeStruct((128, 1024), low),
        ),
        in_specs=[vmem, hbm, hbm, vmem, hbm, hbm, hbm],
        out_specs=(vmem, hbm, vmem, vmem),
        scratch_shapes=[
            pltpu.VMEM((16 * BOTH, 1024), low),
            pltpu.VMEM((16, FULL, 1024), low),
            pltpu.VMEM((2, 1024, 1024), low),
            pltpu.VMEM((2, 512, 1024), low),
            pltpu.VMEM((2, total, 1024), low),
            pltpu.VMEM((2, total, 1024), low),
            pltpu.VMEM((2, total, 512), low),
            pltpu.VMEM((2, total, 1024), low),
            pltpu.VMEM((2, GROUP, 1024), low),
            pltpu.VMEM((2, GROUP, 1024), low),
            pltpu.VMEM((4 * SENT, 1024), low),
            pltpu.VMEM((ROWS, ROWS), low),
            pltpu.VMEM((4, 2 * CAP, ROWS), low),
            pltpu.VMEM((2, GROUP, 128), jnp.float32),
            pltpu.VMEM((2, GROUP, 128), jnp.float32),
            pltpu.VMEM((2, ROWS, 1024), low),
            pltpu.VMEM((6 * 256, 1024), low),
            pltpu.VMEM((4, 256, 1024), low),
            pltpu.VMEM((4, 128, 1024), low),
            pltpu.SemaphoreType.DMA((10, 4)),
            pltpu.SemaphoreType.DMA((10, 4)),
            pltpu.SemaphoreType.DMA((10, 4)),
            pltpu.SemaphoreType.DMA((10, 4)),
            pltpu.SemaphoreType.DMA((3,)),
            pltpu.SemaphoreType.DMA,
            pltpu.SemaphoreType.DMA,
            pltpu.SemaphoreType.DMA((2,)),
            pltpu.SemaphoreType.DMA((6,)),
            pltpu.SemaphoreType.DMA((6,)),
            pltpu.SemaphoreType.DMA((2, 4)),
            pltpu.SemaphoreType.DMA((2, 4)),
            pltpu.SemaphoreType.REGULAR,
        ],
        compiler_params=pltpu.CompilerParams(
            collective_id=1, has_side_effects=True, vmem_limit_bytes=63 * 2**20
        ),
        cost_estimate=pl.CostEstimate(flops=50 * 10**9, bytes_accessed=40 * 10**6, transcendentals=2 * 10**6),
    )(ffn_in, cot_all, own_cot, router_rows, w_gate, w_up, w_down)


def everywhere():
    dp, expert = lax.axis_index("dp"), lax.axis_index("expert")
    here = {"x": dp // 2, "core": dp % 2, "z": expert // RING, "y": expert % RING}

    def device(axis, step):
        there = dict(here)
        size = 2 if axis == "core" else RING
        there[axis] = (here[axis] + step + size) % size
        return (there["x"] * 2 + there["core"], there["z"] * RING + there["y"])

    return here, device


def rms_scale(values):
    return lax.rsqrt(jnp.mean(values * values, axis=-1, keepdims=True) + epsilon)


def as_row(gain):
    return gain[...].astype(jnp.float32).reshape(1, -1)


def turned_rows(values, cosine, sine):
    front, back = values[: HEAD_DIM // 2], values[HEAD_DIM // 2 :]
    return jnp.concatenate([front * cosine - back * sine, back * cosine + front * sine], axis=0)


def kv_order(here, step):
    turn = step // 2
    return (turn % 2) * (3 - turn // 2) + (1 - turn % 2) * (turn // 2)


class Keys:
    def __init__(self, here, device, blocks, send, recv):
        self.here, self.device, self.blocks, self.send, self.recv = here, device, blocks, send, recv
        self.lines = blocks.shape[1]

    def copy(self, which):
        half = self.lines // 2
        offset, start, size, axis, step = (
            (0, 0, self.lines, "core", 1),
            (0, 0, self.lines, "x", 1),
            (0, 0, self.lines, "x", -1),
            (-1, 0, half, "x", 1),
            (1, half, half, "x", -1),
            (-1, 0, self.lines, "core", 1),
            (1, 0, self.lines, "core", 1),
            (2, 0, self.lines, "core", 1),
        )[which]
        block = (self.here["x"] + offset + RING) % RING * 2 + self.here["core"]
        part = self.blocks.at[block, pl.ds(start, size)]
        return pltpu.make_async_remote_copy(
            src_ref=part,
            dst_ref=part,
            send_sem=self.send.at[which],
            recv_sem=self.recv.at[which],
            device_id=self.device(axis, step),
            device_id_type=MESH,
        )

    def start(self, *which):
        for one in which:
            self.copy(one).start()

    def arrive(self, *which):
        for one in which:
            self.copy(one).wait_recv()

    def drain(self):
        for one in range(8):
            self.copy(one).wait_send()


def forward_kernel(
    tokens, cot, routes_t, length, cosine, sine, attn_gain, query_gain, key_gain, ffn_gain,
    w_query, w_key, w_value, w_output,
    ffn_in, hidden, mixed_t, queries, log_total, normed, query_raw, key_raw, kv_all, cot_all,
    wq, wk, wv, wo, kv, turned, most, total, mixed, packed,
    ag_send, ag_recv, kv_send, kv_recv, w_sem, kv_sem, own_sem,
):
    torus = Torus()
    here, device = everywhere()
    me = here["x"] * 2 + here["core"]
    barrier = pltpu.get_barrier_semaphore()
    peers = [*torus.neighbours(), device("core", 1), device("x", 1), device("x", -1)]
    for peer in peers:
        pl.semaphore_signal(barrier, inc=1, device_id=peer, device_id_type=MESH)
    loads = [
        pltpu.make_async_copy(source, target, w_sem.at[n])
        for n, (source, target) in enumerate(((w_query, wq), (w_key, wk), (w_value, wv), (w_output, wo)))
    ]
    for load in loads:
        load.start()

    expert_rows = lax.broadcasted_iota(jnp.int32, (EXPERTS, ROWS), 0)
    member = jnp.zeros((EXPERTS, ROWS), jnp.float32)
    for k in range(TOPK):
        member = member + jnp.where(expert_rows == routes_t[pl.ds(k, 1), :], 1.0, 0.0)
    laid = jnp.concatenate([member[8 * q : 8 * q + 8] for q in range(4)], axis=1)
    packed[...] = jnp.concatenate([laid, jnp.zeros_like(laid)], axis=0).astype(jnp.bfloat16)
    first_row = pl.multiple_of(torus.expert * SENT, 16)
    owns = [
        pltpu.make_async_copy(packed, cot_all.at[pl.ds(first_row, EXTRA)], own_sem.at[0]),
        pltpu.make_async_copy(
            cot.at[pl.ds(0, SENT - EXTRA)],
            cot_all.at[pl.ds(pl.multiple_of(first_row + EXTRA, 16), SENT - EXTRA)],
            own_sem.at[1],
        ),
    ]
    for copy in owns:
        copy.start()
    for copy in owns:
        copy.wait()
    pl.semaphore_wait(barrier, len(peers))

    def gather(number, axis, other, low, first, second):
        return Gather(torus, cot_all, ag_send, ag_recv, number, axis, other, low, first, second, SENT)

    a_first = gather(0, "y", 0, 0, 48, 32)
    b_first = gather(1, "z", 0, 80, 48, 32)
    a_second = {d: gather(2 + d % RING, "z", d, 0, 48, 32) for d in (0, 1, -1, 2)}
    b_second = {d: gather(6 + d % RING, "y", d, 80, 48, 32) for d in (0, 1, -1, 2)}
    gathers = [a_first, b_first, *a_second.values(), *b_second.values()]
    a_first.first()
    b_first.first()
    b_second[0].first()
    a_second[0].first()

    @pl.loop(0, 4)
    def _(n):
        at = pl.ds(pl.multiple_of(n * 64, 64), 64)
        rows = tokens[at].astype(jnp.float32)
        normed[at] = (rows * rms_scale(rows) * as_row(attn_gain)).astype(jnp.bfloat16)

    for load in loads:
        load.wait()

    keys = Keys(here, device, kv, kv_send, kv_recv)
    key_raw[...] = dot_nn(normed[...], wk[...])
    scaled = key_raw[...]
    scaled = (scaled * rms_scale(scaled) * as_row(key_gain)).T
    for j in range(KV_HEADS):
        head = turned_rows(scaled[j * 64 : j * 64 + 64], cosine[...], sine[...])
        kv[me, pl.ds(j * 64, 64)] = head.astype(jnp.bfloat16)
    kv[me, pl.ds(512, 512)] = dot_nn(normed[...], wv[...]).T.astype(jnp.bfloat16)
    keys.start(0, 1, 2)
    query_raw[...] = dot_nn(normed[...], wq[...])
    scaled = query_raw[...]
    turned[...] = (scaled * rms_scale(scaled) * as_row(query_gain)).T

    for j in range(KV_HEADS):
        for r in range(2):
            head = turned[j * 128 + r * 64 : j * 128 + r * 64 + 64]
            head = turned_rows(head, cosine[...], sine[...])
            queries[j, :, r * ROWS : (r + 1) * ROWS] = (head * HEAD_DIM**-0.5).astype(jnp.bfloat16)

    a_first.second()
    b_first.second()
    for d in (1, -1):
        b_second[d].first()
        a_second[d].first()

    key_at = lax.broadcasted_iota(jnp.int32, (ROWS, 2 * ROWS), 0)
    query_at = lax.broadcasted_iota(jnp.int32, (ROWS, 2 * ROWS), 1) % ROWS
    valid = (key_at <= query_at) & (key_at + me * ROWS < length[...])

    def heads_of(block):
        keys_here = [kv[block, j * 64 : j * 64 + 64] for j in range(KV_HEADS)]
        values_here = [kv[block, 512 + j * 64 : 576 + j * 64] for j in range(KV_HEADS)]
        return keys_here, values_here

    keys_here, values_here = heads_of(me)
    scores = [jnp.where(valid, dot_tn(keys_here[j], queries[j]), -1e30) for j in range(KV_HEADS)]
    tops = [jnp.max(one, axis=0, keepdims=True) for one in scores]
    probs = [jnp.exp(one - top) for one, top in zip(scores, tops)]
    parts = [dot_nn(one, prob.astype(jnp.bfloat16)) for one, prob in zip(values_here, probs)]
    for j in range(KV_HEADS):
        most[j] = tops[j]
        total[j] = jnp.sum(probs[j], axis=0, keepdims=True)
        mixed[j] = parts[j]

    @pl.loop(1, 8)
    def _(step):
        @pl.when(step == 1)
        def _():
            a_first.third()
            b_first.third()
            b_second[2].first()
            a_second[2].first()
            keys.arrive(0)

        @pl.when(step == 2)
        def _():
            keys.arrive(1)
            keys.start(3, 5)
            keys.arrive(2)
            keys.start(4, 6)
            b_second[0].second()
            a_second[0].second()

        @pl.when(step == 3)
        def _():
            keys.arrive(5)
            for d in (1, -1):
                b_second[d].second()
                a_second[d].second()

        @pl.when(step == 5)
        def _():
            keys.arrive(3, 4)
            keys.start(7)
            keys.arrive(6)
            b_second[2].second()
            a_second[2].second()

        @pl.when(step == 7)
        def _():
            keys.arrive(7)

        block = (here["x"] + kv_order(here, step) + RING) % RING * 2 + (here["core"] + step) % 2

        @pl.when(block < me)
        def _():
            keys_here, values_here = heads_of(block)
            before = [most[j] for j in range(KV_HEADS)]
            shares = [total[j] for j in range(KV_HEADS)]
            sums = [mixed[j] for j in range(KV_HEADS)]
            scores = [dot_tn(keys_here[j], queries[j]) for j in range(KV_HEADS)]
            tops = [jnp.maximum(old, jnp.max(one, axis=0, keepdims=True)) for old, one in zip(before, scores)]
            probs = [jnp.exp(one - top) for one, top in zip(scores, tops)]
            less = [jnp.exp(old - top) for old, top in zip(before, tops)]
            parts = [dot_nn(one, prob.astype(jnp.bfloat16)) for one, prob in zip(values_here, probs)]
            for j in range(KV_HEADS):
                most[j] = tops[j]
                total[j] = shares[j] * less[j] + jnp.sum(probs[j], axis=0, keepdims=True)
                mixed[j] = sums[j] * less[j] + parts[j]

    save = pltpu.make_async_copy(kv, kv_all, kv_sem)
    save.start()

    for j in range(KV_HEADS):
        share = total[j]
        log_total[j] = most[j] + jnp.log(share)
        head = (mixed[j] * (1.0 / share)).astype(jnp.bfloat16)
        for r in range(2):
            mixed_t[j * 128 + r * 64 : j * 128 + r * 64 + 64, :] = head[:, r * ROWS : (r + 1) * ROWS]

    hidden[...] = dot_tn(mixed_t[...], wo[...])

    @pl.loop(0, 4)
    def _(n):
        at = pl.ds(pl.multiple_of(n * 64, 64), 64)
        rows = hidden[at] + tokens[at].astype(jnp.float32)
        hidden[at] = rows
        ffn_in[at] = (rows * rms_scale(rows) * as_row(ffn_gain)).astype(jnp.bfloat16)

    for d in (0, 1, -1, 2):
        a_second[d].third()
        b_second[d].third()
    save.wait()
    keys.drain()
    for one in gathers:
        one.drain()


def forward(tokens, cot, routes_t, length, cosine, sine, gains, weights):
    vmem, hbm = pl.BlockSpec(memory_space=pltpu.VMEM), pl.BlockSpec(memory_space=pl.ANY)
    low, wide = jnp.bfloat16, jnp.float32
    shape = jax.ShapeDtypeStruct
    return pl.pallas_call(
        forward_kernel,
        name="forward",
        out_shape=(
            shape((ROWS, 1024), low),
            shape((ROWS, 1024), wide),
            shape((1024, ROWS), low),
            shape((KV_HEADS, HEAD_DIM, 2 * ROWS), low),
            shape((KV_HEADS, 1, 2 * ROWS), wide),
            shape((ROWS, 1024), low),
            shape((ROWS, 1024), wide),
            shape((ROWS, 512), wide),
            shape((8, 1024, ROWS), low),
            shape((16 * SENT, 1024), low),
        ),
        in_specs=[vmem] * 10 + [hbm] * 4,
        out_specs=(vmem,) * 8 + (hbm, hbm),
        scratch_shapes=[
            pltpu.VMEM((1024, 1024), low),
            pltpu.VMEM((1024, 512), low),
            pltpu.VMEM((1024, 512), low),
            pltpu.VMEM((1024, 1024), low),
            pltpu.VMEM((8, 1024, ROWS), low),
            pltpu.VMEM((1024, ROWS), wide),
            pltpu.VMEM((KV_HEADS, 1, 2 * ROWS), wide),
            pltpu.VMEM((KV_HEADS, 1, 2 * ROWS), wide),
            pltpu.VMEM((KV_HEADS, HEAD_DIM, 2 * ROWS), wide),
            pltpu.VMEM((EXTRA, 1024), low),
            pltpu.SemaphoreType.DMA((10, 4)),
            pltpu.SemaphoreType.DMA((10, 4)),
            pltpu.SemaphoreType.DMA((8,)),
            pltpu.SemaphoreType.DMA((8,)),
            pltpu.SemaphoreType.DMA((4,)),
            pltpu.SemaphoreType.DMA,
            pltpu.SemaphoreType.DMA((2,)),
        ],
        compiler_params=pltpu.CompilerParams(
            collective_id=3, has_side_effects=True, vmem_limit_bytes=56 * 2**20
        ),
    )(tokens, cot, routes_t, length, cosine, sine, *gains, *weights)


ORDERS = (("x", "y", "z"), ("y", "z", "x"), ("z", "x", "y"))
STREAMS = {2048: ((0, 768), (768, 768), (1536, 512)), 2304: ((0, 768), (768, 768), (1536, 768))}


class Total:
    def __init__(self, here, device, buffer, shift, final, landing, work, send, recv, number, stream, half):
        self.here, self.device, self.buffer, self.shift, self.final = here, device, buffer, shift, final
        self.landing, self.work = landing, work
        self.send, self.recv, self.number, self.order = send, recv, number, ORDERS[(stream + number // 3) % 3]
        self.half = half
        self.start, self.rows = STREAMS[half][stream]
        first = self.start + self.start * 9 // 8
        r = self.rows
        self.lands = (first, first + r, first + r + 3 * (r // 4), first + r + 3 * (r // 4) + 3 * (r // 16))

    def own(self):
        return self.here["core"] * self.half + self.start

    def copy(self, which, source, target, axis, step):
        return pltpu.make_async_remote_copy(
            src_ref=source,
            dst_ref=target,
            send_sem=self.send.at[self.number, which],
            recv_sem=self.recv.at[self.number, which],
            device_id=self.device(axis, step),
            device_id_type=MESH,
        )

    def held(self, at, size):
        return self.buffer.at[pl.ds(pl.multiple_of(at + self.shift, 16), size)]

    def ready(self, at, size):
        return self.final.at[pl.ds(pl.multiple_of(at, 16), size)]

    def land(self, stage, n, size):
        return self.landing.at[pl.ds(self.lands[stage] + n * size, size)]

    def copies(self, stage):
        r, own = self.rows, self.own()
        a, b, c = self.order
        ia, ib = self.here[a], self.here[b]
        second = own + ia * (r // 4)
        third = second + ib * (r // 16)
        if stage == 0:
            there = (1 - self.here["core"]) * self.half + self.start
            return [self.copy(0, self.held(there, r), self.land(0, 0, r), "core", 1)]
        if stage == 6:
            return [self.copy(16, self.ready(own, r), self.ready(own, r), "core", 1)]
        found = []
        for d in (1, 2, 3):
            if stage == 1:
                source, target, axis = self.held(own + (ia + d) % RING * (r // 4), r // 4), self.land(1, d - 1, r // 4), a
            elif stage == 2:
                source = self.held(second + (ib + d) % RING * (r // 16), r // 16)
                target, axis = self.land(2, d - 1, r // 16), b
            elif stage == 3:
                source = self.work.at[self.number, pl.ds(0, r // 16)]
                target, axis = self.land(3, d - 1, r // 16), c
            elif stage == 4:
                source, target, axis = self.ready(third, r // 16), self.ready(third, r // 16), b
            else:
                source, target, axis = self.ready(second, r // 4), self.ready(second, r // 4), a
            found.append(self.copy(1 + (stage - 1) * 3 + d - 1, source, target, axis, d))
        return found

    def begin(self, stage):
        for copy in self.copies(stage):
            copy.start()

    def add(self, stage, load, store, size, count):
        step = 64 if size % 64 == 0 else 16

        @pl.loop(0, size // step)
        def _(k):
            at = k * step
            total = load(at, step).astype(jnp.float32)
            for n in range(count):
                land = pl.ds(pl.multiple_of(self.lands[stage] + n * size + at, 16), step)
                total = total + self.landing[land].astype(jnp.float32)
            store(at, step, total.astype(jnp.bfloat16))

    def finish(self, stage):
        for copy in self.copies(stage):
            copy.wait_recv()
        if stage > 3:
            return
        r, own = self.rows, self.own()
        a, b, _ = self.order
        second = own + self.here[a] * (r // 4)
        third = second + self.here[b] * (r // 16)
        first = (own, second, third, third)[stage] + self.shift

        def in_place(at, step, *value):
            lines = pl.ds(pl.multiple_of(first + at, 16), step)
            if not value:
                return self.buffer[lines]
            self.buffer[lines] = value[0]

        def in_work(at, step, *value):
            lines = pl.ds(pl.multiple_of(at, 16), step)
            if not value:
                return self.work[self.number, lines]
            self.work[self.number, lines] = value[0]

        def in_final(at, step, value):
            self.final[pl.ds(pl.multiple_of(third + at, 16), step)] = value

        if stage == 0:
            self.add(0, in_place, in_place, r, 1)
        elif stage == 1:
            self.add(1, in_place, in_place, r // 4, 3)
        elif stage == 2:
            self.add(2, in_place, in_work, r // 16, 3)
        else:
            self.add(3, in_work, in_final, r // 16, 3)

    def drain(self):
        for stage in range(7):
            for copy in self.copies(stage):
                copy.wait_send()


class Small:
    STAGES = (("core", (1,)), ("x", (1, 2, 3)), ("y", (1, 2, 3)), ("z", (1, 2, 3)))

    def __init__(self, device, value, landing, send, recv):
        self.device, self.value, self.landing, self.send, self.recv = device, value, landing, send, recv

    def copies(self, stage):
        axis, steps = self.STAGES[stage]
        first = sum(len(s) for _, s in self.STAGES[:stage])
        return [
            pltpu.make_async_remote_copy(
                src_ref=self.value.at[stage],
                dst_ref=self.landing.at[first + n],
                send_sem=self.send.at[first + n],
                recv_sem=self.recv.at[first + n],
                device_id=self.device(axis, step),
                device_id_type=MESH,
            )
            for n, step in enumerate(steps)
        ]

    def begin(self, stage):
        for copy in self.copies(stage):
            copy.start()

    def finish(self, stage):
        for copy in self.copies(stage):
            copy.wait_recv()
        first = sum(len(s) for _, s in self.STAGES[:stage])
        total = self.value[stage]
        for n in range(len(self.STAGES[stage][1])):
            total = total + self.landing[first + n]
        self.value[stage + 1] = total

    def drain(self):
        for stage in range(4):
            for copy in self.copies(stage):
                copy.wait_send()


class Line:
    def __init__(self, here, device):
        self.here, self.device = here, device

    def along(self, axis, other, step):
        return (self.here["x"] + step + RING) % RING

    def near(self, axis, step):
        return self.device("x", step)


def rms_back(values, gain, grad):
    scale = rms_scale(values)
    lifted = gain * grad
    inner = jnp.mean(values * lifted, axis=-1, keepdims=True)
    return scale * lifted - values * (scale * scale * scale) * inner, jnp.sum(
        grad * values * scale, axis=0, keepdims=True
    )


def turned_back(grads, cosine, sine):
    front, back = grads[: HEAD_DIM // 2], grads[HEAD_DIM // 2 :]
    return jnp.concatenate([front * cosine + back * sine, back * cosine - front * sine], axis=0)


def backward_kernel(
    hidden, ffn_in, cot, tokens, normed, key_raw, mixed_t, queries, log_total,
    routes_t, length, cosine, sine, attn_gain, query_gain, key_gain, ffn_gain, router_rows, own_gu, own_down,
    returned_all, query_raw_all, mixed_parts, kv_all, w_query, w_key, w_value, w_output,
    mixed_out, token_grad, early_small, late_small, query_sum, key_sum, value_sum, output_sum, all_gu, all_down,
    sums, rows, returned, square, kv, hidden_grad, result, branch, grads, delta, query_grad, turned,
    for_mate, from_mate, kv_sums, kv_rows, key_low, value_low,
    held, final_output, final_query, final_keys, land_output, land_query, land_keys, work, late_values, late_rows,
    rs_send, rs_recv, mate_send, mate_recv, kv_send, kv_recv, ar_send, ar_recv, small_send, small_recv, load_sem, out_sem, ex_send, ex_recv,
):
    torus = Torus()
    here, device = everywhere()
    me = here["x"] * 2 + here["core"]
    barrier = pltpu.get_barrier_semaphore()
    peers = [device("core", 1)] + [device(axis, d) for axis in "xyz" for d in (1, 2, 3)]
    for peer in peers:
        pl.semaphore_signal(barrier, inc=1, device_id=peer, device_id_type=MESH)
    loads = [
        pltpu.make_async_copy(source, target, load_sem.at[n])
        for n, (source, target) in enumerate(
            ((returned_all, returned), (w_output, square), (mixed_parts, sums), (kv_all, kv))
        )
    ]
    for load in loads:
        load.start()
    owns = [
        pltpu.make_async_copy(own_gu, all_gu.at[me], load_sem.at[8]),
        pltpu.make_async_copy(own_down, all_down.at[me], load_sem.at[9]),
    ]
    for copy in owns:
        copy.start()
    order = (2, 1, -1, 0)
    leads = []
    for n, d in enumerate(order):
        leads.append(Scatter(torus, sums, rows, rs_send, rs_recv, n, n * 384, "z", d, 0, 64, 64))
        leads.append(Scatter(torus, sums, rows, rs_send, rs_recv, 4 + n, (5 + n) * 384, "y", d, 128, 64, 64))
    lasts = [
        Scatter(torus, sums, rows, rs_send, rs_recv, 8, 4 * 384, "y", 0, 0, 64, 64),
        Scatter(torus, sums, rows, rs_send, rs_recv, 9, 9 * 384, "z", 0, 128, 64, 64),
    ]
    ring = Scatter(Line(here, device), kv_sums, kv_rows, kv_send, kv_recv, 0, 0, "x", 0, 0, 512, 512)
    experts = [
        Keys(here, device, blocks, ex_send.at[n], ex_recv.at[n]) for n, blocks in enumerate((all_gu, all_down))
    ]
    for copy in owns:
        copy.wait()
    pl.semaphore_wait(barrier, len(peers))
    for one in experts:
        one.start(0, 1, 2)
    loads[2].wait()
    for one in leads:
        one.first()

    expert_rows = lax.broadcasted_iota(jnp.int32, (EXPERTS, ROWS), 0)
    member = jnp.zeros((EXPERTS, ROWS), jnp.float32)
    for k in range(TOPK):
        member = member + jnp.where(expert_rows == routes_t[pl.ds(k, 1), :], 1.0, 0.0)
    named = member > 0.5
    logits = jnp.where(named, dot_nt(router_rows[...], ffn_in[...]), -1e30)
    weight = jnp.where(named, jnp.exp(logits - jnp.max(logits, axis=0, keepdims=True)), 0.0)
    gates = weight / jnp.sum(weight, axis=0, keepdims=True)
    loads[0].wait()
    gate_grad = jnp.concatenate([returned[:8, q * ROWS : (q + 1) * ROWS] for q in range(4)], axis=0)
    logit_grad = (gates * (gate_grad - jnp.sum(gates * gate_grad, axis=0, keepdims=True))).astype(jnp.bfloat16)
    result[...] = dot_tn(logit_grad, router_rows[...])
    router_grad = dot_nn(logit_grad, ffn_in[...]).astype(jnp.bfloat16)
    for q in range(4):
        held[2048 + q * EXPERTS : 2048 + (q + 1) * EXPERTS] = router_grad[:, q * 256 : (q + 1) * 256]

    def ffn_part(n, gain_grad):
        at = pl.ds(pl.multiple_of(n * 64, 64), 64)
        grad = result[at] + returned[pl.ds(pl.multiple_of(n * 64 + EXTRA, 16), 64)]
        part, more = rms_back(hidden[at], as_row(ffn_gain), grad)
        part = part + cot[at].astype(jnp.float32)
        hidden_grad[at] = part
        branch[at] = part.astype(jnp.bfloat16)
        return gain_grad + more

    gain_grad = lax.fori_loop(0, 4, ffn_part, jnp.zeros((1, 1024), jnp.float32))
    gain_lines = [gain_grad[:, q * 256 : (q + 1) * 256] for q in range(4)] + [jnp.zeros((124, 256), jnp.float32)]
    held[2176:2304] = jnp.concatenate(gain_lines, axis=0).astype(jnp.bfloat16)
    held[4352:4608] = jnp.zeros((256, 256), jnp.bfloat16)

    loads[1].wait()
    turned[...] = dot_nt(square[...], branch[...])
    next_load = pltpu.make_async_copy(w_query, square, load_sem.at[6])
    next_load.start()
    query_raw = returned.at[pl.ds(0, ROWS)]
    raw_load = pltpu.make_async_copy(query_raw_all, query_raw, load_sem.at[7])
    raw_load.start()

    for j in range(KV_HEADS):
        for r in range(2):
            at = slice(j * 128 + r * 64, j * 128 + r * 64 + 64)
            low = turned[at].astype(jnp.bfloat16)
            grads[j, :, r * ROWS : (r + 1) * ROWS] = low
            delta[j, :, r * ROWS : (r + 1) * ROWS] = jnp.sum(
                low.astype(jnp.float32) * mixed_t[at].astype(jnp.float32), axis=0, keepdims=True
            )
        query_grad[j] = jnp.zeros((HEAD_DIM, 2 * ROWS), jnp.float32)

    @pl.loop(0, 4)
    def _(n):
        at = pl.ds(pl.multiple_of(n * 256, 256), 256)
        part = dot_nn(mixed_t[at], branch[...]).astype(jnp.bfloat16)
        for q in range(4):
            held[pl.ds(pl.multiple_of(q * 1024 + q // 2 * 256 + n * 256, 256), 256)] = part[:, q * 256 : (q + 1) * 256]

    loads[3].wait()

    def reduction(number, buffer, shift, final, land, half):
        return [
            Total(here, device, buffer, shift, final, land, work, ar_send, ar_recv, 3 * number + s, s, half)
            for s in range(3)
        ]

    early = reduction(0, held, 0, final_output, land_output, 2304)
    of_query = reduction(1, kv, 0, final_query, land_query, 2048)
    of_keys = reduction(2, kv, 4096, final_keys, land_keys, 2048)
    late_few = Small(device, late_values, late_rows, small_send, small_recv)
    for one in early:
        one.begin(0)

    def onward(streams, stage):
        for one in streams:
            one.finish(stage)
            if stage < 6:
                one.begin(stage + 1)

    def write_out(number, final, first, target, at):
        block = final.at[pl.ds(first, 1024)]
        return pltpu.make_async_copy(block, target.at[:, pl.ds(at * 256, 256)], out_sem.at[number])

    outs = [write_out(q, final_output, q * 1024 + q // 2 * 256, output_sum, q) for q in range(4)]
    outs += [write_out(4 + q, final_query, q * 1024, query_sum, q) for q in range(4)]
    outs += [write_out(8 + q, final_keys, q * 1024, key_sum, q) for q in range(2)]
    outs += [write_out(10 + q, final_keys, (2 + q) * 1024, value_sum, q) for q in range(2)]

    def mate_copy(turn, at):
        return pltpu.make_async_remote_copy(
            src_ref=for_mate.at[turn % 2],
            dst_ref=from_mate.at[at],
            send_sem=mate_send.at[turn],
            recv_sem=mate_recv.at[turn],
            device_id=device("core", 1),
            device_id_type=MESH,
        )

    key_at = lax.broadcasted_iota(jnp.int32, (ROWS, 2 * ROWS), 0)
    query_at = lax.broadcasted_iota(jnp.int32, (ROWS, 2 * ROWS), 1) % ROWS
    valid = (key_at <= query_at) & (key_at + me * ROWS < length[...])

    def block_grads(block, target, at, masked):
        for group in range(2):
            heads = range(4 * group, 4 * group + 4)
            key_heads = [kv[pl.ds(pl.multiple_of(block * 1024 + j * 64, 64), 64)] for j in heads]
            value_heads = [kv[pl.ds(pl.multiple_of(block * 1024 + 512 + j * 64, 64), 64)] for j in heads]
            probs = [jnp.exp(dot_tn(one, queries[j]) - log_total[j]) for one, j in zip(key_heads, heads)]
            if masked:
                probs = [jnp.where(valid, one, 0.0) for one in probs]
            probs_grads = [dot_tn(one, grads[j]) for one, j in zip(value_heads, heads)]
            lows = [
                (one * (grad - delta[j])).astype(jnp.bfloat16) for one, grad, j in zip(probs, probs_grads, heads)
            ]
            key_parts = [dot_nt(queries[j], low).astype(jnp.bfloat16) for low, j in zip(lows, heads)]
            value_parts = [
                dot_nt(grads[j], one.astype(jnp.bfloat16)).astype(jnp.bfloat16) for one, j in zip(probs, heads)
            ]
            query_parts = [dot_nn(one, low) for one, low in zip(key_heads, lows)]
            for n, j in enumerate(heads):
                target[at, j * 64 : j * 64 + 64] = key_parts[n]
                target[at, 512 + j * 64 : 576 + j * 64] = value_parts[n]
                query_grad[j] += query_parts[n]

    def from_other(turn, at):
        mate_copy(turn, at).wait_recv()

        @pl.loop(0, 16)
        def _(n):
            lines = pl.ds(pl.multiple_of(n * 64, 64), 64)
            total = kv_sums[at, lines].astype(jnp.float32) + from_mate[at, lines].astype(jnp.float32)
            kv_sums[at, lines] = total.astype(jnp.bfloat16)

    def turn_x(turn):
        offset = (1 - turn % 2) * (2 + turn // 2) + (turn % 2) * (1 - turn // 2)
        return (here["x"] + offset + RING) % RING

    @pl.loop(0, 4)
    def _(turn):
        @pl.when(turn == 1)
        def _():
            for one in leads:
                one.second()
            for one in experts:
                one.arrive(1)
                one.start(3, 5)
                one.arrive(2)
                one.start(4, 6)

        @pl.when(turn == 2)
        def _():
            onward(early, 0)

        @pl.when(turn == 3)
        def _():
            onward(early, 1)

        at = turn_x(turn)
        other = at * 2 + 1 - here["core"]

        @pl.when(turn >= 2)
        def _():
            mate_copy(turn - 2, at).wait_send()

        @pl.when(other < me)
        def _():
            block_grads(other, for_mate, turn % 2, False)

        @pl.when(other >= me)
        def _():
            for_mate[turn % 2] = jnp.zeros((1024, ROWS), jnp.bfloat16)

        mate_copy(turn, at).start()

        own = at * 2 + here["core"]

        @pl.when(own < me)
        def _():
            block_grads(own, kv_sums, at, False)

        @pl.when(own > me)
        def _():
            kv_sums[at] = jnp.zeros((1024, ROWS), jnp.bfloat16)

        @pl.when(own == me)
        def _():
            block_grads(own, kv_sums, at, True)

        from_other(turn, at)

        @pl.when(turn == 0)
        def _():
            ring.first()

        @pl.when(turn == 2)
        def _():
            ring.second()

    for j in range(KV_HEADS):
        for r in range(2):
            head = query_grad[j, :, r * ROWS : (r + 1) * ROWS] * HEAD_DIM**-0.5
            turned[j * 128 + r * 64 : j * 128 + r * 64 + 64] = turned_back(head, cosine[...], sine[...])

    raw_load.wait()
    result[...] = turned[...].T

    def query_part(n, gain_grad):
        at = pl.ds(pl.multiple_of(n * 64, 64), 64)
        part, more = rms_back(query_raw[at], as_row(query_gain), result[at])
        branch[at] = part.astype(jnp.bfloat16)
        return gain_grad + more

    query_gain_grad = lax.fori_loop(0, 4, query_part, jnp.zeros((1, 1024), jnp.float32))

    @pl.loop(0, 4)
    def _(n):
        columns = pl.ds(pl.multiple_of(n * 256, 256), 256)
        part = dot_tn(normed[:, columns], branch[...]).astype(jnp.bfloat16)
        for q in range(4):
            kv[pl.ds(pl.multiple_of(q * 1024 + n * 256, 256), 256)] = part[:, q * 256 : (q + 1) * 256]

    for one in of_query:
        one.begin(0)
    onward(early, 2)
    for one in experts:
        one.arrive(3, 4)
        one.start(7)

    def put(at, total):
        turned[at] = total

    ring.third(put)
    for j in range(KV_HEADS):
        turned[j * 64 : j * 64 + 64] = turned_back(turned[j * 64 : j * 64 + 64], cosine[...], sine[...])
    part, key_gain_grad = rms_back(key_raw[...], as_row(key_gain), turned[:512].T)
    key_low[...] = part.astype(jnp.bfloat16)
    value_low[...] = turned[512:].T.astype(jnp.bfloat16)

    @pl.loop(0, 4)
    def _(n):
        columns = pl.ds(pl.multiple_of(n * 256, 256), 256)
        part = dot_tn(normed[:, columns], jnp.concatenate([key_low[...], value_low[...]], axis=1)).astype(jnp.bfloat16)
        for q in range(4):
            kv[pl.ds(pl.multiple_of(4096 + q * 1024 + n * 256, 256), 256)] = part[:, q * 256 : (q + 1) * 256]

    for one in of_keys:
        one.begin(0)
    next_load.wait()
    result[...] = dot_nt(branch[...], square[...])
    last_loads = [
        pltpu.make_async_copy(w_key, square.at[:, pl.ds(0, 512)], load_sem.at[4]),
        pltpu.make_async_copy(w_value, square.at[:, pl.ds(512, 512)], load_sem.at[5]),
    ]
    for load in last_loads:
        load.start()
    onward(of_query, 0)
    for one in leads:
        one.third()
    for one in lasts:
        one.first()
    for load in last_loads:
        load.wait()
    result[...] += dot_nt(jnp.concatenate([key_low[...], value_low[...]], axis=1), square[...])

    def token_part(n, gain_grad):
        at = pl.ds(pl.multiple_of(n * 64, 64), 64)
        part, more = rms_back(tokens[at].astype(jnp.float32), as_row(attn_gain), result[at])
        token_grad[at] = (hidden_grad[at] + part).astype(jnp.bfloat16)
        return gain_grad + more

    attn_gain_grad = lax.fori_loop(0, 4, token_part, jnp.zeros((1, 1024), jnp.float32))
    key_wide = jnp.concatenate([key_gain_grad, jnp.zeros((1, 512), jnp.float32)], axis=1)
    late_values[0] = jnp.concatenate(
        [attn_gain_grad, query_gain_grad, key_wide, jnp.zeros((5, 1024), jnp.float32)], axis=0
    )
    late_few.begin(0)
    onward(of_keys, 0)
    onward(early, 3)
    for stage in range(1, 4):
        onward(of_query, stage)
        late_few.finish(stage - 1)
        late_few.begin(stage)
        onward(of_keys, stage)
        onward(early, stage + 3)
        if stage == 1:
            for one in lasts:
                one.second()
    for q in range(4):
        outs[q].start()
    late_few.finish(3)
    late_small[...] = late_values[4]
    router = [final_output[2048 + q * EXPERTS : 2048 + (q + 1) * EXPERTS].astype(jnp.float32) for q in range(4)]
    lines = final_output[2176:2192].astype(jnp.float32)
    lines = jnp.concatenate([lines[q : q + 1] for q in range(4)], axis=1)
    early_small[...] = jnp.concatenate(
        [jnp.concatenate(router, axis=1), lines, jnp.zeros((7, 1024), jnp.float32)], axis=0
    )

    def put_mixed(at, total):
        mixed_out[at] = (hidden[at] + total).astype(jnp.bfloat16)

    for stage in range(4, 7):
        onward(of_query, stage)
        onward(of_keys, stage)
        if stage == 4:
            for one in lasts:
                one.third(put_mixed)
    for q in range(4, 12):
        outs[q].start()
    for one in experts:
        one.arrive(0, 5, 6, 7)
    for one in [*experts, *leads, *lasts, ring, *early, *of_query, *of_keys, late_few]:
        one.drain()
    for turn in (2, 3):
        mate_copy(turn, 0).wait_send()
    for out in outs:
        out.wait()


def backward(smalls, larges):
    vmem, hbm = pl.BlockSpec(memory_space=pltpu.VMEM), pl.BlockSpec(memory_space=pl.ANY)
    low, wide = jnp.bfloat16, jnp.float32
    shape = jax.ShapeDtypeStruct
    dma = pltpu.SemaphoreType.DMA
    return pl.pallas_call(
        backward_kernel,
        name="backward",
        out_shape=(
            shape((ROWS, 1024), low),
            shape((ROWS, 1024), low),
            shape((40, 1024), wide),
            shape((8, 1024), wide),
            shape((1024, 1024), low),
            shape((1024, 512), low),
            shape((1024, 512), low),
            shape((1024, 1024), low),
            shape((8, 256, 1024), low),
            shape((8, 128, 1024), low),
        ),
        in_specs=[vmem] * len(smalls) + [hbm] * len(larges),
        out_specs=(vmem,) * 4 + (hbm,) * 6,
        scratch_shapes=[
            pltpu.VMEM((16, ROWS, 1024), low),
            pltpu.VMEM((10 * 384, 1024), low),
            pltpu.VMEM((FULL, 1024), wide),
            pltpu.VMEM((1024, 1024), low),
            pltpu.VMEM((8 * 1024, ROWS), low),
            pltpu.VMEM((ROWS, 1024), wide),
            pltpu.VMEM((ROWS, 1024), wide),
            pltpu.VMEM((ROWS, 1024), low),
            pltpu.VMEM((KV_HEADS, HEAD_DIM, 2 * ROWS), low),
            pltpu.VMEM((KV_HEADS, 1, 2 * ROWS), wide),
            pltpu.VMEM((KV_HEADS, HEAD_DIM, 2 * ROWS), wide),
            pltpu.VMEM((1024, ROWS), wide),
            pltpu.VMEM((2, 1024, ROWS), low),
            pltpu.VMEM((4, 1024, ROWS), low),
            pltpu.VMEM((4, 1024, ROWS), low),
            pltpu.VMEM((3072, ROWS), low),
            pltpu.VMEM((ROWS, 512), low),
            pltpu.VMEM((ROWS, 512), low),
            pltpu.VMEM((4608, 256), low),
            pltpu.VMEM((4608, 256), low),
            pltpu.VMEM((4096, 256), low),
            pltpu.VMEM((4096, 256), low),
            pltpu.VMEM((4896, 256), low),
            pltpu.VMEM((4352, 256), low),
            pltpu.VMEM((4352, 256), low),
            pltpu.VMEM((9, 48, 256), low),
            pltpu.VMEM((5, 8, 1024), wide),
            pltpu.VMEM((10, 8, 1024), wide),
            dma((10, 4)),
            dma((10, 4)),
            dma((4,)),
            dma((4,)),
            dma((1, 4)),
            dma((1, 4)),
            dma((9, 17)),
            dma((9, 17)),
            dma((10,)),
            dma((10,)),
            dma((10,)),
            dma((12,)),
            dma((2, 8)),
            dma((2, 8)),
        ],
        compiler_params=pltpu.CompilerParams(
            collective_id=4, has_side_effects=True, vmem_limit_bytes=66000000
        ),
        cost_estimate=pl.CostEstimate(flops=100 * 10**9, bytes_accessed=60 * 10**6, transcendentals=8 * 10**6),
    )(*smalls, *larges)


def widen_kernel(
    early, late, mixed, tokens, query, key, value, output, gate_up, down,
    ffn_gain, attn_gain, query_gain, key_gain, router,
    mixed_out, token_out, query_out, key_out, value_out, output_out, gate_out, up_out, down_out,
    query_in, key_in, value_in, output_in, gate_up_in, down_in,
    query_wide, key_wide, value_wide, output_wide, gate_up_wide, down_wide,
    in_sem, out_sem,
):
    arrays = (
        (query, query_in, query_wide, query_out),
        (output, output_in, output_wide, output_out),
        (key, key_in, key_wide, key_out),
        (value, value_in, value_wide, value_out),
    )
    parts = []
    for source, low, wide, target in arrays:
        for n in range(0, 1024, 512):
            at = pl.ds(n, 512)
            parts.append((source.at[at], low.at[at], wide.at[at], [(wide.at[at], target.at[at])]))
    for block in range(8):
        rows, e = pl.ds(block // 2 * 256, 256), block % 2
        wide = gate_up_wide.at[block]
        targets = [
            (wide.at[:, pl.ds(0, 512)], gate_out.at[e, rows]),
            (wide.at[:, pl.ds(512, 512)], up_out.at[e, rows]),
        ]
        parts.append((gate_up.at[block], gate_up_in.at[block], wide, targets))
    for block in range(8):
        wide = down_wide.at[block]
        target = down_out.at[block % 2, pl.ds(block // 2 * 128, 128)]
        parts.append((down.at[block], down_in.at[block], wide, [(wide, target)]))
    loads = [pltpu.make_async_copy(source, low, in_sem.at[n]) for n, (source, low, _, _) in enumerate(parts)]
    for load in loads:
        load.start()
    ffn_gain[...] = early[EXPERTS]
    attn_gain[...] = late[0]
    query_gain[...] = late[1]
    key_gain[...] = late[2, :512]
    router[...] = early[:EXPERTS].T
    mixed_out[...] = mixed[...]
    token_out[...] = tokens[...]
    stores = []
    for load, (_, low, wide, targets) in zip(loads, parts):
        load.wait()
        wide[...] = low[...].astype(jnp.float32)
        for source, target in targets:
            stores.append(pltpu.make_async_copy(source, target, out_sem.at[len(stores)]))
            stores[-1].start()
    for copy in stores:
        copy.wait()


def widen(arrays):
    vmem, hbm = pl.BlockSpec(memory_space=pltpu.VMEM), pl.BlockSpec(memory_space=pl.ANY)
    low, wide = jnp.bfloat16, jnp.float32
    shape = jax.ShapeDtypeStruct
    held = ((1024, 1024), (1024, 512), (1024, 512), (1024, 1024), (8, 256, 1024), (8, 128, 1024))
    return pl.pallas_call(
        widen_kernel,
        name="widen",
        out_shape=(
            shape((1024,), wide),
            shape((1024,), wide),
            shape((1024,), wide),
            shape((512,), wide),
            shape((1024, EXPERTS), wide),
            shape((ROWS, 1024), low),
            shape((ROWS, 1024), low),
            shape((1024, 1024), wide),
            shape((1024, 512), wide),
            shape((1024, 512), wide),
            shape((1024, 1024), wide),
            shape((2, 1024, 512), wide),
            shape((2, 1024, 512), wide),
            shape((2, 512, 1024), wide),
        ),
        in_specs=[vmem] * 4 + [hbm] * 6,
        out_specs=(vmem,) * 7 + (hbm,) * 7,
        scratch_shapes=[
            *[pltpu.VMEM(size, low) for size in held],
            *[pltpu.VMEM(size, wide) for size in held],
            pltpu.SemaphoreType.DMA((24,)),
            pltpu.SemaphoreType.DMA((32,)),
        ],
        compiler_params=pltpu.CompilerParams(vmem_limit_bytes=56 * 2**20),
    )(*arrays)


def body(
    tokens,
    cotangent,
    lengths,
    routes,
    attn_gain,
    w_query,
    w_key,
    w_value,
    query_gain,
    key_gain,
    w_output,
    ffn_gain,
    w_router,
    w_gate,
    w_up,
    w_down,
):
    query_pos = lax.axis_index("dp") * ROWS + jnp.arange(ROWS, dtype=jnp.int32)
    cosine, sine_table = rope_tables(query_pos)
    cosine, sine_table = cosine.T, sine_table.T
    routes_t, length = routes[0].T, lengths.reshape(1, 1)
    gains = [attn_gain, query_gain, key_gain, ffn_gain]
    weights = (w_query, w_key, w_value, w_output)
    router_rows = w_router.T
    ffn_in, hidden, mixed_t, queries, log_total, normed, query_raw, key_raw, kv_all, cot_all = forward(
        tokens[0], cotangent[0], routes_t, length, cosine, sine_table, gains, weights
    )
    returned, mixed_parts, own_gu, own_down = moe(
        ffn_in, cot_all, cotangent[0], router_rows, w_gate, w_up, w_down
    )
    mixed_low, token_low, early_small, late_small, *sums = backward(
        (
            hidden, ffn_in, cotangent[0], tokens[0], normed, key_raw, mixed_t, queries, log_total, routes_t,
            length, cosine, sine_table, *gains, router_rows, own_gu, own_down,
        ),
        (returned, query_raw, mixed_parts, kv_all.reshape(8 * 1024, ROWS), *weights),
    )
    (
        ffn_gain_sum, attn_gain_sum, query_gain_sum, key_gain_sum, router_sum, mixed_out, token_grad,
        query_w_sum, key_w_sum, value_w_sum, output_w_sum, gate_w_sum, up_w_sum, down_w_sum,
    ) = widen((early_small, late_small, mixed_low, token_low, *sums))
    return (
        mixed_out[None],
        token_grad[None],
        attn_gain_sum,
        query_w_sum,
        key_w_sum,
        value_w_sum,
        query_gain_sum,
        key_gain_sum,
        output_w_sum,
        ffn_gain_sum,
        router_sum,
        gate_w_sum,
        up_w_sum,
        down_w_sum,
    )


def solution(mesh):
    return jax.shard_map(
        body,
        mesh=mesh,
        in_specs=(
            P("expert", "dp", None),
            P("expert", "dp", None),
            P("expert"),
            P("expert", "dp", None),
            P(),
            P(),
            P(),
            P(),
            P(),
            P(),
            P(),
            P(),
            P(),
            P("expert", None, None),
            P("expert", None, None),
            P("expert", None, None),
        ),
        out_specs=(
            P("expert", "dp", None),
            P("expert", "dp", None),
            P(),
            P(),
            P(),
            P(),
            P(),
            P(),
            P(),
            P(),
            P(),
            P("expert", None, None),
            P("expert", None, None),
            P("expert", None, None),
        ),
        check_vma=False,
    )
```

```python
import math

import jax
import jax.numpy as jnp
from jax import lax
from jax.experimental import pallas as pl
from jax.experimental.pallas import tpu as pltpu
from jax.sharding import PartitionSpec as P

HEADS = 16
KV_HEADS = 8
HEAD_DIM = 64
EXPERTS = 32
TOPK = 8
CAP = 80


epsilon = 1e-06


def rope_tables(positions):
    steps_half = jnp.arange(HEAD_DIM // 2).astype(jnp.float32)
    inverse = jnp.exp(steps_half * (-2.0 * math.log(10000.0) / HEAD_DIM))
    angles = positions.astype(jnp.float32)[:, None] * inverse[None, :]
    return (jnp.cos(angles), jnp.sin(angles))


RING = 4
ROWS = 256
EXTRA = 16
FULL = ROWS + EXTRA
SENT = 192
LEFT = FULL - SENT
BOTH = ROWS + LEFT
GROUP = 4 * CAP
MESH = pl.DeviceIdType.MESH


def dot_nn(a, b):
    return jnp.dot(a, b, preferred_element_type=jnp.float32)


def dot_nt(a, b):
    return lax.dot_general(a, b, (((1,), (1,)), ((), ())), preferred_element_type=jnp.float32)


def dot_tn(a, b):
    return lax.dot_general(a, b, (((0,), (0,)), ((), ())), preferred_element_type=jnp.float32)


def step_of(size):
    return next(step for step in (64, 48, 32, 16) if size % step == 0)


class Torus:
    def __init__(self):
        self.dp = lax.axis_index("dp")
        expert = lax.axis_index("expert")
        self.expert = expert
        self.z, self.y = expert // RING, expert % RING

    def block(self, dz, dy):
        return ((self.z + dz + RING) % RING) * RING + (self.y + dy + RING) % RING

    def near(self, axis, step):
        return (self.dp, self.block(step, 0) if axis == "z" else self.block(0, step))

    def along(self, axis, other, step):
        return self.block(step, other) if axis == "z" else self.block(other, step)

    def neighbours(self):
        return [self.near(axis, step) for axis in "yz" for step in (1, -1)]


ARRIVALS = (
    ((0, 0), (3, 0), (1, 3), (3, 2)),
    ((0, 1), (0, 2), (3, 1), (2, 1)),
    ((0, 3), (2, 0), (3, 3), (2, 3)),
    ((1, 0), (1, 1), (1, 2), (2, 2)),
)


def differences(values):
    found = list(values)
    for level in range(1, len(found)):
        for n in range(len(found) - 1, level - 1, -1):
            found[n] -= found[n - 1]
    return found


def chooses(n):
    return 1, n, n * (n - 1) // 2, n * (n - 1) * (n - 2) // 6


class Gather:
    def __init__(self, torus, buffer, send, recv, number, axis, other, low, first, second, stride):
        self.torus, self.buffer, self.send, self.recv = torus, buffer, send, recv
        self.number, self.axis, self.other, self.stride = number, axis, other, stride
        self.whole, self.front, self.rear = (low, first + second), (low, first), (low + first, second)

    def copy(self, which, offset, part, step):
        at = self.torus.along(self.axis, self.other, offset) * self.stride + part[0]
        rows = self.buffer.at[pl.ds(pl.multiple_of(at, 16), part[1])]
        return pltpu.make_async_remote_copy(
            src_ref=rows,
            dst_ref=rows,
            send_sem=self.send.at[self.number, which],
            recv_sem=self.recv.at[self.number, which],
            device_id=self.torus.near(self.axis, step),
            device_id_type=MESH,
        )

    def first(self):
        self.copy(0, 0, self.whole, 1).start()
        self.copy(1, 0, self.whole, -1).start()

    def second(self):
        self.copy(0, -1, self.whole, 1).wait_recv()
        self.copy(2, -1, self.front, 1).start()
        self.copy(1, 1, self.whole, -1).wait_recv()
        self.copy(3, 1, self.rear, -1).start()

    def third(self):
        self.copy(2, 2, self.front, 1).wait_recv()
        self.copy(3, 2, self.rear, -1).wait_recv()

    def drain(self):
        self.copy(0, 0, self.whole, 1).wait_send()
        self.copy(1, 0, self.whole, -1).wait_send()
        self.copy(2, -1, self.front, 1).wait_send()
        self.copy(3, 1, self.rear, -1).wait_send()


class Scatter:
    def __init__(self, torus, sums, landing, send, recv, number, base, axis, other, low, first, second):
        self.torus, self.sums, self.landing, self.send, self.recv = torus, sums, landing, send, recv
        self.number, self.axis, self.other = number, axis, other
        self.low, self.parts = low, (first, second)
        self.size = first + second
        self.slots = (base, base + first, base + self.size, base + 2 * self.size)

    def rows(self, which):
        if which == 0:
            return self.low, self.parts[0]
        if which == 1:
            return self.low + self.parts[0], self.parts[1]
        return self.low, self.size

    def at(self, offset):
        return self.torus.along(self.axis, self.other, offset)

    def copy(self, which):
        start, size = self.rows(which)
        offset = (2, 2, 1, -1)[which]
        return pltpu.make_async_remote_copy(
            src_ref=self.sums.at[self.at(offset), pl.ds(start, size)],
            dst_ref=self.landing.at[pl.ds(self.slots[which], size)],
            send_sem=self.send.at[self.number, which],
            recv_sem=self.recv.at[self.number, which],
            device_id=self.torus.near(self.axis, (1, -1, 1, -1)[which]),
            device_id_type=MESH,
        )

    def add(self, which, offset):
        start, size = self.rows(which)
        block = self.at(offset)

        many = step_of(size)

        @pl.loop(0, size // many)
        def _(k):
            here = pl.ds(pl.multiple_of(start + k * many, 16), many)
            there = pl.ds(pl.multiple_of(self.slots[which] + k * many, 16), many)
            total = self.sums[block, here].astype(jnp.float32) + self.landing[there].astype(jnp.float32)
            self.sums[block, here] = total.astype(jnp.bfloat16)

    def first(self):
        self.copy(0).start()
        self.copy(1).start()

    def second(self):
        self.copy(0).wait_recv()
        self.add(0, 1)
        self.copy(2).start()
        self.copy(1).wait_recv()
        self.add(1, -1)
        self.copy(3).start()

    def third(self, put=None):
        self.copy(2).wait_recv()
        self.copy(3).wait_recv()
        block = self.at(0)

        many = step_of(self.size)

        @pl.loop(0, self.size // many)
        def _(k):
            here = pl.ds(pl.multiple_of(self.low + k * many, 16), many)
            left = pl.ds(pl.multiple_of(self.slots[2] + k * many, 16), many)
            right = pl.ds(pl.multiple_of(self.slots[3] + k * many, 16), many)
            total = (
                self.sums[block, here].astype(jnp.float32)
                + self.landing[left].astype(jnp.float32)
                + self.landing[right].astype(jnp.float32)
            )
            if put is None:
                self.sums[block, here] = total.astype(jnp.bfloat16)
            else:
                put(here, total)

    def drain(self):
        for which in range(4):
            self.copy(which).wait_send()


def moe_kernel(
    ffn, cot, own_cot, wr, w_gate, w_up, w_down,
    ret, mixed, own_gu, own_down,
    rows, sums, wgu, wd, held, pair, inner, dgu, mixing, back, cotv, before, chosen, gate_rows, grad_rows, stage,
    mate_rows, gu_sums, down_sums,
    ag_send, ag_recv, rs_send, rs_recv, w_sem, cot_sem, own_sem, stage_sem, mate_send, mate_recv, x_send, x_recv, credit,
):
    torus = Torus()
    place, place_of = everywhere()
    barrier = pltpu.get_barrier_semaphore()
    peers = [*torus.neighbours(), place_of("core", 1), place_of("x", 1), place_of("x", -1)]
    for device in peers:
        pl.semaphore_signal(barrier, inc=1, device_id=device, device_id_type=MESH)

    weights = [
        pltpu.make_async_copy(w_gate, wgu.at[:, :, pl.ds(0, 512)], w_sem.at[0]),
        pltpu.make_async_copy(w_up, wgu.at[:, :, pl.ds(512, 512)], w_sem.at[1]),
        pltpu.make_async_copy(w_down, wd, w_sem.at[2]),
    ]
    for copy in weights:
        copy.start()

    def source_of(g, j):
        of_g, of_j = chooses(g), chooses(j)
        offsets = []
        for axis in range(2):
            table = [differences([at[axis] for at in line]) for line in ARRIVALS]
            table = [differences(column) for column in zip(*table)]
            offsets.append(sum(table[a][b] * of_g[a] * of_j[b] for a in range(4) for b in range(4) if table[a][b]))
        return torus.block(*offsets)

    def cot_copy(g, j):
        at = pl.multiple_of(source_of(g, j) * SENT, 16)
        return pltpu.make_async_copy(cot.at[pl.ds(at, SENT)], cotv.at[pl.ds(j * SENT, SENT)], cot_sem.at[j])

    for j in range(4):
        cot_copy(0, j).start()
    first_row = torus.expert * BOTH
    own_copy = pltpu.make_async_copy(
        own_cot.at[pl.ds(ROWS - LEFT, LEFT)], rows.at[pl.ds(pl.multiple_of(first_row + ROWS, 16), LEFT)], own_sem
    )
    own_copy.start()
    rows[pl.ds(pl.multiple_of(first_row, 16), ROWS)] = ffn[...]
    own_copy.wait()
    pl.semaphore_wait(barrier, len(peers))

    def gather(number, axis, other, low, first, second):
        return Gather(torus, rows, ag_send, ag_recv, number, axis, other, low, first, second, BOTH)

    a_first = gather(0, "y", 0, 0, 96, 80)
    b_first = gather(1, "z", 0, 176, 80, 80)
    a_second = {d: gather(2 + d % RING, "z", d, 0, 96, 80) for d in (0, 1, -1, 2)}
    b_second = {d: gather(6 + d % RING, "y", d, 176, 80, 80) for d in (0, 1, -1, 2)}
    gathers = [a_first, b_first, *a_second.values(), *b_second.values()]

    a_first.first()
    b_first.first()
    b_second[0].first()
    a_second[0].first()
    a_first.second()
    b_first.second()
    b_second[0].second()
    a_second[0].second()
    for d in (1, -1):
        b_second[d].first()
        a_second[d].first()
    for copy in weights:
        copy.wait()

    earlier = lax.broadcasted_iota(jnp.int32, (ROWS, ROWS), 0) < lax.broadcasted_iota(jnp.int32, (ROWS, ROWS), 1)
    before[...] = jnp.where(earlier, 1.0, 0.0).astype(jnp.bfloat16)
    slot_at = lax.broadcasted_iota(jnp.int32, (CAP, ROWS), 0).astype(jnp.float32)

    def stage_copy(slot, target):
        return pltpu.make_async_copy(stage.at[slot], target, stage_sem.at[slot])

    expert_rows = lax.broadcasted_iota(jnp.int32, (EXPERTS, ROWS), 0)
    order = (2, 1, -1, 0)
    a_lead = {
        d: Scatter(torus, sums, rows, rs_send, rs_recv, n, n * 384, "z", d, 0, 64, 64) for n, d in enumerate(order)
    }
    b_lead = {
        d: Scatter(torus, sums, rows, rs_send, rs_recv, 4 + n, 1920 + n * 432, "y", d, 128, 80, 64)
        for n, d in enumerate(order)
    }
    a_last = Scatter(torus, sums, rows, rs_send, rs_recv, 8, 4 * 384, "y", 0, 0, 64, 64)
    b_last = Scatter(torus, sums, rows, rs_send, rs_recv, 9, 1920 + 4 * 432, "z", 0, 128, 80, 64)

    @pl.loop(0, 4)
    def _(g):
        @pl.when(g == 1)
        def _():
            a_first.third()
            b_first.third()
            b_second[2].first()
            a_second[2].first()
            b_second[0].third()
            a_second[0].third()
            for d in (1, -1):
                b_second[d].second()
                a_second[d].second()

        @pl.when(g == 2)
        def _():
            b_second[2].second()
            a_second[2].second()
            b_second[1].third()

        @pl.when(g == 3)
        def _():
            b_second[-1].third()
            for d in (1, -1, 2):
                a_second[d].third()
            b_second[2].third()

        for j in range(4):
            cot_copy(g, j).wait()

        @pl.loop(0, 4)
        def _(j):
            source = source_of(g, j)
            block = rows[pl.ds(pl.multiple_of(source * BOTH, 16), ROWS)]
            laid = cotv[pl.ds(pl.multiple_of(j * SENT, 16), EXTRA)].astype(jnp.float32)
            member = jnp.concatenate([laid[:8, q * ROWS : (q + 1) * ROWS] for q in range(4)], axis=0)
            named = member > 0.5
            slots = dot_nn(member.astype(jnp.bfloat16), before[...])
            slots = jnp.where(named, slots, -1.0)
            logits = jnp.where(named, dot_nt(wr[...], block), -1e30)
            weight = jnp.where(named, jnp.exp(logits - jnp.max(logits, axis=0, keepdims=True)), 0.0)
            gates = weight / jnp.sum(weight, axis=0, keepdims=True)
            picked = []
            for e in range(2):
                own = jnp.sum(
                    jnp.where(expert_rows == torus.expert * 2 + e, slots, 0.0), axis=0, keepdims=True
                )
                picked.append(jnp.where(slot_at == own, 1.0, 0.0))
            both = jnp.concatenate(picked, axis=0).astype(jnp.bfloat16)
            chosen[j] = both
            grad_block = jnp.concatenate(
                [
                    cotv[pl.ds(pl.multiple_of(j * SENT + EXTRA, 16), SENT - EXTRA)],
                    rows[pl.ds(pl.multiple_of(source * BOTH + ROWS, 16), LEFT)],
                ],
                axis=0,
            )
            took = dot_nn(both, jnp.concatenate([block, grad_block], axis=1)).astype(jnp.bfloat16)
            here = pl.ds(pl.multiple_of(j * CAP, 16), CAP)
            there = pl.ds(pl.multiple_of(g * GROUP + j * CAP, 16), CAP)
            for e in range(2):
                own = jnp.sum(
                    jnp.where(expert_rows == torus.expert * 2 + e, gates, 0.0), axis=0, keepdims=True
                )
                of_rows = jnp.sum(picked[e] * own, axis=1, keepdims=True)
                gate_rows[e, here] = jnp.broadcast_to(of_rows, (CAP, 128))
                held[e, there] = took[e * CAP : (e + 1) * CAP, :1024]
                mixing[e, here] = took[e * CAP : (e + 1) * CAP, 1024:]

        @pl.when(g < 3)
        def _():
            for j in range(4):
                cot_copy(g + 1, j).start()

        @pl.when(g == 3)
        def _():
            for one in gathers:
                one.drain()
            for device in peers:
                pl.semaphore_signal(credit, inc=1, device_id=device, device_id_type=MESH)
            pl.semaphore_wait(credit, len(peers))
            b_lead[0].first()
            a_lead[0].first()

        @pl.loop(0, 2)
        def _(e):
            there = pl.ds(pl.multiple_of(g * GROUP, 16), GROUP)
            both = dot_nn(held[e, there], wgu[e])
            gate, up = both[:, :512], both[:, 512:]
            sig = jax.nn.sigmoid(gate)
            silu = gate * sig
            act = (silu * up).astype(jnp.bfloat16)
            inner[e, there] = act
            out = dot_nn(act, wd[e]).astype(jnp.bfloat16).astype(jnp.float32)
            grad = mixing[e].astype(jnp.float32)
            weight = gate_rows[e][:, :1]
            grad_rows[e] = jnp.broadcast_to(jnp.sum(grad * out, axis=1, keepdims=True), (GROUP, 128))
            pair[e, there] = (weight * grad).astype(jnp.bfloat16)
            mixing[e] = (weight * out).astype(jnp.bfloat16)
            inner_grad = dot_nt(pair[e, there], wd[e])
            dgu[e, there, :512] = (inner_grad * up * sig * (1.0 + gate * (1.0 - sig))).astype(jnp.bfloat16)
            dgu[e, there, 512:] = (inner_grad * silu).astype(jnp.bfloat16)
            back[e] = dot_nt(dgu[e, there], wgu[e]).astype(jnp.bfloat16)

        @pl.loop(0, 4)
        def _(j):
            source = source_of(g, j)
            both = chosen[j]
            picked = both.astype(jnp.float32)
            here = pl.ds(pl.multiple_of(j * CAP, 16), CAP)
            compact = jnp.concatenate(
                [jnp.concatenate([back[e, here], mixing[e, here]], axis=1) for e in range(2)], axis=0
            )
            spread = dot_tn(both, compact).astype(jnp.bfloat16)
            sums[source, pl.ds(EXTRA, ROWS)] = spread[:, :1024]
            grads = jnp.zeros((EXPERTS, ROWS), jnp.float32)
            for e in range(2):
                own = jnp.sum(
                    picked[e * CAP : (e + 1) * CAP] * grad_rows[e, here][:, :1], axis=0, keepdims=True
                )
                grads = grads + jnp.where(expert_rows == torus.expert * 2 + e, own, 0.0)
            laid = jnp.concatenate([grads[8 * q : 8 * q + 8] for q in range(4)], axis=1)
            sums[source, pl.ds(0, EXTRA)] = jnp.concatenate([laid, jnp.zeros_like(laid)], axis=0).astype(
                jnp.bfloat16
            )
            slot = j % 2

            @pl.when((g > 0) | (j > 1))
            def _():
                stage_copy(slot, mixed.at[source]).wait()

            stage[slot] = spread[:, 1024:]
            stage_copy(slot, mixed.at[source]).start()

    def chunk(e, k):
        if k < 4:
            return dot_tn(held[e, :, k * 256 : (k + 1) * 256], dgu[e]).astype(jnp.bfloat16)
        return dot_tn(inner[e, :, (k - 4) * 256 : (k - 3) * 256], pair[e]).astype(jnp.bfloat16)

    def mate_copy(k):
        return pltpu.make_async_remote_copy(
            src_ref=stage.at[k % 2],
            dst_ref=mate_rows.at[pl.ds(k * 256, 256)],
            send_sem=mate_send.at[k],
            recv_sem=mate_recv.at[k],
            device_id=place_of("core", 1),
            device_id_type=MESH,
        )

    line = Line(place, place_of)
    rings = [
        Scatter(line, gu_sums, rows, x_send, x_recv, 0, 4080, "x", 0, 0, 128, 128),
        Scatter(line, down_sums, rows, x_send, x_recv, 1, 4848, "x", 0, 0, 64, 64),
    ]

    for d in (2, 1, -1):
        b_lead[d].first()
        a_lead[d].first()
    b_lead[0].second()
    a_lead[0].second()
    for k in range(6):
        if k < 2:
            stage_copy(k, mixed.at[0]).wait()
        else:
            mate_copy(k - 2).wait_send()
        stage[k % 2] = chunk(1 - place["core"], k)
        mate_copy(k).start()
        own = chunk(place["core"], k)
        if k < 4:
            gu_sums[k] = own
        else:
            down_sums[2 * k - 8] = own[:128]
            down_sums[2 * k - 7] = own[128:]
    for d in (2, 1, -1):
        b_lead[d].second()
        a_lead[d].second()
    for k in range(6):
        mate_copy(k).wait_recv()

        @pl.loop(0, 4)
        def _(n):
            other = mate_rows[pl.ds(pl.multiple_of(k * 256 + n * 64, 64), 64)].astype(jnp.float32)
            if k < 4:
                at = (k, pl.ds(pl.multiple_of(n * 64, 64), 64))
                gu_sums[at] = (gu_sums[at].astype(jnp.float32) + other).astype(jnp.bfloat16)
            else:
                at = (2 * k - 8 + n // 2, pl.ds(pl.multiple_of(n % 2 * 64, 64), 64))
                down_sums[at] = (down_sums[at].astype(jnp.float32) + other).astype(jnp.bfloat16)

    for one in rings:
        one.first()
    for one in rings:
        one.second()
    for d in order:
        b_lead[d].third()
        a_lead[d].third()
        if d == 2:
            b_last.first()
            a_last.first()
    b_last.second()
    a_last.second()

    def put(at, total):
        ret[at] = total

    b_last.third(put)
    a_last.third(put)

    def put_gu(at, total):
        own_gu[at] = total.astype(jnp.bfloat16)

    def put_down(at, total):
        own_down[at] = total.astype(jnp.bfloat16)

    rings[0].third(put_gu)
    rings[1].third(put_down)
    for one in [*a_lead.values(), *b_lead.values(), a_last, b_last, *rings]:
        one.drain()
    for k in (4, 5):
        mate_copy(k).wait_send()


def moe(ffn_in, cot_all, own_cot, router_rows, w_gate, w_up, w_down):
    vmem, hbm = pl.BlockSpec(memory_space=pltpu.VMEM), pl.BlockSpec(memory_space=pl.ANY)
    low, total = jnp.bfloat16, 4 * GROUP
    return pl.pallas_call(
        moe_kernel,
        name="moe",
        out_shape=(
            jax.ShapeDtypeStruct((FULL, 1024), jnp.float32),
            jax.ShapeDtypeStruct((16, ROWS, 1024), low),
            jax.ShapeDtypeStruct((256, 1024), low),
            jax.ShapeDtypeStruct((128, 1024), low),
        ),
        in_specs=[vmem, hbm, hbm, vmem, hbm, hbm, hbm],
        out_specs=(vmem, hbm, vmem, vmem),
        scratch_shapes=[
            pltpu.VMEM((16 * BOTH, 1024), low),
            pltpu.VMEM((16, FULL, 1024), low),
            pltpu.VMEM((2, 1024, 1024), low),
            pltpu.VMEM((2, 512, 1024), low),
            pltpu.VMEM((2, total, 1024), low),
            pltpu.VMEM((2, total, 1024), low),
            pltpu.VMEM((2, total, 512), low),
            pltpu.VMEM((2, total, 1024), low),
            pltpu.VMEM((2, GROUP, 1024), low),
            pltpu.VMEM((2, GROUP, 1024), low),
            pltpu.VMEM((4 * SENT, 1024), low),
            pltpu.VMEM((ROWS, ROWS), low),
            pltpu.VMEM((4, 2 * CAP, ROWS), low),
            pltpu.VMEM((2, GROUP, 128), jnp.float32),
            pltpu.VMEM((2, GROUP, 128), jnp.float32),
            pltpu.VMEM((2, ROWS, 1024), low),
            pltpu.VMEM((6 * 256, 1024), low),
            pltpu.VMEM((4, 256, 1024), low),
            pltpu.VMEM((4, 128, 1024), low),
            pltpu.SemaphoreType.DMA((10, 4)),
            pltpu.SemaphoreType.DMA((10, 4)),
            pltpu.SemaphoreType.DMA((10, 4)),
            pltpu.SemaphoreType.DMA((10, 4)),
            pltpu.SemaphoreType.DMA((3,)),
            pltpu.SemaphoreType.DMA((4,)),
            pltpu.SemaphoreType.DMA,
            pltpu.SemaphoreType.DMA((2,)),
            pltpu.SemaphoreType.DMA((6,)),
            pltpu.SemaphoreType.DMA((6,)),
            pltpu.SemaphoreType.DMA((2, 4)),
            pltpu.SemaphoreType.DMA((2, 4)),
            pltpu.SemaphoreType.REGULAR,
        ],
        compiler_params=pltpu.CompilerParams(
            collective_id=1, has_side_effects=True, vmem_limit_bytes=63 * 2**20
        ),
        cost_estimate=pl.CostEstimate(flops=50 * 10**9, bytes_accessed=40 * 10**6, transcendentals=2 * 10**6),
    )(ffn_in, cot_all, own_cot, router_rows, w_gate, w_up, w_down)


def everywhere():
    dp, expert = lax.axis_index("dp"), lax.axis_index("expert")
    here = {"x": dp // 2, "core": dp % 2, "z": expert // RING, "y": expert % RING}

    def device(axis, step):
        there = dict(here)
        size = 2 if axis == "core" else RING
        there[axis] = (here[axis] + step + size) % size
        return (there["x"] * 2 + there["core"], there["z"] * RING + there["y"])

    return here, device


def rms_scale(values):
    return lax.rsqrt(jnp.mean(values * values, axis=-1, keepdims=True) + epsilon)


def as_row(gain):
    return gain[...].astype(jnp.float32).reshape(1, -1)


def turned_rows(values, cosine, sine):
    front, back = values[: HEAD_DIM // 2], values[HEAD_DIM // 2 :]
    return jnp.concatenate([front * cosine - back * sine, back * cosine + front * sine], axis=0)


def kv_order(here, step):
    turn = step // 2
    return (turn % 2) * (3 - turn // 2) + (1 - turn % 2) * (turn // 2)


class Keys:
    def __init__(self, here, device, blocks, send, recv):
        self.here, self.device, self.blocks, self.send, self.recv = here, device, blocks, send, recv
        self.lines = blocks.shape[1]

    def copy(self, which):
        half = self.lines // 2
        offset, start, size, axis, step = (
            (0, 0, self.lines, "core", 1),
            (0, 0, self.lines, "x", 1),
            (0, 0, self.lines, "x", -1),
            (-1, 0, half, "x", 1),
            (1, half, half, "x", -1),
            (-1, 0, self.lines, "core", 1),
            (1, 0, self.lines, "core", 1),
            (2, 0, self.lines, "core", 1),
        )[which]
        block = (self.here["x"] + offset + RING) % RING * 2 + self.here["core"]
        part = self.blocks.at[block, pl.ds(start, size)]
        return pltpu.make_async_remote_copy(
            src_ref=part,
            dst_ref=part,
            send_sem=self.send.at[which],
            recv_sem=self.recv.at[which],
            device_id=self.device(axis, step),
            device_id_type=MESH,
        )

    def start(self, *which):
        for one in which:
            self.copy(one).start()

    def arrive(self, *which):
        for one in which:
            self.copy(one).wait_recv()

    def drain(self):
        for one in range(8):
            self.copy(one).wait_send()


def forward_kernel(
    tokens, cot, routes_t, length, cosine, sine, attn_gain, query_gain, key_gain, ffn_gain,
    w_query, w_key, w_value, w_output,
    ffn_in, hidden, mixed_t, queries, log_total, normed, query_raw, key_raw, kv_all, cot_all,
    wq, wk, wv, wo, kv, turned, most, total, mixed, packed,
    ag_send, ag_recv, kv_send, kv_recv, w_sem, kv_sem, own_sem,
):
    torus = Torus()
    here, device = everywhere()
    me = here["x"] * 2 + here["core"]
    barrier = pltpu.get_barrier_semaphore()
    peers = [*torus.neighbours(), device("core", 1), device("x", 1), device("x", -1)]
    for peer in peers:
        pl.semaphore_signal(barrier, inc=1, device_id=peer, device_id_type=MESH)
    loads = [
        pltpu.make_async_copy(source, target, w_sem.at[n])
        for n, (source, target) in enumerate(((w_query, wq), (w_key, wk), (w_value, wv), (w_output, wo)))
    ]
    for load in loads:
        load.start()

    expert_rows = lax.broadcasted_iota(jnp.int32, (EXPERTS, ROWS), 0)
    member = jnp.zeros((EXPERTS, ROWS), jnp.float32)
    for k in range(TOPK):
        member = member + jnp.where(expert_rows == routes_t[pl.ds(k, 1), :], 1.0, 0.0)
    laid = jnp.concatenate([member[8 * q : 8 * q + 8] for q in range(4)], axis=1)
    packed[...] = jnp.concatenate([laid, jnp.zeros_like(laid)], axis=0).astype(jnp.bfloat16)
    first_row = pl.multiple_of(torus.expert * SENT, 16)
    owns = [
        pltpu.make_async_copy(packed, cot_all.at[pl.ds(first_row, EXTRA)], own_sem.at[0]),
        pltpu.make_async_copy(
            cot.at[pl.ds(0, SENT - EXTRA)],
            cot_all.at[pl.ds(pl.multiple_of(first_row + EXTRA, 16), SENT - EXTRA)],
            own_sem.at[1],
        ),
    ]
    for copy in owns:
        copy.start()
    for copy in owns:
        copy.wait()
    pl.semaphore_wait(barrier, len(peers))

    def gather(number, axis, other, low, first, second):
        return Gather(torus, cot_all, ag_send, ag_recv, number, axis, other, low, first, second, SENT)

    a_first = gather(0, "y", 0, 0, 48, 48)
    b_first = gather(1, "z", 0, 96, 48, 48)
    a_second = {d: gather(2 + d % RING, "z", d, 0, 48, 48) for d in (0, 1, -1, 2)}
    b_second = {d: gather(6 + d % RING, "y", d, 96, 48, 48) for d in (0, 1, -1, 2)}
    gathers = [a_first, b_first, *a_second.values(), *b_second.values()]
    a_first.first()
    b_first.first()
    b_second[0].first()
    a_second[0].first()

    @pl.loop(0, 4)
    def _(n):
        at = pl.ds(pl.multiple_of(n * 64, 64), 64)
        rows = tokens[at].astype(jnp.float32)
        normed[at] = (rows * rms_scale(rows) * as_row(attn_gain)).astype(jnp.bfloat16)

    for load in loads:
        load.wait()

    keys = Keys(here, device, kv, kv_send, kv_recv)
    key_raw[...] = dot_nn(normed[...], wk[...])
    scaled = key_raw[...]
    scaled = (scaled * rms_scale(scaled) * as_row(key_gain)).T
    for j in range(KV_HEADS):
        head = turned_rows(scaled[j * 64 : j * 64 + 64], cosine[...], sine[...])
        kv[me, pl.ds(j * 64, 64)] = head.astype(jnp.bfloat16)
    kv[me, pl.ds(512, 512)] = dot_nn(normed[...], wv[...]).T.astype(jnp.bfloat16)
    keys.start(0, 1, 2)
    query_raw[...] = dot_nn(normed[...], wq[...])
    scaled = query_raw[...]
    turned[...] = (scaled * rms_scale(scaled) * as_row(query_gain)).T

    for j in range(KV_HEADS):
        for r in range(2):
            head = turned[j * 128 + r * 64 : j * 128 + r * 64 + 64]
            head = turned_rows(head, cosine[...], sine[...])
            queries[j, :, r * ROWS : (r + 1) * ROWS] = (head * HEAD_DIM**-0.5).astype(jnp.bfloat16)

    a_first.second()
    b_first.second()
    for d in (1, -1):
        b_second[d].first()
        a_second[d].first()

    key_at = lax.broadcasted_iota(jnp.int32, (ROWS, 2 * ROWS), 0)
    query_at = lax.broadcasted_iota(jnp.int32, (ROWS, 2 * ROWS), 1) % ROWS
    valid = (key_at <= query_at) & (key_at + me * ROWS < length[...])

    def heads_of(block):
        keys_here = [kv[block, j * 64 : j * 64 + 64] for j in range(KV_HEADS)]
        values_here = [kv[block, 512 + j * 64 : 576 + j * 64] for j in range(KV_HEADS)]
        return keys_here, values_here

    keys_here, values_here = heads_of(me)
    scores = [jnp.where(valid, dot_tn(keys_here[j], queries[j]), -1e30) for j in range(KV_HEADS)]
    tops = [jnp.max(one, axis=0, keepdims=True) for one in scores]
    probs = [jnp.exp(one - top) for one, top in zip(scores, tops)]
    parts = [dot_nn(one, prob.astype(jnp.bfloat16)) for one, prob in zip(values_here, probs)]
    for j in range(KV_HEADS):
        most[j] = tops[j]
        total[j] = jnp.sum(probs[j], axis=0, keepdims=True)
        mixed[j] = parts[j]

    @pl.loop(1, 8)
    def _(step):
        @pl.when(step == 1)
        def _():
            a_first.third()
            b_first.third()
            b_second[2].first()
            a_second[2].first()
            keys.arrive(0)

        @pl.when(step == 2)
        def _():
            keys.arrive(1)
            keys.start(3, 5)
            keys.arrive(2)
            keys.start(4, 6)
            b_second[0].second()
            a_second[0].second()

        @pl.when(step == 3)
        def _():
            keys.arrive(5)
            for d in (1, -1):
                b_second[d].second()
                a_second[d].second()

        @pl.when(step == 5)
        def _():
            keys.arrive(3, 4)
            keys.start(7)
            keys.arrive(6)
            b_second[2].second()
            a_second[2].second()

        @pl.when(step == 7)
        def _():
            keys.arrive(7)

        block = (here["x"] + kv_order(here, step) + RING) % RING * 2 + (here["core"] + step) % 2

        @pl.when(block < me)
        def _():
            keys_here, values_here = heads_of(block)
            before = [most[j] for j in range(KV_HEADS)]
            shares = [total[j] for j in range(KV_HEADS)]
            sums = [mixed[j] for j in range(KV_HEADS)]
            scores = [dot_tn(keys_here[j], queries[j]) for j in range(KV_HEADS)]
            tops = [jnp.maximum(old, jnp.max(one, axis=0, keepdims=True)) for old, one in zip(before, scores)]
            probs = [jnp.exp(one - top) for one, top in zip(scores, tops)]
            less = [jnp.exp(old - top) for old, top in zip(before, tops)]
            parts = [dot_nn(one, prob.astype(jnp.bfloat16)) for one, prob in zip(values_here, probs)]
            for j in range(KV_HEADS):
                most[j] = tops[j]
                total[j] = shares[j] * less[j] + jnp.sum(probs[j], axis=0, keepdims=True)
                mixed[j] = sums[j] * less[j] + parts[j]

    save = pltpu.make_async_copy(kv, kv_all, kv_sem)
    save.start()

    for j in range(KV_HEADS):
        share = total[j]
        log_total[j] = most[j] + jnp.log(share)
        head = (mixed[j] * (1.0 / share)).astype(jnp.bfloat16)
        for r in range(2):
            mixed_t[j * 128 + r * 64 : j * 128 + r * 64 + 64, :] = head[:, r * ROWS : (r + 1) * ROWS]

    hidden[...] = dot_tn(mixed_t[...], wo[...])

    @pl.loop(0, 4)
    def _(n):
        at = pl.ds(pl.multiple_of(n * 64, 64), 64)
        rows = hidden[at] + tokens[at].astype(jnp.float32)
        hidden[at] = rows
        ffn_in[at] = (rows * rms_scale(rows) * as_row(ffn_gain)).astype(jnp.bfloat16)

    for d in (0, 1, -1, 2):
        a_second[d].third()
        b_second[d].third()
    save.wait()
    keys.drain()
    for one in gathers:
        one.drain()


def forward(tokens, cot, routes_t, length, cosine, sine, gains, weights):
    vmem, hbm = pl.BlockSpec(memory_space=pltpu.VMEM), pl.BlockSpec(memory_space=pl.ANY)
    low, wide = jnp.bfloat16, jnp.float32
    shape = jax.ShapeDtypeStruct
    return pl.pallas_call(
        forward_kernel,
        name="forward",
        out_shape=(
            shape((ROWS, 1024), low),
            shape((ROWS, 1024), wide),
            shape((1024, ROWS), low),
            shape((KV_HEADS, HEAD_DIM, 2 * ROWS), low),
            shape((KV_HEADS, 1, 2 * ROWS), wide),
            shape((ROWS, 1024), low),
            shape((ROWS, 1024), wide),
            shape((ROWS, 512), wide),
            shape((8, 1024, ROWS), low),
            shape((16 * SENT, 1024), low),
        ),
        in_specs=[vmem] * 10 + [hbm] * 4,
        out_specs=(vmem,) * 8 + (hbm, hbm),
        scratch_shapes=[
            pltpu.VMEM((1024, 1024), low),
            pltpu.VMEM((1024, 512), low),
            pltpu.VMEM((1024, 512), low),
            pltpu.VMEM((1024, 1024), low),
            pltpu.VMEM((8, 1024, ROWS), low),
            pltpu.VMEM((1024, ROWS), wide),
            pltpu.VMEM((KV_HEADS, 1, 2 * ROWS), wide),
            pltpu.VMEM((KV_HEADS, 1, 2 * ROWS), wide),
            pltpu.VMEM((KV_HEADS, HEAD_DIM, 2 * ROWS), wide),
            pltpu.VMEM((EXTRA, 1024), low),
            pltpu.SemaphoreType.DMA((10, 4)),
            pltpu.SemaphoreType.DMA((10, 4)),
            pltpu.SemaphoreType.DMA((8,)),
            pltpu.SemaphoreType.DMA((8,)),
            pltpu.SemaphoreType.DMA((4,)),
            pltpu.SemaphoreType.DMA,
            pltpu.SemaphoreType.DMA((2,)),
        ],
        compiler_params=pltpu.CompilerParams(
            collective_id=3, has_side_effects=True, vmem_limit_bytes=56 * 2**20
        ),
    )(tokens, cot, routes_t, length, cosine, sine, *gains, *weights)


ORDERS = (("x", "y", "z"), ("y", "z", "x"), ("z", "x", "y"))
STREAMS = {2048: ((0, 768), (768, 768), (1536, 512)), 2304: ((0, 768), (768, 768), (1536, 768))}


class Total:
    def __init__(self, here, device, buffer, shift, final, landing, work, send, recv, number, stream, half):
        self.here, self.device, self.buffer, self.shift, self.final = here, device, buffer, shift, final
        self.landing, self.work = landing, work
        self.send, self.recv, self.number, self.order = send, recv, number, ORDERS[(stream + number // 3) % 3]
        self.half = half
        self.start, self.rows = STREAMS[half][stream]
        first = self.start + self.start * 9 // 8
        r = self.rows
        self.lands = (first, first + r, first + r + 3 * (r // 4), first + r + 3 * (r // 4) + 3 * (r // 16))

    def own(self):
        return self.here["core"] * self.half + self.start

    def copy(self, which, source, target, axis, step):
        return pltpu.make_async_remote_copy(
            src_ref=source,
            dst_ref=target,
            send_sem=self.send.at[self.number, which],
            recv_sem=self.recv.at[self.number, which],
            device_id=self.device(axis, step),
            device_id_type=MESH,
        )

    def held(self, at, size):
        return self.buffer.at[pl.ds(pl.multiple_of(at + self.shift, 16), size)]

    def ready(self, at, size):
        return self.final.at[pl.ds(pl.multiple_of(at, 16), size)]

    def land(self, stage, n, size):
        return self.landing.at[pl.ds(self.lands[stage] + n * size, size)]

    def copies(self, stage):
        r, own = self.rows, self.own()
        a, b, c = self.order
        ia, ib = self.here[a], self.here[b]
        second = own + ia * (r // 4)
        third = second + ib * (r // 16)
        if stage == 0:
            there = (1 - self.here["core"]) * self.half + self.start
            return [self.copy(0, self.held(there, r), self.land(0, 0, r), "core", 1)]
        if stage == 6:
            return [self.copy(16, self.ready(own, r), self.ready(own, r), "core", 1)]
        found = []
        for d in (1, 2, 3):
            if stage == 1:
                source, target, axis = self.held(own + (ia + d) % RING * (r // 4), r // 4), self.land(1, d - 1, r // 4), a
            elif stage == 2:
                source = self.held(second + (ib + d) % RING * (r // 16), r // 16)
                target, axis = self.land(2, d - 1, r // 16), b
            elif stage == 3:
                source = self.work.at[self.number, pl.ds(0, r // 16)]
                target, axis = self.land(3, d - 1, r // 16), c
            elif stage == 4:
                source, target, axis = self.ready(third, r // 16), self.ready(third, r // 16), b
            else:
                source, target, axis = self.ready(second, r // 4), self.ready(second, r // 4), a
            found.append(self.copy(1 + (stage - 1) * 3 + d - 1, source, target, axis, d))
        return found

    def begin(self, stage):
        for copy in self.copies(stage):
            copy.start()

    def add(self, stage, load, store, size, count):
        step = 64 if size % 64 == 0 else 16

        @pl.loop(0, size // step)
        def _(k):
            at = k * step
            total = load(at, step).astype(jnp.float32)
            for n in range(count):
                land = pl.ds(pl.multiple_of(self.lands[stage] + n * size + at, 16), step)
                total = total + self.landing[land].astype(jnp.float32)
            store(at, step, total.astype(jnp.bfloat16))

    def finish(self, stage):
        for copy in self.copies(stage):
            copy.wait_recv()
        if stage > 3:
            return
        r, own = self.rows, self.own()
        a, b, _ = self.order
        second = own + self.here[a] * (r // 4)
        third = second + self.here[b] * (r // 16)
        first = (own, second, third, third)[stage] + self.shift

        def in_place(at, step, *value):
            lines = pl.ds(pl.multiple_of(first + at, 16), step)
            if not value:
                return self.buffer[lines]
            self.buffer[lines] = value[0]

        def in_work(at, step, *value):
            lines = pl.ds(pl.multiple_of(at, 16), step)
            if not value:
                return self.work[self.number, lines]
            self.work[self.number, lines] = value[0]

        def in_final(at, step, value):
            self.final[pl.ds(pl.multiple_of(third + at, 16), step)] = value

        if stage == 0:
            self.add(0, in_place, in_place, r, 1)
        elif stage == 1:
            self.add(1, in_place, in_place, r // 4, 3)
        elif stage == 2:
            self.add(2, in_place, in_work, r // 16, 3)
        else:
            self.add(3, in_work, in_final, r // 16, 3)

    def drain(self):
        for stage in range(7):
            for copy in self.copies(stage):
                copy.wait_send()


class Small:
    STAGES = (("core", (1,)), ("x", (1, 2, 3)), ("y", (1, 2, 3)), ("z", (1, 2, 3)))

    def __init__(self, device, value, landing, send, recv):
        self.device, self.value, self.landing, self.send, self.recv = device, value, landing, send, recv

    def copies(self, stage):
        axis, steps = self.STAGES[stage]
        first = sum(len(s) for _, s in self.STAGES[:stage])
        return [
            pltpu.make_async_remote_copy(
                src_ref=self.value.at[stage],
                dst_ref=self.landing.at[first + n],
                send_sem=self.send.at[first + n],
                recv_sem=self.recv.at[first + n],
                device_id=self.device(axis, step),
                device_id_type=MESH,
            )
            for n, step in enumerate(steps)
        ]

    def begin(self, stage):
        for copy in self.copies(stage):
            copy.start()

    def finish(self, stage):
        for copy in self.copies(stage):
            copy.wait_recv()
        first = sum(len(s) for _, s in self.STAGES[:stage])
        total = self.value[stage]
        for n in range(len(self.STAGES[stage][1])):
            total = total + self.landing[first + n]
        self.value[stage + 1] = total

    def drain(self):
        for stage in range(4):
            for copy in self.copies(stage):
                copy.wait_send()


class Line:
    def __init__(self, here, device):
        self.here, self.device = here, device

    def along(self, axis, other, step):
        return (self.here["x"] + step + RING) % RING

    def near(self, axis, step):
        return self.device("x", step)


def rms_back(values, gain, grad):
    scale = rms_scale(values)
    lifted = gain * grad
    inner = jnp.mean(values * lifted, axis=-1, keepdims=True)
    return scale * lifted - values * (scale * scale * scale) * inner, jnp.sum(
        grad * values * scale, axis=0, keepdims=True
    )


def turned_back(grads, cosine, sine):
    front, back = grads[: HEAD_DIM // 2], grads[HEAD_DIM // 2 :]
    return jnp.concatenate([front * cosine + back * sine, back * cosine - front * sine], axis=0)


def backward_kernel(
    hidden, ffn_in, cot, tokens, normed, key_raw, mixed_t, queries, log_total,
    routes_t, length, cosine, sine, attn_gain, query_gain, key_gain, ffn_gain, router_rows, own_gu, own_down,
    returned_all, query_raw_all, mixed_parts, kv_all, w_query, w_key, w_value, w_output,
    mixed_out, token_grad, early_small, late_small, query_sum, key_sum, value_sum, output_sum, all_gu, all_down,
    sums, rows, returned, square, kv, hidden_grad, result, branch, grads, delta, query_grad, turned,
    for_mate, from_mate, kv_sums, kv_rows, key_low, value_low,
    held, final_output, final_query, final_keys, land_output, land_query, land_keys, work, late_values, late_rows,
    rs_send, rs_recv, mate_send, mate_recv, kv_send, kv_recv, ar_send, ar_recv, small_send, small_recv, load_sem, out_sem, ex_send, ex_recv,
):
    torus = Torus()
    here, device = everywhere()
    me = here["x"] * 2 + here["core"]
    barrier = pltpu.get_barrier_semaphore()
    peers = [device("core", 1)] + [device(axis, d) for axis in "xyz" for d in (1, 2, 3)]
    for peer in peers:
        pl.semaphore_signal(barrier, inc=1, device_id=peer, device_id_type=MESH)
    loads = [
        pltpu.make_async_copy(source, target, load_sem.at[n])
        for n, (source, target) in enumerate(
            ((returned_all, returned), (w_output, square), (mixed_parts, sums), (kv_all, kv))
        )
    ]
    for load in loads:
        load.start()
    owns = [
        pltpu.make_async_copy(own_gu, all_gu.at[me], load_sem.at[8]),
        pltpu.make_async_copy(own_down, all_down.at[me], load_sem.at[9]),
    ]
    for copy in owns:
        copy.start()
    order = (2, 1, -1, 0)
    leads = []
    for n, d in enumerate(order):
        leads.append(Scatter(torus, sums, rows, rs_send, rs_recv, n, n * 384, "z", d, 0, 64, 64))
        leads.append(Scatter(torus, sums, rows, rs_send, rs_recv, 4 + n, (5 + n) * 384, "y", d, 128, 64, 64))
    lasts = [
        Scatter(torus, sums, rows, rs_send, rs_recv, 8, 4 * 384, "y", 0, 0, 64, 64),
        Scatter(torus, sums, rows, rs_send, rs_recv, 9, 9 * 384, "z", 0, 128, 64, 64),
    ]
    ring = Scatter(Line(here, device), kv_sums, kv_rows, kv_send, kv_recv, 0, 0, "x", 0, 0, 512, 512)
    experts = [
        Keys(here, device, blocks, ex_send.at[n], ex_recv.at[n]) for n, blocks in enumerate((all_gu, all_down))
    ]
    for copy in owns:
        copy.wait()
    pl.semaphore_wait(barrier, len(peers))
    for one in experts:
        one.start(0, 1, 2)
    loads[2].wait()
    for one in leads:
        one.first()

    expert_rows = lax.broadcasted_iota(jnp.int32, (EXPERTS, ROWS), 0)
    member = jnp.zeros((EXPERTS, ROWS), jnp.float32)
    for k in range(TOPK):
        member = member + jnp.where(expert_rows == routes_t[pl.ds(k, 1), :], 1.0, 0.0)
    named = member > 0.5
    logits = jnp.where(named, dot_nt(router_rows[...], ffn_in[...]), -1e30)
    weight = jnp.where(named, jnp.exp(logits - jnp.max(logits, axis=0, keepdims=True)), 0.0)
    gates = weight / jnp.sum(weight, axis=0, keepdims=True)
    loads[0].wait()
    gate_grad = jnp.concatenate([returned[:8, q * ROWS : (q + 1) * ROWS] for q in range(4)], axis=0)
    logit_grad = (gates * (gate_grad - jnp.sum(gates * gate_grad, axis=0, keepdims=True))).astype(jnp.bfloat16)
    result[...] = dot_tn(logit_grad, router_rows[...])
    router_grad = dot_nn(logit_grad, ffn_in[...]).astype(jnp.bfloat16)
    for q in range(4):
        held[2048 + q * EXPERTS : 2048 + (q + 1) * EXPERTS] = router_grad[:, q * 256 : (q + 1) * 256]

    def ffn_part(n, gain_grad):
        at = pl.ds(pl.multiple_of(n * 64, 64), 64)
        grad = result[at] + returned[pl.ds(pl.multiple_of(n * 64 + EXTRA, 16), 64)]
        part, more = rms_back(hidden[at], as_row(ffn_gain), grad)
        part = part + cot[at].astype(jnp.float32)
        hidden_grad[at] = part
        branch[at] = part.astype(jnp.bfloat16)
        return gain_grad + more

    gain_grad = lax.fori_loop(0, 4, ffn_part, jnp.zeros((1, 1024), jnp.float32))
    gain_lines = [gain_grad[:, q * 256 : (q + 1) * 256] for q in range(4)] + [jnp.zeros((124, 256), jnp.float32)]
    held[2176:2304] = jnp.concatenate(gain_lines, axis=0).astype(jnp.bfloat16)
    held[4352:4608] = jnp.zeros((256, 256), jnp.bfloat16)

    loads[1].wait()
    turned[...] = dot_nt(square[...], branch[...])
    next_load = pltpu.make_async_copy(w_query, square, load_sem.at[6])
    next_load.start()
    query_raw = returned.at[pl.ds(0, ROWS)]
    raw_load = pltpu.make_async_copy(query_raw_all, query_raw, load_sem.at[7])
    raw_load.start()

    for j in range(KV_HEADS):
        for r in range(2):
            at = slice(j * 128 + r * 64, j * 128 + r * 64 + 64)
            low = turned[at].astype(jnp.bfloat16)
            grads[j, :, r * ROWS : (r + 1) * ROWS] = low
            delta[j, :, r * ROWS : (r + 1) * ROWS] = jnp.sum(
                low.astype(jnp.float32) * mixed_t[at].astype(jnp.float32), axis=0, keepdims=True
            )
        query_grad[j] = jnp.zeros((HEAD_DIM, 2 * ROWS), jnp.float32)

    @pl.loop(0, 4)
    def _(n):
        at = pl.ds(pl.multiple_of(n * 256, 256), 256)
        part = dot_nn(mixed_t[at], branch[...]).astype(jnp.bfloat16)
        for q in range(4):
            held[pl.ds(pl.multiple_of(q * 1024 + q // 2 * 256 + n * 256, 256), 256)] = part[:, q * 256 : (q + 1) * 256]

    loads[3].wait()

    def reduction(number, buffer, shift, final, land, half):
        return [
            Total(here, device, buffer, shift, final, land, work, ar_send, ar_recv, 3 * number + s, s, half)
            for s in range(3)
        ]

    early = reduction(0, held, 0, final_output, land_output, 2304)
    of_query = reduction(1, kv, 0, final_query, land_query, 2048)
    of_keys = reduction(2, kv, 4096, final_keys, land_keys, 2048)
    late_few = Small(device, late_values, late_rows, small_send, small_recv)
    for one in early:
        one.begin(0)

    def onward(streams, stage):
        for one in streams:
            one.finish(stage)
            if stage < 6:
                one.begin(stage + 1)

    def write_out(number, final, first, target, at):
        block = final.at[pl.ds(first, 1024)]
        return pltpu.make_async_copy(block, target.at[:, pl.ds(at * 256, 256)], out_sem.at[number])

    outs = [write_out(q, final_output, q * 1024 + q // 2 * 256, output_sum, q) for q in range(4)]
    outs += [write_out(4 + q, final_query, q * 1024, query_sum, q) for q in range(4)]
    outs += [write_out(8 + q, final_keys, q * 1024, key_sum, q) for q in range(2)]
    outs += [write_out(10 + q, final_keys, (2 + q) * 1024, value_sum, q) for q in range(2)]

    def mate_copy(turn, at):
        return pltpu.make_async_remote_copy(
            src_ref=for_mate.at[turn % 2],
            dst_ref=from_mate.at[at],
            send_sem=mate_send.at[turn],
            recv_sem=mate_recv.at[turn],
            device_id=device("core", 1),
            device_id_type=MESH,
        )

    key_at = lax.broadcasted_iota(jnp.int32, (ROWS, 2 * ROWS), 0)
    query_at = lax.broadcasted_iota(jnp.int32, (ROWS, 2 * ROWS), 1) % ROWS
    valid = (key_at <= query_at) & (key_at + me * ROWS < length[...])

    def block_grads(block, target, at, masked):
        for group in range(2):
            heads = range(4 * group, 4 * group + 4)
            key_heads = [kv[pl.ds(pl.multiple_of(block * 1024 + j * 64, 64), 64)] for j in heads]
            value_heads = [kv[pl.ds(pl.multiple_of(block * 1024 + 512 + j * 64, 64), 64)] for j in heads]
            probs = [jnp.exp(dot_tn(one, queries[j]) - log_total[j]) for one, j in zip(key_heads, heads)]
            if masked:
                probs = [jnp.where(valid, one, 0.0) for one in probs]
            probs_grads = [dot_tn(one, grads[j]) for one, j in zip(value_heads, heads)]
            lows = [
                (one * (grad - delta[j])).astype(jnp.bfloat16) for one, grad, j in zip(probs, probs_grads, heads)
            ]
            key_parts = [dot_nt(queries[j], low).astype(jnp.bfloat16) for low, j in zip(lows, heads)]
            value_parts = [
                dot_nt(grads[j], one.astype(jnp.bfloat16)).astype(jnp.bfloat16) for one, j in zip(probs, heads)
            ]
            query_parts = [dot_nn(one, low) for one, low in zip(key_heads, lows)]
            for n, j in enumerate(heads):
                target[at, j * 64 : j * 64 + 64] = key_parts[n]
                target[at, 512 + j * 64 : 576 + j * 64] = value_parts[n]
                query_grad[j] += query_parts[n]

    def from_other(turn, at):
        mate_copy(turn, at).wait_recv()

        @pl.loop(0, 16)
        def _(n):
            lines = pl.ds(pl.multiple_of(n * 64, 64), 64)
            total = kv_sums[at, lines].astype(jnp.float32) + from_mate[at, lines].astype(jnp.float32)
            kv_sums[at, lines] = total.astype(jnp.bfloat16)

    def turn_x(turn):
        offset = (1 - turn % 2) * (2 + turn // 2) + (turn % 2) * (1 - turn // 2)
        return (here["x"] + offset + RING) % RING

    @pl.loop(0, 4)
    def _(turn):
        @pl.when(turn == 1)
        def _():
            for one in leads:
                one.second()
            for one in experts:
                one.arrive(1)
                one.start(3, 5)
                one.arrive(2)
                one.start(4, 6)

        @pl.when(turn == 2)
        def _():
            onward(early, 0)

        @pl.when(turn == 3)
        def _():
            onward(early, 1)

        at = turn_x(turn)
        other = at * 2 + 1 - here["core"]

        @pl.when(turn >= 2)
        def _():
            mate_copy(turn - 2, at).wait_send()

        @pl.when(other < me)
        def _():
            block_grads(other, for_mate, turn % 2, False)

        @pl.when(other >= me)
        def _():
            for_mate[turn % 2] = jnp.zeros((1024, ROWS), jnp.bfloat16)

        mate_copy(turn, at).start()

        own = at * 2 + here["core"]

        @pl.when(own < me)
        def _():
            block_grads(own, kv_sums, at, False)

        @pl.when(own > me)
        def _():
            kv_sums[at] = jnp.zeros((1024, ROWS), jnp.bfloat16)

        @pl.when(own == me)
        def _():
            block_grads(own, kv_sums, at, True)

        from_other(turn, at)

        @pl.when(turn == 0)
        def _():
            ring.first()

        @pl.when(turn == 2)
        def _():
            ring.second()

    for j in range(KV_HEADS):
        for r in range(2):
            head = query_grad[j, :, r * ROWS : (r + 1) * ROWS] * HEAD_DIM**-0.5
            turned[j * 128 + r * 64 : j * 128 + r * 64 + 64] = turned_back(head, cosine[...], sine[...])

    raw_load.wait()
    result[...] = turned[...].T

    def query_part(n, gain_grad):
        at = pl.ds(pl.multiple_of(n * 64, 64), 64)
        part, more = rms_back(query_raw[at], as_row(query_gain), result[at])
        branch[at] = part.astype(jnp.bfloat16)
        return gain_grad + more

    query_gain_grad = lax.fori_loop(0, 4, query_part, jnp.zeros((1, 1024), jnp.float32))

    @pl.loop(0, 4)
    def _(n):
        columns = pl.ds(pl.multiple_of(n * 256, 256), 256)
        part = dot_tn(normed[:, columns], branch[...]).astype(jnp.bfloat16)
        for q in range(4):
            kv[pl.ds(pl.multiple_of(q * 1024 + n * 256, 256), 256)] = part[:, q * 256 : (q + 1) * 256]

    for one in of_query:
        one.begin(0)
    onward(early, 2)
    for one in experts:
        one.arrive(3, 4)
        one.start(7)

    def put(at, total):
        turned[at] = total

    ring.third(put)
    for j in range(KV_HEADS):
        turned[j * 64 : j * 64 + 64] = turned_back(turned[j * 64 : j * 64 + 64], cosine[...], sine[...])
    part, key_gain_grad = rms_back(key_raw[...], as_row(key_gain), turned[:512].T)
    key_low[...] = part.astype(jnp.bfloat16)
    value_low[...] = turned[512:].T.astype(jnp.bfloat16)

    @pl.loop(0, 4)
    def _(n):
        columns = pl.ds(pl.multiple_of(n * 256, 256), 256)
        part = dot_tn(normed[:, columns], jnp.concatenate([key_low[...], value_low[...]], axis=1)).astype(jnp.bfloat16)
        for q in range(4):
            kv[pl.ds(pl.multiple_of(4096 + q * 1024 + n * 256, 256), 256)] = part[:, q * 256 : (q + 1) * 256]

    for one in of_keys:
        one.begin(0)
    next_load.wait()
    result[...] = dot_nt(branch[...], square[...])
    last_loads = [
        pltpu.make_async_copy(w_key, square.at[:, pl.ds(0, 512)], load_sem.at[4]),
        pltpu.make_async_copy(w_value, square.at[:, pl.ds(512, 512)], load_sem.at[5]),
    ]
    for load in last_loads:
        load.start()
    onward(of_query, 0)
    for load in last_loads:
        load.wait()
    result[...] += dot_nt(jnp.concatenate([key_low[...], value_low[...]], axis=1), square[...])

    def token_part(n, gain_grad):
        at = pl.ds(pl.multiple_of(n * 64, 64), 64)
        part, more = rms_back(tokens[at].astype(jnp.float32), as_row(attn_gain), result[at])
        token_grad[at] = (hidden_grad[at] + part).astype(jnp.bfloat16)
        return gain_grad + more

    attn_gain_grad = lax.fori_loop(0, 4, token_part, jnp.zeros((1, 1024), jnp.float32))
    key_wide = jnp.concatenate([key_gain_grad, jnp.zeros((1, 512), jnp.float32)], axis=1)
    late_values[0] = jnp.concatenate(
        [attn_gain_grad, query_gain_grad, key_wide, jnp.zeros((5, 1024), jnp.float32)], axis=0
    )
    late_few.begin(0)
    onward(of_keys, 0)
    onward(early, 3)
    for stage in range(1, 4):
        onward(of_query, stage)
        late_few.finish(stage - 1)
        late_few.begin(stage)
        onward(of_keys, stage)
        onward(early, stage + 3)
        if stage == 1:
            for one in leads:
                one.third()
            for one in lasts:
                one.first()
        if stage == 3:
            for one in lasts:
                one.second()
    for q in range(4):
        outs[q].start()
    late_few.finish(3)
    late_small[...] = late_values[4]
    router = [final_output[2048 + q * EXPERTS : 2048 + (q + 1) * EXPERTS].astype(jnp.float32) for q in range(4)]
    lines = final_output[2176:2192].astype(jnp.float32)
    lines = jnp.concatenate([lines[q : q + 1] for q in range(4)], axis=1)
    early_small[...] = jnp.concatenate(
        [jnp.concatenate(router, axis=1), lines, jnp.zeros((7, 1024), jnp.float32)], axis=0
    )

    def put_mixed(at, total):
        mixed_out[at] = (hidden[at] + total).astype(jnp.bfloat16)

    for stage in range(4, 7):
        onward(of_query, stage)
        onward(of_keys, stage)
        if stage == 5:
            for one in lasts:
                one.third(put_mixed)
    for q in range(4, 12):
        outs[q].start()
    for one in experts:
        one.arrive(0, 5, 6, 7)
    for one in [*experts, *leads, *lasts, ring, *early, *of_query, *of_keys, late_few]:
        one.drain()
    for turn in (2, 3):
        mate_copy(turn, 0).wait_send()
    for out in outs:
        out.wait()


def backward(smalls, larges):
    vmem, hbm = pl.BlockSpec(memory_space=pltpu.VMEM), pl.BlockSpec(memory_space=pl.ANY)
    low, wide = jnp.bfloat16, jnp.float32
    shape = jax.ShapeDtypeStruct
    dma = pltpu.SemaphoreType.DMA
    return pl.pallas_call(
        backward_kernel,
        name="backward",
        out_shape=(
            shape((ROWS, 1024), low),
            shape((ROWS, 1024), low),
            shape((40, 1024), wide),
            shape((8, 1024), wide),
            shape((1024, 1024), low),
            shape((1024, 512), low),
            shape((1024, 512), low),
            shape((1024, 1024), low),
            shape((8, 256, 1024), low),
            shape((8, 128, 1024), low),
        ),
        in_specs=[vmem] * len(smalls) + [hbm] * len(larges),
        out_specs=(vmem,) * 4 + (hbm,) * 6,
        scratch_shapes=[
            pltpu.VMEM((16, ROWS, 1024), low),
            pltpu.VMEM((10 * 384, 1024), low),
            pltpu.VMEM((FULL, 1024), wide),
            pltpu.VMEM((1024, 1024), low),
            pltpu.VMEM((8 * 1024, ROWS), low),
            pltpu.VMEM((ROWS, 1024), wide),
            pltpu.VMEM((ROWS, 1024), wide),
            pltpu.VMEM((ROWS, 1024), low),
            pltpu.VMEM((KV_HEADS, HEAD_DIM, 2 * ROWS), low),
            pltpu.VMEM((KV_HEADS, 1, 2 * ROWS), wide),
            pltpu.VMEM((KV_HEADS, HEAD_DIM, 2 * ROWS), wide),
            pltpu.VMEM((1024, ROWS), wide),
            pltpu.VMEM((2, 1024, ROWS), low),
            pltpu.VMEM((4, 1024, ROWS), low),
            pltpu.VMEM((4, 1024, ROWS), low),
            pltpu.VMEM((3072, ROWS), low),
            pltpu.VMEM((ROWS, 512), low),
            pltpu.VMEM((ROWS, 512), low),
            pltpu.VMEM((4608, 256), low),
            pltpu.VMEM((4608, 256), low),
            pltpu.VMEM((4096, 256), low),
            pltpu.VMEM((4096, 256), low),
            pltpu.VMEM((4896, 256), low),
            pltpu.VMEM((4352, 256), low),
            pltpu.VMEM((4352, 256), low),
            pltpu.VMEM((9, 48, 256), low),
            pltpu.VMEM((5, 8, 1024), wide),
            pltpu.VMEM((10, 8, 1024), wide),
            dma((10, 4)),
            dma((10, 4)),
            dma((4,)),
            dma((4,)),
            dma((1, 4)),
            dma((1, 4)),
            dma((9, 17)),
            dma((9, 17)),
            dma((10,)),
            dma((10,)),
            dma((10,)),
            dma((12,)),
            dma((2, 8)),
            dma((2, 8)),
        ],
        compiler_params=pltpu.CompilerParams(
            collective_id=4, has_side_effects=True, vmem_limit_bytes=66000000
        ),
        cost_estimate=pl.CostEstimate(flops=100 * 10**9, bytes_accessed=60 * 10**6, transcendentals=8 * 10**6),
    )(*smalls, *larges)


def widen_kernel(
    early, late, mixed, tokens, query, key, value, output, gate_up, down,
    ffn_gain, attn_gain, query_gain, key_gain, router,
    mixed_out, token_out, query_out, key_out, value_out, output_out, gate_out, up_out, down_out,
    query_in, key_in, value_in, output_in, gate_up_in, down_in,
    query_wide, key_wide, value_wide, output_wide, gate_up_wide, down_wide,
    in_sem, out_sem,
):
    arrays = (
        (query, query_in, query_wide, query_out),
        (output, output_in, output_wide, output_out),
        (key, key_in, key_wide, key_out),
        (value, value_in, value_wide, value_out),
    )
    parts = []
    for source, low, wide, target in arrays:
        for n in range(0, 1024, 512):
            at = pl.ds(n, 512)
            parts.append((source.at[at], low.at[at], wide.at[at], [(wide.at[at], target.at[at])]))
    for block in range(8):
        rows, e = pl.ds(block // 2 * 256, 256), block % 2
        wide = gate_up_wide.at[block]
        targets = [
            (wide.at[:, pl.ds(0, 512)], gate_out.at[e, rows]),
            (wide.at[:, pl.ds(512, 512)], up_out.at[e, rows]),
        ]
        parts.append((gate_up.at[block], gate_up_in.at[block], wide, targets))
    for block in range(8):
        wide = down_wide.at[block]
        target = down_out.at[block % 2, pl.ds(block // 2 * 128, 128)]
        parts.append((down.at[block], down_in.at[block], wide, [(wide, target)]))
    loads = [pltpu.make_async_copy(source, low, in_sem.at[n]) for n, (source, low, _, _) in enumerate(parts)]
    for load in loads:
        load.start()
    ffn_gain[...] = early[EXPERTS]
    attn_gain[...] = late[0]
    query_gain[...] = late[1]
    key_gain[...] = late[2, :512]
    router[...] = early[:EXPERTS].T
    mixed_out[...] = mixed[...]
    token_out[...] = tokens[...]
    stores = []
    for load, (_, low, wide, targets) in zip(loads, parts):
        load.wait()
        wide[...] = low[...].astype(jnp.float32)
        for source, target in targets:
            stores.append(pltpu.make_async_copy(source, target, out_sem.at[len(stores)]))
            stores[-1].start()
    for copy in stores:
        copy.wait()


def widen(arrays):
    vmem, hbm = pl.BlockSpec(memory_space=pltpu.VMEM), pl.BlockSpec(memory_space=pl.ANY)
    low, wide = jnp.bfloat16, jnp.float32
    shape = jax.ShapeDtypeStruct
    held = ((1024, 1024), (1024, 512), (1024, 512), (1024, 1024), (8, 256, 1024), (8, 128, 1024))
    return pl.pallas_call(
        widen_kernel,
        name="widen",
        out_shape=(
            shape((1024,), wide),
            shape((1024,), wide),
            shape((1024,), wide),
            shape((512,), wide),
            shape((1024, EXPERTS), wide),
            shape((ROWS, 1024), low),
            shape((ROWS, 1024), low),
            shape((1024, 1024), wide),
            shape((1024, 512), wide),
            shape((1024, 512), wide),
            shape((1024, 1024), wide),
            shape((2, 1024, 512), wide),
            shape((2, 1024, 512), wide),
            shape((2, 512, 1024), wide),
        ),
        in_specs=[vmem] * 4 + [hbm] * 6,
        out_specs=(vmem,) * 7 + (hbm,) * 7,
        scratch_shapes=[
            *[pltpu.VMEM(size, low) for size in held],
            *[pltpu.VMEM(size, wide) for size in held],
            pltpu.SemaphoreType.DMA((24,)),
            pltpu.SemaphoreType.DMA((32,)),
        ],
        compiler_params=pltpu.CompilerParams(vmem_limit_bytes=56 * 2**20),
    )(*arrays)


def body(
    tokens,
    cotangent,
    lengths,
    routes,
    attn_gain,
    w_query,
    w_key,
    w_value,
    query_gain,
    key_gain,
    w_output,
    ffn_gain,
    w_router,
    w_gate,
    w_up,
    w_down,
):
    query_pos = lax.axis_index("dp") * ROWS + jnp.arange(ROWS, dtype=jnp.int32)
    cosine, sine_table = rope_tables(query_pos)
    cosine, sine_table = cosine.T, sine_table.T
    routes_t, length = routes[0].T, lengths.reshape(1, 1)
    gains = [attn_gain, query_gain, key_gain, ffn_gain]
    weights = (w_query, w_key, w_value, w_output)
    router_rows = w_router.T
    ffn_in, hidden, mixed_t, queries, log_total, normed, query_raw, key_raw, kv_all, cot_all = forward(
        tokens[0], cotangent[0], routes_t, length, cosine, sine_table, gains, weights
    )
    returned, mixed_parts, own_gu, own_down = moe(
        ffn_in, cot_all, cotangent[0], router_rows, w_gate, w_up, w_down
    )
    mixed_low, token_low, early_small, late_small, *sums = backward(
        (
            hidden, ffn_in, cotangent[0], tokens[0], normed, key_raw, mixed_t, queries, log_total, routes_t,
            length, cosine, sine_table, *gains, router_rows, own_gu, own_down,
        ),
        (returned, query_raw, mixed_parts, kv_all.reshape(8 * 1024, ROWS), *weights),
    )
    (
        ffn_gain_sum, attn_gain_sum, query_gain_sum, key_gain_sum, router_sum, mixed_out, token_grad,
        query_w_sum, key_w_sum, value_w_sum, output_w_sum, gate_w_sum, up_w_sum, down_w_sum,
    ) = widen((early_small, late_small, mixed_low, token_low, *sums))
    return (
        mixed_out[None],
        token_grad[None],
        attn_gain_sum,
        query_w_sum,
        key_w_sum,
        value_w_sum,
        query_gain_sum,
        key_gain_sum,
        output_w_sum,
        ffn_gain_sum,
        router_sum,
        gate_w_sum,
        up_w_sum,
        down_w_sum,
    )


def solution(mesh):
    return jax.shard_map(
        body,
        mesh=mesh,
        in_specs=(
            P("expert", "dp", None),
            P("expert", "dp", None),
            P("expert"),
            P("expert", "dp", None),
            P(),
            P(),
            P(),
            P(),
            P(),
            P(),
            P(),
            P(),
            P(),
            P("expert", None, None),
            P("expert", None, None),
            P("expert", None, None),
        ),
        out_specs=(
            P("expert", "dp", None),
            P("expert", "dp", None),
            P(),
            P(),
            P(),
            P(),
            P(),
            P(),
            P(),
            P(),
            P(),
            P("expert", None, None),
            P("expert", None, None),
            P("expert", None, None),
        ),
        check_vma=False,
    )
```

```python
import math

import jax
import jax.numpy as jnp
from jax import lax
from jax.experimental import pallas as pl
from jax.experimental.pallas import tpu as pltpu
from jax.sharding import PartitionSpec as P

HEADS = 16
KV_HEADS = 8
HEAD_DIM = 64
EXPERTS = 32
TOPK = 8
CAP = 80


epsilon = 1e-06


def rope_tables(positions):
    steps_half = jnp.arange(HEAD_DIM // 2).astype(jnp.float32)
    inverse = jnp.exp(steps_half * (-2.0 * math.log(10000.0) / HEAD_DIM))
    angles = positions.astype(jnp.float32)[:, None] * inverse[None, :]
    return (jnp.cos(angles), jnp.sin(angles))


RING = 4
ROWS = 256
EXTRA = 16
FULL = ROWS + EXTRA
SENT = 192
LEFT = FULL - SENT
BOTH = ROWS + LEFT
GROUP = 2 * CAP
MESH = pl.DeviceIdType.MESH


def dot_nn(a, b):
    return jnp.dot(a, b, preferred_element_type=jnp.float32)


def dot_nt(a, b):
    return lax.dot_general(a, b, (((1,), (1,)), ((), ())), preferred_element_type=jnp.float32)


def dot_tn(a, b):
    return lax.dot_general(a, b, (((0,), (0,)), ((), ())), preferred_element_type=jnp.float32)


def step_of(size):
    return next(step for step in (64, 48, 32, 16) if size % step == 0)


class Torus:
    def __init__(self):
        self.dp = lax.axis_index("dp")
        expert = lax.axis_index("expert")
        self.expert = expert
        self.z, self.y = expert // RING, expert % RING

    def block(self, dz, dy):
        return ((self.z + dz + RING) % RING) * RING + (self.y + dy + RING) % RING

    def near(self, axis, step):
        return (self.dp, self.block(step, 0) if axis == "z" else self.block(0, step))

    def along(self, axis, other, step):
        return self.block(step, other) if axis == "z" else self.block(other, step)

    def neighbours(self):
        return [self.near(axis, step) for axis in "yz" for step in (1, -1)]


ARRIVALS = (
    ((0, 0), (3, 0), (1, 3), (3, 2)),
    ((0, 1), (0, 2), (3, 1), (2, 1)),
    ((0, 3), (2, 0), (3, 3), (2, 3)),
    ((1, 0), (1, 1), (1, 2), (2, 2)),
)


def differences(values):
    found = list(values)
    for level in range(1, len(found)):
        for n in range(len(found) - 1, level - 1, -1):
            found[n] -= found[n - 1]
    return found


def chooses(n):
    return 1, n, n * (n - 1) // 2, n * (n - 1) * (n - 2) // 6


class Gather:
    def __init__(self, torus, buffer, send, recv, number, axis, other, low, first, second, stride):
        self.torus, self.buffer, self.send, self.recv = torus, buffer, send, recv
        self.number, self.axis, self.other, self.stride = number, axis, other, stride
        self.whole, self.front, self.rear = (low, first + second), (low, first), (low + first, second)

    def copy(self, which, offset, part, step):
        at = self.torus.along(self.axis, self.other, offset) * self.stride + part[0]
        rows = self.buffer.at[pl.ds(pl.multiple_of(at, 16), part[1])]
        return pltpu.make_async_remote_copy(
            src_ref=rows,
            dst_ref=rows,
            send_sem=self.send.at[self.number, which],
            recv_sem=self.recv.at[self.number, which],
            device_id=self.torus.near(self.axis, step),
            device_id_type=MESH,
        )

    def first(self):
        self.copy(0, 0, self.whole, 1).start()
        self.copy(1, 0, self.whole, -1).start()

    def second(self):
        self.copy(0, -1, self.whole, 1).wait_recv()
        self.copy(2, -1, self.front, 1).start()
        self.copy(1, 1, self.whole, -1).wait_recv()
        self.copy(3, 1, self.rear, -1).start()

    def third(self):
        self.copy(2, 2, self.front, 1).wait_recv()
        self.copy(3, 2, self.rear, -1).wait_recv()

    def drain(self):
        self.copy(0, 0, self.whole, 1).wait_send()
        self.copy(1, 0, self.whole, -1).wait_send()
        self.copy(2, -1, self.front, 1).wait_send()
        self.copy(3, 1, self.rear, -1).wait_send()


class Scatter:
    def __init__(self, torus, sums, landing, send, recv, number, base, axis, other, low, first, second, origin=None):
        self.torus, self.sums, self.landing, self.send, self.recv = torus, sums, landing, send, recv
        self.number, self.axis, self.other = number, axis, other
        self.origin = sums if origin is None else origin
        self.low, self.parts = low, (first, second)
        self.size = first + second
        self.slots = (base, base + first, base + self.size, base + 2 * self.size)

    def rows(self, which):
        if which == 0:
            return self.low, self.parts[0]
        if which == 1:
            return self.low + self.parts[0], self.parts[1]
        return self.low, self.size

    def at(self, offset):
        return self.torus.along(self.axis, self.other, offset)

    def copy(self, which):
        start, size = self.rows(which)
        offset = (2, 2, 1, -1)[which]
        return pltpu.make_async_remote_copy(
            src_ref=(self.origin if which < 2 else self.sums).at[self.at(offset), pl.ds(start, size)],
            dst_ref=self.landing.at[pl.ds(self.slots[which], size)],
            send_sem=self.send.at[self.number, which],
            recv_sem=self.recv.at[self.number, which],
            device_id=self.torus.near(self.axis, (1, -1, 1, -1)[which]),
            device_id_type=MESH,
        )

    def add(self, which, offset):
        start, size = self.rows(which)
        block = self.at(offset)

        many = step_of(size)

        @pl.loop(0, size // many)
        def _(k):
            here = pl.ds(pl.multiple_of(start + k * many, 16), many)
            there = pl.ds(pl.multiple_of(self.slots[which] + k * many, 16), many)
            total = self.sums[block, here].astype(jnp.float32) + self.landing[there].astype(jnp.float32)
            self.sums[block, here] = total.astype(jnp.bfloat16)

    def first(self):
        self.copy(0).start()
        self.copy(1).start()

    def second(self):
        self.copy(0).wait_recv()
        self.add(0, 1)
        self.copy(2).start()
        self.copy(1).wait_recv()
        self.add(1, -1)
        self.copy(3).start()

    def third(self, put=None):
        self.copy(2).wait_recv()
        self.copy(3).wait_recv()
        block = self.at(0)

        many = step_of(self.size)

        @pl.loop(0, self.size // many)
        def _(k):
            here = pl.ds(pl.multiple_of(self.low + k * many, 16), many)
            left = pl.ds(pl.multiple_of(self.slots[2] + k * many, 16), many)
            right = pl.ds(pl.multiple_of(self.slots[3] + k * many, 16), many)
            total = (
                self.sums[block, here].astype(jnp.float32)
                + self.landing[left].astype(jnp.float32)
                + self.landing[right].astype(jnp.float32)
            )
            if put is None:
                self.sums[block, here] = total.astype(jnp.bfloat16)
            else:
                put(here, total)

    def drain(self):
        for which in range(4):
            self.copy(which).wait_send()


def moe_kernel(
    ffn, cot, own_cot, wr, w_gate, w_up, w_down,
    ret, mixed, own_gu, own_down,
    rows, sums, wgu, wd, held, pair, inner, dgu, mixing, back, cotv, before, chosen, gate_rows, grad_rows, stage,
    mate_rows, gu_sums, down_sums,
    ag_send, ag_recv, rs_send, rs_recv, w_sem, cot_sem, own_sem, stage_sem, mate_send, mate_recv, x_send, x_recv, credit,
):
    torus = Torus()
    place, place_of = everywhere()
    barrier = pltpu.get_barrier_semaphore()
    peers = [*torus.neighbours(), place_of("core", 1), place_of("x", 1), place_of("x", -1)]
    for device in peers:
        pl.semaphore_signal(barrier, inc=1, device_id=device, device_id_type=MESH)

    weights = [
        pltpu.make_async_copy(w_gate, wgu.at[:, :, pl.ds(0, 512)], w_sem.at[0]),
        pltpu.make_async_copy(w_up, wgu.at[:, :, pl.ds(512, 512)], w_sem.at[1]),
        pltpu.make_async_copy(w_down, wd, w_sem.at[2]),
    ]
    for copy in weights:
        copy.start()

    def source_of(g, j):
        of_g, of_j = chooses(g // 2), chooses(g % 2 * 2 + j)
        offsets = []
        for axis in range(2):
            table = [differences([at[axis] for at in line]) for line in ARRIVALS]
            table = [differences(column) for column in zip(*table)]
            offsets.append(sum(table[a][b] * of_g[a] * of_j[b] for a in range(4) for b in range(4) if table[a][b]))
        return torus.block(*offsets)

    def slot_rows(g, j, start, count):
        return pl.ds(pl.multiple_of((g % 2 * 2 + j) * SENT + start, 16), count)

    def cot_copy(g, j):
        at = pl.multiple_of(source_of(g, j) * SENT, 16)
        return pltpu.make_async_copy(cot.at[pl.ds(at, SENT)], cotv.at[slot_rows(g, j, 0, SENT)], cot_sem.at[g % 2 * 2 + j])

    for j in range(2):
        cot_copy(0, j).start()
    first_row = torus.expert * BOTH
    own_copy = pltpu.make_async_copy(
        own_cot.at[pl.ds(ROWS - LEFT, LEFT)], rows.at[pl.ds(pl.multiple_of(first_row + ROWS, 16), LEFT)], own_sem
    )
    own_copy.start()
    rows[pl.ds(pl.multiple_of(first_row, 16), ROWS)] = ffn[...]
    own_copy.wait()
    pl.semaphore_wait(barrier, len(peers))

    def gather(number, axis, other, low, first, second):
        return Gather(torus, rows, ag_send, ag_recv, number, axis, other, low, first, second, BOTH)

    a_first = gather(0, "y", 0, 0, 96, 80)
    b_first = gather(1, "z", 0, 176, 80, 80)
    a_second = {d: gather(2 + d % RING, "z", d, 0, 96, 80) for d in (0, 1, -1, 2)}
    b_second = {d: gather(6 + d % RING, "y", d, 176, 80, 80) for d in (0, 1, -1, 2)}
    gathers = [a_first, b_first, *a_second.values(), *b_second.values()]

    a_first.first()
    b_first.first()
    b_second[0].first()
    a_second[0].first()
    a_first.second()
    b_first.second()
    b_second[0].second()
    a_second[0].second()
    for d in (1, -1):
        b_second[d].first()
        a_second[d].first()
    for copy in weights:
        copy.wait()

    earlier = lax.broadcasted_iota(jnp.int32, (ROWS, ROWS), 0) < lax.broadcasted_iota(jnp.int32, (ROWS, ROWS), 1)
    before[...] = jnp.where(earlier, 1.0, 0.0).astype(jnp.bfloat16)
    slot_at = lax.broadcasted_iota(jnp.int32, (CAP, ROWS), 0).astype(jnp.float32)

    def stage_copy(slot, target):
        return pltpu.make_async_copy(stage.at[slot], target, stage_sem.at[slot])

    expert_rows = lax.broadcasted_iota(jnp.int32, (EXPERTS, ROWS), 0)
    order = (2, 1, -1, 0)
    a_lead = {
        d: Scatter(torus, sums, rows, rs_send, rs_recv, n, n * 384, "z", d, 0, 64, 64) for n, d in enumerate(order)
    }
    b_lead = {
        d: Scatter(torus, sums, rows, rs_send, rs_recv, 4 + n, 1920 + n * 432, "y", d, 128, 80, 64)
        for n, d in enumerate(order)
    }
    a_last = Scatter(torus, sums, rows, rs_send, rs_recv, 8, 4 * 384, "y", 0, 0, 64, 64)
    b_last = Scatter(torus, sums, rows, rs_send, rs_recv, 9, 1920 + 4 * 432, "z", 0, 128, 80, 64)

    @pl.loop(0, 8)
    def _(g):
        @pl.when(g == 2)
        def _():
            a_first.third()
            b_first.third()
            b_second[2].first()
            a_second[2].first()
            b_second[0].third()
            a_second[0].third()
            for d in (1, -1):
                b_second[d].second()
                a_second[d].second()

        @pl.when(g == 4)
        def _():
            b_second[2].second()
            a_second[2].second()
            b_second[1].third()

        @pl.when(g == 6)
        def _():
            b_second[-1].third()
            a_second[1].third()

        @pl.when(g == 7)
        def _():
            a_second[-1].third()
            a_second[2].third()
            b_second[2].third()

        @pl.when(g < 7)
        def _():
            for j in range(2):
                cot_copy(g + 1, j).start()

        for j in range(2):
            cot_copy(g, j).wait()

        @pl.loop(0, 2)
        def _(j):
            source = source_of(g, j)
            block = rows[pl.ds(pl.multiple_of(source * BOTH, 16), ROWS)]
            laid = cotv[slot_rows(g, j, 0, EXTRA)].astype(jnp.float32)
            member = jnp.concatenate([laid[:8, q * ROWS : (q + 1) * ROWS] for q in range(4)], axis=0)
            named = member > 0.5
            slots = dot_nn(member.astype(jnp.bfloat16), before[...])
            slots = jnp.where(named, slots, -1.0)
            logits = jnp.where(named, dot_nt(wr[...], block), -1e30)
            weight = jnp.where(named, jnp.exp(logits - jnp.max(logits, axis=0, keepdims=True)), 0.0)
            gates = weight / jnp.sum(weight, axis=0, keepdims=True)
            picked = []
            for e in range(2):
                own = jnp.sum(
                    jnp.where(expert_rows == torus.expert * 2 + e, slots, 0.0), axis=0, keepdims=True
                )
                picked.append(jnp.where(slot_at == own, 1.0, 0.0))
            both = jnp.concatenate(picked, axis=0).astype(jnp.bfloat16)
            chosen[j] = both
            grad_block = jnp.concatenate(
                [
                    cotv[slot_rows(g, j, EXTRA, SENT - EXTRA)],
                    rows[pl.ds(pl.multiple_of(source * BOTH + ROWS, 16), LEFT)],
                ],
                axis=0,
            )
            took = dot_nn(both, jnp.concatenate([block, grad_block], axis=1)).astype(jnp.bfloat16)
            here = pl.ds(pl.multiple_of(j * CAP, 16), CAP)
            there = pl.ds(pl.multiple_of(g * GROUP + j * CAP, 16), CAP)
            for e in range(2):
                own = jnp.sum(
                    jnp.where(expert_rows == torus.expert * 2 + e, gates, 0.0), axis=0, keepdims=True
                )
                of_rows = jnp.sum(picked[e] * own, axis=1, keepdims=True)
                gate_rows[e, here] = jnp.broadcast_to(of_rows, (CAP, 128))
                held[e, there] = took[e * CAP : (e + 1) * CAP, :1024]
                mixing[e, here] = took[e * CAP : (e + 1) * CAP, 1024:]

        @pl.when(g == 7)
        def _():
            for one in gathers:
                one.drain()
            for device in peers:
                pl.semaphore_signal(credit, inc=1, device_id=device, device_id_type=MESH)
            pl.semaphore_wait(credit, len(peers))
            b_lead[0].first()
            a_lead[0].first()

        @pl.loop(0, 2)
        def _(e):
            there = pl.ds(pl.multiple_of(g * GROUP, 16), GROUP)
            both = dot_nn(held[e, there], wgu[e])
            gate, up = both[:, :512], both[:, 512:]
            sig = jax.nn.sigmoid(gate)
            silu = gate * sig
            act = (silu * up).astype(jnp.bfloat16)
            inner[e, there] = act
            out = dot_nn(act, wd[e]).astype(jnp.bfloat16).astype(jnp.float32)
            grad = mixing[e].astype(jnp.float32)
            weight = gate_rows[e][:, :1]
            grad_rows[e] = jnp.broadcast_to(jnp.sum(grad * out, axis=1, keepdims=True), (GROUP, 128))
            pair[e, there] = (weight * grad).astype(jnp.bfloat16)
            mixing[e] = (weight * out).astype(jnp.bfloat16)
            inner_grad = dot_nt(pair[e, there], wd[e])
            dgu[e, there, :512] = (inner_grad * up * sig * (1.0 + gate * (1.0 - sig))).astype(jnp.bfloat16)
            dgu[e, there, 512:] = (inner_grad * silu).astype(jnp.bfloat16)
            back[e] = dot_nt(dgu[e, there], wgu[e]).astype(jnp.bfloat16)

        @pl.loop(0, 2)
        def _(j):
            source = source_of(g, j)
            both = chosen[j]
            picked = both.astype(jnp.float32)
            here = pl.ds(pl.multiple_of(j * CAP, 16), CAP)
            compact = jnp.concatenate(
                [jnp.concatenate([back[e, here], mixing[e, here]], axis=1) for e in range(2)], axis=0
            )
            spread = dot_tn(both, compact).astype(jnp.bfloat16)
            sums[source, pl.ds(EXTRA, ROWS)] = spread[:, :1024]
            grads = jnp.zeros((EXPERTS, ROWS), jnp.float32)
            for e in range(2):
                own = jnp.sum(
                    picked[e * CAP : (e + 1) * CAP] * grad_rows[e, here][:, :1], axis=0, keepdims=True
                )
                grads = grads + jnp.where(expert_rows == torus.expert * 2 + e, own, 0.0)
            laid = jnp.concatenate([grads[8 * q : 8 * q + 8] for q in range(4)], axis=1)
            sums[source, pl.ds(0, EXTRA)] = jnp.concatenate([laid, jnp.zeros_like(laid)], axis=0).astype(
                jnp.bfloat16
            )
            slot = j

            @pl.when(g > 0)
            def _():
                stage_copy(slot, mixed.at[source]).wait()

            stage[slot] = spread[:, 1024:]
            stage_copy(slot, mixed.at[source]).start()

    def chunk(e, k):
        if k < 4:
            return dot_tn(held[e, :, k * 256 : (k + 1) * 256], dgu[e]).astype(jnp.bfloat16)
        return dot_tn(inner[e, :, (k - 4) * 256 : (k - 3) * 256], pair[e]).astype(jnp.bfloat16)

    def mate_copy(k):
        return pltpu.make_async_remote_copy(
            src_ref=stage.at[k % 2],
            dst_ref=mate_rows.at[pl.ds(k * 256, 256)],
            send_sem=mate_send.at[k],
            recv_sem=mate_recv.at[k],
            device_id=place_of("core", 1),
            device_id_type=MESH,
        )

    line = Line(place, place_of)
    rings = [
        Scatter(line, gu_sums, rows, x_send, x_recv, 0, 4080, "x", 0, 0, 128, 128),
        Scatter(line, down_sums, rows, x_send, x_recv, 1, 4848, "x", 0, 0, 64, 64),
    ]

    for d in (2, 1, -1):
        b_lead[d].first()
        a_lead[d].first()
    b_lead[0].second()
    a_lead[0].second()
    for k in range(6):
        if k < 2:
            stage_copy(k, mixed.at[0]).wait()
        else:
            mate_copy(k - 2).wait_send()
        stage[k % 2] = chunk(1 - place["core"], k)
        mate_copy(k).start()
        own = chunk(place["core"], k)
        if k < 4:
            gu_sums[k] = own
        else:
            down_sums[2 * k - 8] = own[:128]
            down_sums[2 * k - 7] = own[128:]
    for d in (2, 1, -1):
        b_lead[d].second()
        a_lead[d].second()
    for k in range(6):
        mate_copy(k).wait_recv()

        @pl.loop(0, 4)
        def _(n):
            other = mate_rows[pl.ds(pl.multiple_of(k * 256 + n * 64, 64), 64)].astype(jnp.float32)
            if k < 4:
                at = (k, pl.ds(pl.multiple_of(n * 64, 64), 64))
                gu_sums[at] = (gu_sums[at].astype(jnp.float32) + other).astype(jnp.bfloat16)
            else:
                at = (2 * k - 8 + n // 2, pl.ds(pl.multiple_of(n % 2 * 64, 64), 64))
                down_sums[at] = (down_sums[at].astype(jnp.float32) + other).astype(jnp.bfloat16)

    for one in rings:
        one.first()
    for one in rings:
        one.second()
    for d in order:
        b_lead[d].third()
        a_lead[d].third()
        if d == 2:
            b_last.first()
            a_last.first()
    b_last.second()
    a_last.second()

    def put(at, total):
        ret[at] = total

    b_last.third(put)
    a_last.third(put)

    def put_gu(at, total):
        own_gu[at] = total.astype(jnp.bfloat16)

    def put_down(at, total):
        own_down[at] = total.astype(jnp.bfloat16)

    rings[0].third(put_gu)
    rings[1].third(put_down)
    for one in [*a_lead.values(), *b_lead.values(), a_last, b_last, *rings]:
        one.drain()
    for k in (4, 5):
        mate_copy(k).wait_send()


def moe(ffn_in, cot_all, own_cot, router_rows, w_gate, w_up, w_down):
    vmem, hbm = pl.BlockSpec(memory_space=pltpu.VMEM), pl.BlockSpec(memory_space=pl.ANY)
    low, total = jnp.bfloat16, 8 * GROUP
    return pl.pallas_call(
        moe_kernel,
        name="moe",
        out_shape=(
            jax.ShapeDtypeStruct((FULL, 1024), jnp.float32),
            jax.ShapeDtypeStruct((16, ROWS, 1024), low),
            jax.ShapeDtypeStruct((256, 1024), low),
            jax.ShapeDtypeStruct((128, 1024), low),
        ),
        in_specs=[vmem, hbm, hbm, vmem, hbm, hbm, hbm],
        out_specs=(vmem, hbm, vmem, vmem),
        scratch_shapes=[
            pltpu.VMEM((16 * BOTH, 1024), low),
            pltpu.VMEM((16, FULL, 1024), low),
            pltpu.VMEM((2, 1024, 1024), low),
            pltpu.VMEM((2, 512, 1024), low),
            pltpu.VMEM((2, total, 1024), low),
            pltpu.VMEM((2, total, 1024), low),
            pltpu.VMEM((2, total, 512), low),
            pltpu.VMEM((2, total, 1024), low),
            pltpu.VMEM((2, GROUP, 1024), low),
            pltpu.VMEM((2, GROUP, 1024), low),
            pltpu.VMEM((4 * SENT, 1024), low),
            pltpu.VMEM((ROWS, ROWS), low),
            pltpu.VMEM((2, 2 * CAP, ROWS), low),
            pltpu.VMEM((2, GROUP, 128), jnp.float32),
            pltpu.VMEM((2, GROUP, 128), jnp.float32),
            pltpu.VMEM((2, ROWS, 1024), low),
            pltpu.VMEM((6 * 256, 1024), low),
            pltpu.VMEM((4, 256, 1024), low),
            pltpu.VMEM((4, 128, 1024), low),
            pltpu.SemaphoreType.DMA((10, 4)),
            pltpu.SemaphoreType.DMA((10, 4)),
            pltpu.SemaphoreType.DMA((10, 4)),
            pltpu.SemaphoreType.DMA((10, 4)),
            pltpu.SemaphoreType.DMA((3,)),
            pltpu.SemaphoreType.DMA((4,)),
            pltpu.SemaphoreType.DMA,
            pltpu.SemaphoreType.DMA((2,)),
            pltpu.SemaphoreType.DMA((6,)),
            pltpu.SemaphoreType.DMA((6,)),
            pltpu.SemaphoreType.DMA((2, 4)),
            pltpu.SemaphoreType.DMA((2, 4)),
            pltpu.SemaphoreType.REGULAR,
        ],
        compiler_params=pltpu.CompilerParams(
            collective_id=1, has_side_effects=True, vmem_limit_bytes=63 * 2**20
        ),
        cost_estimate=pl.CostEstimate(flops=50 * 10**9, bytes_accessed=40 * 10**6, transcendentals=2 * 10**6),
    )(ffn_in, cot_all, own_cot, router_rows, w_gate, w_up, w_down)


def everywhere():
    dp, expert = lax.axis_index("dp"), lax.axis_index("expert")
    here = {"x": dp // 2, "core": dp % 2, "z": expert // RING, "y": expert % RING}

    def device(axis, step):
        there = dict(here)
        size = 2 if axis == "core" else RING
        there[axis] = (here[axis] + step + size) % size
        return (there["x"] * 2 + there["core"], there["z"] * RING + there["y"])

    return here, device


def rms_scale(values):
    return lax.rsqrt(jnp.mean(values * values, axis=-1, keepdims=True) + epsilon)


def as_row(gain):
    return gain[...].astype(jnp.float32).reshape(1, -1)


def turned_rows(values, cosine, sine):
    front, back = values[: HEAD_DIM // 2], values[HEAD_DIM // 2 :]
    return jnp.concatenate([front * cosine - back * sine, back * cosine + front * sine], axis=0)


def kv_order(here, step):
    turn = step // 2
    return (turn % 2) * (3 - turn // 2) + (1 - turn % 2) * (turn // 2)


class Keys:
    def __init__(self, here, device, blocks, send, recv):
        self.here, self.device, self.blocks, self.send, self.recv = here, device, blocks, send, recv
        self.lines = blocks.shape[1]

    def copy(self, which):
        half = self.lines // 2
        offset, start, size, axis, step = (
            (0, 0, self.lines, "core", 1),
            (0, 0, self.lines, "x", 1),
            (0, 0, self.lines, "x", -1),
            (-1, 0, half, "x", 1),
            (1, half, half, "x", -1),
            (-1, 0, self.lines, "core", 1),
            (1, 0, self.lines, "core", 1),
            (2, 0, self.lines, "core", 1),
        )[which]
        block = (self.here["x"] + offset + RING) % RING * 2 + self.here["core"]
        part = self.blocks.at[block, pl.ds(start, size)]
        return pltpu.make_async_remote_copy(
            src_ref=part,
            dst_ref=part,
            send_sem=self.send.at[which],
            recv_sem=self.recv.at[which],
            device_id=self.device(axis, step),
            device_id_type=MESH,
        )

    def start(self, *which):
        for one in which:
            self.copy(one).start()

    def arrive(self, *which):
        for one in which:
            self.copy(one).wait_recv()

    def drain(self):
        for one in range(8):
            self.copy(one).wait_send()


def forward_kernel(
    tokens, cot, routes_t, length, cosine, sine, attn_gain, query_gain, key_gain, ffn_gain,
    w_query, w_key, w_value, w_output,
    ffn_in, hidden, mixed_t, queries, log_total, normed, query_raw, key_raw, kv_all, cot_all,
    wq, wk, wv, wo, kv, turned, most, total, mixed, packed,
    ag_send, ag_recv, kv_send, kv_recv, w_sem, kv_sem, own_sem,
):
    torus = Torus()
    here, device = everywhere()
    me = here["x"] * 2 + here["core"]
    barrier = pltpu.get_barrier_semaphore()
    peers = [*torus.neighbours(), device("core", 1), device("x", 1), device("x", -1)]
    for peer in peers:
        pl.semaphore_signal(barrier, inc=1, device_id=peer, device_id_type=MESH)
    loads = [
        pltpu.make_async_copy(source, target, w_sem.at[n])
        for n, (source, target) in enumerate(((w_query, wq), (w_key, wk), (w_value, wv), (w_output, wo)))
    ]
    for load in loads:
        load.start()

    expert_rows = lax.broadcasted_iota(jnp.int32, (EXPERTS, ROWS), 0)
    member = jnp.zeros((EXPERTS, ROWS), jnp.float32)
    for k in range(TOPK):
        member = member + jnp.where(expert_rows == routes_t[pl.ds(k, 1), :], 1.0, 0.0)
    laid = jnp.concatenate([member[8 * q : 8 * q + 8] for q in range(4)], axis=1)
    packed[...] = jnp.concatenate([laid, jnp.zeros_like(laid)], axis=0).astype(jnp.bfloat16)
    first_row = pl.multiple_of(torus.expert * SENT, 16)
    owns = [
        pltpu.make_async_copy(packed, cot_all.at[pl.ds(first_row, EXTRA)], own_sem.at[0]),
        pltpu.make_async_copy(
            cot.at[pl.ds(0, SENT - EXTRA)],
            cot_all.at[pl.ds(pl.multiple_of(first_row + EXTRA, 16), SENT - EXTRA)],
            own_sem.at[1],
        ),
    ]
    for copy in owns:
        copy.start()
    for copy in owns:
        copy.wait()
    pl.semaphore_wait(barrier, len(peers))

    def gather(number, axis, other, low, first, second):
        return Gather(torus, cot_all, ag_send, ag_recv, number, axis, other, low, first, second, SENT)

    a_first = gather(0, "y", 0, 0, 48, 48)
    b_first = gather(1, "z", 0, 96, 48, 48)
    a_second = {d: gather(2 + d % RING, "z", d, 0, 48, 48) for d in (0, 1, -1, 2)}
    b_second = {d: gather(6 + d % RING, "y", d, 96, 48, 48) for d in (0, 1, -1, 2)}
    gathers = [a_first, b_first, *a_second.values(), *b_second.values()]
    a_first.first()
    b_first.first()
    b_second[0].first()
    a_second[0].first()

    @pl.loop(0, 4)
    def _(n):
        at = pl.ds(pl.multiple_of(n * 64, 64), 64)
        rows = tokens[at].astype(jnp.float32)
        normed[at] = (rows * rms_scale(rows) * as_row(attn_gain)).astype(jnp.bfloat16)

    for load in loads:
        load.wait()

    keys = Keys(here, device, kv, kv_send, kv_recv)
    key_raw[...] = dot_nn(normed[...], wk[...])
    scaled = key_raw[...]
    scaled = (scaled * rms_scale(scaled) * as_row(key_gain)).T
    for j in range(KV_HEADS):
        head = turned_rows(scaled[j * 64 : j * 64 + 64], cosine[...], sine[...])
        kv[me, pl.ds(j * 64, 64)] = head.astype(jnp.bfloat16)
    kv[me, pl.ds(512, 512)] = dot_nn(normed[...], wv[...]).T.astype(jnp.bfloat16)
    keys.start(0, 1, 2)
    query_raw[...] = dot_nn(normed[...], wq[...])
    scaled = query_raw[...]
    turned[...] = (scaled * rms_scale(scaled) * as_row(query_gain)).T

    for j in range(KV_HEADS):
        for r in range(2):
            head = turned[j * 128 + r * 64 : j * 128 + r * 64 + 64]
            head = turned_rows(head, cosine[...], sine[...])
            queries[j, :, r * ROWS : (r + 1) * ROWS] = (head * HEAD_DIM**-0.5).astype(jnp.bfloat16)

    a_first.second()
    b_first.second()
    for d in (1, -1):
        b_second[d].first()
        a_second[d].first()

    key_at = lax.broadcasted_iota(jnp.int32, (ROWS, 2 * ROWS), 0)
    query_at = lax.broadcasted_iota(jnp.int32, (ROWS, 2 * ROWS), 1) % ROWS
    valid = (key_at <= query_at) & (key_at + me * ROWS < length[...])

    def heads_of(block):
        keys_here = [kv[block, j * 64 : j * 64 + 64] for j in range(KV_HEADS)]
        values_here = [kv[block, 512 + j * 64 : 576 + j * 64] for j in range(KV_HEADS)]
        return keys_here, values_here

    keys_here, values_here = heads_of(me)
    scores = [jnp.where(valid, dot_tn(keys_here[j], queries[j]), -1e30) for j in range(KV_HEADS)]
    tops = [jnp.max(one, axis=0, keepdims=True) for one in scores]
    probs = [jnp.exp(one - top) for one, top in zip(scores, tops)]
    parts = [dot_nn(one, prob.astype(jnp.bfloat16)) for one, prob in zip(values_here, probs)]
    for j in range(KV_HEADS):
        most[j] = tops[j]
        total[j] = jnp.sum(probs[j], axis=0, keepdims=True)
        mixed[j] = parts[j]

    @pl.loop(1, 8)
    def _(step):
        @pl.when(step == 1)
        def _():
            a_first.third()
            b_first.third()
            b_second[2].first()
            a_second[2].first()
            keys.arrive(0)

        @pl.when(step == 2)
        def _():
            keys.arrive(1)
            keys.start(3, 5)
            keys.arrive(2)
            keys.start(4, 6)
            b_second[0].second()
            a_second[0].second()

        @pl.when(step == 3)
        def _():
            keys.arrive(5)
            for d in (1, -1):
                b_second[d].second()
                a_second[d].second()

        @pl.when(step == 5)
        def _():
            keys.arrive(3, 4)
            keys.start(7)
            keys.arrive(6)
            b_second[2].second()
            a_second[2].second()

        @pl.when(step == 7)
        def _():
            keys.arrive(7)

        block = (here["x"] + kv_order(here, step) + RING) % RING * 2 + (here["core"] + step) % 2

        @pl.when(block < me)
        def _():
            keys_here, values_here = heads_of(block)
            before = [most[j] for j in range(KV_HEADS)]
            shares = [total[j] for j in range(KV_HEADS)]
            sums = [mixed[j] for j in range(KV_HEADS)]
            scores = [dot_tn(keys_here[j], queries[j]) for j in range(KV_HEADS)]
            tops = [jnp.maximum(old, jnp.max(one, axis=0, keepdims=True)) for old, one in zip(before, scores)]
            probs = [jnp.exp(one - top) for one, top in zip(scores, tops)]
            less = [jnp.exp(old - top) for old, top in zip(before, tops)]
            parts = [dot_nn(one, prob.astype(jnp.bfloat16)) for one, prob in zip(values_here, probs)]
            for j in range(KV_HEADS):
                most[j] = tops[j]
                total[j] = shares[j] * less[j] + jnp.sum(probs[j], axis=0, keepdims=True)
                mixed[j] = sums[j] * less[j] + parts[j]

    save = pltpu.make_async_copy(kv, kv_all, kv_sem)
    save.start()

    for j in range(KV_HEADS):
        share = total[j]
        log_total[j] = most[j] + jnp.log(share)
        head = (mixed[j] * (1.0 / share)).astype(jnp.bfloat16)
        for r in range(2):
            mixed_t[j * 128 + r * 64 : j * 128 + r * 64 + 64, :] = head[:, r * ROWS : (r + 1) * ROWS]

    hidden[...] = dot_tn(mixed_t[...], wo[...])

    @pl.loop(0, 4)
    def _(n):
        at = pl.ds(pl.multiple_of(n * 64, 64), 64)
        rows = hidden[at] + tokens[at].astype(jnp.float32)
        hidden[at] = rows
        ffn_in[at] = (rows * rms_scale(rows) * as_row(ffn_gain)).astype(jnp.bfloat16)

    for d in (0, 1, -1, 2):
        a_second[d].third()
        b_second[d].third()
    save.wait()
    keys.drain()
    for one in gathers:
        one.drain()


def forward(tokens, cot, routes_t, length, cosine, sine, gains, weights):
    vmem, hbm = pl.BlockSpec(memory_space=pltpu.VMEM), pl.BlockSpec(memory_space=pl.ANY)
    low, wide = jnp.bfloat16, jnp.float32
    shape = jax.ShapeDtypeStruct
    return pl.pallas_call(
        forward_kernel,
        name="forward",
        out_shape=(
            shape((ROWS, 1024), low),
            shape((ROWS, 1024), wide),
            shape((1024, ROWS), low),
            shape((KV_HEADS, HEAD_DIM, 2 * ROWS), low),
            shape((KV_HEADS, 1, 2 * ROWS), wide),
            shape((ROWS, 1024), low),
            shape((ROWS, 1024), wide),
            shape((ROWS, 512), wide),
            shape((8, 1024, ROWS), low),
            shape((16 * SENT, 1024), low),
        ),
        in_specs=[vmem] * 10 + [hbm] * 4,
        out_specs=(vmem,) * 8 + (hbm, hbm),
        scratch_shapes=[
            pltpu.VMEM((1024, 1024), low),
            pltpu.VMEM((1024, 512), low),
            pltpu.VMEM((1024, 512), low),
            pltpu.VMEM((1024, 1024), low),
            pltpu.VMEM((8, 1024, ROWS), low),
            pltpu.VMEM((1024, ROWS), wide),
            pltpu.VMEM((KV_HEADS, 1, 2 * ROWS), wide),
            pltpu.VMEM((KV_HEADS, 1, 2 * ROWS), wide),
            pltpu.VMEM((KV_HEADS, HEAD_DIM, 2 * ROWS), wide),
            pltpu.VMEM((EXTRA, 1024), low),
            pltpu.SemaphoreType.DMA((10, 4)),
            pltpu.SemaphoreType.DMA((10, 4)),
            pltpu.SemaphoreType.DMA((8,)),
            pltpu.SemaphoreType.DMA((8,)),
            pltpu.SemaphoreType.DMA((4,)),
            pltpu.SemaphoreType.DMA,
            pltpu.SemaphoreType.DMA((2,)),
        ],
        compiler_params=pltpu.CompilerParams(
            collective_id=3, has_side_effects=True, vmem_limit_bytes=56 * 2**20
        ),
    )(tokens, cot, routes_t, length, cosine, sine, *gains, *weights)


ORDERS = (("x", "y", "z"), ("y", "z", "x"), ("z", "x", "y"))
STREAMS = {2048: ((0, 768), (768, 768), (1536, 512)), 2304: ((0, 768), (768, 768), (1536, 768))}


class Total:
    def __init__(self, here, device, buffer, shift, final, landing, work, send, recv, number, stream, half, begin=0):
        self.here, self.device, self.buffer, self.shift, self.final = here, device, buffer, shift, final
        self.landing, self.work = landing, work
        self.send, self.recv, self.number, self.order = send, recv, number, ORDERS[(stream + number // 3) % 3]
        self.half = half
        self.start, self.rows = STREAMS[half][stream]
        self.stages = range(begin, 7)
        r, own = self.rows, 0 if begin else self.rows
        first = self.start * 9 // 8 + (0 if begin else self.start)
        self.lands = (first, first + own, first + own + 3 * (r // 4), first + own + 3 * (r // 4) + 3 * (r // 16))

    def own(self):
        return self.here["core"] * self.half + self.start

    def copy(self, which, source, target, axis, step):
        return pltpu.make_async_remote_copy(
            src_ref=source,
            dst_ref=target,
            send_sem=self.send.at[self.number, which],
            recv_sem=self.recv.at[self.number, which],
            device_id=self.device(axis, step),
            device_id_type=MESH,
        )

    def held(self, at, size):
        return self.buffer.at[pl.ds(pl.multiple_of(at + self.shift, 16), size)]

    def ready(self, at, size):
        return self.final.at[pl.ds(pl.multiple_of(at, 16), size)]

    def land(self, stage, n, size):
        return self.landing.at[pl.ds(self.lands[stage] + n * size, size)]

    def copies(self, stage):
        r, own = self.rows, self.own()
        a, b, c = self.order
        ia, ib = self.here[a], self.here[b]
        second = own + ia * (r // 4)
        third = second + ib * (r // 16)
        if stage == 0:
            there = (1 - self.here["core"]) * self.half + self.start
            return [self.copy(0, self.held(there, r), self.land(0, 0, r), "core", 1)]
        if stage == 6:
            return [self.copy(16, self.ready(own, r), self.ready(own, r), "core", 1)]
        found = []
        for d in (1, 2, 3):
            if stage == 1:
                source, target, axis = self.held(own + (ia + d) % RING * (r // 4), r // 4), self.land(1, d - 1, r // 4), a
            elif stage == 2:
                source = self.held(second + (ib + d) % RING * (r // 16), r // 16)
                target, axis = self.land(2, d - 1, r // 16), b
            elif stage == 3:
                source = self.work.at[self.number, pl.ds(0, r // 16)]
                target, axis = self.land(3, d - 1, r // 16), c
            elif stage == 4:
                source, target, axis = self.ready(third, r // 16), self.ready(third, r // 16), b
            else:
                source, target, axis = self.ready(second, r // 4), self.ready(second, r // 4), a
            found.append(self.copy(1 + (stage - 1) * 3 + d - 1, source, target, axis, d))
        return found

    def begin(self, stage):
        for copy in self.copies(stage):
            copy.start()

    def add(self, stage, load, store, size, count):
        step = 64 if size % 64 == 0 else 16

        @pl.loop(0, size // step)
        def _(k):
            at = k * step
            total = load(at, step).astype(jnp.float32)
            for n in range(count):
                land = pl.ds(pl.multiple_of(self.lands[stage] + n * size + at, 16), step)
                total = total + self.landing[land].astype(jnp.float32)
            store(at, step, total.astype(jnp.bfloat16))

    def finish(self, stage):
        for copy in self.copies(stage):
            copy.wait_recv()
        if stage > 3:
            return
        r, own = self.rows, self.own()
        a, b, _ = self.order
        second = own + self.here[a] * (r // 4)
        third = second + self.here[b] * (r // 16)
        first = (own, second, third, third)[stage] + self.shift

        def in_place(at, step, *value):
            lines = pl.ds(pl.multiple_of(first + at, 16), step)
            if not value:
                return self.buffer[lines]
            self.buffer[lines] = value[0]

        def in_work(at, step, *value):
            lines = pl.ds(pl.multiple_of(at, 16), step)
            if not value:
                return self.work[self.number, lines]
            self.work[self.number, lines] = value[0]

        def in_final(at, step, value):
            self.final[pl.ds(pl.multiple_of(third + at, 16), step)] = value

        if stage == 0:
            self.add(0, in_place, in_place, r, 1)
        elif stage == 1:
            self.add(1, in_place, in_place, r // 4, 3)
        elif stage == 2:
            self.add(2, in_place, in_work, r // 16, 3)
        else:
            self.add(3, in_work, in_final, r // 16, 3)

    def drain(self):
        for stage in self.stages:
            for copy in self.copies(stage):
                copy.wait_send()


class Small:
    STAGES = (("core", (1,)), ("x", (1, 2, 3)), ("y", (1, 2, 3)), ("z", (1, 2, 3)))

    def __init__(self, device, value, landing, send, recv):
        self.device, self.value, self.landing, self.send, self.recv = device, value, landing, send, recv

    def copies(self, stage):
        axis, steps = self.STAGES[stage]
        first = sum(len(s) for _, s in self.STAGES[:stage])
        return [
            pltpu.make_async_remote_copy(
                src_ref=self.value.at[stage],
                dst_ref=self.landing.at[first + n],
                send_sem=self.send.at[first + n],
                recv_sem=self.recv.at[first + n],
                device_id=self.device(axis, step),
                device_id_type=MESH,
            )
            for n, step in enumerate(steps)
        ]

    def begin(self, stage):
        for copy in self.copies(stage):
            copy.start()

    def finish(self, stage):
        for copy in self.copies(stage):
            copy.wait_recv()
        first = sum(len(s) for _, s in self.STAGES[:stage])
        total = self.value[stage]
        for n in range(len(self.STAGES[stage][1])):
            total = total + self.landing[first + n]
        self.value[stage + 1] = total

    def drain(self):
        for stage in range(4):
            for copy in self.copies(stage):
                copy.wait_send()


class Line:
    def __init__(self, here, device):
        self.here, self.device = here, device

    def along(self, axis, other, step):
        return (self.here["x"] + step + RING) % RING

    def near(self, axis, step):
        return self.device("x", step)


def rms_back(values, gain, grad):
    scale = rms_scale(values)
    lifted = gain * grad
    inner = jnp.mean(values * lifted, axis=-1, keepdims=True)
    return scale * lifted - values * (scale * scale * scale) * inner, jnp.sum(
        grad * values * scale, axis=0, keepdims=True
    )


def turned_back(grads, cosine, sine):
    front, back = grads[: HEAD_DIM // 2], grads[HEAD_DIM // 2 :]
    return jnp.concatenate([front * cosine + back * sine, back * cosine - front * sine], axis=0)


def backward_kernel(
    hidden, ffn_in, cot, tokens, normed, key_raw, mixed_t, queries, log_total,
    routes_t, length, cosine, sine, attn_gain, query_gain, key_gain, ffn_gain, router_rows, own_gu, own_down,
    returned_all, query_raw_all, mixed_parts, kv_all, w_query, w_key, w_value, w_output,
    mixed_out, token_grad, early_small, late_small, query_sum, key_sum, value_sum, output_sum, all_gu, all_down,
    sums, rows, returned, square, kv, hidden_grad, result, branch, grads, delta, query_grad, turned,
    for_mate, from_mate, kv_sums, kv_rows, key_value, normed_other, query_other, key_value_other,
    held, final_output, final_query, final_keys, land_output, land_query, land_keys, work, late_values, late_rows,
    rs_send, rs_recv, mate_send, mate_recv, kv_send, kv_recv, ar_send, ar_recv, small_send, small_recv, load_sem, out_sem, ex_send, ex_recv, pair_send, pair_recv,
):
    torus = Torus()
    here, device = everywhere()
    me = here["x"] * 2 + here["core"]
    barrier = pltpu.get_barrier_semaphore()
    peers = [device("core", 1)] + [device(axis, d) for axis in "xyz" for d in (1, 2, 3)]
    for peer in peers:
        pl.semaphore_signal(barrier, inc=1, device_id=peer, device_id_type=MESH)
    loads = [
        pltpu.make_async_copy(source, target, load_sem.at[n])
        for n, (source, target) in enumerate(
            ((returned_all, returned), (w_output, square), (mixed_parts, sums), (kv_all, kv))
        )
    ]
    for load in loads:
        load.start()
    owns = [
        pltpu.make_async_copy(own_gu, all_gu.at[me], load_sem.at[8]),
        pltpu.make_async_copy(own_down, all_down.at[me], load_sem.at[9]),
    ]
    for copy in owns:
        copy.start()
    order = (2, 1, -1, 0)
    leads = []
    for n, d in enumerate(order):
        leads.append(Scatter(torus, sums, rows, rs_send, rs_recv, n, n * 384, "z", d, 0, 64, 64, mixed_parts))
        leads.append(Scatter(torus, sums, rows, rs_send, rs_recv, 4 + n, (5 + n) * 384, "y", d, 128, 64, 64, mixed_parts))
    lasts = [
        Scatter(torus, sums, rows, rs_send, rs_recv, 8, 4 * 384, "y", 0, 0, 64, 64),
        Scatter(torus, sums, rows, rs_send, rs_recv, 9, 9 * 384, "z", 0, 128, 64, 64),
    ]
    ring = Scatter(Line(here, device), kv_sums, kv_rows, kv_send, kv_recv, 0, 0, "x", 0, 0, 512, 512)
    experts = [
        Keys(here, device, blocks, ex_send.at[n], ex_recv.at[n]) for n, blocks in enumerate((all_gu, all_down))
    ]
    for copy in owns:
        copy.wait()
    pl.semaphore_wait(barrier, len(peers))
    for one in leads:
        one.first()
    for one in experts:
        one.start(0, 1, 2)

    def to_other(number, source, target):
        return pltpu.make_async_remote_copy(
            src_ref=source,
            dst_ref=target,
            send_sem=pair_send.at[number],
            recv_sem=pair_recv.at[number],
            device_id=device("core", 1),
            device_id_type=MESH,
        )

    own_half = pl.ds(pl.multiple_of(here["core"] * 512, 512), 512)
    other_half = pl.ds(pl.multiple_of((1 - here["core"]) * 512, 512), 512)
    pairs = [
        to_other(0, normed, normed_other),
        to_other(1, branch.at[:, other_half], query_other),
        to_other(2, key_value.at[:, other_half], key_value_other),
    ]
    pairs[0].start()

    expert_rows = lax.broadcasted_iota(jnp.int32, (EXPERTS, ROWS), 0)
    member = jnp.zeros((EXPERTS, ROWS), jnp.float32)
    for k in range(TOPK):
        member = member + jnp.where(expert_rows == routes_t[pl.ds(k, 1), :], 1.0, 0.0)
    named = member > 0.5
    logits = jnp.where(named, dot_nt(router_rows[...], ffn_in[...]), -1e30)
    weight = jnp.where(named, jnp.exp(logits - jnp.max(logits, axis=0, keepdims=True)), 0.0)
    gates = weight / jnp.sum(weight, axis=0, keepdims=True)
    loads[0].wait()
    gate_grad = jnp.concatenate([returned[:8, q * ROWS : (q + 1) * ROWS] for q in range(4)], axis=0)
    logit_grad = (gates * (gate_grad - jnp.sum(gates * gate_grad, axis=0, keepdims=True))).astype(jnp.bfloat16)
    result[...] = dot_tn(logit_grad, router_rows[...])
    router_grad = dot_nn(logit_grad, ffn_in[...]).astype(jnp.bfloat16)
    for q in range(4):
        held[2048 + q * EXPERTS : 2048 + (q + 1) * EXPERTS] = router_grad[:, q * 256 : (q + 1) * 256]

    def ffn_part(n, gain_grad):
        at = pl.ds(pl.multiple_of(n * 64, 64), 64)
        grad = result[at] + returned[pl.ds(pl.multiple_of(n * 64 + EXTRA, 16), 64)]
        part, more = rms_back(hidden[at], as_row(ffn_gain), grad)
        part = part + cot[at].astype(jnp.float32)
        hidden_grad[at] = part
        branch[at] = part.astype(jnp.bfloat16)
        return gain_grad + more

    gain_grad = lax.fori_loop(0, 4, ffn_part, jnp.zeros((1, 1024), jnp.float32))
    gain_lines = [gain_grad[:, q * 256 : (q + 1) * 256] for q in range(4)] + [jnp.zeros((124, 256), jnp.float32)]
    held[2176:2304] = jnp.concatenate(gain_lines, axis=0).astype(jnp.bfloat16)
    held[4352:4608] = jnp.zeros((256, 256), jnp.bfloat16)

    loads[1].wait()
    turned[...] = dot_nt(square[...], branch[...])
    next_load = pltpu.make_async_copy(w_query, square, load_sem.at[6])
    next_load.start()
    query_raw = returned.at[pl.ds(0, ROWS)]
    raw_load = pltpu.make_async_copy(query_raw_all, query_raw, load_sem.at[7])
    raw_load.start()

    for j in range(KV_HEADS):
        for r in range(2):
            at = slice(j * 128 + r * 64, j * 128 + r * 64 + 64)
            low = turned[at].astype(jnp.bfloat16)
            grads[j, :, r * ROWS : (r + 1) * ROWS] = low
            delta[j, :, r * ROWS : (r + 1) * ROWS] = jnp.sum(
                low.astype(jnp.float32) * mixed_t[at].astype(jnp.float32), axis=0, keepdims=True
            )
        query_grad[j] = jnp.zeros((HEAD_DIM, 2 * ROWS), jnp.float32)

    @pl.loop(0, 4)
    def _(n):
        at = pl.ds(pl.multiple_of(n * 256, 256), 256)
        part = dot_nn(mixed_t[at], branch[...]).astype(jnp.bfloat16)
        for q in range(4):
            held[pl.ds(pl.multiple_of(q * 1024 + q // 2 * 256 + n * 256, 256), 256)] = part[:, q * 256 : (q + 1) * 256]

    loads[3].wait()

    def reduction(number, buffer, shift, final, land, half, begin):
        return [
            Total(here, device, buffer, shift, final, land, work, ar_send, ar_recv, 3 * number + s, s, half, begin)
            for s in range(3)
        ]

    early = reduction(0, held, 0, final_output, land_output, 2304, 0)
    of_query = reduction(1, kv, 0, final_query, land_query, 2048, 1)
    of_keys = reduction(2, kv, 4096, final_keys, land_keys, 2048, 1)
    late_few = Small(device, late_values, late_rows, small_send, small_recv)
    for one in early:
        one.begin(0)
    loads[2].wait()
    for one in leads:
        one.second()

    def onward(streams, stage):
        for one in streams:
            one.finish(stage)
            if stage < 6:
                one.begin(stage + 1)

    def write_out(number, final, first, target, at):
        block = final.at[pl.ds(first, 1024)]
        return pltpu.make_async_copy(block, target.at[:, pl.ds(at * 256, 256)], out_sem.at[number])

    outs = [write_out(q, final_output, q * 1024 + q // 2 * 256, output_sum, q) for q in range(4)]
    outs += [write_out(4 + q, final_query, q * 1024, query_sum, q) for q in range(4)]
    outs += [write_out(8 + q, final_keys, q * 1024, key_sum, q) for q in range(2)]
    outs += [write_out(10 + q, final_keys, (2 + q) * 1024, value_sum, q) for q in range(2)]

    def mate_copy(turn, at):
        return pltpu.make_async_remote_copy(
            src_ref=for_mate.at[turn % 2],
            dst_ref=from_mate.at[at],
            send_sem=mate_send.at[turn],
            recv_sem=mate_recv.at[turn],
            device_id=device("core", 1),
            device_id_type=MESH,
        )

    key_at = lax.broadcasted_iota(jnp.int32, (ROWS, 2 * ROWS), 0)
    query_at = lax.broadcasted_iota(jnp.int32, (ROWS, 2 * ROWS), 1) % ROWS
    valid = (key_at <= query_at) & (key_at + me * ROWS < length[...])

    def block_grads(block, target, at, masked):
        for group in range(2):
            heads = range(4 * group, 4 * group + 4)
            key_heads = [kv[pl.ds(pl.multiple_of(block * 1024 + j * 64, 64), 64)] for j in heads]
            value_heads = [kv[pl.ds(pl.multiple_of(block * 1024 + 512 + j * 64, 64), 64)] for j in heads]
            probs = [jnp.exp(dot_tn(one, queries[j]) - log_total[j]) for one, j in zip(key_heads, heads)]
            if masked:
                probs = [jnp.where(valid, one, 0.0) for one in probs]
            probs_grads = [dot_tn(one, grads[j]) for one, j in zip(value_heads, heads)]
            lows = [
                (one * (grad - delta[j])).astype(jnp.bfloat16) for one, grad, j in zip(probs, probs_grads, heads)
            ]
            key_parts = [dot_nt(queries[j], low).astype(jnp.bfloat16) for low, j in zip(lows, heads)]
            value_parts = [
                dot_nt(grads[j], one.astype(jnp.bfloat16)).astype(jnp.bfloat16) for one, j in zip(probs, heads)
            ]
            query_parts = [dot_nn(one, low) for one, low in zip(key_heads, lows)]
            for n, j in enumerate(heads):
                target[at, j * 64 : j * 64 + 64] = key_parts[n]
                target[at, 512 + j * 64 : 576 + j * 64] = value_parts[n]
                query_grad[j] += query_parts[n]

    def from_other(turn, at):
        mate_copy(turn, at).wait_recv()

        @pl.loop(0, 16)
        def _(n):
            lines = pl.ds(pl.multiple_of(n * 64, 64), 64)
            total = kv_sums[at, lines].astype(jnp.float32) + from_mate[at, lines].astype(jnp.float32)
            kv_sums[at, lines] = total.astype(jnp.bfloat16)

    def turn_x(turn):
        offset = (1 - turn % 2) * (2 + turn // 2) + (turn % 2) * (1 - turn // 2)
        return (here["x"] + offset + RING) % RING

    @pl.loop(0, 4)
    def _(turn):
        @pl.when(turn == 1)
        def _():
            for one in experts:
                one.arrive(1)
                one.start(3, 5)
                one.arrive(2)
                one.start(4, 6)

        @pl.when(turn == 2)
        def _():
            onward(early, 0)

        @pl.when(turn == 3)
        def _():
            onward(early, 1)

        at = turn_x(turn)
        other = at * 2 + 1 - here["core"]

        @pl.when(turn >= 2)
        def _():
            mate_copy(turn - 2, at).wait_send()

        @pl.when(other < me)
        def _():
            block_grads(other, for_mate, turn % 2, False)

        @pl.when(other >= me)
        def _():
            for_mate[turn % 2] = jnp.zeros((1024, ROWS), jnp.bfloat16)

        mate_copy(turn, at).start()

        own = at * 2 + here["core"]

        @pl.when(own < me)
        def _():
            block_grads(own, kv_sums, at, False)

        @pl.when(own > me)
        def _():
            kv_sums[at] = jnp.zeros((1024, ROWS), jnp.bfloat16)

        @pl.when(own == me)
        def _():
            block_grads(own, kv_sums, at, True)

        from_other(turn, at)

        @pl.when(turn == 0)
        def _():
            ring.first()

        @pl.when(turn == 2)
        def _():
            ring.second()

    for j in range(KV_HEADS):
        for r in range(2):
            head = query_grad[j, :, r * ROWS : (r + 1) * ROWS] * HEAD_DIM**-0.5
            turned[j * 128 + r * 64 : j * 128 + r * 64 + 64] = turned_back(head, cosine[...], sine[...])

    raw_load.wait()
    result[...] = turned[...].T

    def query_part(n, gain_grad):
        at = pl.ds(pl.multiple_of(n * 64, 64), 64)
        part, more = rms_back(query_raw[at], as_row(query_gain), result[at])
        branch[at] = part.astype(jnp.bfloat16)
        return gain_grad + more

    query_gain_grad = lax.fori_loop(0, 4, query_part, jnp.zeros((1, 1024), jnp.float32))

    def half_of_columns(raw, raw_other, shift):
        both = jnp.concatenate([raw[:, own_half], raw_other[...]], axis=0)

        @pl.loop(0, 4)
        def _(n):
            columns = pl.ds(pl.multiple_of(n * 256, 256), 256)
            left = jnp.concatenate([normed[:, columns], normed_other[:, columns]], axis=0)
            part = dot_tn(left, both).astype(jnp.bfloat16)
            for q in range(2):
                first = shift + (here["core"] * 2 + q) * 1024 + n * 256
                kv[pl.ds(pl.multiple_of(first, 256), 256)] = part[:, q * 256 : (q + 1) * 256]

    pairs[1].start()
    onward(early, 2)
    for one in experts:
        one.arrive(3, 4)
        one.start(7)
    pairs[0].wait_recv()
    pairs[1].wait_recv()
    half_of_columns(branch, query_other, 0)
    for one in of_query:
        one.begin(1)

    def put(at, total):
        turned[at] = total

    ring.third(put)
    for j in range(KV_HEADS):
        turned[j * 64 : j * 64 + 64] = turned_back(turned[j * 64 : j * 64 + 64], cosine[...], sine[...])
    part, key_gain_grad = rms_back(key_raw[...], as_row(key_gain), turned[:512].T)
    key_value[:, :512] = part.astype(jnp.bfloat16)
    key_value[:, 512:] = turned[512:].T.astype(jnp.bfloat16)
    pairs[2].start()
    for one in leads:
        one.third()
    for one in lasts:
        one.first()
    pairs[2].wait_recv()
    half_of_columns(key_value, key_value_other, 4096)
    for one in of_keys:
        one.begin(1)

    next_load.wait()
    result[...] = dot_nt(branch[...], square[...])
    last_loads = [
        pltpu.make_async_copy(w_key, square.at[:, pl.ds(0, 512)], load_sem.at[4]),
        pltpu.make_async_copy(w_value, square.at[:, pl.ds(512, 512)], load_sem.at[5]),
    ]
    for load in last_loads:
        load.start()
    onward(of_query, 1)
    for load in last_loads:
        load.wait()
    result[...] += dot_nt(key_value[...], square[...])

    def token_part(n, gain_grad):
        at = pl.ds(pl.multiple_of(n * 64, 64), 64)
        part, more = rms_back(tokens[at].astype(jnp.float32), as_row(attn_gain), result[at])
        token_grad[at] = (hidden_grad[at] + part).astype(jnp.bfloat16)
        return gain_grad + more

    attn_gain_grad = lax.fori_loop(0, 4, token_part, jnp.zeros((1, 1024), jnp.float32))
    key_wide = jnp.concatenate([key_gain_grad, jnp.zeros((1, 512), jnp.float32)], axis=1)
    late_values[0] = jnp.concatenate(
        [attn_gain_grad, query_gain_grad, key_wide, jnp.zeros((5, 1024), jnp.float32)], axis=0
    )
    late_few.begin(0)
    onward(of_keys, 1)
    onward(early, 3)
    for stage in range(2, 5):
        onward(of_query, stage)
        late_few.finish(stage - 2)
        late_few.begin(stage - 1)
        onward(of_keys, stage)
        onward(early, stage + 2)
        if stage == 3:
            for one in lasts:
                one.second()
    for q in range(4):
        outs[q].start()
    late_few.finish(3)
    late_small[...] = late_values[4]
    router = [final_output[2048 + q * EXPERTS : 2048 + (q + 1) * EXPERTS].astype(jnp.float32) for q in range(4)]
    lines = final_output[2176:2192].astype(jnp.float32)
    lines = jnp.concatenate([lines[q : q + 1] for q in range(4)], axis=1)
    early_small[...] = jnp.concatenate(
        [jnp.concatenate(router, axis=1), lines, jnp.zeros((7, 1024), jnp.float32)], axis=0
    )

    def put_mixed(at, total):
        mixed_out[at] = (hidden[at] + total).astype(jnp.bfloat16)

    for stage in range(5, 7):
        onward(of_query, stage)
        onward(of_keys, stage)
        if stage == 5:
            for one in lasts:
                one.third(put_mixed)
    for q in range(4, 12):
        outs[q].start()
    for one in experts:
        one.arrive(0, 5, 6, 7)
    for one in [*experts, *leads, *lasts, ring, *early, *of_query, *of_keys, late_few]:
        one.drain()
    for turn in (2, 3):
        mate_copy(turn, 0).wait_send()
    for pair in pairs:
        pair.wait_send()
    for out in outs:
        out.wait()


def backward(smalls, larges):
    vmem, hbm = pl.BlockSpec(memory_space=pltpu.VMEM), pl.BlockSpec(memory_space=pl.ANY)
    low, wide = jnp.bfloat16, jnp.float32
    shape = jax.ShapeDtypeStruct
    dma = pltpu.SemaphoreType.DMA
    return pl.pallas_call(
        backward_kernel,
        name="backward",
        out_shape=(
            shape((ROWS, 1024), low),
            shape((ROWS, 1024), low),
            shape((40, 1024), wide),
            shape((8, 1024), wide),
            shape((1024, 1024), low),
            shape((1024, 512), low),
            shape((1024, 512), low),
            shape((1024, 1024), low),
            shape((8, 256, 1024), low),
            shape((8, 128, 1024), low),
        ),
        in_specs=[vmem] * len(smalls) + [hbm] * len(larges),
        out_specs=(vmem,) * 4 + (hbm,) * 6,
        scratch_shapes=[
            pltpu.VMEM((16, ROWS, 1024), low),
            pltpu.VMEM((10 * 384, 1024), low),
            pltpu.VMEM((FULL, 1024), wide),
            pltpu.VMEM((1024, 1024), low),
            pltpu.VMEM((8 * 1024, ROWS), low),
            pltpu.VMEM((ROWS, 1024), wide),
            pltpu.VMEM((ROWS, 1024), wide),
            pltpu.VMEM((ROWS, 1024), low),
            pltpu.VMEM((KV_HEADS, HEAD_DIM, 2 * ROWS), low),
            pltpu.VMEM((KV_HEADS, 1, 2 * ROWS), wide),
            pltpu.VMEM((KV_HEADS, HEAD_DIM, 2 * ROWS), wide),
            pltpu.VMEM((1024, ROWS), wide),
            pltpu.VMEM((2, 1024, ROWS), low),
            pltpu.VMEM((4, 1024, ROWS), low),
            pltpu.VMEM((4, 1024, ROWS), low),
            pltpu.VMEM((3072, ROWS), low),
            pltpu.VMEM((ROWS, 1024), low),
            pltpu.VMEM((ROWS, 1024), low),
            pltpu.VMEM((ROWS, 512), low),
            pltpu.VMEM((ROWS, 512), low),
            pltpu.VMEM((4608, 256), low),
            pltpu.VMEM((4608, 256), low),
            pltpu.VMEM((4096, 256), low),
            pltpu.VMEM((4096, 256), low),
            pltpu.VMEM((4896, 256), low),
            pltpu.VMEM((2304, 256), low),
            pltpu.VMEM((2304, 256), low),
            pltpu.VMEM((9, 48, 256), low),
            pltpu.VMEM((5, 8, 1024), wide),
            pltpu.VMEM((10, 8, 1024), wide),
            dma((10, 4)),
            dma((10, 4)),
            dma((4,)),
            dma((4,)),
            dma((1, 4)),
            dma((1, 4)),
            dma((9, 17)),
            dma((9, 17)),
            dma((10,)),
            dma((10,)),
            dma((10,)),
            dma((12,)),
            dma((2, 8)),
            dma((2, 8)),
            dma((3,)),
            dma((3,)),
        ],
        compiler_params=pltpu.CompilerParams(
            collective_id=4, has_side_effects=True, vmem_limit_bytes=66000000
        ),
        cost_estimate=pl.CostEstimate(flops=100 * 10**9, bytes_accessed=60 * 10**6, transcendentals=8 * 10**6),
    )(*smalls, *larges)


def widen_kernel(
    early, late, mixed, tokens, query, key, value, output, gate_up, down,
    ffn_gain, attn_gain, query_gain, key_gain, router,
    mixed_out, token_out, query_out, key_out, value_out, output_out, gate_out, up_out, down_out,
    query_in, key_in, value_in, output_in, gate_up_in, down_in,
    query_wide, key_wide, value_wide, output_wide, gate_up_wide, down_wide,
    in_sem, out_sem,
):
    arrays = (
        (query, query_in, query_wide, query_out),
        (output, output_in, output_wide, output_out),
        (key, key_in, key_wide, key_out),
        (value, value_in, value_wide, value_out),
    )
    parts = []
    for source, low, wide, target in arrays:
        for n in range(0, 1024, 512):
            at = pl.ds(n, 512)
            parts.append((source.at[at], low.at[at], wide.at[at], [(wide.at[at], target.at[at])]))
    for block in range(8):
        rows, e = pl.ds(block // 2 * 256, 256), block % 2
        wide = gate_up_wide.at[block]
        targets = [
            (wide.at[:, pl.ds(0, 512)], gate_out.at[e, rows]),
            (wide.at[:, pl.ds(512, 512)], up_out.at[e, rows]),
        ]
        parts.append((gate_up.at[block], gate_up_in.at[block], wide, targets))
    for block in range(8):
        wide = down_wide.at[block]
        target = down_out.at[block % 2, pl.ds(block // 2 * 128, 128)]
        parts.append((down.at[block], down_in.at[block], wide, [(wide, target)]))
    loads = [pltpu.make_async_copy(source, low, in_sem.at[n]) for n, (source, low, _, _) in enumerate(parts)]
    for load in loads:
        load.start()
    ffn_gain[...] = early[EXPERTS]
    attn_gain[...] = late[0]
    query_gain[...] = late[1]
    key_gain[...] = late[2, :512]
    router[...] = early[:EXPERTS]
    mixed_out[...] = mixed[...]
    token_out[...] = tokens[...]
    stores = []
    for load, (_, low, wide, targets) in zip(loads, parts):
        load.wait()
        wide[...] = low[...].astype(jnp.float32)
        for source, target in targets:
            stores.append(pltpu.make_async_copy(source, target, out_sem.at[len(stores)]))
            stores[-1].start()
    for copy in stores:
        copy.wait()


def widen(arrays):
    vmem, hbm = pl.BlockSpec(memory_space=pltpu.VMEM), pl.BlockSpec(memory_space=pl.ANY)
    low, wide = jnp.bfloat16, jnp.float32
    shape = jax.ShapeDtypeStruct
    held = ((1024, 1024), (1024, 512), (1024, 512), (1024, 1024), (8, 256, 1024), (8, 128, 1024))
    return pl.pallas_call(
        widen_kernel,
        name="widen",
        out_shape=(
            shape((1024,), wide),
            shape((1024,), wide),
            shape((1024,), wide),
            shape((512,), wide),
            shape((EXPERTS, 1024), wide),
            shape((ROWS, 1024), low),
            shape((ROWS, 1024), low),
            shape((1024, 1024), wide),
            shape((1024, 512), wide),
            shape((1024, 512), wide),
            shape((1024, 1024), wide),
            shape((2, 1024, 512), wide),
            shape((2, 1024, 512), wide),
            shape((2, 512, 1024), wide),
        ),
        in_specs=[vmem] * 4 + [hbm] * 6,
        out_specs=(vmem,) * 7 + (hbm,) * 7,
        scratch_shapes=[
            *[pltpu.VMEM(size, low) for size in held],
            *[pltpu.VMEM(size, wide) for size in held],
            pltpu.SemaphoreType.DMA((24,)),
            pltpu.SemaphoreType.DMA((32,)),
        ],
        compiler_params=pltpu.CompilerParams(vmem_limit_bytes=56 * 2**20),
    )(*arrays)


def body(
    tokens,
    cotangent,
    lengths,
    routes,
    attn_gain,
    w_query,
    w_key,
    w_value,
    query_gain,
    key_gain,
    w_output,
    ffn_gain,
    w_router,
    w_gate,
    w_up,
    w_down,
):
    query_pos = lax.axis_index("dp") * ROWS + jnp.arange(ROWS, dtype=jnp.int32)
    cosine, sine_table = rope_tables(query_pos)
    cosine, sine_table = cosine.T, sine_table.T
    routes_t, length = routes[0].T, lengths.reshape(1, 1)
    gains = [attn_gain, query_gain, key_gain, ffn_gain]
    weights = (w_query, w_key, w_value, w_output)
    router_rows = w_router.T
    ffn_in, hidden, mixed_t, queries, log_total, normed, query_raw, key_raw, kv_all, cot_all = forward(
        tokens[0], cotangent[0], routes_t, length, cosine, sine_table, gains, weights
    )
    returned, mixed_parts, own_gu, own_down = moe(
        ffn_in, cot_all, cotangent[0], router_rows, w_gate, w_up, w_down
    )
    mixed_low, token_low, early_small, late_small, *sums = backward(
        (
            hidden, ffn_in, cotangent[0], tokens[0], normed, key_raw, mixed_t, queries, log_total, routes_t,
            length, cosine, sine_table, *gains, router_rows, own_gu, own_down,
        ),
        (returned, query_raw, mixed_parts, kv_all.reshape(8 * 1024, ROWS), *weights),
    )
    (
        ffn_gain_sum, attn_gain_sum, query_gain_sum, key_gain_sum, router_sum, mixed_out, token_grad,
        query_w_sum, key_w_sum, value_w_sum, output_w_sum, gate_w_sum, up_w_sum, down_w_sum,
    ) = widen((early_small, late_small, mixed_low, token_low, *sums))
    return (
        mixed_out[None],
        token_grad[None],
        attn_gain_sum,
        query_w_sum,
        key_w_sum,
        value_w_sum,
        query_gain_sum,
        key_gain_sum,
        output_w_sum,
        ffn_gain_sum,
        router_sum.T,
        gate_w_sum,
        up_w_sum,
        down_w_sum,
    )


def solution(mesh):
    return jax.shard_map(
        body,
        mesh=mesh,
        in_specs=(
            P("expert", "dp", None),
            P("expert", "dp", None),
            P("expert"),
            P("expert", "dp", None),
            P(),
            P(),
            P(),
            P(),
            P(),
            P(),
            P(),
            P(),
            P(),
            P("expert", None, None),
            P("expert", None, None),
            P("expert", None, None),
        ),
        out_specs=(
            P("expert", "dp", None),
            P("expert", "dp", None),
            P(),
            P(),
            P(),
            P(),
            P(),
            P(),
            P(),
            P(),
            P(),
            P("expert", None, None),
            P("expert", None, None),
            P("expert", None, None),
        ),
        check_vma=False,
    )
```

```python
import math

import jax
import jax.numpy as jnp
from jax import lax
from jax.experimental import pallas as pl
from jax.experimental.pallas import tpu as pltpu
from jax.sharding import PartitionSpec as P

HEADS = 16
KV_HEADS = 8
HEAD_DIM = 64
EXPERTS = 32
TOPK = 8
CAP = 80


epsilon = 1e-06


def rope_tables(positions):
    steps_half = jnp.arange(HEAD_DIM // 2).astype(jnp.float32)
    inverse = jnp.exp(steps_half * (-2.0 * math.log(10000.0) / HEAD_DIM))
    angles = positions.astype(jnp.float32)[:, None] * inverse[None, :]
    return (jnp.cos(angles), jnp.sin(angles))


RING = 4
ROWS = 256
EXTRA = 16
FULL = ROWS + EXTRA
SENT = 192
LEFT = FULL - SENT
BOTH = ROWS + LEFT
GROUP = 4 * CAP
MESH = pl.DeviceIdType.MESH


def dot_nn(a, b):
    return jnp.dot(a, b, preferred_element_type=jnp.float32)


def dot_nt(a, b):
    return lax.dot_general(a, b, (((1,), (1,)), ((), ())), preferred_element_type=jnp.float32)


def dot_tn(a, b):
    return lax.dot_general(a, b, (((0,), (0,)), ((), ())), preferred_element_type=jnp.float32)


def step_of(size):
    return next(step for step in (64, 48, 32, 16) if size % step == 0)


class Torus:
    def __init__(self):
        self.dp = lax.axis_index("dp")
        expert = lax.axis_index("expert")
        self.expert = expert
        self.z, self.y = expert // RING, expert % RING

    def block(self, dz, dy):
        return ((self.z + dz + RING) % RING) * RING + (self.y + dy + RING) % RING

    def near(self, axis, step):
        return (self.dp, self.block(step, 0) if axis == "z" else self.block(0, step))

    def along(self, axis, other, step):
        return self.block(step, other) if axis == "z" else self.block(other, step)

    def neighbours(self):
        return [self.near(axis, step) for axis in "yz" for step in (1, -1)]


ARRIVALS = (
    ((0, 0), (3, 0), (1, 3), (3, 2)),
    ((0, 1), (0, 2), (3, 1), (2, 1)),
    ((0, 3), (2, 0), (3, 3), (2, 3)),
    ((1, 0), (1, 1), (1, 2), (2, 2)),
)


def differences(values):
    found = list(values)
    for level in range(1, len(found)):
        for n in range(len(found) - 1, level - 1, -1):
            found[n] -= found[n - 1]
    return found


def chooses(n):
    return 1, n, n * (n - 1) // 2, n * (n - 1) * (n - 2) // 6


class Gather:
    def __init__(self, torus, buffer, send, recv, number, axis, other, low, first, second, stride):
        self.torus, self.buffer, self.send, self.recv = torus, buffer, send, recv
        self.number, self.axis, self.other, self.stride = number, axis, other, stride
        self.whole, self.front, self.rear = (low, first + second), (low, first), (low + first, second)

    def copy(self, which, offset, part, step):
        at = self.torus.along(self.axis, self.other, offset) * self.stride + part[0]
        rows = self.buffer.at[pl.ds(pl.multiple_of(at, 16), part[1])]
        return pltpu.make_async_remote_copy(
            src_ref=rows,
            dst_ref=rows,
            send_sem=self.send.at[self.number, which],
            recv_sem=self.recv.at[self.number, which],
            device_id=self.torus.near(self.axis, step),
            device_id_type=MESH,
        )

    def first(self):
        self.copy(0, 0, self.whole, 1).start()
        self.copy(1, 0, self.whole, -1).start()

    def second(self):
        self.copy(0, -1, self.whole, 1).wait_recv()
        self.copy(2, -1, self.front, 1).start()
        self.copy(1, 1, self.whole, -1).wait_recv()
        self.copy(3, 1, self.rear, -1).start()

    def third(self):
        self.copy(2, 2, self.front, 1).wait_recv()
        self.copy(3, 2, self.rear, -1).wait_recv()

    def drain(self):
        self.copy(0, 0, self.whole, 1).wait_send()
        self.copy(1, 0, self.whole, -1).wait_send()
        self.copy(2, -1, self.front, 1).wait_send()
        self.copy(3, 1, self.rear, -1).wait_send()


class Scatter:
    def __init__(self, torus, sums, landing, send, recv, number, base, axis, other, low, first, second, origin=None):
        self.torus, self.sums, self.landing, self.send, self.recv = torus, sums, landing, send, recv
        self.number, self.axis, self.other = number, axis, other
        self.origin = sums if origin is None else origin
        self.low, self.parts = low, (first, second)
        self.size = first + second
        self.slots = (base, base + first, base + self.size, base + 2 * self.size)

    def rows(self, which):
        if which == 0:
            return self.low, self.parts[0]
        if which == 1:
            return self.low + self.parts[0], self.parts[1]
        return self.low, self.size

    def at(self, offset):
        return self.torus.along(self.axis, self.other, offset)

    def copy(self, which):
        start, size = self.rows(which)
        offset = (2, 2, 1, -1)[which]
        return pltpu.make_async_remote_copy(
            src_ref=(self.origin if which < 2 else self.sums).at[self.at(offset), pl.ds(start, size)],
            dst_ref=self.landing.at[pl.ds(self.slots[which], size)],
            send_sem=self.send.at[self.number, which],
            recv_sem=self.recv.at[self.number, which],
            device_id=self.torus.near(self.axis, (1, -1, 1, -1)[which]),
            device_id_type=MESH,
        )

    def add(self, which, offset):
        start, size = self.rows(which)
        block = self.at(offset)

        many = step_of(size)

        @pl.loop(0, size // many)
        def _(k):
            here = pl.ds(pl.multiple_of(start + k * many, 16), many)
            there = pl.ds(pl.multiple_of(self.slots[which] + k * many, 16), many)
            total = self.sums[block, here].astype(jnp.float32) + self.landing[there].astype(jnp.float32)
            self.sums[block, here] = total.astype(jnp.bfloat16)

    def first(self):
        self.copy(0).start()
        self.copy(1).start()

    def second(self):
        self.copy(0).wait_recv()
        self.add(0, 1)
        self.copy(2).start()
        self.copy(1).wait_recv()
        self.add(1, -1)
        self.copy(3).start()

    def third(self, put=None):
        self.copy(2).wait_recv()
        self.copy(3).wait_recv()
        block = self.at(0)

        many = step_of(self.size)

        @pl.loop(0, self.size // many)
        def _(k):
            here = pl.ds(pl.multiple_of(self.low + k * many, 16), many)
            left = pl.ds(pl.multiple_of(self.slots[2] + k * many, 16), many)
            right = pl.ds(pl.multiple_of(self.slots[3] + k * many, 16), many)
            total = (
                self.sums[block, here].astype(jnp.float32)
                + self.landing[left].astype(jnp.float32)
                + self.landing[right].astype(jnp.float32)
            )
            if put is None:
                self.sums[block, here] = total.astype(jnp.bfloat16)
            else:
                put(here, total)

    def drain(self):
        for which in range(4):
            self.copy(which).wait_send()


def moe_kernel(
    ffn, cot, own_cot, wr, w_gate, w_up, w_down,
    ret, mixed, own_gu, own_down,
    rows, sums, wgu, wd, held, pair, inner, dgu, mixing, back, cotv, before, chosen, gate_rows, grad_rows, stage,
    mate_rows, gu_sums, down_sums,
    ag_send, ag_recv, rs_send, rs_recv, w_sem, cot_sem, own_sem, stage_sem, mate_send, mate_recv, x_send, x_recv, credit,
):
    torus = Torus()
    place, place_of = everywhere()
    barrier = pltpu.get_barrier_semaphore()
    peers = [*torus.neighbours(), place_of("core", 1), place_of("x", 1), place_of("x", -1)]
    for device in peers:
        pl.semaphore_signal(barrier, inc=1, device_id=device, device_id_type=MESH)

    weights = [
        pltpu.make_async_copy(w_gate, wgu.at[:, :, pl.ds(0, 512)], w_sem.at[0]),
        pltpu.make_async_copy(w_up, wgu.at[:, :, pl.ds(512, 512)], w_sem.at[1]),
        pltpu.make_async_copy(w_down, wd, w_sem.at[2]),
    ]
    for copy in weights:
        copy.start()

    def source_of(g, j):
        of_g, of_j = chooses(g), chooses(j)
        offsets = []
        for axis in range(2):
            table = [differences([at[axis] for at in line]) for line in ARRIVALS]
            table = [differences(column) for column in zip(*table)]
            offsets.append(sum(table[a][b] * of_g[a] * of_j[b] for a in range(4) for b in range(4) if table[a][b]))
        return torus.block(*offsets)

    def cot_copy(g, j):
        at = pl.multiple_of(source_of(g, j) * SENT, 16)
        return pltpu.make_async_copy(cot.at[pl.ds(at, SENT)], cotv.at[pl.ds(j * SENT, SENT)], cot_sem.at[j])

    for j in range(4):
        cot_copy(0, j).start()
    first_row = torus.expert * BOTH
    own_copy = pltpu.make_async_copy(
        own_cot.at[pl.ds(ROWS - LEFT, LEFT)], rows.at[pl.ds(pl.multiple_of(first_row + ROWS, 16), LEFT)], own_sem
    )
    own_copy.start()
    rows[pl.ds(pl.multiple_of(first_row, 16), ROWS)] = ffn[...]
    own_copy.wait()
    pl.semaphore_wait(barrier, len(peers))

    def gather(number, axis, other, low, first, second):
        return Gather(torus, rows, ag_send, ag_recv, number, axis, other, low, first, second, BOTH)

    a_first = gather(0, "y", 0, 0, 96, 80)
    b_first = gather(1, "z", 0, 176, 80, 80)
    a_second = {d: gather(2 + d % RING, "z", d, 0, 96, 80) for d in (0, 1, -1, 2)}
    b_second = {d: gather(6 + d % RING, "y", d, 176, 80, 80) for d in (0, 1, -1, 2)}
    gathers = [a_first, b_first, *a_second.values(), *b_second.values()]

    a_first.first()
    b_first.first()
    b_second[0].first()
    a_second[0].first()
    a_first.second()
    b_first.second()
    b_second[0].second()
    a_second[0].second()
    for d in (1, -1):
        b_second[d].first()
        a_second[d].first()
    for copy in weights:
        copy.wait()

    earlier = lax.broadcasted_iota(jnp.int32, (ROWS, ROWS), 0) < lax.broadcasted_iota(jnp.int32, (ROWS, ROWS), 1)
    before[...] = jnp.where(earlier, 1.0, 0.0).astype(jnp.bfloat16)
    slot_at = lax.broadcasted_iota(jnp.int32, (CAP, ROWS), 0).astype(jnp.float32)

    def stage_copy(slot, target):
        return pltpu.make_async_copy(stage.at[slot], target, stage_sem.at[slot])

    expert_rows = lax.broadcasted_iota(jnp.int32, (EXPERTS, ROWS), 0)
    order = (2, 1, -1, 0)
    a_lead = {
        d: Scatter(torus, sums, rows, rs_send, rs_recv, n, n * 384, "z", d, 0, 64, 64) for n, d in enumerate(order)
    }
    b_lead = {
        d: Scatter(torus, sums, rows, rs_send, rs_recv, 4 + n, 1920 + n * 432, "y", d, 128, 80, 64)
        for n, d in enumerate(order)
    }
    a_last = Scatter(torus, sums, rows, rs_send, rs_recv, 8, 4 * 384, "y", 0, 0, 64, 64)
    b_last = Scatter(torus, sums, rows, rs_send, rs_recv, 9, 1920 + 4 * 432, "z", 0, 128, 80, 64)

    @pl.loop(0, 4)
    def _(g):
        @pl.when(g == 1)
        def _():
            a_first.third()
            b_first.third()
            b_second[2].first()
            a_second[2].first()
            b_second[0].third()
            a_second[0].third()
            for d in (1, -1):
                b_second[d].second()
                a_second[d].second()

        @pl.when(g == 2)
        def _():
            b_second[2].second()
            a_second[2].second()
            b_second[1].third()

        @pl.when(g == 3)
        def _():
            b_second[-1].third()
            for d in (1, -1, 2):
                a_second[d].third()
            b_second[2].third()

        for j in range(4):
            cot_copy(g, j).wait()

        @pl.loop(0, 4)
        def _(j):
            source = source_of(g, j)
            block = rows[pl.ds(pl.multiple_of(source * BOTH, 16), ROWS)]
            laid = cotv[pl.ds(pl.multiple_of(j * SENT, 16), EXTRA)].astype(jnp.float32)
            member = jnp.concatenate([laid[:8, q * ROWS : (q + 1) * ROWS] for q in range(4)], axis=0)
            named = member > 0.5
            slots = dot_nn(member.astype(jnp.bfloat16), before[...])
            slots = jnp.where(named, slots, -1.0)
            logits = jnp.where(named, dot_nt(wr[...], block), -1e30)
            weight = jnp.where(named, jnp.exp(logits - jnp.max(logits, axis=0, keepdims=True)), 0.0)
            gates = weight / jnp.sum(weight, axis=0, keepdims=True)
            picked = []
            for e in range(2):
                own = jnp.sum(
                    jnp.where(expert_rows == torus.expert * 2 + e, slots, 0.0), axis=0, keepdims=True
                )
                picked.append(jnp.where(slot_at == own, 1.0, 0.0))
            both = jnp.concatenate(picked, axis=0).astype(jnp.bfloat16)
            chosen[j] = both
            grad_block = jnp.concatenate(
                [
                    cotv[pl.ds(pl.multiple_of(j * SENT + EXTRA, 16), SENT - EXTRA)],
                    rows[pl.ds(pl.multiple_of(source * BOTH + ROWS, 16), LEFT)],
                ],
                axis=0,
            )
            took = dot_nn(both, jnp.concatenate([block, grad_block], axis=1)).astype(jnp.bfloat16)
            here = pl.ds(pl.multiple_of(j * CAP, 16), CAP)
            there = pl.ds(pl.multiple_of(g * GROUP + j * CAP, 16), CAP)
            for e in range(2):
                own = jnp.sum(
                    jnp.where(expert_rows == torus.expert * 2 + e, gates, 0.0), axis=0, keepdims=True
                )
                of_rows = jnp.sum(picked[e] * own, axis=1, keepdims=True)
                gate_rows[e, here] = jnp.broadcast_to(of_rows, (CAP, 128))
                held[e, there] = took[e * CAP : (e + 1) * CAP, :1024]
                mixing[e, here] = took[e * CAP : (e + 1) * CAP, 1024:]

        @pl.when(g < 3)
        def _():
            for j in range(4):
                cot_copy(g + 1, j).start()

        @pl.when(g == 3)
        def _():
            for one in gathers:
                one.drain()
            for device in peers:
                pl.semaphore_signal(credit, inc=1, device_id=device, device_id_type=MESH)
            pl.semaphore_wait(credit, len(peers))
            b_lead[0].first()
            a_lead[0].first()

        @pl.loop(0, 2)
        def _(e):
            there = pl.ds(pl.multiple_of(g * GROUP, 16), GROUP)
            both = dot_nn(held[e, there], wgu[e])
            gate, up = both[:, :512], both[:, 512:]
            sig = jax.nn.sigmoid(gate)
            silu = gate * sig
            act = (silu * up).astype(jnp.bfloat16)
            inner[e, there] = act
            out = dot_nn(act, wd[e]).astype(jnp.bfloat16).astype(jnp.float32)
            grad = mixing[e].astype(jnp.float32)
            weight = gate_rows[e][:, :1]
            grad_rows[e] = jnp.broadcast_to(jnp.sum(grad * out, axis=1, keepdims=True), (GROUP, 128))
            pair[e, there] = (weight * grad).astype(jnp.bfloat16)
            mixing[e] = (weight * out).astype(jnp.bfloat16)
            inner_grad = dot_nt(pair[e, there], wd[e])
            dgu[e, there, :512] = (inner_grad * up * sig * (1.0 + gate * (1.0 - sig))).astype(jnp.bfloat16)
            dgu[e, there, 512:] = (inner_grad * silu).astype(jnp.bfloat16)
            back[e] = dot_nt(dgu[e, there], wgu[e]).astype(jnp.bfloat16)

        @pl.loop(0, 4)
        def _(j):
            source = source_of(g, j)
            both = chosen[j]
            picked = both.astype(jnp.float32)
            here = pl.ds(pl.multiple_of(j * CAP, 16), CAP)
            compact = jnp.concatenate(
                [jnp.concatenate([back[e, here], mixing[e, here]], axis=1) for e in range(2)], axis=0
            )
            spread = dot_tn(both, compact).astype(jnp.bfloat16)
            sums[source, pl.ds(EXTRA, ROWS)] = spread[:, :1024]
            grads = jnp.zeros((EXPERTS, ROWS), jnp.float32)
            for e in range(2):
                own = jnp.sum(
                    picked[e * CAP : (e + 1) * CAP] * grad_rows[e, here][:, :1], axis=0, keepdims=True
                )
                grads = grads + jnp.where(expert_rows == torus.expert * 2 + e, own, 0.0)
            laid = jnp.concatenate([grads[8 * q : 8 * q + 8] for q in range(4)], axis=1)
            sums[source, pl.ds(0, EXTRA)] = jnp.concatenate([laid, jnp.zeros_like(laid)], axis=0).astype(
                jnp.bfloat16
            )
            slot = j % 2

            @pl.when((g > 0) | (j > 1))
            def _():
                stage_copy(slot, mixed.at[source]).wait()

            stage[slot] = spread[:, 1024:]
            stage_copy(slot, mixed.at[source]).start()

    def chunk(e, k):
        if k < 4:
            return dot_tn(held[e, :, k * 256 : (k + 1) * 256], dgu[e]).astype(jnp.bfloat16)
        return dot_tn(inner[e, :, (k - 4) * 256 : (k - 3) * 256], pair[e]).astype(jnp.bfloat16)

    def mate_copy(k):
        return pltpu.make_async_remote_copy(
            src_ref=stage.at[k % 2],
            dst_ref=mate_rows.at[pl.ds(k * 256, 256)],
            send_sem=mate_send.at[k],
            recv_sem=mate_recv.at[k],
            device_id=place_of("core", 1),
            device_id_type=MESH,
        )

    line = Line(place, place_of)
    rings = [
        Scatter(line, gu_sums, rows, x_send, x_recv, 0, 4080, "x", 0, 0, 128, 128),
        Scatter(line, down_sums, rows, x_send, x_recv, 1, 4848, "x", 0, 0, 64, 64),
    ]

    for d in (2, 1, -1):
        b_lead[d].first()
        a_lead[d].first()
    b_lead[0].second()
    a_lead[0].second()
    for k in range(6):
        if k < 2:
            stage_copy(k, mixed.at[0]).wait()
        else:
            mate_copy(k - 2).wait_send()
        stage[k % 2] = chunk(1 - place["core"], k)
        mate_copy(k).start()
        own = chunk(place["core"], k)
        if k < 4:
            gu_sums[k] = own
        else:
            down_sums[2 * k - 8] = own[:128]
            down_sums[2 * k - 7] = own[128:]
    for d in (2, 1, -1):
        b_lead[d].second()
        a_lead[d].second()
    for k in range(6):
        mate_copy(k).wait_recv()

        @pl.loop(0, 4)
        def _(n):
            other = mate_rows[pl.ds(pl.multiple_of(k * 256 + n * 64, 64), 64)].astype(jnp.float32)
            if k < 4:
                at = (k, pl.ds(pl.multiple_of(n * 64, 64), 64))
                gu_sums[at] = (gu_sums[at].astype(jnp.float32) + other).astype(jnp.bfloat16)
            else:
                at = (2 * k - 8 + n // 2, pl.ds(pl.multiple_of(n % 2 * 64, 64), 64))
                down_sums[at] = (down_sums[at].astype(jnp.float32) + other).astype(jnp.bfloat16)

    for one in rings:
        one.first()
    for one in rings:
        one.second()
    for d in order:
        b_lead[d].third()
        a_lead[d].third()
        if d == 2:
            b_last.first()
            a_last.first()
    b_last.second()
    a_last.second()

    def put(at, total):
        ret[at] = total

    b_last.third(put)
    a_last.third(put)

    def put_gu(at, total):
        own_gu[at] = total.astype(jnp.bfloat16)

    def put_down(at, total):
        own_down[at] = total.astype(jnp.bfloat16)

    rings[0].third(put_gu)
    rings[1].third(put_down)
    for one in [*a_lead.values(), *b_lead.values(), a_last, b_last, *rings]:
        one.drain()
    for k in (4, 5):
        mate_copy(k).wait_send()


def moe(ffn_in, cot_all, own_cot, router_rows, w_gate, w_up, w_down):
    vmem, hbm = pl.BlockSpec(memory_space=pltpu.VMEM), pl.BlockSpec(memory_space=pl.ANY)
    low, total = jnp.bfloat16, 4 * GROUP
    return pl.pallas_call(
        moe_kernel,
        name="moe",
        out_shape=(
            jax.ShapeDtypeStruct((FULL, 1024), jnp.float32),
            jax.ShapeDtypeStruct((16, ROWS, 1024), low),
            jax.ShapeDtypeStruct((256, 1024), low),
            jax.ShapeDtypeStruct((128, 1024), low),
        ),
        in_specs=[vmem, hbm, hbm, vmem, hbm, hbm, hbm],
        out_specs=(vmem, hbm, vmem, vmem),
        scratch_shapes=[
            pltpu.VMEM((16 * BOTH, 1024), low),
            pltpu.VMEM((16, FULL, 1024), low),
            pltpu.VMEM((2, 1024, 1024), low),
            pltpu.VMEM((2, 512, 1024), low),
            pltpu.VMEM((2, total, 1024), low),
            pltpu.VMEM((2, total, 1024), low),
            pltpu.VMEM((2, total, 512), low),
            pltpu.VMEM((2, total, 1024), low),
            pltpu.VMEM((2, GROUP, 1024), low),
            pltpu.VMEM((2, GROUP, 1024), low),
            pltpu.VMEM((4 * SENT, 1024), low),
            pltpu.VMEM((ROWS, ROWS), low),
            pltpu.VMEM((4, 2 * CAP, ROWS), low),
            pltpu.VMEM((2, GROUP, 128), jnp.float32),
            pltpu.VMEM((2, GROUP, 128), jnp.float32),
            pltpu.VMEM((2, ROWS, 1024), low),
            pltpu.VMEM((6 * 256, 1024), low),
            pltpu.VMEM((4, 256, 1024), low),
            pltpu.VMEM((4, 128, 1024), low),
            pltpu.SemaphoreType.DMA((10, 4)),
            pltpu.SemaphoreType.DMA((10, 4)),
            pltpu.SemaphoreType.DMA((10, 4)),
            pltpu.SemaphoreType.DMA((10, 4)),
            pltpu.SemaphoreType.DMA((3,)),
            pltpu.SemaphoreType.DMA((4,)),
            pltpu.SemaphoreType.DMA,
            pltpu.SemaphoreType.DMA((2,)),
            pltpu.SemaphoreType.DMA((6,)),
            pltpu.SemaphoreType.DMA((6,)),
            pltpu.SemaphoreType.DMA((2, 4)),
            pltpu.SemaphoreType.DMA((2, 4)),
            pltpu.SemaphoreType.REGULAR,
        ],
        compiler_params=pltpu.CompilerParams(
            collective_id=1, has_side_effects=True, vmem_limit_bytes=63 * 2**20
        ),
        cost_estimate=pl.CostEstimate(flops=50 * 10**9, bytes_accessed=40 * 10**6, transcendentals=2 * 10**6),
    )(ffn_in, cot_all, own_cot, router_rows, w_gate, w_up, w_down)


def everywhere():
    dp, expert = lax.axis_index("dp"), lax.axis_index("expert")
    here = {"x": dp // 2, "core": dp % 2, "z": expert // RING, "y": expert % RING}

    def device(axis, step):
        there = dict(here)
        size = 2 if axis == "core" else RING
        there[axis] = (here[axis] + step + size) % size
        return (there["x"] * 2 + there["core"], there["z"] * RING + there["y"])

    return here, device


def rms_scale(values):
    return lax.rsqrt(jnp.mean(values * values, axis=-1, keepdims=True) + epsilon)


def as_row(gain):
    return gain[...].astype(jnp.float32).reshape(1, -1)


def turned_rows(values, cosine, sine):
    front, back = values[: HEAD_DIM // 2], values[HEAD_DIM // 2 :]
    return jnp.concatenate([front * cosine - back * sine, back * cosine + front * sine], axis=0)


def kv_order(here, step):
    turn = step // 2
    return (turn % 2) * (3 - turn // 2) + (1 - turn % 2) * (turn // 2)


class Keys:
    def __init__(self, here, device, blocks, send, recv, origin=None):
        self.here, self.device, self.blocks, self.send, self.recv = here, device, blocks, send, recv
        self.origin = origin
        self.lines = blocks.shape[1]

    def copy(self, which):
        half = self.lines // 2
        offset, start, size, axis, step = (
            (0, 0, self.lines, "core", 1),
            (0, 0, self.lines, "x", 1),
            (0, 0, self.lines, "x", -1),
            (-1, 0, half, "x", 1),
            (1, half, half, "x", -1),
            (-1, 0, self.lines, "core", 1),
            (1, 0, self.lines, "core", 1),
            (2, 0, self.lines, "core", 1),
        )[which]
        block = (self.here["x"] + offset + RING) % RING * 2 + self.here["core"]
        part = self.blocks.at[block, pl.ds(start, size)]
        return pltpu.make_async_remote_copy(
            src_ref=part if which > 2 or self.origin is None else self.origin,
            dst_ref=part,
            send_sem=self.send.at[which],
            recv_sem=self.recv.at[which],
            device_id=self.device(axis, step),
            device_id_type=MESH,
        )

    def start(self, *which):
        for one in which:
            self.copy(one).start()

    def arrive(self, *which):
        for one in which:
            self.copy(one).wait_recv()

    def drain(self):
        for one in range(8):
            self.copy(one).wait_send()


def forward_kernel(
    tokens, cot, routes_t, length, cosine, sine, attn_gain, query_gain, key_gain, ffn_gain,
    w_query, w_key, w_value, w_output,
    ffn_in, hidden, mixed_t, queries, log_total, normed, query_raw, key_raw, kv_all, cot_all,
    wq, wk, wv, wo, kv, turned, most, total, mixed, packed,
    ag_send, ag_recv, kv_send, kv_recv, w_sem, kv_sem, own_sem,
):
    torus = Torus()
    here, device = everywhere()
    me = here["x"] * 2 + here["core"]
    barrier = pltpu.get_barrier_semaphore()
    peers = [*torus.neighbours(), device("core", 1), device("x", 1), device("x", -1)]
    for peer in peers:
        pl.semaphore_signal(barrier, inc=1, device_id=peer, device_id_type=MESH)
    loads = [
        pltpu.make_async_copy(source, target, w_sem.at[n])
        for n, (source, target) in enumerate(((w_query, wq), (w_key, wk), (w_value, wv), (w_output, wo)))
    ]
    for load in loads:
        load.start()

    expert_rows = lax.broadcasted_iota(jnp.int32, (EXPERTS, ROWS), 0)
    member = jnp.zeros((EXPERTS, ROWS), jnp.float32)
    for k in range(TOPK):
        member = member + jnp.where(expert_rows == routes_t[pl.ds(k, 1), :], 1.0, 0.0)
    laid = jnp.concatenate([member[8 * q : 8 * q + 8] for q in range(4)], axis=1)
    packed[...] = jnp.concatenate([laid, jnp.zeros_like(laid)], axis=0).astype(jnp.bfloat16)
    first_row = pl.multiple_of(torus.expert * SENT, 16)
    owns = [
        pltpu.make_async_copy(packed, cot_all.at[pl.ds(first_row, EXTRA)], own_sem.at[0]),
        pltpu.make_async_copy(
            cot.at[pl.ds(0, SENT - EXTRA)],
            cot_all.at[pl.ds(pl.multiple_of(first_row + EXTRA, 16), SENT - EXTRA)],
            own_sem.at[1],
        ),
    ]
    for copy in owns:
        copy.start()
    for copy in owns:
        copy.wait()
    pl.semaphore_wait(barrier, len(peers))

    def gather(number, axis, other, low, first, second):
        return Gather(torus, cot_all, ag_send, ag_recv, number, axis, other, low, first, second, SENT)

    a_first = gather(0, "y", 0, 0, 48, 48)
    b_first = gather(1, "z", 0, 96, 48, 48)
    a_second = {d: gather(2 + d % RING, "z", d, 0, 48, 48) for d in (0, 1, -1, 2)}
    b_second = {d: gather(6 + d % RING, "y", d, 96, 48, 48) for d in (0, 1, -1, 2)}
    gathers = [a_first, b_first, *a_second.values(), *b_second.values()]
    a_first.first()
    b_first.first()
    b_second[0].first()
    a_second[0].first()

    @pl.loop(0, 4)
    def _(n):
        at = pl.ds(pl.multiple_of(n * 64, 64), 64)
        rows = tokens[at].astype(jnp.float32)
        normed[at] = (rows * rms_scale(rows) * as_row(attn_gain)).astype(jnp.bfloat16)

    for load in loads:
        load.wait()

    keys = Keys(here, device, kv, kv_send, kv_recv)
    key_raw[...] = dot_nn(normed[...], wk[...])
    scaled = key_raw[...]
    scaled = (scaled * rms_scale(scaled) * as_row(key_gain)).T
    for j in range(KV_HEADS):
        head = turned_rows(scaled[j * 64 : j * 64 + 64], cosine[...], sine[...])
        kv[me, pl.ds(j * 64, 64)] = head.astype(jnp.bfloat16)
    kv[me, pl.ds(512, 512)] = dot_nn(normed[...], wv[...]).T.astype(jnp.bfloat16)
    keys.start(0, 1, 2)
    query_raw[...] = dot_nn(normed[...], wq[...])
    scaled = query_raw[...]
    turned[...] = (scaled * rms_scale(scaled) * as_row(query_gain)).T

    for j in range(KV_HEADS):
        for r in range(2):
            head = turned[j * 128 + r * 64 : j * 128 + r * 64 + 64]
            head = turned_rows(head, cosine[...], sine[...])
            queries[j, :, r * ROWS : (r + 1) * ROWS] = (head * HEAD_DIM**-0.5).astype(jnp.bfloat16)

    a_first.second()
    b_first.second()
    for d in (1, -1):
        b_second[d].first()
        a_second[d].first()

    key_at = lax.broadcasted_iota(jnp.int32, (ROWS, 2 * ROWS), 0)
    query_at = lax.broadcasted_iota(jnp.int32, (ROWS, 2 * ROWS), 1) % ROWS
    valid = (key_at <= query_at) & (key_at + me * ROWS < length[...])

    def heads_of(block):
        keys_here = [kv[block, j * 64 : j * 64 + 64] for j in range(KV_HEADS)]
        values_here = [kv[block, 512 + j * 64 : 576 + j * 64] for j in range(KV_HEADS)]
        return keys_here, values_here

    keys_here, values_here = heads_of(me)
    scores = [jnp.where(valid, dot_tn(keys_here[j], queries[j]), -1e30) for j in range(KV_HEADS)]
    tops = [jnp.max(one, axis=0, keepdims=True) for one in scores]
    probs = [jnp.exp(one - top) for one, top in zip(scores, tops)]
    parts = [dot_nn(one, prob.astype(jnp.bfloat16)) for one, prob in zip(values_here, probs)]
    for j in range(KV_HEADS):
        most[j] = tops[j]
        total[j] = jnp.sum(probs[j], axis=0, keepdims=True)
        mixed[j] = parts[j]

    @pl.loop(1, 8)
    def _(step):
        @pl.when(step == 1)
        def _():
            a_first.third()
            b_first.third()
            b_second[2].first()
            a_second[2].first()
            keys.arrive(0)

        @pl.when(step == 2)
        def _():
            b_second[0].second()
            a_second[0].second()
            keys.arrive(1)
            keys.start(3, 5)
            keys.arrive(2)
            keys.start(4, 6)

        @pl.when(step == 3)
        def _():
            for d in (1, -1):
                b_second[d].second()
                a_second[d].second()
            keys.arrive(5)

        @pl.when(step == 5)
        def _():
            keys.arrive(3, 4)
            keys.start(7)
            b_second[2].second()
            a_second[2].second()
            keys.arrive(6)

        @pl.when(step == 7)
        def _():
            keys.arrive(7)

        block = (here["x"] + kv_order(here, step) + RING) % RING * 2 + (here["core"] + step) % 2

        @pl.when(block < me)
        def _():
            keys_here, values_here = heads_of(block)
            before = [most[j] for j in range(KV_HEADS)]
            shares = [total[j] for j in range(KV_HEADS)]
            sums = [mixed[j] for j in range(KV_HEADS)]
            scores = [dot_tn(keys_here[j], queries[j]) for j in range(KV_HEADS)]
            tops = [jnp.maximum(old, jnp.max(one, axis=0, keepdims=True)) for old, one in zip(before, scores)]
            probs = [jnp.exp(one - top) for one, top in zip(scores, tops)]
            less = [jnp.exp(old - top) for old, top in zip(before, tops)]
            parts = [dot_nn(one, prob.astype(jnp.bfloat16)) for one, prob in zip(values_here, probs)]
            for j in range(KV_HEADS):
                most[j] = tops[j]
                total[j] = shares[j] * less[j] + jnp.sum(probs[j], axis=0, keepdims=True)
                mixed[j] = sums[j] * less[j] + parts[j]

    save = pltpu.make_async_copy(kv, kv_all, kv_sem)
    save.start()

    for j in range(KV_HEADS):
        share = total[j]
        log_total[j] = most[j] + jnp.log(share)
        head = (mixed[j] * (1.0 / share)).astype(jnp.bfloat16)
        for r in range(2):
            mixed_t[j * 128 + r * 64 : j * 128 + r * 64 + 64, :] = head[:, r * ROWS : (r + 1) * ROWS]

    hidden[...] = dot_tn(mixed_t[...], wo[...])

    @pl.loop(0, 4)
    def _(n):
        at = pl.ds(pl.multiple_of(n * 64, 64), 64)
        rows = hidden[at] + tokens[at].astype(jnp.float32)
        hidden[at] = rows
        ffn_in[at] = (rows * rms_scale(rows) * as_row(ffn_gain)).astype(jnp.bfloat16)

    for d in (0, 1, -1, 2):
        a_second[d].third()
        b_second[d].third()
    save.wait()
    keys.drain()
    for one in gathers:
        one.drain()


def forward(tokens, cot, routes_t, length, cosine, sine, gains, weights):
    vmem, hbm = pl.BlockSpec(memory_space=pltpu.VMEM), pl.BlockSpec(memory_space=pl.ANY)
    low, wide = jnp.bfloat16, jnp.float32
    shape = jax.ShapeDtypeStruct
    return pl.pallas_call(
        forward_kernel,
        name="forward",
        out_shape=(
            shape((ROWS, 1024), low),
            shape((ROWS, 1024), wide),
            shape((1024, ROWS), low),
            shape((KV_HEADS, HEAD_DIM, 2 * ROWS), low),
            shape((KV_HEADS, 1, 2 * ROWS), wide),
            shape((ROWS, 1024), low),
            shape((ROWS, 1024), wide),
            shape((ROWS, 512), wide),
            shape((8, 1024, ROWS), low),
            shape((16 * SENT, 1024), low),
        ),
        in_specs=[vmem] * 10 + [hbm] * 4,
        out_specs=(vmem,) * 8 + (hbm, hbm),
        scratch_shapes=[
            pltpu.VMEM((1024, 1024), low),
            pltpu.VMEM((1024, 512), low),
            pltpu.VMEM((1024, 512), low),
            pltpu.VMEM((1024, 1024), low),
            pltpu.VMEM((8, 1024, ROWS), low),
            pltpu.VMEM((1024, ROWS), wide),
            pltpu.VMEM((KV_HEADS, 1, 2 * ROWS), wide),
            pltpu.VMEM((KV_HEADS, 1, 2 * ROWS), wide),
            pltpu.VMEM((KV_HEADS, HEAD_DIM, 2 * ROWS), wide),
            pltpu.VMEM((EXTRA, 1024), low),
            pltpu.SemaphoreType.DMA((10, 4)),
            pltpu.SemaphoreType.DMA((10, 4)),
            pltpu.SemaphoreType.DMA((8,)),
            pltpu.SemaphoreType.DMA((8,)),
            pltpu.SemaphoreType.DMA((4,)),
            pltpu.SemaphoreType.DMA,
            pltpu.SemaphoreType.DMA((2,)),
        ],
        compiler_params=pltpu.CompilerParams(
            collective_id=3, has_side_effects=True, vmem_limit_bytes=56 * 2**20
        ),
    )(tokens, cot, routes_t, length, cosine, sine, *gains, *weights)


ORDERS = (("x", "y", "z"), ("y", "z", "x"), ("z", "x", "y"))
STREAMS = {2048: ((0, 768), (768, 768), (1536, 512)), 2304: ((0, 768), (768, 768), (1536, 768))}


class Total:
    def __init__(self, here, device, buffer, shift, final, landing, work, send, recv, number, stream, half, begin=0):
        self.here, self.device, self.buffer, self.shift, self.final = here, device, buffer, shift, final
        self.landing, self.work = landing, work
        self.send, self.recv, self.number, self.order = send, recv, number, ORDERS[(stream + number // 3) % 3]
        self.half = half
        self.start, self.rows = STREAMS[half][stream]
        self.stages = range(begin, 7)
        r, own = self.rows, 0 if begin else self.rows
        first = self.start * 9 // 8 + (0 if begin else self.start)
        self.lands = (first, first + own, first + own + 3 * (r // 4), first + own + 3 * (r // 4) + 3 * (r // 16))

    def own(self):
        return self.here["core"] * self.half + self.start

    def copy(self, which, source, target, axis, step):
        return pltpu.make_async_remote_copy(
            src_ref=source,
            dst_ref=target,
            send_sem=self.send.at[self.number, which],
            recv_sem=self.recv.at[self.number, which],
            device_id=self.device(axis, step),
            device_id_type=MESH,
        )

    def held(self, at, size):
        return self.buffer.at[pl.ds(pl.multiple_of(at + self.shift, 16), size)]

    def ready(self, at, size):
        return self.final.at[pl.ds(pl.multiple_of(at, 16), size)]

    def land(self, stage, n, size):
        return self.landing.at[pl.ds(self.lands[stage] + n * size, size)]

    def copies(self, stage):
        r, own = self.rows, self.own()
        a, b, c = self.order
        ia, ib = self.here[a], self.here[b]
        second = own + ia * (r // 4)
        third = second + ib * (r // 16)
        if stage == 0:
            there = (1 - self.here["core"]) * self.half + self.start
            return [self.copy(0, self.held(there, r), self.land(0, 0, r), "core", 1)]
        if stage == 6:
            return [self.copy(16, self.ready(own, r), self.ready(own, r), "core", 1)]
        found = []
        for d in (1, 2, 3):
            if stage == 1:
                source, target, axis = self.held(own + (ia + d) % RING * (r // 4), r // 4), self.land(1, d - 1, r // 4), a
            elif stage == 2:
                source = self.held(second + (ib + d) % RING * (r // 16), r // 16)
                target, axis = self.land(2, d - 1, r // 16), b
            elif stage == 3:
                source = self.work.at[self.number, pl.ds(0, r // 16)]
                target, axis = self.land(3, d - 1, r // 16), c
            elif stage == 4:
                source, target, axis = self.ready(third, r // 16), self.ready(third, r // 16), b
            else:
                source, target, axis = self.ready(second, r // 4), self.ready(second, r // 4), a
            found.append(self.copy(1 + (stage - 1) * 3 + d - 1, source, target, axis, d))
        return found

    def begin(self, stage):
        for copy in self.copies(stage):
            copy.start()

    def add(self, stage, load, store, size, count):
        step = 64 if size % 64 == 0 else 16

        @pl.loop(0, size // step)
        def _(k):
            at = k * step
            total = load(at, step).astype(jnp.float32)
            for n in range(count):
                land = pl.ds(pl.multiple_of(self.lands[stage] + n * size + at, 16), step)
                total = total + self.landing[land].astype(jnp.float32)
            store(at, step, total.astype(jnp.bfloat16))

    def finish(self, stage):
        for copy in self.copies(stage):
            copy.wait_recv()
        if stage > 3:
            return
        r, own = self.rows, self.own()
        a, b, _ = self.order
        second = own + self.here[a] * (r // 4)
        third = second + self.here[b] * (r // 16)
        first = (own, second, third, third)[stage] + self.shift

        def in_place(at, step, *value):
            lines = pl.ds(pl.multiple_of(first + at, 16), step)
            if not value:
                return self.buffer[lines]
            self.buffer[lines] = value[0]

        def in_work(at, step, *value):
            lines = pl.ds(pl.multiple_of(at, 16), step)
            if not value:
                return self.work[self.number, lines]
            self.work[self.number, lines] = value[0]

        def in_final(at, step, value):
            self.final[pl.ds(pl.multiple_of(third + at, 16), step)] = value

        if stage == 0:
            self.add(0, in_place, in_place, r, 1)
        elif stage == 1:
            self.add(1, in_place, in_place, r // 4, 3)
        elif stage == 2:
            self.add(2, in_place, in_work, r // 16, 3)
        else:
            self.add(3, in_work, in_final, r // 16, 3)

    def drain(self):
        for stage in self.stages:
            for copy in self.copies(stage):
                copy.wait_send()


class Small:
    STAGES = (("core", (1,)), ("x", (1, 2, 3)), ("y", (1, 2, 3)), ("z", (1, 2, 3)))

    def __init__(self, device, value, landing, send, recv):
        self.device, self.value, self.landing, self.send, self.recv = device, value, landing, send, recv

    def copies(self, stage):
        axis, steps = self.STAGES[stage]
        first = sum(len(s) for _, s in self.STAGES[:stage])
        return [
            pltpu.make_async_remote_copy(
                src_ref=self.value.at[stage],
                dst_ref=self.landing.at[first + n],
                send_sem=self.send.at[first + n],
                recv_sem=self.recv.at[first + n],
                device_id=self.device(axis, step),
                device_id_type=MESH,
            )
            for n, step in enumerate(steps)
        ]

    def begin(self, stage):
        for copy in self.copies(stage):
            copy.start()

    def finish(self, stage):
        for copy in self.copies(stage):
            copy.wait_recv()
        first = sum(len(s) for _, s in self.STAGES[:stage])
        total = self.value[stage]
        for n in range(len(self.STAGES[stage][1])):
            total = total + self.landing[first + n]
        self.value[stage + 1] = total

    def drain(self):
        for stage in range(4):
            for copy in self.copies(stage):
                copy.wait_send()


class Line:
    def __init__(self, here, device):
        self.here, self.device = here, device

    def along(self, axis, other, step):
        return (self.here["x"] + step + RING) % RING

    def near(self, axis, step):
        return self.device("x", step)


def rms_back(values, gain, grad):
    scale = rms_scale(values)
    lifted = gain * grad
    inner = jnp.mean(values * lifted, axis=-1, keepdims=True)
    return scale * lifted - values * (scale * scale * scale) * inner, jnp.sum(
        grad * values * scale, axis=0, keepdims=True
    )


def turned_back(grads, cosine, sine):
    front, back = grads[: HEAD_DIM // 2], grads[HEAD_DIM // 2 :]
    return jnp.concatenate([front * cosine + back * sine, back * cosine - front * sine], axis=0)


def backward_kernel(
    routes_t, length, cosine, sine, attn_gain, query_gain, key_gain, ffn_gain, router_rows,
    hidden_all, ffn_in_all, cot_all, tokens_all, normed_all, key_raw_all, mixed_t_all, queries_all, log_total_all,
    own_gu, own_down, returned_all, query_raw_all, mixed_parts, kv_all, w_query, w_key, w_value, w_output,
    mixed_out, token_grad, early_small, late_small, query_sum, key_sum, value_sum, output_sum, all_gu, all_down,
    sums, rows, returned, square, kv, hidden_grad, result, branch, grads, delta, query_grad, turned,
    for_mate, from_mate, kv_sums, kv_rows, key_value, normed_other, query_other, key_value_other,
    hidden, ffn_in, cot, tokens, normed, key_raw, mixed_t, queries, log_total, share_gu, share_down,
    held, final_output, final_query, final_keys, land_output, land_query, land_keys, work, late_values, late_rows,
    rs_send, rs_recv, mate_send, mate_recv, kv_send, kv_recv, ar_send, ar_recv, small_send, small_recv, load_sem, out_sem, ex_send, ex_recv, pair_send, pair_recv,
):
    torus = Torus()
    here, device = everywhere()
    me = here["x"] * 2 + here["core"]
    barrier = pltpu.get_barrier_semaphore()
    peers = [device("core", 1)] + [device(axis, d) for axis in "xyz" for d in (1, 2, 3)]
    for peer in peers:
        pl.semaphore_signal(barrier, inc=1, device_id=peer, device_id_type=MESH)
    wanted = (
        ((returned_all, returned), (ffn_in_all, ffn_in), (hidden_all, hidden), (cot_all, cot)),
        ((w_output, square), (mixed_t_all, mixed_t), (queries_all, queries), (log_total_all, log_total)),
        ((normed_all, normed), (kv_all, kv), (own_gu, share_gu), (own_down, share_down)),
        ((mixed_parts, sums), (tokens_all, tokens), (key_raw_all, key_raw)),
    )
    loads, number = [], 0
    for group in wanted:
        loads.append([])
        for source, target in group:
            loads[-1].append(pltpu.make_async_copy(source, target, load_sem.at[number]))
            loads[-1][-1].start()
            number += 1

    order = (2, 1, -1, 0)
    leads = []
    for n, d in enumerate(order):
        leads.append(Scatter(torus, sums, rows, rs_send, rs_recv, n, n * 384, "z", d, 0, 64, 64, mixed_parts))
        leads.append(Scatter(torus, sums, rows, rs_send, rs_recv, 4 + n, (5 + n) * 384, "y", d, 128, 64, 64, mixed_parts))
    lasts = [
        Scatter(torus, sums, rows, rs_send, rs_recv, 8, 4 * 384, "y", 0, 0, 64, 64),
        Scatter(torus, sums, rows, rs_send, rs_recv, 9, 9 * 384, "z", 0, 128, 64, 64),
    ]
    ring = Scatter(Line(here, device), kv_sums, kv_rows, kv_send, kv_recv, 0, 0, "x", 0, 0, 512, 512)
    experts = [
        Keys(here, device, blocks, ex_send.at[n], ex_recv.at[n], origin)
        for n, (blocks, origin) in enumerate(((all_gu, own_gu), (all_down, own_down)))
    ]
    pl.semaphore_wait(barrier, len(peers))
    for one in leads:
        one.first()
    for one in experts:
        one.start(0, 1, 2)

    def to_other(number, source, target):
        return pltpu.make_async_remote_copy(
            src_ref=source,
            dst_ref=target,
            send_sem=pair_send.at[number],
            recv_sem=pair_recv.at[number],
            device_id=device("core", 1),
            device_id_type=MESH,
        )

    own_half = pl.ds(pl.multiple_of(here["core"] * 512, 512), 512)
    other_half = pl.ds(pl.multiple_of((1 - here["core"]) * 512, 512), 512)
    pairs = [
        to_other(0, normed, normed_other),
        to_other(1, branch.at[:, other_half], query_other),
        to_other(2, key_value.at[:, other_half], key_value_other),
    ]
    for load in loads[0]:
        load.wait()

    expert_rows = lax.broadcasted_iota(jnp.int32, (EXPERTS, ROWS), 0)
    member = jnp.zeros((EXPERTS, ROWS), jnp.float32)
    for k in range(TOPK):
        member = member + jnp.where(expert_rows == routes_t[pl.ds(k, 1), :], 1.0, 0.0)
    named = member > 0.5
    logits = jnp.where(named, dot_nt(router_rows[...], ffn_in[...]), -1e30)
    weight = jnp.where(named, jnp.exp(logits - jnp.max(logits, axis=0, keepdims=True)), 0.0)
    gates = weight / jnp.sum(weight, axis=0, keepdims=True)
    gate_grad = jnp.concatenate([returned[:8, q * ROWS : (q + 1) * ROWS] for q in range(4)], axis=0)
    logit_grad = (gates * (gate_grad - jnp.sum(gates * gate_grad, axis=0, keepdims=True))).astype(jnp.bfloat16)
    result[...] = dot_tn(logit_grad, router_rows[...])
    router_grad = dot_nn(logit_grad, ffn_in[...]).astype(jnp.bfloat16)
    for q in range(4):
        held[2048 + q * EXPERTS : 2048 + (q + 1) * EXPERTS] = router_grad[:, q * 256 : (q + 1) * 256]

    def ffn_part(n, gain_grad):
        at = pl.ds(pl.multiple_of(n * 64, 64), 64)
        grad = result[at] + returned[pl.ds(pl.multiple_of(n * 64 + EXTRA, 16), 64)]
        part, more = rms_back(hidden[at], as_row(ffn_gain), grad)
        part = part + cot[at].astype(jnp.float32)
        hidden_grad[at] = part
        branch[at] = part.astype(jnp.bfloat16)
        return gain_grad + more

    gain_grad = lax.fori_loop(0, 4, ffn_part, jnp.zeros((1, 1024), jnp.float32))
    gain_lines = [gain_grad[:, q * 256 : (q + 1) * 256] for q in range(4)] + [jnp.zeros((124, 256), jnp.float32)]
    held[2176:2304] = jnp.concatenate(gain_lines, axis=0).astype(jnp.bfloat16)
    held[4352:4608] = jnp.zeros((256, 256), jnp.bfloat16)

    for load in [*loads[1], *loads[2]]:
        load.wait()
    pairs[0].start()
    owns = [
        pltpu.make_async_copy(share_gu, all_gu.at[me], load_sem.at[19]),
        pltpu.make_async_copy(share_down, all_down.at[me], load_sem.at[20]),
    ]
    for copy in owns:
        copy.start()
    turned[...] = dot_nt(square[...], branch[...])
    next_load = pltpu.make_async_copy(w_query, square, load_sem.at[15])
    next_load.start()
    query_raw = returned.at[pl.ds(0, ROWS)]
    raw_load = pltpu.make_async_copy(query_raw_all, query_raw, load_sem.at[16])
    raw_load.start()

    for j in range(KV_HEADS):
        for r in range(2):
            at = slice(j * 128 + r * 64, j * 128 + r * 64 + 64)
            low = turned[at].astype(jnp.bfloat16)
            grads[j, :, r * ROWS : (r + 1) * ROWS] = low
            delta[j, :, r * ROWS : (r + 1) * ROWS] = jnp.sum(
                low.astype(jnp.float32) * mixed_t[at].astype(jnp.float32), axis=0, keepdims=True
            )
        query_grad[j] = jnp.zeros((HEAD_DIM, 2 * ROWS), jnp.float32)

    @pl.loop(0, 4)
    def _(n):
        at = pl.ds(pl.multiple_of(n * 256, 256), 256)
        part = dot_nn(mixed_t[at], branch[...]).astype(jnp.bfloat16)
        for q in range(4):
            held[pl.ds(pl.multiple_of(q * 1024 + q // 2 * 256 + n * 256, 256), 256)] = part[:, q * 256 : (q + 1) * 256]

    def reduction(number, buffer, shift, final, land, half, begin):
        return [
            Total(here, device, buffer, shift, final, land, work, ar_send, ar_recv, 3 * number + s, s, half, begin)
            for s in range(3)
        ]

    early = reduction(0, held, 0, final_output, land_output, 2304, 0)
    of_query = reduction(1, kv, 0, final_query, land_query, 2048, 1)
    of_keys = reduction(2, kv, 4096, final_keys, land_keys, 2048, 1)
    late_few = Small(device, late_values, late_rows, small_send, small_recv)
    for one in early:
        one.begin(0)
    def onward(streams, stage):
        for one in streams:
            one.finish(stage)
            if stage < 6:
                one.begin(stage + 1)

    def write_out(number, final, first, target, at):
        block = final.at[pl.ds(first, 1024)]
        return pltpu.make_async_copy(block, target.at[:, pl.ds(at * 256, 256)], out_sem.at[number])

    outs = [write_out(q, final_output, q * 1024 + q // 2 * 256, output_sum, q) for q in range(4)]
    outs += [write_out(4 + q, final_query, q * 1024, query_sum, q) for q in range(4)]
    outs += [write_out(8 + q, final_keys, q * 1024, key_sum, q) for q in range(2)]
    outs += [write_out(10 + q, final_keys, (2 + q) * 1024, value_sum, q) for q in range(2)]

    def mate_copy(turn, at):
        return pltpu.make_async_remote_copy(
            src_ref=for_mate.at[turn % 2],
            dst_ref=from_mate.at[at],
            send_sem=mate_send.at[turn],
            recv_sem=mate_recv.at[turn],
            device_id=device("core", 1),
            device_id_type=MESH,
        )

    key_at = lax.broadcasted_iota(jnp.int32, (ROWS, 2 * ROWS), 0)
    query_at = lax.broadcasted_iota(jnp.int32, (ROWS, 2 * ROWS), 1) % ROWS
    valid = (key_at <= query_at) & (key_at + me * ROWS < length[...])

    def block_grads(block, target, at, masked):
        for group in range(2):
            heads = range(4 * group, 4 * group + 4)
            key_heads = [kv[pl.ds(pl.multiple_of(block * 1024 + j * 64, 64), 64)] for j in heads]
            value_heads = [kv[pl.ds(pl.multiple_of(block * 1024 + 512 + j * 64, 64), 64)] for j in heads]
            probs = [jnp.exp(dot_tn(one, queries[j]) - log_total[j]) for one, j in zip(key_heads, heads)]
            if masked:
                probs = [jnp.where(valid, one, 0.0) for one in probs]
            probs_grads = [dot_tn(one, grads[j]) for one, j in zip(value_heads, heads)]
            lows = [
                (one * (grad - delta[j])).astype(jnp.bfloat16) for one, grad, j in zip(probs, probs_grads, heads)
            ]
            key_parts = [dot_nt(queries[j], low).astype(jnp.bfloat16) for low, j in zip(lows, heads)]
            value_parts = [
                dot_nt(grads[j], one.astype(jnp.bfloat16)).astype(jnp.bfloat16) for one, j in zip(probs, heads)
            ]
            query_parts = [dot_nn(one, low) for one, low in zip(key_heads, lows)]
            for n, j in enumerate(heads):
                target[at, j * 64 : j * 64 + 64] = key_parts[n]
                target[at, 512 + j * 64 : 576 + j * 64] = value_parts[n]
                query_grad[j] += query_parts[n]

    def from_other(turn, at):
        mate_copy(turn, at).wait_recv()

        @pl.loop(0, 16)
        def _(n):
            lines = pl.ds(pl.multiple_of(n * 64, 64), 64)
            total = kv_sums[at, lines].astype(jnp.float32) + from_mate[at, lines].astype(jnp.float32)
            kv_sums[at, lines] = total.astype(jnp.bfloat16)

    def turn_x(turn):
        offset = (1 - turn % 2) * (2 + turn // 2) + (turn % 2) * (1 - turn // 2)
        return (here["x"] + offset + RING) % RING

    @pl.loop(0, 4)
    def _(turn):
        @pl.when(turn == 1)
        def _():
            for load in loads[3]:
                load.wait()
            for one in leads:
                one.second()
            for one in experts:
                one.arrive(1)
                one.start(3, 5)
                one.arrive(2)
                one.start(4, 6)

        @pl.when(turn == 2)
        def _():
            onward(early, 0)

        @pl.when(turn == 3)
        def _():
            onward(early, 1)

        at = turn_x(turn)
        other = at * 2 + 1 - here["core"]

        @pl.when(turn >= 2)
        def _():
            mate_copy(turn - 2, at).wait_send()

        @pl.when(other < me)
        def _():
            block_grads(other, for_mate, turn % 2, False)

        @pl.when(other >= me)
        def _():
            for_mate[turn % 2] = jnp.zeros((1024, ROWS), jnp.bfloat16)

        mate_copy(turn, at).start()

        own = at * 2 + here["core"]

        @pl.when(own < me)
        def _():
            block_grads(own, kv_sums, at, False)

        @pl.when(own > me)
        def _():
            kv_sums[at] = jnp.zeros((1024, ROWS), jnp.bfloat16)

        @pl.when(own == me)
        def _():
            block_grads(own, kv_sums, at, True)

        from_other(turn, at)

        @pl.when(turn == 0)
        def _():
            ring.first()

        @pl.when(turn == 2)
        def _():
            ring.second()

    for j in range(KV_HEADS):
        for r in range(2):
            head = query_grad[j, :, r * ROWS : (r + 1) * ROWS] * HEAD_DIM**-0.5
            turned[j * 128 + r * 64 : j * 128 + r * 64 + 64] = turned_back(head, cosine[...], sine[...])

    raw_load.wait()
    result[...] = turned[...].T

    def query_part(n, gain_grad):
        at = pl.ds(pl.multiple_of(n * 64, 64), 64)
        part, more = rms_back(query_raw[at], as_row(query_gain), result[at])
        branch[at] = part.astype(jnp.bfloat16)
        return gain_grad + more

    query_gain_grad = lax.fori_loop(0, 4, query_part, jnp.zeros((1, 1024), jnp.float32))

    def half_of_columns(raw, raw_other, shift):
        both = jnp.concatenate([raw[:, own_half], raw_other[...]], axis=0)

        @pl.loop(0, 4)
        def _(n):
            columns = pl.ds(pl.multiple_of(n * 256, 256), 256)
            left = jnp.concatenate([normed[:, columns], normed_other[:, columns]], axis=0)
            part = dot_tn(left, both).astype(jnp.bfloat16)
            for q in range(2):
                first = shift + (here["core"] * 2 + q) * 1024 + n * 256
                kv[pl.ds(pl.multiple_of(first, 256), 256)] = part[:, q * 256 : (q + 1) * 256]

    pairs[1].start()
    onward(early, 2)
    for one in experts:
        one.arrive(3, 4)
        one.start(7)
    pairs[0].wait_recv()
    pairs[1].wait_recv()
    half_of_columns(branch, query_other, 0)
    for one in of_query:
        one.begin(1)

    def put(at, total):
        turned[at] = total

    ring.third(put)
    for j in range(KV_HEADS):
        turned[j * 64 : j * 64 + 64] = turned_back(turned[j * 64 : j * 64 + 64], cosine[...], sine[...])
    part, key_gain_grad = rms_back(key_raw[...], as_row(key_gain), turned[:512].T)
    key_value[:, :512] = part.astype(jnp.bfloat16)
    key_value[:, 512:] = turned[512:].T.astype(jnp.bfloat16)
    pairs[2].start()
    pairs[2].wait_recv()
    half_of_columns(key_value, key_value_other, 4096)
    for one in of_keys:
        one.begin(1)

    next_load.wait()
    result[...] = dot_nt(branch[...], square[...])
    last_loads = [
        pltpu.make_async_copy(w_key, square.at[:, pl.ds(0, 512)], load_sem.at[17]),
        pltpu.make_async_copy(w_value, square.at[:, pl.ds(512, 512)], load_sem.at[18]),
    ]
    for load in last_loads:
        load.start()
    onward(of_query, 1)
    for load in last_loads:
        load.wait()
    result[...] += dot_nt(key_value[...], square[...])

    def token_part(n, gain_grad):
        at = pl.ds(pl.multiple_of(n * 64, 64), 64)
        part, more = rms_back(tokens[at].astype(jnp.float32), as_row(attn_gain), result[at])
        token_grad[at] = (hidden_grad[at] + part).astype(jnp.bfloat16)
        return gain_grad + more

    attn_gain_grad = lax.fori_loop(0, 4, token_part, jnp.zeros((1, 1024), jnp.float32))
    key_wide = jnp.concatenate([key_gain_grad, jnp.zeros((1, 512), jnp.float32)], axis=1)
    late_values[0] = jnp.concatenate(
        [attn_gain_grad, query_gain_grad, key_wide, jnp.zeros((5, 1024), jnp.float32)], axis=0
    )
    late_few.begin(0)
    onward(of_keys, 1)
    onward(early, 3)
    for stage in range(2, 5):
        onward(of_query, stage)
        late_few.finish(stage - 2)
        late_few.begin(stage - 1)
        onward(of_keys, stage)
        onward(early, stage + 2)
        if stage == 2:
            for one in leads:
                one.third()
            for one in lasts:
                one.first()
        if stage == 4:
            for one in lasts:
                one.second()
    for q in range(4):
        outs[q].start()
    late_few.finish(3)
    late_small[...] = late_values[4]
    router = [final_output[2048 + q * EXPERTS : 2048 + (q + 1) * EXPERTS].astype(jnp.float32) for q in range(4)]
    lines = final_output[2176:2192].astype(jnp.float32)
    lines = jnp.concatenate([lines[q : q + 1] for q in range(4)], axis=1)
    early_small[...] = jnp.concatenate(
        [jnp.concatenate(router, axis=1), lines, jnp.zeros((7, 1024), jnp.float32)], axis=0
    )

    def put_mixed(at, total):
        mixed_out[at] = (hidden[at] + total).astype(jnp.bfloat16)

    for stage in range(5, 7):
        onward(of_query, stage)
        onward(of_keys, stage)
        if stage == 6:
            for one in lasts:
                one.third(put_mixed)
    for q in range(4, 12):
        outs[q].start()
    for one in experts:
        one.arrive(0, 5, 6, 7)
    for one in [*experts, *leads, *lasts, ring, *early, *of_query, *of_keys, late_few]:
        one.drain()
    for turn in (2, 3):
        mate_copy(turn, 0).wait_send()
    for pair in pairs:
        pair.wait_send()
    for out in [*outs, *owns]:
        out.wait()


def backward(smalls, larges):
    vmem, hbm = pl.BlockSpec(memory_space=pltpu.VMEM), pl.BlockSpec(memory_space=pl.ANY)
    low, wide = jnp.bfloat16, jnp.float32
    shape = jax.ShapeDtypeStruct
    dma = pltpu.SemaphoreType.DMA
    return pl.pallas_call(
        backward_kernel,
        name="backward",
        out_shape=(
            shape((ROWS, 1024), low),
            shape((ROWS, 1024), low),
            shape((40, 1024), wide),
            shape((8, 1024), wide),
            shape((1024, 1024), low),
            shape((1024, 512), low),
            shape((1024, 512), low),
            shape((1024, 1024), low),
            shape((8, 256, 1024), low),
            shape((8, 128, 1024), low),
        ),
        in_specs=[vmem] * len(smalls) + [hbm] * len(larges),
        out_specs=(vmem,) * 4 + (hbm,) * 6,
        scratch_shapes=[
            pltpu.VMEM((16, ROWS, 1024), low),
            pltpu.VMEM((10 * 384, 1024), low),
            pltpu.VMEM((FULL, 1024), wide),
            pltpu.VMEM((1024, 1024), low),
            pltpu.VMEM((8 * 1024, ROWS), low),
            pltpu.VMEM((ROWS, 1024), wide),
            pltpu.VMEM((ROWS, 1024), wide),
            pltpu.VMEM((ROWS, 1024), low),
            pltpu.VMEM((KV_HEADS, HEAD_DIM, 2 * ROWS), low),
            pltpu.VMEM((KV_HEADS, 1, 2 * ROWS), wide),
            pltpu.VMEM((KV_HEADS, HEAD_DIM, 2 * ROWS), wide),
            pltpu.VMEM((1024, ROWS), wide),
            pltpu.VMEM((2, 1024, ROWS), low),
            pltpu.VMEM((4, 1024, ROWS), low),
            pltpu.VMEM((4, 1024, ROWS), low),
            pltpu.VMEM((3072, ROWS), low),
            pltpu.VMEM((ROWS, 1024), low),
            pltpu.VMEM((ROWS, 1024), low),
            pltpu.VMEM((ROWS, 512), low),
            pltpu.VMEM((ROWS, 512), low),
            pltpu.VMEM((ROWS, 1024), wide),
            pltpu.VMEM((ROWS, 1024), low),
            pltpu.VMEM((ROWS, 1024), low),
            pltpu.VMEM((ROWS, 1024), low),
            pltpu.VMEM((ROWS, 1024), low),
            pltpu.VMEM((ROWS, 512), wide),
            pltpu.VMEM((1024, ROWS), low),
            pltpu.VMEM((KV_HEADS, HEAD_DIM, 2 * ROWS), low),
            pltpu.VMEM((KV_HEADS, 1, 2 * ROWS), wide),
            pltpu.VMEM((256, 1024), low),
            pltpu.VMEM((128, 1024), low),
            pltpu.VMEM((4608, 256), low),
            pltpu.VMEM((4608, 256), low),
            pltpu.VMEM((4096, 256), low),
            pltpu.VMEM((4096, 256), low),
            pltpu.VMEM((4896, 256), low),
            pltpu.VMEM((2304, 256), low),
            pltpu.VMEM((2304, 256), low),
            pltpu.VMEM((9, 48, 256), low),
            pltpu.VMEM((5, 8, 1024), wide),
            pltpu.VMEM((10, 8, 1024), wide),
            dma((10, 4)),
            dma((10, 4)),
            dma((4,)),
            dma((4,)),
            dma((1, 4)),
            dma((1, 4)),
            dma((9, 17)),
            dma((9, 17)),
            dma((10,)),
            dma((10,)),
            dma((21,)),
            dma((12,)),
            dma((2, 8)),
            dma((2, 8)),
            dma((3,)),
            dma((3,)),
        ],
        compiler_params=pltpu.CompilerParams(
            collective_id=4, has_side_effects=True, vmem_limit_bytes=66000000
        ),
        cost_estimate=pl.CostEstimate(flops=100 * 10**9, bytes_accessed=60 * 10**6, transcendentals=8 * 10**6),
    )(*smalls, *larges)


def widen_kernel(
    early, late, mixed, tokens, query, key, value, output, gate_up, down,
    ffn_gain, attn_gain, query_gain, key_gain, router,
    mixed_out, token_out, query_out, key_out, value_out, output_out, gate_out, up_out, down_out,
    query_in, key_in, value_in, output_in, gate_up_in, down_in,
    query_wide, key_wide, value_wide, output_wide, gate_up_wide, down_wide,
    in_sem, out_sem,
):
    arrays = (
        (query, query_in, query_wide, query_out),
        (output, output_in, output_wide, output_out),
        (key, key_in, key_wide, key_out),
        (value, value_in, value_wide, value_out),
    )
    parts = []
    for source, low, wide, target in arrays:
        for n in range(0, 1024, 512):
            at = pl.ds(n, 512)
            parts.append((source.at[at], low.at[at], wide.at[at], [(wide.at[at], target.at[at])]))
    for block in range(8):
        rows, e = pl.ds(block // 2 * 256, 256), block % 2
        wide = gate_up_wide.at[block]
        targets = [
            (wide.at[:, pl.ds(0, 512)], gate_out.at[e, rows]),
            (wide.at[:, pl.ds(512, 512)], up_out.at[e, rows]),
        ]
        parts.append((gate_up.at[block], gate_up_in.at[block], wide, targets))
    for block in range(8):
        wide = down_wide.at[block]
        target = down_out.at[block % 2, pl.ds(block // 2 * 128, 128)]
        parts.append((down.at[block], down_in.at[block], wide, [(wide, target)]))
    loads = [pltpu.make_async_copy(source, low, in_sem.at[n]) for n, (source, low, _, _) in enumerate(parts)]
    for load in loads:
        load.start()
    ffn_gain[...] = early[EXPERTS]
    attn_gain[...] = late[0]
    query_gain[...] = late[1]
    key_gain[...] = late[2, :512]
    router[...] = early[:EXPERTS]
    mixed_out[...] = mixed[...]
    token_out[...] = tokens[...]
    stores = []
    for load, (_, low, wide, targets) in zip(loads, parts):
        load.wait()

        @pl.loop(0, low.shape[0] // 32)
        def _(n):
            at = pl.ds(pl.multiple_of(n * 32, 32), 32)
            wide[at] = low[at].astype(jnp.float32)

        for source, target in targets:
            stores.append(pltpu.make_async_copy(source, target, out_sem.at[len(stores)]))
            stores[-1].start()
    for copy in stores:
        copy.wait()


def widen(arrays):
    vmem, hbm = pl.BlockSpec(memory_space=pltpu.VMEM), pl.BlockSpec(memory_space=pl.ANY)
    low, wide = jnp.bfloat16, jnp.float32
    shape = jax.ShapeDtypeStruct
    held = ((1024, 1024), (1024, 512), (1024, 512), (1024, 1024), (8, 256, 1024), (8, 128, 1024))
    return pl.pallas_call(
        widen_kernel,
        name="widen",
        out_shape=(
            shape((1024,), wide),
            shape((1024,), wide),
            shape((1024,), wide),
            shape((512,), wide),
            shape((EXPERTS, 1024), wide),
            shape((ROWS, 1024), low),
            shape((ROWS, 1024), low),
            shape((1024, 1024), wide),
            shape((1024, 512), wide),
            shape((1024, 512), wide),
            shape((1024, 1024), wide),
            shape((2, 1024, 512), wide),
            shape((2, 1024, 512), wide),
            shape((2, 512, 1024), wide),
        ),
        in_specs=[vmem] * 4 + [hbm] * 6,
        out_specs=(vmem,) * 7 + (hbm,) * 7,
        scratch_shapes=[
            *[pltpu.VMEM(size, low) for size in held],
            *[pltpu.VMEM(size, wide) for size in held],
            pltpu.SemaphoreType.DMA((24,)),
            pltpu.SemaphoreType.DMA((32,)),
        ],
        compiler_params=pltpu.CompilerParams(vmem_limit_bytes=56 * 2**20),
    )(*arrays)


def body(
    tokens,
    cotangent,
    lengths,
    routes,
    attn_gain,
    w_query,
    w_key,
    w_value,
    query_gain,
    key_gain,
    w_output,
    ffn_gain,
    w_router,
    w_gate,
    w_up,
    w_down,
):
    query_pos = lax.axis_index("dp") * ROWS + jnp.arange(ROWS, dtype=jnp.int32)
    cosine, sine_table = rope_tables(query_pos)
    cosine, sine_table = cosine.T, sine_table.T
    routes_t, length = routes[0].T, lengths.reshape(1, 1)
    gains = [attn_gain, query_gain, key_gain, ffn_gain]
    weights = (w_query, w_key, w_value, w_output)
    router_rows = w_router.T
    ffn_in, hidden, mixed_t, queries, log_total, normed, query_raw, key_raw, kv_all, cot_all = forward(
        tokens[0], cotangent[0], routes_t, length, cosine, sine_table, gains, weights
    )
    returned, mixed_parts, own_gu, own_down = moe(
        ffn_in, cot_all, cotangent[0], router_rows, w_gate, w_up, w_down
    )
    mixed_low, token_low, early_small, late_small, *sums = backward(
        (routes_t, length, cosine, sine_table, *gains, router_rows),
        (
            hidden, ffn_in, cotangent[0], tokens[0], normed, key_raw, mixed_t, queries, log_total, own_gu, own_down,
            returned, query_raw, mixed_parts, kv_all.reshape(8 * 1024, ROWS), *weights,
        ),
    )
    (
        ffn_gain_sum, attn_gain_sum, query_gain_sum, key_gain_sum, router_sum, mixed_out, token_grad,
        query_w_sum, key_w_sum, value_w_sum, output_w_sum, gate_w_sum, up_w_sum, down_w_sum,
    ) = widen((early_small, late_small, mixed_low, token_low, *sums))
    return (
        mixed_out[None],
        token_grad[None],
        attn_gain_sum,
        query_w_sum,
        key_w_sum,
        value_w_sum,
        query_gain_sum,
        key_gain_sum,
        output_w_sum,
        ffn_gain_sum,
        router_sum.T,
        gate_w_sum,
        up_w_sum,
        down_w_sum,
    )


def solution(mesh):
    return jax.shard_map(
        body,
        mesh=mesh,
        in_specs=(
            P("expert", "dp", None),
            P("expert", "dp", None),
            P("expert"),
            P("expert", "dp", None),
            P(),
            P(),
            P(),
            P(),
            P(),
            P(),
            P(),
            P(),
            P(),
            P("expert", None, None),
            P("expert", None, None),
            P("expert", None, None),
        ),
        out_specs=(
            P("expert", "dp", None),
            P("expert", "dp", None),
            P(),
            P(),
            P(),
            P(),
            P(),
            P(),
            P(),
            P(),
            P(),
            P("expert", None, None),
            P("expert", None, None),
            P("expert", None, None),
        ),
        check_vma=False,
    )
```

```python
import math

import jax
import jax.numpy as jnp
from jax import lax
from jax.experimental import pallas as pl
from jax.experimental.pallas import tpu as pltpu
from jax.sharding import PartitionSpec as P

HEADS = 16
KV_HEADS = 8
HEAD_DIM = 64
EXPERTS = 32
TOPK = 8
CAP = 80


epsilon = 1e-06


def rope_tables(positions):
    steps_half = jnp.arange(HEAD_DIM // 2).astype(jnp.float32)
    inverse = jnp.exp(steps_half * (-2.0 * math.log(10000.0) / HEAD_DIM))
    angles = positions.astype(jnp.float32)[:, None] * inverse[None, :]
    return (jnp.cos(angles), jnp.sin(angles))


RING = 4
ROWS = 256
EXTRA = 16
FULL = ROWS + EXTRA
SENT = 192
LEFT = FULL - SENT
BOTH = ROWS + LEFT
GROUP = 4 * CAP
MESH = pl.DeviceIdType.MESH


def dot_nn(a, b):
    return jnp.dot(a, b, preferred_element_type=jnp.float32)


def dot_nt(a, b):
    return lax.dot_general(a, b, (((1,), (1,)), ((), ())), preferred_element_type=jnp.float32)


def dot_tn(a, b):
    return lax.dot_general(a, b, (((0,), (0,)), ((), ())), preferred_element_type=jnp.float32)


def step_of(size):
    return next(step for step in (64, 48, 32, 16) if size % step == 0)


class Torus:
    def __init__(self):
        self.dp = lax.axis_index("dp")
        expert = lax.axis_index("expert")
        self.expert = expert
        self.z, self.y = expert // RING, expert % RING

    def block(self, dz, dy):
        return ((self.z + dz + RING) % RING) * RING + (self.y + dy + RING) % RING

    def near(self, axis, step):
        return (self.dp, self.block(step, 0) if axis == "z" else self.block(0, step))

    def along(self, axis, other, step):
        return self.block(step, other) if axis == "z" else self.block(other, step)

    def neighbours(self):
        return [self.near(axis, step) for axis in "yz" for step in (1, -1)]


ARRIVALS = (
    ((0, 0), (3, 0), (1, 3), (3, 2)),
    ((0, 1), (0, 2), (3, 1), (3, 3)),
    ((0, 3), (2, 0), (2, 1), (2, 3)),
    ((1, 0), (1, 1), (1, 2), (2, 2)),
)


def differences(values):
    found = list(values)
    for level in range(1, len(found)):
        for n in range(len(found) - 1, level - 1, -1):
            found[n] -= found[n - 1]
    return found


def chooses(n):
    return 1, n, n * (n - 1) // 2, n * (n - 1) * (n - 2) // 6


class Gather:
    def __init__(self, torus, buffer, send, recv, number, axis, other, low, first, second, stride):
        self.torus, self.buffer, self.send, self.recv = torus, buffer, send, recv
        self.number, self.axis, self.other, self.stride = number, axis, other, stride
        self.whole, self.front, self.rear = (low, first + second), (low, first), (low + first, second)

    def copy(self, which, offset, part, step):
        at = self.torus.along(self.axis, self.other, offset) * self.stride + part[0]
        rows = self.buffer.at[pl.ds(pl.multiple_of(at, 16), part[1])]
        return pltpu.make_async_remote_copy(
            src_ref=rows,
            dst_ref=rows,
            send_sem=self.send.at[self.number, which],
            recv_sem=self.recv.at[self.number, which],
            device_id=self.torus.near(self.axis, step),
            device_id_type=MESH,
        )

    def first(self):
        self.copy(0, 0, self.whole, 1).start()
        self.copy(1, 0, self.whole, -1).start()

    def second(self):
        self.copy(0, -1, self.whole, 1).wait_recv()
        self.copy(2, -1, self.front, 1).start()
        self.copy(1, 1, self.whole, -1).wait_recv()
        self.copy(3, 1, self.rear, -1).start()

    def third(self):
        self.copy(2, 2, self.front, 1).wait_recv()
        self.copy(3, 2, self.rear, -1).wait_recv()

    def drain(self):
        self.copy(0, 0, self.whole, 1).wait_send()
        self.copy(1, 0, self.whole, -1).wait_send()
        self.copy(2, -1, self.front, 1).wait_send()
        self.copy(3, 1, self.rear, -1).wait_send()


class Scatter:
    def __init__(self, torus, sums, landing, send, recv, number, base, axis, other, low, first, second, origin=None):
        self.torus, self.sums, self.landing, self.send, self.recv = torus, sums, landing, send, recv
        self.number, self.axis, self.other = number, axis, other
        self.origin = sums if origin is None else origin
        self.low, self.parts = low, (first, second)
        self.size = first + second
        self.slots = (base, base + first, base + self.size, base + 2 * self.size)

    def rows(self, which):
        if which == 0:
            return self.low, self.parts[0]
        if which == 1:
            return self.low + self.parts[0], self.parts[1]
        return self.low, self.size

    def at(self, offset):
        return self.torus.along(self.axis, self.other, offset)

    def copy(self, which):
        start, size = self.rows(which)
        offset = (2, 2, 1, -1)[which]
        return pltpu.make_async_remote_copy(
            src_ref=(self.origin if which < 2 else self.sums).at[self.at(offset), pl.ds(start, size)],
            dst_ref=self.landing.at[pl.ds(self.slots[which], size)],
            send_sem=self.send.at[self.number, which],
            recv_sem=self.recv.at[self.number, which],
            device_id=self.torus.near(self.axis, (1, -1, 1, -1)[which]),
            device_id_type=MESH,
        )

    def add(self, which, offset):
        start, size = self.rows(which)
        block = self.at(offset)

        many = step_of(size)

        @pl.loop(0, size // many)
        def _(k):
            here = pl.ds(pl.multiple_of(start + k * many, 16), many)
            there = pl.ds(pl.multiple_of(self.slots[which] + k * many, 16), many)
            total = self.sums[block, here].astype(jnp.float32) + self.landing[there].astype(jnp.float32)
            self.sums[block, here] = total.astype(jnp.bfloat16)

    def first(self):
        self.copy(0).start()
        self.copy(1).start()

    def second(self):
        self.copy(0).wait_recv()
        self.add(0, 1)
        self.copy(2).start()
        self.copy(1).wait_recv()
        self.add(1, -1)
        self.copy(3).start()

    def third(self, put=None):
        self.copy(2).wait_recv()
        self.copy(3).wait_recv()
        block = self.at(0)

        many = step_of(self.size)

        @pl.loop(0, self.size // many)
        def _(k):
            here = pl.ds(pl.multiple_of(self.low + k * many, 16), many)
            left = pl.ds(pl.multiple_of(self.slots[2] + k * many, 16), many)
            right = pl.ds(pl.multiple_of(self.slots[3] + k * many, 16), many)
            total = (
                self.sums[block, here].astype(jnp.float32)
                + self.landing[left].astype(jnp.float32)
                + self.landing[right].astype(jnp.float32)
            )
            if put is None:
                self.sums[block, here] = total.astype(jnp.bfloat16)
            else:
                put(here, total)

    def drain(self):
        for which in range(4):
            self.copy(which).wait_send()


def moe_kernel(
    ffn, cot, own_cot, wr, w_gate, w_up, w_down,
    ret, mixed, own_gu, own_down,
    rows, sums, wgu, wd, held, pair, inner, dgu, mixing, back, cotv, before, chosen, gate_rows, grad_rows, stage,
    mate_rows, gu_sums, down_sums,
    ag_send, ag_recv, rs_send, rs_recv, w_sem, cot_sem, own_sem, stage_sem, mate_send, mate_recv, x_send, x_recv, credit,
):
    torus = Torus()
    place, place_of = everywhere()
    barrier = pltpu.get_barrier_semaphore()
    peers = [*torus.neighbours(), place_of("core", 1), place_of("x", 1), place_of("x", -1)]
    for device in peers:
        pl.semaphore_signal(barrier, inc=1, device_id=device, device_id_type=MESH)

    weights = [
        pltpu.make_async_copy(w_gate, wgu.at[:, :, pl.ds(0, 512)], w_sem.at[0]),
        pltpu.make_async_copy(w_up, wgu.at[:, :, pl.ds(512, 512)], w_sem.at[1]),
        pltpu.make_async_copy(w_down, wd, w_sem.at[2]),
    ]
    for copy in weights:
        copy.start()

    def source_of(g, j):
        of_g, of_j = chooses(g), chooses(j)
        offsets = []
        for axis in range(2):
            table = [differences([at[axis] for at in line]) for line in ARRIVALS]
            table = [differences(column) for column in zip(*table)]
            offsets.append(sum(table[a][b] * of_g[a] * of_j[b] for a in range(4) for b in range(4) if table[a][b]))
        return torus.block(*offsets)

    def cot_copy(g, j):
        at = pl.multiple_of(source_of(g, j) * SENT, 16)
        return pltpu.make_async_copy(cot.at[pl.ds(at, SENT)], cotv.at[pl.ds(j * SENT, SENT)], cot_sem.at[j])

    for j in range(4):
        cot_copy(0, j).start()
    first_row = torus.expert * BOTH
    own_copy = pltpu.make_async_copy(
        own_cot.at[pl.ds(ROWS - LEFT, LEFT)], rows.at[pl.ds(pl.multiple_of(first_row + ROWS, 16), LEFT)], own_sem
    )
    own_copy.start()
    rows[pl.ds(pl.multiple_of(first_row, 16), ROWS)] = ffn[...]
    own_copy.wait()
    pl.semaphore_wait(barrier, len(peers))

    def gather(number, axis, other, low, first, second):
        return Gather(torus, rows, ag_send, ag_recv, number, axis, other, low, first, second, BOTH)

    a_first = gather(0, "y", 0, 0, 96, 80)
    b_first = gather(1, "z", 0, 176, 80, 80)
    a_second = {d: gather(2 + d % RING, "z", d, 0, 96, 80) for d in (0, 1, -1, 2)}
    b_second = {d: gather(6 + d % RING, "y", d, 176, 80, 80) for d in (0, 1, -1, 2)}
    gathers = [a_first, b_first, *a_second.values(), *b_second.values()]

    a_first.first()
    b_first.first()
    b_second[0].first()
    a_second[0].first()
    a_first.second()
    b_first.second()
    b_second[0].second()
    a_second[0].second()
    for d in (1, -1):
        b_second[d].first()
        a_second[d].first()
    for copy in weights:
        copy.wait()

    earlier = lax.broadcasted_iota(jnp.int32, (ROWS, ROWS), 0) < lax.broadcasted_iota(jnp.int32, (ROWS, ROWS), 1)
    before[...] = jnp.where(earlier, 1.0, 0.0).astype(jnp.bfloat16)
    slot_at = lax.broadcasted_iota(jnp.int32, (CAP, ROWS), 0).astype(jnp.float32)

    def stage_copy(slot, target):
        return pltpu.make_async_copy(stage.at[slot], target, stage_sem.at[slot])

    expert_rows = lax.broadcasted_iota(jnp.int32, (EXPERTS, ROWS), 0)
    order = (2, 1, -1, 0)
    a_lead = {
        d: Scatter(torus, sums, rows, rs_send, rs_recv, n, n * 384, "z", d, 0, 64, 64) for n, d in enumerate(order)
    }
    b_lead = {
        d: Scatter(torus, sums, rows, rs_send, rs_recv, 4 + n, 1920 + n * 432, "y", d, 128, 80, 64)
        for n, d in enumerate(order)
    }
    a_last = Scatter(torus, sums, rows, rs_send, rs_recv, 8, 4 * 384, "y", 0, 0, 64, 64)
    b_last = Scatter(torus, sums, rows, rs_send, rs_recv, 9, 1920 + 4 * 432, "z", 0, 128, 80, 64)

    @pl.loop(0, 4)
    def _(g):
        @pl.when(g == 1)
        def _():
            a_first.third()
            b_first.third()
            b_second[2].first()
            a_second[2].first()
            b_second[0].third()
            a_second[0].third()
            for d in (1, -1):
                b_second[d].second()
                a_second[d].second()

        @pl.when(g == 2)
        def _():
            b_second[2].second()
            a_second[2].second()
            b_second[1].third()
            a_second[1].third()

        @pl.when(g == 3)
        def _():
            for d in (-1, 2):
                b_second[d].third()
                a_second[d].third()

        for j in range(4):
            cot_copy(g, j).wait()

        @pl.loop(0, 4)
        def _(j):
            source = source_of(g, j)
            block = rows[pl.ds(pl.multiple_of(source * BOTH, 16), ROWS)]
            laid = cotv[pl.ds(pl.multiple_of(j * SENT, 16), EXTRA)].astype(jnp.float32)
            member = jnp.concatenate([laid[:8, q * ROWS : (q + 1) * ROWS] for q in range(4)], axis=0)
            named = member > 0.5
            slots = dot_nn(member.astype(jnp.bfloat16), before[...])
            slots = jnp.where(named, slots, -1.0)
            logits = jnp.where(named, dot_nt(wr[...], block), -1e30)
            weight = jnp.where(named, jnp.exp(logits - jnp.max(logits, axis=0, keepdims=True)), 0.0)
            gates = weight / jnp.sum(weight, axis=0, keepdims=True)
            picked = []
            for e in range(2):
                own = jnp.sum(
                    jnp.where(expert_rows == torus.expert * 2 + e, slots, 0.0), axis=0, keepdims=True
                )
                picked.append(jnp.where(slot_at == own, 1.0, 0.0))
            both = jnp.concatenate(picked, axis=0).astype(jnp.bfloat16)
            chosen[j] = both
            grad_block = jnp.concatenate(
                [
                    cotv[pl.ds(pl.multiple_of(j * SENT + EXTRA, 16), SENT - EXTRA)],
                    rows[pl.ds(pl.multiple_of(source * BOTH + ROWS, 16), LEFT)],
                ],
                axis=0,
            )
            took = dot_nn(both, jnp.concatenate([block, grad_block], axis=1)).astype(jnp.bfloat16)
            here = pl.ds(pl.multiple_of(j * CAP, 16), CAP)
            there = pl.ds(pl.multiple_of(g * GROUP + j * CAP, 16), CAP)
            for e in range(2):
                own = jnp.sum(
                    jnp.where(expert_rows == torus.expert * 2 + e, gates, 0.0), axis=0, keepdims=True
                )
                of_rows = jnp.sum(picked[e] * own, axis=1, keepdims=True)
                gate_rows[e, here] = jnp.broadcast_to(of_rows, (CAP, 128))
                held[e, there] = took[e * CAP : (e + 1) * CAP, :1024]
                mixing[e, here] = took[e * CAP : (e + 1) * CAP, 1024:]

        @pl.when(g < 3)
        def _():
            for j in range(4):
                cot_copy(g + 1, j).start()

        @pl.when(g == 3)
        def _():
            for one in gathers:
                one.drain()
            for device in peers:
                pl.semaphore_signal(credit, inc=1, device_id=device, device_id_type=MESH)
            pl.semaphore_wait(credit, len(peers))
            for d in (0, 1):
                b_lead[d].first()
                a_lead[d].first()

        @pl.loop(0, 2)
        def _(e):
            there = pl.ds(pl.multiple_of(g * GROUP, 16), GROUP)
            both = dot_nn(held[e, there], wgu[e])
            gate, up = both[:, :512], both[:, 512:]
            sig = jax.nn.sigmoid(gate)
            silu = gate * sig
            act = (silu * up).astype(jnp.bfloat16)
            inner[e, there] = act
            out = dot_nn(act, wd[e]).astype(jnp.bfloat16).astype(jnp.float32)
            grad = mixing[e].astype(jnp.float32)
            weight = gate_rows[e][:, :1]
            grad_rows[e] = jnp.broadcast_to(jnp.sum(grad * out, axis=1, keepdims=True), (GROUP, 128))
            pair[e, there] = (weight * grad).astype(jnp.bfloat16)
            mixing[e] = (weight * out).astype(jnp.bfloat16)
            inner_grad = dot_nt(pair[e, there], wd[e])
            dgu[e, there, :512] = (inner_grad * up * sig * (1.0 + gate * (1.0 - sig))).astype(jnp.bfloat16)
            dgu[e, there, 512:] = (inner_grad * silu).astype(jnp.bfloat16)
            back[e] = dot_nt(dgu[e, there], wgu[e]).astype(jnp.bfloat16)

        @pl.when(g == 3)
        def _():
            for d in (0, 1):
                b_lead[d].second()
                a_lead[d].second()

        @pl.loop(0, 4)
        def _(j):
            source = source_of(g, j)
            both = chosen[j]
            picked = both.astype(jnp.float32)
            here = pl.ds(pl.multiple_of(j * CAP, 16), CAP)
            compact = jnp.concatenate(
                [jnp.concatenate([back[e, here], mixing[e, here]], axis=1) for e in range(2)], axis=0
            )
            spread = dot_tn(both, compact).astype(jnp.bfloat16)
            sums[source, pl.ds(EXTRA, ROWS)] = spread[:, :1024]
            grads = jnp.zeros((EXPERTS, ROWS), jnp.float32)
            for e in range(2):
                own = jnp.sum(
                    picked[e * CAP : (e + 1) * CAP] * grad_rows[e, here][:, :1], axis=0, keepdims=True
                )
                grads = grads + jnp.where(expert_rows == torus.expert * 2 + e, own, 0.0)
            laid = jnp.concatenate([grads[8 * q : 8 * q + 8] for q in range(4)], axis=1)
            sums[source, pl.ds(0, EXTRA)] = jnp.concatenate([laid, jnp.zeros_like(laid)], axis=0).astype(
                jnp.bfloat16
            )
            slot = j % 2

            @pl.when((g > 0) | (j > 1))
            def _():
                stage_copy(slot, mixed.at[source]).wait()

            stage[slot] = spread[:, 1024:]
            stage_copy(slot, mixed.at[source]).start()

    def chunk(e, k):
        if k < 4:
            return dot_tn(held[e, :, k * 256 : (k + 1) * 256], dgu[e]).astype(jnp.bfloat16)
        return dot_tn(inner[e, :, (k - 4) * 256 : (k - 3) * 256], pair[e]).astype(jnp.bfloat16)

    def mate_copy(k):
        return pltpu.make_async_remote_copy(
            src_ref=stage.at[k % 2],
            dst_ref=mate_rows.at[pl.ds(k * 256, 256)],
            send_sem=mate_send.at[k],
            recv_sem=mate_recv.at[k],
            device_id=place_of("core", 1),
            device_id_type=MESH,
        )

    line = Line(place, place_of)
    rings = [
        Scatter(line, gu_sums, rows, x_send, x_recv, 0, 4080, "x", 0, 0, 128, 128),
        Scatter(line, down_sums, rows, x_send, x_recv, 1, 4848, "x", 0, 0, 64, 64),
    ]

    for d in (2, -1):
        b_lead[d].first()
        a_lead[d].first()
    for k in range(6):
        if k < 2:
            stage_copy(k, mixed.at[0]).wait()
        else:
            mate_copy(k - 2).wait_send()
        stage[k % 2] = chunk(1 - place["core"], k)
        mate_copy(k).start()
        own = chunk(place["core"], k)
        if k < 4:
            gu_sums[k] = own
        else:
            down_sums[2 * k - 8] = own[:128]
            down_sums[2 * k - 7] = own[128:]
    for d in (2, -1):
        b_lead[d].second()
        a_lead[d].second()
    for k in range(6):
        mate_copy(k).wait_recv()

        @pl.loop(0, 4)
        def _(n):
            other = mate_rows[pl.ds(pl.multiple_of(k * 256 + n * 64, 64), 64)].astype(jnp.float32)
            if k < 4:
                at = (k, pl.ds(pl.multiple_of(n * 64, 64), 64))
                gu_sums[at] = (gu_sums[at].astype(jnp.float32) + other).astype(jnp.bfloat16)
            else:
                at = (2 * k - 8 + n // 2, pl.ds(pl.multiple_of(n % 2 * 64, 64), 64))
                down_sums[at] = (down_sums[at].astype(jnp.float32) + other).astype(jnp.bfloat16)

    for one in rings:
        one.first()
    for one in rings:
        one.second()
    for d in order:
        b_lead[d].third()
        a_lead[d].third()
        if d == 2:
            b_last.first()
            a_last.first()
    b_last.second()
    a_last.second()

    def put(at, total):
        ret[at] = total

    b_last.third(put)
    a_last.third(put)

    def put_gu(at, total):
        own_gu[at] = total.astype(jnp.bfloat16)

    def put_down(at, total):
        own_down[at] = total.astype(jnp.bfloat16)

    rings[0].third(put_gu)
    rings[1].third(put_down)
    for one in [*a_lead.values(), *b_lead.values(), a_last, b_last, *rings]:
        one.drain()
    for k in (4, 5):
        mate_copy(k).wait_send()


def moe(ffn_in, cot_all, own_cot, router_rows, w_gate, w_up, w_down):
    vmem, hbm = pl.BlockSpec(memory_space=pltpu.VMEM), pl.BlockSpec(memory_space=pl.ANY)
    low, total = jnp.bfloat16, 4 * GROUP
    return pl.pallas_call(
        moe_kernel,
        name="moe",
        out_shape=(
            jax.ShapeDtypeStruct((FULL, 1024), jnp.float32),
            jax.ShapeDtypeStruct((16, ROWS, 1024), low),
            jax.ShapeDtypeStruct((256, 1024), low),
            jax.ShapeDtypeStruct((128, 1024), low),
        ),
        in_specs=[vmem, hbm, hbm, vmem, hbm, hbm, hbm],
        out_specs=(vmem, hbm, vmem, vmem),
        scratch_shapes=[
            pltpu.VMEM((16 * BOTH, 1024), low),
            pltpu.VMEM((16, FULL, 1024), low),
            pltpu.VMEM((2, 1024, 1024), low),
            pltpu.VMEM((2, 512, 1024), low),
            pltpu.VMEM((2, total, 1024), low),
            pltpu.VMEM((2, total, 1024), low),
            pltpu.VMEM((2, total, 512), low),
            pltpu.VMEM((2, total, 1024), low),
            pltpu.VMEM((2, GROUP, 1024), low),
            pltpu.VMEM((2, GROUP, 1024), low),
            pltpu.VMEM((4 * SENT, 1024), low),
            pltpu.VMEM((ROWS, ROWS), low),
            pltpu.VMEM((4, 2 * CAP, ROWS), low),
            pltpu.VMEM((2, GROUP, 128), jnp.float32),
            pltpu.VMEM((2, GROUP, 128), jnp.float32),
            pltpu.VMEM((2, ROWS, 1024), low),
            pltpu.VMEM((6 * 256, 1024), low),
            pltpu.VMEM((4, 256, 1024), low),
            pltpu.VMEM((4, 128, 1024), low),
            pltpu.SemaphoreType.DMA((10, 4)),
            pltpu.SemaphoreType.DMA((10, 4)),
            pltpu.SemaphoreType.DMA((10, 4)),
            pltpu.SemaphoreType.DMA((10, 4)),
            pltpu.SemaphoreType.DMA((3,)),
            pltpu.SemaphoreType.DMA((4,)),
            pltpu.SemaphoreType.DMA,
            pltpu.SemaphoreType.DMA((2,)),
            pltpu.SemaphoreType.DMA((6,)),
            pltpu.SemaphoreType.DMA((6,)),
            pltpu.SemaphoreType.DMA((2, 4)),
            pltpu.SemaphoreType.DMA((2, 4)),
            pltpu.SemaphoreType.REGULAR,
        ],
        compiler_params=pltpu.CompilerParams(
            collective_id=1, has_side_effects=True, vmem_limit_bytes=63 * 2**20
        ),
        cost_estimate=pl.CostEstimate(flops=50 * 10**9, bytes_accessed=40 * 10**6, transcendentals=2 * 10**6),
    )(ffn_in, cot_all, own_cot, router_rows, w_gate, w_up, w_down)


def everywhere():
    dp, expert = lax.axis_index("dp"), lax.axis_index("expert")
    here = {"x": dp // 2, "core": dp % 2, "z": expert // RING, "y": expert % RING}

    def device(axis, step):
        there = dict(here)
        size = 2 if axis == "core" else RING
        there[axis] = (here[axis] + step + size) % size
        return (there["x"] * 2 + there["core"], there["z"] * RING + there["y"])

    return here, device


def rms_scale(values):
    return lax.rsqrt(jnp.mean(values * values, axis=-1, keepdims=True) + epsilon)


def as_row(gain):
    return gain[...].astype(jnp.float32).reshape(1, -1)


def turned_rows(values, cosine, sine):
    front, back = values[: HEAD_DIM // 2], values[HEAD_DIM // 2 :]
    return jnp.concatenate([front * cosine - back * sine, back * cosine + front * sine], axis=0)


def kv_order(here, step):
    turn = step // 2
    return (turn % 2) * (3 - turn // 2) + (1 - turn % 2) * (turn // 2)


class Keys:
    def __init__(self, here, device, blocks, send, recv, origin=None):
        self.here, self.device, self.blocks, self.send, self.recv = here, device, blocks, send, recv
        self.origin = origin
        self.lines = blocks.shape[1]

    def copy(self, which):
        half = self.lines // 2
        offset, start, size, axis, step = (
            (0, 0, self.lines, "core", 1),
            (0, 0, self.lines, "x", 1),
            (0, 0, self.lines, "x", -1),
            (-1, 0, half, "x", 1),
            (1, half, half, "x", -1),
            (-1, 0, self.lines, "core", 1),
            (1, 0, self.lines, "core", 1),
            (2, 0, self.lines, "core", 1),
        )[which]
        block = (self.here["x"] + offset + RING) % RING * 2 + self.here["core"]
        part = self.blocks.at[block, pl.ds(start, size)]
        return pltpu.make_async_remote_copy(
            src_ref=part if which > 2 or self.origin is None else self.origin,
            dst_ref=part,
            send_sem=self.send.at[which],
            recv_sem=self.recv.at[which],
            device_id=self.device(axis, step),
            device_id_type=MESH,
        )

    def start(self, *which):
        for one in which:
            self.copy(one).start()

    def arrive(self, *which):
        for one in which:
            self.copy(one).wait_recv()

    def drain(self):
        for one in range(8):
            self.copy(one).wait_send()


def forward_kernel(
    tokens, cot, routes_t, length, cosine, sine, attn_gain, query_gain, key_gain, ffn_gain,
    w_query, w_key, w_value, w_output,
    ffn_in, hidden, mixed_t, queries, log_total, normed, query_raw, key_raw, kv_all, cot_all,
    wq, wk, wv, wo, kv, turned, most, total, mixed, packed,
    ag_send, ag_recv, kv_send, kv_recv, w_sem, kv_sem, own_sem,
):
    torus = Torus()
    here, device = everywhere()
    me = here["x"] * 2 + here["core"]
    barrier = pltpu.get_barrier_semaphore()
    peers = [*torus.neighbours(), device("core", 1), device("x", 1), device("x", -1)]
    for peer in peers:
        pl.semaphore_signal(barrier, inc=1, device_id=peer, device_id_type=MESH)
    loads = [
        pltpu.make_async_copy(source, target, w_sem.at[n])
        for n, (source, target) in enumerate(((w_query, wq), (w_key, wk), (w_value, wv), (w_output, wo)))
    ]
    for load in loads:
        load.start()

    expert_rows = lax.broadcasted_iota(jnp.int32, (EXPERTS, ROWS), 0)
    member = jnp.zeros((EXPERTS, ROWS), jnp.float32)
    for k in range(TOPK):
        member = member + jnp.where(expert_rows == routes_t[pl.ds(k, 1), :], 1.0, 0.0)
    laid = jnp.concatenate([member[8 * q : 8 * q + 8] for q in range(4)], axis=1)
    packed[...] = jnp.concatenate([laid, jnp.zeros_like(laid)], axis=0).astype(jnp.bfloat16)
    first_row = pl.multiple_of(torus.expert * SENT, 16)
    owns = [
        pltpu.make_async_copy(packed, cot_all.at[pl.ds(first_row, EXTRA)], own_sem.at[0]),
        pltpu.make_async_copy(
            cot.at[pl.ds(0, SENT - EXTRA)],
            cot_all.at[pl.ds(pl.multiple_of(first_row + EXTRA, 16), SENT - EXTRA)],
            own_sem.at[1],
        ),
    ]
    for copy in owns:
        copy.start()
    for copy in owns:
        copy.wait()
    pl.semaphore_wait(barrier, len(peers))

    def gather(number, axis, other, low, first, second):
        return Gather(torus, cot_all, ag_send, ag_recv, number, axis, other, low, first, second, SENT)

    a_first = gather(0, "y", 0, 0, 48, 48)
    b_first = gather(1, "z", 0, 96, 48, 48)
    a_second = {d: gather(2 + d % RING, "z", d, 0, 48, 48) for d in (0, 1, -1, 2)}
    b_second = {d: gather(6 + d % RING, "y", d, 96, 48, 48) for d in (0, 1, -1, 2)}
    gathers = [a_first, b_first, *a_second.values(), *b_second.values()]
    a_first.first()
    b_first.first()
    b_second[0].first()
    a_second[0].first()

    @pl.loop(0, 4)
    def _(n):
        at = pl.ds(pl.multiple_of(n * 64, 64), 64)
        rows = tokens[at].astype(jnp.float32)
        normed[at] = (rows * rms_scale(rows) * as_row(attn_gain)).astype(jnp.bfloat16)

    for load in loads:
        load.wait()

    keys = Keys(here, device, kv, kv_send, kv_recv)
    key_raw[...] = dot_nn(normed[...], wk[...])
    scaled = key_raw[...]
    scaled = (scaled * rms_scale(scaled) * as_row(key_gain)).T
    for j in range(KV_HEADS):
        head = turned_rows(scaled[j * 64 : j * 64 + 64], cosine[...], sine[...])
        kv[me, pl.ds(j * 64, 64)] = head.astype(jnp.bfloat16)
    kv[me, pl.ds(512, 512)] = dot_nn(normed[...], wv[...]).T.astype(jnp.bfloat16)
    keys.start(0, 1, 2)
    query_raw[...] = dot_nn(normed[...], wq[...])
    scaled = query_raw[...]
    turned[...] = (scaled * rms_scale(scaled) * as_row(query_gain)).T

    for j in range(KV_HEADS):
        for r in range(2):
            head = turned[j * 128 + r * 64 : j * 128 + r * 64 + 64]
            head = turned_rows(head, cosine[...], sine[...])
            queries[j, :, r * ROWS : (r + 1) * ROWS] = (head * HEAD_DIM**-0.5).astype(jnp.bfloat16)

    a_first.second()
    b_first.second()
    for d in (1, -1):
        b_second[d].first()
        a_second[d].first()

    key_at = lax.broadcasted_iota(jnp.int32, (ROWS, 2 * ROWS), 0)
    query_at = lax.broadcasted_iota(jnp.int32, (ROWS, 2 * ROWS), 1) % ROWS
    valid = (key_at <= query_at) & (key_at + me * ROWS < length[...])

    def heads_of(block):
        keys_here = [kv[block, j * 64 : j * 64 + 64] for j in range(KV_HEADS)]
        values_here = [kv[block, 512 + j * 64 : 576 + j * 64] for j in range(KV_HEADS)]
        return keys_here, values_here

    keys_here, values_here = heads_of(me)
    scores = [jnp.where(valid, dot_tn(keys_here[j], queries[j]), -1e30) for j in range(KV_HEADS)]
    tops = [jnp.max(one, axis=0, keepdims=True) for one in scores]
    probs = [jnp.exp(one - top) for one, top in zip(scores, tops)]
    parts = [dot_nn(one, prob.astype(jnp.bfloat16)) for one, prob in zip(values_here, probs)]
    for j in range(KV_HEADS):
        most[j] = tops[j]
        total[j] = jnp.sum(probs[j], axis=0, keepdims=True)
        mixed[j] = parts[j]

    @pl.loop(1, 8)
    def _(step):
        @pl.when(step == 1)
        def _():
            a_first.third()
            b_first.third()
            b_second[2].first()
            a_second[2].first()
            keys.arrive(0)

        @pl.when(step == 2)
        def _():
            b_second[0].second()
            a_second[0].second()
            keys.arrive(1)
            keys.start(3, 5)
            keys.arrive(2)
            keys.start(4, 6)

        @pl.when(step == 3)
        def _():
            for d in (1, -1):
                b_second[d].second()
                a_second[d].second()
            keys.arrive(5)

        @pl.when(step == 5)
        def _():
            keys.arrive(3, 4)
            keys.start(7)
            b_second[2].second()
            a_second[2].second()
            keys.arrive(6)

        @pl.when(step == 7)
        def _():
            keys.arrive(7)

        block = (here["x"] + kv_order(here, step) + RING) % RING * 2 + (here["core"] + step) % 2

        @pl.when(block < me)
        def _():
            keys_here, values_here = heads_of(block)
            before = [most[j] for j in range(KV_HEADS)]
            shares = [total[j] for j in range(KV_HEADS)]
            sums = [mixed[j] for j in range(KV_HEADS)]
            scores = [dot_tn(keys_here[j], queries[j]) for j in range(KV_HEADS)]
            tops = [jnp.maximum(old, jnp.max(one, axis=0, keepdims=True)) for old, one in zip(before, scores)]
            probs = [jnp.exp(one - top) for one, top in zip(scores, tops)]
            less = [jnp.exp(old - top) for old, top in zip(before, tops)]
            parts = [dot_nn(one, prob.astype(jnp.bfloat16)) for one, prob in zip(values_here, probs)]
            for j in range(KV_HEADS):
                most[j] = tops[j]
                total[j] = shares[j] * less[j] + jnp.sum(probs[j], axis=0, keepdims=True)
                mixed[j] = sums[j] * less[j] + parts[j]

    save = pltpu.make_async_copy(kv, kv_all, kv_sem)
    save.start()

    for j in range(KV_HEADS):
        share = total[j]
        log_total[j] = most[j] + jnp.log(share)
        head = (mixed[j] * (1.0 / share)).astype(jnp.bfloat16)
        for r in range(2):
            mixed_t[j * 128 + r * 64 : j * 128 + r * 64 + 64, :] = head[:, r * ROWS : (r + 1) * ROWS]

    hidden[...] = dot_tn(mixed_t[...], wo[...])

    @pl.loop(0, 4)
    def _(n):
        at = pl.ds(pl.multiple_of(n * 64, 64), 64)
        rows = hidden[at] + tokens[at].astype(jnp.float32)
        hidden[at] = rows
        ffn_in[at] = (rows * rms_scale(rows) * as_row(ffn_gain)).astype(jnp.bfloat16)

    for d in (0, 1, -1, 2):
        a_second[d].third()
        b_second[d].third()
    save.wait()
    keys.drain()
    for one in gathers:
        one.drain()


def forward(tokens, cot, routes_t, length, cosine, sine, gains, weights):
    vmem, hbm = pl.BlockSpec(memory_space=pltpu.VMEM), pl.BlockSpec(memory_space=pl.ANY)
    low, wide = jnp.bfloat16, jnp.float32
    shape = jax.ShapeDtypeStruct
    return pl.pallas_call(
        forward_kernel,
        name="forward",
        out_shape=(
            shape((ROWS, 1024), low),
            shape((ROWS, 1024), wide),
            shape((1024, ROWS), low),
            shape((KV_HEADS, HEAD_DIM, 2 * ROWS), low),
            shape((KV_HEADS, 1, 2 * ROWS), wide),
            shape((ROWS, 1024), low),
            shape((ROWS, 1024), wide),
            shape((ROWS, 512), wide),
            shape((8, 1024, ROWS), low),
            shape((16 * SENT, 1024), low),
        ),
        in_specs=[vmem] * 10 + [hbm] * 4,
        out_specs=(vmem,) * 8 + (hbm, hbm),
        scratch_shapes=[
            pltpu.VMEM((1024, 1024), low),
            pltpu.VMEM((1024, 512), low),
            pltpu.VMEM((1024, 512), low),
            pltpu.VMEM((1024, 1024), low),
            pltpu.VMEM((8, 1024, ROWS), low),
            pltpu.VMEM((1024, ROWS), wide),
            pltpu.VMEM((KV_HEADS, 1, 2 * ROWS), wide),
            pltpu.VMEM((KV_HEADS, 1, 2 * ROWS), wide),
            pltpu.VMEM((KV_HEADS, HEAD_DIM, 2 * ROWS), wide),
            pltpu.VMEM((EXTRA, 1024), low),
            pltpu.SemaphoreType.DMA((10, 4)),
            pltpu.SemaphoreType.DMA((10, 4)),
            pltpu.SemaphoreType.DMA((8,)),
            pltpu.SemaphoreType.DMA((8,)),
            pltpu.SemaphoreType.DMA((4,)),
            pltpu.SemaphoreType.DMA,
            pltpu.SemaphoreType.DMA((2,)),
        ],
        compiler_params=pltpu.CompilerParams(
            collective_id=3, has_side_effects=True, vmem_limit_bytes=56 * 2**20
        ),
    )(tokens, cot, routes_t, length, cosine, sine, *gains, *weights)


ORDERS = (("x", "y", "z"), ("y", "z", "x"), ("z", "x", "y"))
STREAMS = {2048: ((0, 768), (768, 768), (1536, 512)), 2304: ((0, 768), (768, 768), (1536, 768))}


class Total:
    def __init__(self, here, device, buffer, shift, final, landing, work, send, recv, number, stream, half, begin=0):
        self.here, self.device, self.buffer, self.shift, self.final = here, device, buffer, shift, final
        self.landing, self.work = landing, work
        self.send, self.recv, self.number, self.order = send, recv, number, ORDERS[(stream + number // 3) % 3]
        self.half = half
        self.start, self.rows = STREAMS[half][stream]
        self.stages = range(begin, 7)
        r, own = self.rows, 0 if begin else self.rows
        first = self.start * 9 // 8 + (0 if begin else self.start)
        self.lands = (first, first + own, first + own + 3 * (r // 4), first + own + 3 * (r // 4) + 3 * (r // 16))

    def own(self):
        return self.here["core"] * self.half + self.start

    def copy(self, which, source, target, axis, step):
        return pltpu.make_async_remote_copy(
            src_ref=source,
            dst_ref=target,
            send_sem=self.send.at[self.number, which],
            recv_sem=self.recv.at[self.number, which],
            device_id=self.device(axis, step),
            device_id_type=MESH,
        )

    def held(self, at, size):
        return self.buffer.at[pl.ds(pl.multiple_of(at + self.shift, 16), size)]

    def ready(self, at, size):
        return self.final.at[pl.ds(pl.multiple_of(at, 16), size)]

    def land(self, stage, n, size):
        return self.landing.at[pl.ds(self.lands[stage] + n * size, size)]

    def copies(self, stage):
        r, own = self.rows, self.own()
        a, b, c = self.order
        ia, ib = self.here[a], self.here[b]
        second = own + ia * (r // 4)
        third = second + ib * (r // 16)
        if stage == 0:
            there = (1 - self.here["core"]) * self.half + self.start
            return [self.copy(0, self.held(there, r), self.land(0, 0, r), "core", 1)]
        if stage == 6:
            return [self.copy(16, self.ready(own, r), self.ready(own, r), "core", 1)]
        found = []
        for d in (1, 2, 3):
            if stage == 1:
                source, target, axis = self.held(own + (ia + d) % RING * (r // 4), r // 4), self.land(1, d - 1, r // 4), a
            elif stage == 2:
                source = self.held(second + (ib + d) % RING * (r // 16), r // 16)
                target, axis = self.land(2, d - 1, r // 16), b
            elif stage == 3:
                source = self.work.at[self.number, pl.ds(0, r // 16)]
                target, axis = self.land(3, d - 1, r // 16), c
            elif stage == 4:
                source, target, axis = self.ready(third, r // 16), self.ready(third, r // 16), b
            else:
                source, target, axis = self.ready(second, r // 4), self.ready(second, r // 4), a
            found.append(self.copy(1 + (stage - 1) * 3 + d - 1, source, target, axis, d))
        return found

    def begin(self, stage):
        for copy in self.copies(stage):
            copy.start()

    def add(self, stage, load, store, size, count):
        step = 64 if size % 64 == 0 else 16

        @pl.loop(0, size // step)
        def _(k):
            at = k * step
            total = load(at, step).astype(jnp.float32)
            for n in range(count):
                land = pl.ds(pl.multiple_of(self.lands[stage] + n * size + at, 16), step)
                total = total + self.landing[land].astype(jnp.float32)
            store(at, step, total.astype(jnp.bfloat16))

    def finish(self, stage):
        for copy in self.copies(stage):
            copy.wait_recv()
        if stage > 3:
            return
        r, own = self.rows, self.own()
        a, b, _ = self.order
        second = own + self.here[a] * (r // 4)
        third = second + self.here[b] * (r // 16)
        first = (own, second, third, third)[stage] + self.shift

        def in_place(at, step, *value):
            lines = pl.ds(pl.multiple_of(first + at, 16), step)
            if not value:
                return self.buffer[lines]
            self.buffer[lines] = value[0]

        def in_work(at, step, *value):
            lines = pl.ds(pl.multiple_of(at, 16), step)
            if not value:
                return self.work[self.number, lines]
            self.work[self.number, lines] = value[0]

        def in_final(at, step, value):
            self.final[pl.ds(pl.multiple_of(third + at, 16), step)] = value

        if stage == 0:
            self.add(0, in_place, in_place, r, 1)
        elif stage == 1:
            self.add(1, in_place, in_place, r // 4, 3)
        elif stage == 2:
            self.add(2, in_place, in_work, r // 16, 3)
        else:
            self.add(3, in_work, in_final, r // 16, 3)

    def drain(self):
        for stage in self.stages:
            for copy in self.copies(stage):
                copy.wait_send()


class Small:
    STAGES = (("core", (1,)), ("x", (1, 2, 3)), ("y", (1, 2, 3)), ("z", (1, 2, 3)))

    def __init__(self, device, value, landing, send, recv):
        self.device, self.value, self.landing, self.send, self.recv = device, value, landing, send, recv

    def copies(self, stage):
        axis, steps = self.STAGES[stage]
        first = sum(len(s) for _, s in self.STAGES[:stage])
        return [
            pltpu.make_async_remote_copy(
                src_ref=self.value.at[stage],
                dst_ref=self.landing.at[first + n],
                send_sem=self.send.at[first + n],
                recv_sem=self.recv.at[first + n],
                device_id=self.device(axis, step),
                device_id_type=MESH,
            )
            for n, step in enumerate(steps)
        ]

    def begin(self, stage):
        for copy in self.copies(stage):
            copy.start()

    def finish(self, stage):
        for copy in self.copies(stage):
            copy.wait_recv()
        first = sum(len(s) for _, s in self.STAGES[:stage])
        total = self.value[stage]
        for n in range(len(self.STAGES[stage][1])):
            total = total + self.landing[first + n]
        self.value[stage + 1] = total

    def drain(self):
        for stage in range(4):
            for copy in self.copies(stage):
                copy.wait_send()


class Line:
    def __init__(self, here, device):
        self.here, self.device = here, device

    def along(self, axis, other, step):
        return (self.here["x"] + step + RING) % RING

    def near(self, axis, step):
        return self.device("x", step)


def rms_back(values, gain, grad):
    scale = rms_scale(values)
    lifted = gain * grad
    inner = jnp.mean(values * lifted, axis=-1, keepdims=True)
    return scale * lifted - values * (scale * scale * scale) * inner, jnp.sum(
        grad * values * scale, axis=0, keepdims=True
    )


def turned_back(grads, cosine, sine):
    front, back = grads[: HEAD_DIM // 2], grads[HEAD_DIM // 2 :]
    return jnp.concatenate([front * cosine + back * sine, back * cosine - front * sine], axis=0)


def backward_kernel(
    routes_t, length, cosine, sine, attn_gain, query_gain, key_gain, ffn_gain, router_rows,
    hidden_all, ffn_in_all, cot_all, tokens_all, normed_all, key_raw_all, mixed_t_all, queries_all, log_total_all,
    own_gu, own_down, returned_all, query_raw_all, mixed_parts, kv_all, w_query, w_key, w_value, w_output,
    mixed_out, token_grad, early_small, late_small, query_sum, key_sum, value_sum, output_sum, all_gu, all_down,
    sums, rows, returned, square, kv, hidden_grad, result, branch, grads, delta, query_grad, turned,
    for_mate, from_mate, kv_sums, kv_rows, key_value, normed_other, query_other, key_value_other,
    hidden, ffn_in, cot, tokens, normed, key_raw, mixed_t, queries, log_total, share_gu, share_down,
    held, final_output, final_query, final_keys, land_output, land_query, land_keys, work, late_values, late_rows,
    rs_send, rs_recv, mate_send, mate_recv, kv_send, kv_recv, ar_send, ar_recv, small_send, small_recv, load_sem, out_sem, ex_send, ex_recv, pair_send, pair_recv,
):
    torus = Torus()
    here, device = everywhere()
    me = here["x"] * 2 + here["core"]
    barrier = pltpu.get_barrier_semaphore()
    peers = [device("core", 1)] + [device(axis, d) for axis in "xyz" for d in (1, 2, 3)]
    for peer in peers:
        pl.semaphore_signal(barrier, inc=1, device_id=peer, device_id_type=MESH)
    wanted = (
        ((returned_all, returned), (ffn_in_all, ffn_in), (hidden_all, hidden), (cot_all, cot)),
        ((w_output, square), (mixed_t_all, mixed_t), (queries_all, queries), (log_total_all, log_total)),
        ((normed_all, normed), (kv_all, kv), (own_gu, share_gu), (own_down, share_down)),
        ((mixed_parts, sums), (tokens_all, tokens), (key_raw_all, key_raw)),
    )
    loads, number = [], 0
    for group in wanted:
        loads.append([])
        for source, target in group:
            loads[-1].append(pltpu.make_async_copy(source, target, load_sem.at[number]))
            loads[-1][-1].start()
            number += 1

    order = (2, 1, -1, 0)
    leads = []
    for n, d in enumerate(order):
        leads.append(Scatter(torus, sums, rows, rs_send, rs_recv, n, n * 384, "z", d, 0, 64, 64, mixed_parts))
        leads.append(Scatter(torus, sums, rows, rs_send, rs_recv, 4 + n, (5 + n) * 384, "y", d, 128, 64, 64, mixed_parts))
    lasts = [
        Scatter(torus, sums, rows, rs_send, rs_recv, 8, 4 * 384, "y", 0, 0, 64, 64),
        Scatter(torus, sums, rows, rs_send, rs_recv, 9, 9 * 384, "z", 0, 128, 64, 64),
    ]
    ring = Scatter(Line(here, device), kv_sums, kv_rows, kv_send, kv_recv, 0, 0, "x", 0, 0, 512, 512)
    experts = [
        Keys(here, device, blocks, ex_send.at[n], ex_recv.at[n], origin)
        for n, (blocks, origin) in enumerate(((all_gu, own_gu), (all_down, own_down)))
    ]
    pl.semaphore_wait(barrier, len(peers))
    for one in leads:
        one.first()
    for one in experts:
        one.start(0, 1, 2)

    def to_other(number, source, target):
        return pltpu.make_async_remote_copy(
            src_ref=source,
            dst_ref=target,
            send_sem=pair_send.at[number],
            recv_sem=pair_recv.at[number],
            device_id=device("core", 1),
            device_id_type=MESH,
        )

    own_half = pl.ds(pl.multiple_of(here["core"] * 512, 512), 512)
    other_half = pl.ds(pl.multiple_of((1 - here["core"]) * 512, 512), 512)
    pairs = [
        to_other(0, normed, normed_other),
        to_other(1, branch.at[:, other_half], query_other),
        to_other(2, key_value.at[:, other_half], key_value_other),
    ]
    for load in loads[0]:
        load.wait()

    expert_rows = lax.broadcasted_iota(jnp.int32, (EXPERTS, ROWS), 0)
    member = jnp.zeros((EXPERTS, ROWS), jnp.float32)
    for k in range(TOPK):
        member = member + jnp.where(expert_rows == routes_t[pl.ds(k, 1), :], 1.0, 0.0)
    named = member > 0.5
    logits = jnp.where(named, dot_nt(router_rows[...], ffn_in[...]), -1e30)
    weight = jnp.where(named, jnp.exp(logits - jnp.max(logits, axis=0, keepdims=True)), 0.0)
    gates = weight / jnp.sum(weight, axis=0, keepdims=True)
    gate_grad = jnp.concatenate([returned[:8, q * ROWS : (q + 1) * ROWS] for q in range(4)], axis=0)
    logit_grad = (gates * (gate_grad - jnp.sum(gates * gate_grad, axis=0, keepdims=True))).astype(jnp.bfloat16)
    result[...] = dot_tn(logit_grad, router_rows[...])
    router_grad = dot_nn(logit_grad, ffn_in[...]).astype(jnp.bfloat16)
    for q in range(4):
        held[2048 + q * EXPERTS : 2048 + (q + 1) * EXPERTS] = router_grad[:, q * 256 : (q + 1) * 256]

    def ffn_part(n, gain_grad):
        at = pl.ds(pl.multiple_of(n * 64, 64), 64)
        grad = result[at] + returned[pl.ds(pl.multiple_of(n * 64 + EXTRA, 16), 64)]
        part, more = rms_back(hidden[at], as_row(ffn_gain), grad)
        part = part + cot[at].astype(jnp.float32)
        hidden_grad[at] = part
        branch[at] = part.astype(jnp.bfloat16)
        return gain_grad + more

    gain_grad = lax.fori_loop(0, 4, ffn_part, jnp.zeros((1, 1024), jnp.float32))
    gain_lines = [gain_grad[:, q * 256 : (q + 1) * 256] for q in range(4)] + [jnp.zeros((124, 256), jnp.float32)]
    held[2176:2304] = jnp.concatenate(gain_lines, axis=0).astype(jnp.bfloat16)
    held[4352:4608] = jnp.zeros((256, 256), jnp.bfloat16)

    for load in [*loads[1], *loads[2]]:
        load.wait()
    pairs[0].start()
    owns = [
        pltpu.make_async_copy(share_gu, all_gu.at[me], load_sem.at[19]),
        pltpu.make_async_copy(share_down, all_down.at[me], load_sem.at[20]),
    ]
    for copy in owns:
        copy.start()
    turned[...] = dot_nt(square[...], branch[...])
    next_load = pltpu.make_async_copy(w_query, square, load_sem.at[15])
    next_load.start()
    query_raw = returned.at[pl.ds(0, ROWS)]
    raw_load = pltpu.make_async_copy(query_raw_all, query_raw, load_sem.at[16])
    raw_load.start()

    for j in range(KV_HEADS):
        for r in range(2):
            at = slice(j * 128 + r * 64, j * 128 + r * 64 + 64)
            low = turned[at].astype(jnp.bfloat16)
            grads[j, :, r * ROWS : (r + 1) * ROWS] = low
            delta[j, :, r * ROWS : (r + 1) * ROWS] = jnp.sum(
                low.astype(jnp.float32) * mixed_t[at].astype(jnp.float32), axis=0, keepdims=True
            )
        query_grad[j] = jnp.zeros((HEAD_DIM, 2 * ROWS), jnp.float32)

    @pl.loop(0, 4)
    def _(n):
        at = pl.ds(pl.multiple_of(n * 256, 256), 256)
        part = dot_nn(mixed_t[at], branch[...]).astype(jnp.bfloat16)
        for q in range(4):
            held[pl.ds(pl.multiple_of(q * 1024 + q // 2 * 256 + n * 256, 256), 256)] = part[:, q * 256 : (q + 1) * 256]

    def reduction(number, buffer, shift, final, land, half, begin):
        return [
            Total(here, device, buffer, shift, final, land, work, ar_send, ar_recv, 3 * number + s, s, half, begin)
            for s in range(3)
        ]

    early = reduction(0, held, 0, final_output, land_output, 2304, 0)
    of_query = reduction(1, kv, 0, final_query, land_query, 2048, 1)
    of_keys = reduction(2, kv, 4096, final_keys, land_keys, 2048, 1)
    late_few = Small(device, late_values, late_rows, small_send, small_recv)
    for one in early:
        one.begin(0)
    def onward(streams, stage):
        for one in streams:
            one.finish(stage)
            if stage < 6:
                one.begin(stage + 1)

    def write_out(number, final, first, target, at):
        block = final.at[pl.ds(first, 1024)]
        return pltpu.make_async_copy(block, target.at[:, pl.ds(at * 256, 256)], out_sem.at[number])

    outs = [write_out(q, final_output, q * 1024 + q // 2 * 256, output_sum, q) for q in range(4)]
    outs += [write_out(4 + q, final_query, q * 1024, query_sum, q) for q in range(4)]
    outs += [write_out(8 + q, final_keys, q * 1024, key_sum, q) for q in range(2)]
    outs += [write_out(10 + q, final_keys, (2 + q) * 1024, value_sum, q) for q in range(2)]

    def mate_copy(turn, at):
        return pltpu.make_async_remote_copy(
            src_ref=for_mate.at[turn % 2],
            dst_ref=from_mate.at[at],
            send_sem=mate_send.at[turn],
            recv_sem=mate_recv.at[turn],
            device_id=device("core", 1),
            device_id_type=MESH,
        )

    key_at = lax.broadcasted_iota(jnp.int32, (ROWS, 2 * ROWS), 0)
    query_at = lax.broadcasted_iota(jnp.int32, (ROWS, 2 * ROWS), 1) % ROWS
    valid = (key_at <= query_at) & (key_at + me * ROWS < length[...])

    def block_grads(block, target, at, masked):
        for group in range(2):
            heads = range(4 * group, 4 * group + 4)
            key_heads = [kv[pl.ds(pl.multiple_of(block * 1024 + j * 64, 64), 64)] for j in heads]
            value_heads = [kv[pl.ds(pl.multiple_of(block * 1024 + 512 + j * 64, 64), 64)] for j in heads]
            probs = [jnp.exp(dot_tn(one, queries[j]) - log_total[j]) for one, j in zip(key_heads, heads)]
            if masked:
                probs = [jnp.where(valid, one, 0.0) for one in probs]
            probs_grads = [dot_tn(one, grads[j]) for one, j in zip(value_heads, heads)]
            lows = [
                (one * (grad - delta[j])).astype(jnp.bfloat16) for one, grad, j in zip(probs, probs_grads, heads)
            ]
            key_parts = [dot_nt(queries[j], low).astype(jnp.bfloat16) for low, j in zip(lows, heads)]
            value_parts = [
                dot_nt(grads[j], one.astype(jnp.bfloat16)).astype(jnp.bfloat16) for one, j in zip(probs, heads)
            ]
            query_parts = [dot_nn(one, low) for one, low in zip(key_heads, lows)]
            for n, j in enumerate(heads):
                target[at, j * 64 : j * 64 + 64] = key_parts[n]
                target[at, 512 + j * 64 : 576 + j * 64] = value_parts[n]
                query_grad[j] += query_parts[n]

    def from_other(turn, at):
        mate_copy(turn, at).wait_recv()

        @pl.loop(0, 16)
        def _(n):
            lines = pl.ds(pl.multiple_of(n * 64, 64), 64)
            total = kv_sums[at, lines].astype(jnp.float32) + from_mate[at, lines].astype(jnp.float32)
            kv_sums[at, lines] = total.astype(jnp.bfloat16)

    def turn_x(turn):
        offset = (1 - turn % 2) * (2 + turn // 2) + (turn % 2) * (1 - turn // 2)
        return (here["x"] + offset + RING) % RING

    @pl.loop(0, 4)
    def _(turn):
        @pl.when(turn == 1)
        def _():
            for load in loads[3]:
                load.wait()
            for one in leads:
                one.second()
            for one in experts:
                one.arrive(1)
                one.start(3, 5)
                one.arrive(2)
                one.start(4, 6)

        at = turn_x(turn)
        other = at * 2 + 1 - here["core"]

        @pl.when(turn >= 2)
        def _():
            mate_copy(turn - 2, at).wait_send()

        @pl.when(other < me)
        def _():
            block_grads(other, for_mate, turn % 2, False)

        @pl.when(other >= me)
        def _():
            for_mate[turn % 2] = jnp.zeros((1024, ROWS), jnp.bfloat16)

        mate_copy(turn, at).start()

        own = at * 2 + here["core"]

        @pl.when(own < me)
        def _():
            block_grads(own, kv_sums, at, False)

        @pl.when(own > me)
        def _():
            kv_sums[at] = jnp.zeros((1024, ROWS), jnp.bfloat16)

        @pl.when(own == me)
        def _():
            block_grads(own, kv_sums, at, True)

        from_other(turn, at)

        @pl.when(turn == 0)
        def _():
            ring.first()

        @pl.when(turn == 2)
        def _():
            ring.second()

    for j in range(KV_HEADS):
        for r in range(2):
            head = query_grad[j, :, r * ROWS : (r + 1) * ROWS] * HEAD_DIM**-0.5
            turned[j * 128 + r * 64 : j * 128 + r * 64 + 64] = turned_back(head, cosine[...], sine[...])

    raw_load.wait()
    result[...] = turned[...].T

    def query_part(n, gain_grad):
        at = pl.ds(pl.multiple_of(n * 64, 64), 64)
        part, more = rms_back(query_raw[at], as_row(query_gain), result[at])
        branch[at] = part.astype(jnp.bfloat16)
        return gain_grad + more

    query_gain_grad = lax.fori_loop(0, 4, query_part, jnp.zeros((1, 1024), jnp.float32))

    def half_of_columns(raw, raw_other, shift):
        both = jnp.concatenate([raw[:, own_half], raw_other[...]], axis=0)

        @pl.loop(0, 4)
        def _(n):
            columns = pl.ds(pl.multiple_of(n * 256, 256), 256)
            left = jnp.concatenate([normed[:, columns], normed_other[:, columns]], axis=0)
            part = dot_tn(left, both).astype(jnp.bfloat16)
            for q in range(2):
                first = shift + (here["core"] * 2 + q) * 1024 + n * 256
                kv[pl.ds(pl.multiple_of(first, 256), 256)] = part[:, q * 256 : (q + 1) * 256]

    pairs[1].start()
    onward(early, 0)
    for one in experts:
        one.arrive(3, 4)
        one.start(7)
    pairs[0].wait_recv()
    pairs[1].wait_recv()
    half_of_columns(branch, query_other, 0)
    for one in of_query:
        one.begin(1)

    def put(at, total):
        turned[at] = total

    ring.third(put)
    for j in range(KV_HEADS):
        turned[j * 64 : j * 64 + 64] = turned_back(turned[j * 64 : j * 64 + 64], cosine[...], sine[...])
    part, key_gain_grad = rms_back(key_raw[...], as_row(key_gain), turned[:512].T)
    key_value[:, :512] = part.astype(jnp.bfloat16)
    key_value[:, 512:] = turned[512:].T.astype(jnp.bfloat16)
    pairs[2].start()
    pairs[2].wait_recv()
    half_of_columns(key_value, key_value_other, 4096)
    for one in of_keys:
        one.begin(1)

    next_load.wait()
    result[...] = dot_nt(branch[...], square[...])
    last_loads = [
        pltpu.make_async_copy(w_key, square.at[:, pl.ds(0, 512)], load_sem.at[17]),
        pltpu.make_async_copy(w_value, square.at[:, pl.ds(512, 512)], load_sem.at[18]),
    ]
    for load in last_loads:
        load.start()
    onward(of_query, 1)
    for load in last_loads:
        load.wait()
    result[...] += dot_nt(key_value[...], square[...])

    def token_part(n, gain_grad):
        at = pl.ds(pl.multiple_of(n * 64, 64), 64)
        part, more = rms_back(tokens[at].astype(jnp.float32), as_row(attn_gain), result[at])
        token_grad[at] = (hidden_grad[at] + part).astype(jnp.bfloat16)
        return gain_grad + more

    attn_gain_grad = lax.fori_loop(0, 4, token_part, jnp.zeros((1, 1024), jnp.float32))
    key_wide = jnp.concatenate([key_gain_grad, jnp.zeros((1, 512), jnp.float32)], axis=1)
    late_values[0] = jnp.concatenate(
        [attn_gain_grad, query_gain_grad, key_wide, jnp.zeros((5, 1024), jnp.float32)], axis=0
    )
    late_few.begin(0)
    onward(of_keys, 1)
    onward(early, 1)
    for stage in range(2, 5):
        onward(of_query, stage)
        late_few.finish(stage - 2)
        late_few.begin(stage - 1)
        onward(of_keys, stage)
        onward(early, stage)
        if stage == 2:
            for one in leads:
                one.third()
            for one in lasts:
                one.first()
        if stage == 4:
            for one in lasts:
                one.second()
    onward(early, 5)
    onward(early, 6)
    for q in range(4):
        outs[q].start()
    late_few.finish(3)
    late_small[...] = late_values[4]
    router = [final_output[2048 + q * EXPERTS : 2048 + (q + 1) * EXPERTS].astype(jnp.float32) for q in range(4)]
    lines = final_output[2176:2192].astype(jnp.float32)
    lines = jnp.concatenate([lines[q : q + 1] for q in range(4)], axis=1)
    early_small[...] = jnp.concatenate(
        [jnp.concatenate(router, axis=1), lines, jnp.zeros((7, 1024), jnp.float32)], axis=0
    )

    def put_mixed(at, total):
        mixed_out[at] = (hidden[at] + total).astype(jnp.bfloat16)

    for stage in range(5, 7):
        onward(of_query, stage)
        onward(of_keys, stage)
        if stage == 6:
            for one in lasts:
                one.third(put_mixed)
    for q in range(4, 12):
        outs[q].start()
    for one in experts:
        one.arrive(0, 5, 6, 7)
    for one in [*experts, *leads, *lasts, ring, *early, *of_query, *of_keys, late_few]:
        one.drain()
    for turn in (2, 3):
        mate_copy(turn, 0).wait_send()
    for pair in pairs:
        pair.wait_send()
    for out in [*outs, *owns]:
        out.wait()


def backward(smalls, larges):
    vmem, hbm = pl.BlockSpec(memory_space=pltpu.VMEM), pl.BlockSpec(memory_space=pl.ANY)
    low, wide = jnp.bfloat16, jnp.float32
    shape = jax.ShapeDtypeStruct
    dma = pltpu.SemaphoreType.DMA
    return pl.pallas_call(
        backward_kernel,
        name="backward",
        out_shape=(
            shape((ROWS, 1024), low),
            shape((ROWS, 1024), low),
            shape((40, 1024), wide),
            shape((8, 1024), wide),
            shape((1024, 1024), low),
            shape((1024, 512), low),
            shape((1024, 512), low),
            shape((1024, 1024), low),
            shape((8, 256, 1024), low),
            shape((8, 128, 1024), low),
        ),
        in_specs=[vmem] * len(smalls) + [hbm] * len(larges),
        out_specs=(vmem,) * 4 + (hbm,) * 6,
        scratch_shapes=[
            pltpu.VMEM((16, ROWS, 1024), low),
            pltpu.VMEM((10 * 384, 1024), low),
            pltpu.VMEM((FULL, 1024), wide),
            pltpu.VMEM((1024, 1024), low),
            pltpu.VMEM((8 * 1024, ROWS), low),
            pltpu.VMEM((ROWS, 1024), wide),
            pltpu.VMEM((ROWS, 1024), wide),
            pltpu.VMEM((ROWS, 1024), low),
            pltpu.VMEM((KV_HEADS, HEAD_DIM, 2 * ROWS), low),
            pltpu.VMEM((KV_HEADS, 1, 2 * ROWS), wide),
            pltpu.VMEM((KV_HEADS, HEAD_DIM, 2 * ROWS), wide),
            pltpu.VMEM((1024, ROWS), wide),
            pltpu.VMEM((2, 1024, ROWS), low),
            pltpu.VMEM((4, 1024, ROWS), low),
            pltpu.VMEM((4, 1024, ROWS), low),
            pltpu.VMEM((3072, ROWS), low),
            pltpu.VMEM((ROWS, 1024), low),
            pltpu.VMEM((ROWS, 1024), low),
            pltpu.VMEM((ROWS, 512), low),
            pltpu.VMEM((ROWS, 512), low),
            pltpu.VMEM((ROWS, 1024), wide),
            pltpu.VMEM((ROWS, 1024), low),
            pltpu.VMEM((ROWS, 1024), low),
            pltpu.VMEM((ROWS, 1024), low),
            pltpu.VMEM((ROWS, 1024), low),
            pltpu.VMEM((ROWS, 512), wide),
            pltpu.VMEM((1024, ROWS), low),
            pltpu.VMEM((KV_HEADS, HEAD_DIM, 2 * ROWS), low),
            pltpu.VMEM((KV_HEADS, 1, 2 * ROWS), wide),
            pltpu.VMEM((256, 1024), low),
            pltpu.VMEM((128, 1024), low),
            pltpu.VMEM((4608, 256), low),
            pltpu.VMEM((4608, 256), low),
            pltpu.VMEM((4096, 256), low),
            pltpu.VMEM((4096, 256), low),
            pltpu.VMEM((4896, 256), low),
            pltpu.VMEM((2304, 256), low),
            pltpu.VMEM((2304, 256), low),
            pltpu.VMEM((9, 48, 256), low),
            pltpu.VMEM((5, 8, 1024), wide),
            pltpu.VMEM((10, 8, 1024), wide),
            dma((10, 4)),
            dma((10, 4)),
            dma((4,)),
            dma((4,)),
            dma((1, 4)),
            dma((1, 4)),
            dma((9, 17)),
            dma((9, 17)),
            dma((10,)),
            dma((10,)),
            dma((21,)),
            dma((12,)),
            dma((2, 8)),
            dma((2, 8)),
            dma((3,)),
            dma((3,)),
        ],
        compiler_params=pltpu.CompilerParams(
            collective_id=4, has_side_effects=True, vmem_limit_bytes=66000000
        ),
        cost_estimate=pl.CostEstimate(flops=100 * 10**9, bytes_accessed=60 * 10**6, transcendentals=8 * 10**6),
    )(*smalls, *larges)


def widen_kernel(
    early, late, mixed, tokens, query, key, value, output, gate_up, down,
    ffn_gain, attn_gain, query_gain, key_gain, router,
    mixed_out, token_out, query_out, key_out, value_out, output_out, gate_out, up_out, down_out,
    query_in, key_in, value_in, output_in, gate_up_in, down_in,
    query_wide, key_wide, value_wide, output_wide, gate_up_wide, down_wide,
    in_sem, out_sem,
):
    arrays = (
        (query, query_in, query_wide, query_out),
        (output, output_in, output_wide, output_out),
        (key, key_in, key_wide, key_out),
        (value, value_in, value_wide, value_out),
    )
    parts = []
    for source, low, wide, target in arrays:
        for n in range(0, 1024, 512):
            at = pl.ds(n, 512)
            parts.append((source.at[at], low.at[at], wide.at[at], [(wide.at[at], target.at[at])]))
    for block in range(8):
        rows, e = pl.ds(block // 2 * 256, 256), block % 2
        wide = gate_up_wide.at[block]
        targets = [
            (wide.at[:, pl.ds(0, 512)], gate_out.at[e, rows]),
            (wide.at[:, pl.ds(512, 512)], up_out.at[e, rows]),
        ]
        parts.append((gate_up.at[block], gate_up_in.at[block], wide, targets))
    for block in range(8):
        wide = down_wide.at[block]
        target = down_out.at[block % 2, pl.ds(block // 2 * 128, 128)]
        parts.append((down.at[block], down_in.at[block], wide, [(wide, target)]))
    loads = [pltpu.make_async_copy(source, low, in_sem.at[n]) for n, (source, low, _, _) in enumerate(parts)]
    for load in loads:
        load.start()
    ffn_gain[...] = early[EXPERTS]
    attn_gain[...] = late[0]
    query_gain[...] = late[1]
    key_gain[...] = late[2, :512]
    router[...] = early[:EXPERTS]
    mixed_out[...] = mixed[...]
    token_out[...] = tokens[...]
    stores = []
    for load, (_, low, wide, targets) in zip(loads, parts):
        load.wait()

        @pl.loop(0, low.shape[0] // 32)
        def _(n):
            at = pl.ds(pl.multiple_of(n * 32, 32), 32)
            wide[at] = low[at].astype(jnp.float32)

        for source, target in targets:
            stores.append(pltpu.make_async_copy(source, target, out_sem.at[len(stores)]))
            stores[-1].start()
    for copy in stores:
        copy.wait()


def widen(arrays):
    vmem, hbm = pl.BlockSpec(memory_space=pltpu.VMEM), pl.BlockSpec(memory_space=pl.ANY)
    low, wide = jnp.bfloat16, jnp.float32
    shape = jax.ShapeDtypeStruct
    held = ((1024, 1024), (1024, 512), (1024, 512), (1024, 1024), (8, 256, 1024), (8, 128, 1024))
    return pl.pallas_call(
        widen_kernel,
        name="widen",
        out_shape=(
            shape((1024,), wide),
            shape((1024,), wide),
            shape((1024,), wide),
            shape((512,), wide),
            shape((EXPERTS, 1024), wide),
            shape((ROWS, 1024), low),
            shape((ROWS, 1024), low),
            shape((1024, 1024), wide),
            shape((1024, 512), wide),
            shape((1024, 512), wide),
            shape((1024, 1024), wide),
            shape((2, 1024, 512), wide),
            shape((2, 1024, 512), wide),
            shape((2, 512, 1024), wide),
        ),
        in_specs=[vmem] * 4 + [hbm] * 6,
        out_specs=(vmem,) * 7 + (hbm,) * 7,
        scratch_shapes=[
            *[pltpu.VMEM(size, low) for size in held],
            *[pltpu.VMEM(size, wide) for size in held],
            pltpu.SemaphoreType.DMA((24,)),
            pltpu.SemaphoreType.DMA((32,)),
        ],
        compiler_params=pltpu.CompilerParams(vmem_limit_bytes=56 * 2**20),
    )(*arrays)


def body(
    tokens,
    cotangent,
    lengths,
    routes,
    attn_gain,
    w_query,
    w_key,
    w_value,
    query_gain,
    key_gain,
    w_output,
    ffn_gain,
    w_router,
    w_gate,
    w_up,
    w_down,
):
    query_pos = lax.axis_index("dp") * ROWS + jnp.arange(ROWS, dtype=jnp.int32)
    cosine, sine_table = rope_tables(query_pos)
    cosine, sine_table = cosine.T, sine_table.T
    routes_t, length = routes[0].T, lengths.reshape(1, 1)
    gains = [attn_gain, query_gain, key_gain, ffn_gain]
    weights = (w_query, w_key, w_value, w_output)
    router_rows = w_router.T
    ffn_in, hidden, mixed_t, queries, log_total, normed, query_raw, key_raw, kv_all, cot_all = forward(
        tokens[0], cotangent[0], routes_t, length, cosine, sine_table, gains, weights
    )
    returned, mixed_parts, own_gu, own_down = moe(
        ffn_in, cot_all, cotangent[0], router_rows, w_gate, w_up, w_down
    )
    mixed_low, token_low, early_small, late_small, *sums = backward(
        (routes_t, length, cosine, sine_table, *gains, router_rows),
        (
            hidden, ffn_in, cotangent[0], tokens[0], normed, key_raw, mixed_t, queries, log_total, own_gu, own_down,
            returned, query_raw, mixed_parts, kv_all.reshape(8 * 1024, ROWS), *weights,
        ),
    )
    (
        ffn_gain_sum, attn_gain_sum, query_gain_sum, key_gain_sum, router_sum, mixed_out, token_grad,
        query_w_sum, key_w_sum, value_w_sum, output_w_sum, gate_w_sum, up_w_sum, down_w_sum,
    ) = widen((early_small, late_small, mixed_low, token_low, *sums))
    return (
        mixed_out[None],
        token_grad[None],
        attn_gain_sum,
        query_w_sum,
        key_w_sum,
        value_w_sum,
        query_gain_sum,
        key_gain_sum,
        output_w_sum,
        ffn_gain_sum,
        router_sum.T,
        gate_w_sum,
        up_w_sum,
        down_w_sum,
    )


def solution(mesh):
    return jax.shard_map(
        body,
        mesh=mesh,
        in_specs=(
            P("expert", "dp", None),
            P("expert", "dp", None),
            P("expert"),
            P("expert", "dp", None),
            P(),
            P(),
            P(),
            P(),
            P(),
            P(),
            P(),
            P(),
            P(),
            P("expert", None, None),
            P("expert", None, None),
            P("expert", None, None),
        ),
        out_specs=(
            P("expert", "dp", None),
            P("expert", "dp", None),
            P(),
            P(),
            P(),
            P(),
            P(),
            P(),
            P(),
            P(),
            P(),
            P("expert", None, None),
            P("expert", None, None),
            P("expert", None, None),
        ),
        check_vma=False,
    )
```

```python
import math

import jax
import jax.numpy as jnp
from jax import lax
from jax.experimental import pallas as pl
from jax.experimental.pallas import tpu as pltpu
from jax.sharding import PartitionSpec as P

HEADS = 16
KV_HEADS = 8
HEAD_DIM = 64
EXPERTS = 32
TOPK = 8
CAP = 80


epsilon = 1e-06


def rope_tables(positions):
    steps_half = jnp.arange(HEAD_DIM // 2).astype(jnp.float32)
    inverse = jnp.exp(steps_half * (-2.0 * math.log(10000.0) / HEAD_DIM))
    angles = positions.astype(jnp.float32)[:, None] * inverse[None, :]
    return (jnp.cos(angles), jnp.sin(angles))


RING = 4
ROWS = 256
EXTRA = 16
FULL = ROWS + EXTRA
SENT = 192
LEFT = FULL - SENT
BOTH = ROWS + LEFT
GROUP = 4 * CAP
MESH = pl.DeviceIdType.MESH


def dot_nn(a, b):
    return jnp.dot(a, b, preferred_element_type=jnp.float32)


def dot_nt(a, b):
    return lax.dot_general(a, b, (((1,), (1,)), ((), ())), preferred_element_type=jnp.float32)


def dot_tn(a, b):
    return lax.dot_general(a, b, (((0,), (0,)), ((), ())), preferred_element_type=jnp.float32)


def step_of(size):
    return next(step for step in (64, 48, 32, 16) if size % step == 0)


class Torus:
    def __init__(self):
        self.dp = lax.axis_index("dp")
        expert = lax.axis_index("expert")
        self.expert = expert
        self.z, self.y = expert // RING, expert % RING

    def block(self, dz, dy):
        return ((self.z + dz + RING) % RING) * RING + (self.y + dy + RING) % RING

    def near(self, axis, step):
        return (self.dp, self.block(step, 0) if axis == "z" else self.block(0, step))

    def along(self, axis, other, step):
        return self.block(step, other) if axis == "z" else self.block(other, step)

    def neighbours(self):
        return [self.near(axis, step) for axis in "yz" for step in (1, -1)]


ARRIVALS = (
    ((0, 0), (3, 0), (1, 3), (3, 2)),
    ((0, 1), (0, 2), (3, 1), (2, 1)),
    ((0, 3), (2, 0), (3, 3), (2, 3)),
    ((1, 0), (1, 1), (1, 2), (2, 2)),
)


def differences(values):
    found = list(values)
    for level in range(1, len(found)):
        for n in range(len(found) - 1, level - 1, -1):
            found[n] -= found[n - 1]
    return found


def chooses(n):
    return 1, n, n * (n - 1) // 2, n * (n - 1) * (n - 2) // 6


class Gather:
    def __init__(self, torus, buffer, send, recv, number, axis, other, low, first, second, stride):
        self.torus, self.buffer, self.send, self.recv = torus, buffer, send, recv
        self.number, self.axis, self.other, self.stride = number, axis, other, stride
        self.whole, self.front, self.rear = (low, first + second), (low, first), (low + first, second)

    def copy(self, which, offset, part, step):
        at = self.torus.along(self.axis, self.other, offset) * self.stride + part[0]
        rows = self.buffer.at[pl.ds(pl.multiple_of(at, 16), part[1])]
        return pltpu.make_async_remote_copy(
            src_ref=rows,
            dst_ref=rows,
            send_sem=self.send.at[self.number, which],
            recv_sem=self.recv.at[self.number, which],
            device_id=self.torus.near(self.axis, step),
            device_id_type=MESH,
        )

    def first(self):
        self.copy(0, 0, self.whole, 1).start()
        self.copy(1, 0, self.whole, -1).start()

    def second(self):
        self.copy(0, -1, self.whole, 1).wait_recv()
        self.copy(2, -1, self.front, 1).start()
        self.copy(1, 1, self.whole, -1).wait_recv()
        self.copy(3, 1, self.rear, -1).start()

    def third(self):
        self.copy(2, 2, self.front, 1).wait_recv()
        self.copy(3, 2, self.rear, -1).wait_recv()

    def drain(self):
        self.copy(0, 0, self.whole, 1).wait_send()
        self.copy(1, 0, self.whole, -1).wait_send()
        self.copy(2, -1, self.front, 1).wait_send()
        self.copy(3, 1, self.rear, -1).wait_send()


class Scatter:
    def __init__(self, torus, sums, landing, send, recv, number, base, axis, other, low, first, second, origin=None):
        self.torus, self.sums, self.landing, self.send, self.recv = torus, sums, landing, send, recv
        self.number, self.axis, self.other = number, axis, other
        self.origin = sums if origin is None else origin
        self.low, self.parts = low, (first, second)
        self.size = first + second
        self.slots = (base, base + first, base + self.size, base + 2 * self.size)

    def rows(self, which):
        if which == 0:
            return self.low, self.parts[0]
        if which == 1:
            return self.low + self.parts[0], self.parts[1]
        return self.low, self.size

    def at(self, offset):
        return self.torus.along(self.axis, self.other, offset)

    def copy(self, which):
        start, size = self.rows(which)
        offset = (2, 2, 1, -1)[which]
        return pltpu.make_async_remote_copy(
            src_ref=(self.origin if which < 2 else self.sums).at[self.at(offset), pl.ds(start, size)],
            dst_ref=self.landing.at[pl.ds(self.slots[which], size)],
            send_sem=self.send.at[self.number, which],
            recv_sem=self.recv.at[self.number, which],
            device_id=self.torus.near(self.axis, (1, -1, 1, -1)[which]),
            device_id_type=MESH,
        )

    def add(self, which, offset):
        start, size = self.rows(which)
        block = self.at(offset)

        many = step_of(size)

        @pl.loop(0, size // many)
        def _(k):
            here = pl.ds(pl.multiple_of(start + k * many, 16), many)
            there = pl.ds(pl.multiple_of(self.slots[which] + k * many, 16), many)
            total = self.sums[block, here].astype(jnp.float32) + self.landing[there].astype(jnp.float32)
            self.sums[block, here] = total.astype(jnp.bfloat16)

    def first(self):
        self.copy(0).start()
        self.copy(1).start()

    def second(self):
        self.copy(0).wait_recv()
        self.add(0, 1)
        self.copy(2).start()
        self.copy(1).wait_recv()
        self.add(1, -1)
        self.copy(3).start()

    def third(self, put=None):
        self.copy(2).wait_recv()
        self.copy(3).wait_recv()
        block = self.at(0)

        many = step_of(self.size)

        @pl.loop(0, self.size // many)
        def _(k):
            here = pl.ds(pl.multiple_of(self.low + k * many, 16), many)
            left = pl.ds(pl.multiple_of(self.slots[2] + k * many, 16), many)
            right = pl.ds(pl.multiple_of(self.slots[3] + k * many, 16), many)
            total = (
                self.sums[block, here].astype(jnp.float32)
                + self.landing[left].astype(jnp.float32)
                + self.landing[right].astype(jnp.float32)
            )
            if put is None:
                self.sums[block, here] = total.astype(jnp.bfloat16)
            else:
                put(here, total)

    def drain(self):
        for which in range(4):
            self.copy(which).wait_send()


def moe_kernel(
    ffn, cot, own_cot, wr, w_gate, w_up, w_down,
    ret, mixed, own_gu, own_down,
    rows, sums, wgu, wd, held, pair, inner, dgu, mixing, back, cotv, before, chosen, gate_rows, grad_rows, stage,
    mate_rows, gu_sums, down_sums,
    ag_send, ag_recv, rs_send, rs_recv, w_sem, cot_sem, own_sem, stage_sem, mate_send, mate_recv, x_send, x_recv, credit,
):
    torus = Torus()
    place, place_of = everywhere()
    barrier = pltpu.get_barrier_semaphore()
    peers = [*torus.neighbours(), place_of("core", 1), place_of("x", 1), place_of("x", -1)]
    for device in peers:
        pl.semaphore_signal(barrier, inc=1, device_id=device, device_id_type=MESH)

    weights = [
        pltpu.make_async_copy(w_gate, wgu.at[:, :, pl.ds(0, 512)], w_sem.at[0]),
        pltpu.make_async_copy(w_up, wgu.at[:, :, pl.ds(512, 512)], w_sem.at[1]),
        pltpu.make_async_copy(w_down, wd, w_sem.at[2]),
    ]
    for copy in weights:
        copy.start()

    def source_of(g, j):
        of_g, of_j = chooses(g), chooses(j)
        offsets = []
        for axis in range(2):
            table = [differences([at[axis] for at in line]) for line in ARRIVALS]
            table = [differences(column) for column in zip(*table)]
            offsets.append(sum(table[a][b] * of_g[a] * of_j[b] for a in range(4) for b in range(4) if table[a][b]))
        return torus.block(*offsets)

    def cot_copy(g, j):
        at = pl.multiple_of(source_of(g, j) * SENT, 16)
        return pltpu.make_async_copy(cot.at[pl.ds(at, SENT)], cotv.at[pl.ds(j * SENT, SENT)], cot_sem.at[j])

    for j in range(4):
        cot_copy(0, j).start()
    first_row = torus.expert * BOTH
    own_copy = pltpu.make_async_copy(
        own_cot.at[pl.ds(ROWS - LEFT, LEFT)], rows.at[pl.ds(pl.multiple_of(first_row + ROWS, 16), LEFT)], own_sem
    )
    own_copy.start()
    rows[pl.ds(pl.multiple_of(first_row, 16), ROWS)] = ffn[...]
    own_copy.wait()
    pl.semaphore_wait(barrier, len(peers))

    def gather(number, axis, other, low, first, second):
        return Gather(torus, rows, ag_send, ag_recv, number, axis, other, low, first, second, BOTH)

    a_first = gather(0, "y", 0, 0, 96, 80)
    b_first = gather(1, "z", 0, 176, 80, 80)
    a_second = {d: gather(2 + d % RING, "z", d, 0, 96, 80) for d in (0, 1, -1, 2)}
    b_second = {d: gather(6 + d % RING, "y", d, 176, 80, 80) for d in (0, 1, -1, 2)}
    gathers = [a_first, b_first, *a_second.values(), *b_second.values()]

    a_first.first()
    b_first.first()
    b_second[0].first()
    a_second[0].first()
    a_first.second()
    b_first.second()
    b_second[0].second()
    a_second[0].second()
    for d in (1, -1):
        b_second[d].first()
        a_second[d].first()
    for copy in weights:
        copy.wait()

    earlier = lax.broadcasted_iota(jnp.int32, (ROWS, ROWS), 0) < lax.broadcasted_iota(jnp.int32, (ROWS, ROWS), 1)
    before[...] = jnp.where(earlier, 1.0, 0.0).astype(jnp.bfloat16)
    slot_at = lax.broadcasted_iota(jnp.int32, (CAP, ROWS), 0).astype(jnp.float32)

    def stage_copy(slot, target):
        return pltpu.make_async_copy(stage.at[slot], target, stage_sem.at[slot])

    expert_rows = lax.broadcasted_iota(jnp.int32, (EXPERTS, ROWS), 0)
    order = (2, 1, -1, 0)
    a_lead = {
        d: Scatter(torus, sums, rows, rs_send, rs_recv, n, n * 384, "z", d, 0, 64, 64) for n, d in enumerate(order)
    }
    b_lead = {
        d: Scatter(torus, sums, rows, rs_send, rs_recv, 4 + n, 1920 + n * 432, "y", d, 128, 80, 64)
        for n, d in enumerate(order)
    }
    a_last = Scatter(torus, sums, rows, rs_send, rs_recv, 8, 4 * 384, "y", 0, 0, 64, 64)
    b_last = Scatter(torus, sums, rows, rs_send, rs_recv, 9, 1920 + 4 * 432, "z", 0, 128, 80, 64)

    @pl.loop(0, 4)
    def _(g):
        @pl.when(g == 1)
        def _():
            a_first.third()
            b_first.third()
            b_second[2].first()
            a_second[2].first()
            b_second[0].third()
            a_second[0].third()
            for d in (1, -1):
                b_second[d].second()
                a_second[d].second()

        @pl.when(g == 2)
        def _():
            b_second[2].second()
            a_second[2].second()
            b_second[1].third()

        @pl.when(g == 3)
        def _():
            b_second[-1].third()
            for d in (1, -1, 2):
                a_second[d].third()
            b_second[2].third()

        for j in range(4):
            cot_copy(g, j).wait()

        @pl.loop(0, 4)
        def _(j):
            source = source_of(g, j)
            block = rows[pl.ds(pl.multiple_of(source * BOTH, 16), ROWS)]
            laid = cotv[pl.ds(pl.multiple_of(j * SENT, 16), EXTRA)].astype(jnp.float32)
            member = jnp.concatenate([laid[:8, q * ROWS : (q + 1) * ROWS] for q in range(4)], axis=0)
            named = member > 0.5
            slots = dot_nn(member.astype(jnp.bfloat16), before[...])
            slots = jnp.where(named, slots, -1.0)
            logits = jnp.where(named, dot_nt(wr[...], block), -1e30)
            weight = jnp.where(named, jnp.exp(logits - jnp.max(logits, axis=0, keepdims=True)), 0.0)
            gates = weight / jnp.sum(weight, axis=0, keepdims=True)
            picked = []
            for e in range(2):
                own = jnp.sum(
                    jnp.where(expert_rows == torus.expert * 2 + e, slots, 0.0), axis=0, keepdims=True
                )
                picked.append(jnp.where(slot_at == own, 1.0, 0.0))
            both = jnp.concatenate(picked, axis=0).astype(jnp.bfloat16)
            chosen[j] = both
            grad_block = jnp.concatenate(
                [
                    cotv[pl.ds(pl.multiple_of(j * SENT + EXTRA, 16), SENT - EXTRA)],
                    rows[pl.ds(pl.multiple_of(source * BOTH + ROWS, 16), LEFT)],
                ],
                axis=0,
            )
            took = dot_nn(both, jnp.concatenate([block, grad_block], axis=1)).astype(jnp.bfloat16)
            here = pl.ds(pl.multiple_of(j * CAP, 16), CAP)
            there = pl.ds(pl.multiple_of(g * GROUP + j * CAP, 16), CAP)
            for e in range(2):
                own = jnp.sum(
                    jnp.where(expert_rows == torus.expert * 2 + e, gates, 0.0), axis=0, keepdims=True
                )
                of_rows = jnp.sum(picked[e] * own, axis=1, keepdims=True)
                gate_rows[e, here] = jnp.broadcast_to(of_rows, (CAP, 128))
                held[e, there] = took[e * CAP : (e + 1) * CAP, :1024]
                mixing[e, here] = took[e * CAP : (e + 1) * CAP, 1024:]

        @pl.when(g < 3)
        def _():
            for j in range(4):
                cot_copy(g + 1, j).start()

        @pl.when(g == 3)
        def _():
            for one in gathers:
                one.drain()
            for device in peers:
                pl.semaphore_signal(credit, inc=1, device_id=device, device_id_type=MESH)
            pl.semaphore_wait(credit, len(peers))
            b_lead[0].first()
            a_lead[0].first()

        @pl.loop(0, 2)
        def _(e):
            there = pl.ds(pl.multiple_of(g * GROUP, 16), GROUP)
            both = dot_nn(held[e, there], wgu[e])
            gate, up = both[:, :512], both[:, 512:]
            sig = jax.nn.sigmoid(gate)
            silu = gate * sig
            act = (silu * up).astype(jnp.bfloat16)
            inner[e, there] = act
            out = dot_nn(act, wd[e]).astype(jnp.bfloat16).astype(jnp.float32)
            grad = mixing[e].astype(jnp.float32)
            weight = gate_rows[e][:, :1]
            grad_rows[e] = jnp.broadcast_to(jnp.sum(grad * out, axis=1, keepdims=True), (GROUP, 128))
            pair[e, there] = (weight * grad).astype(jnp.bfloat16)
            mixing[e] = (weight * out).astype(jnp.bfloat16)
            inner_grad = dot_nt(pair[e, there], wd[e])
            dgu[e, there, :512] = (inner_grad * up * sig * (1.0 + gate * (1.0 - sig))).astype(jnp.bfloat16)
            dgu[e, there, 512:] = (inner_grad * silu).astype(jnp.bfloat16)
            back[e] = dot_nt(dgu[e, there], wgu[e]).astype(jnp.bfloat16)

        @pl.loop(0, 4)
        def _(j):
            source = source_of(g, j)
            both = chosen[j]
            picked = both.astype(jnp.float32)
            here = pl.ds(pl.multiple_of(j * CAP, 16), CAP)
            compact = jnp.concatenate(
                [jnp.concatenate([back[e, here], mixing[e, here]], axis=1) for e in range(2)], axis=0
            )
            spread = dot_tn(both, compact).astype(jnp.bfloat16)
            sums[source, pl.ds(EXTRA, ROWS)] = spread[:, :1024]
            grads = jnp.zeros((EXPERTS, ROWS), jnp.float32)
            for e in range(2):
                own = jnp.sum(
                    picked[e * CAP : (e + 1) * CAP] * grad_rows[e, here][:, :1], axis=0, keepdims=True
                )
                grads = grads + jnp.where(expert_rows == torus.expert * 2 + e, own, 0.0)
            laid = jnp.concatenate([grads[8 * q : 8 * q + 8] for q in range(4)], axis=1)
            sums[source, pl.ds(0, EXTRA)] = jnp.concatenate([laid, jnp.zeros_like(laid)], axis=0).astype(
                jnp.bfloat16
            )
            slot = j % 2

            @pl.when((g > 0) | (j > 1))
            def _():
                stage_copy(slot, mixed.at[source]).wait()

            stage[slot] = spread[:, 1024:]
            stage_copy(slot, mixed.at[source]).start()

    def chunk(e, k):
        if k < 4:
            return dot_tn(held[e, :, k * 256 : (k + 1) * 256], dgu[e]).astype(jnp.bfloat16)
        return dot_tn(inner[e, :, (k - 4) * 256 : (k - 3) * 256], pair[e]).astype(jnp.bfloat16)

    def mate_copy(k):
        return pltpu.make_async_remote_copy(
            src_ref=stage.at[k % 2],
            dst_ref=mate_rows.at[pl.ds(k * 256, 256)],
            send_sem=mate_send.at[k],
            recv_sem=mate_recv.at[k],
            device_id=place_of("core", 1),
            device_id_type=MESH,
        )

    line = Line(place, place_of)
    rings = [
        Scatter(line, gu_sums, rows, x_send, x_recv, 0, 4080, "x", 0, 0, 128, 128),
        Scatter(line, down_sums, rows, x_send, x_recv, 1, 4848, "x", 0, 0, 64, 64),
    ]

    for d in (2, 1, -1):
        b_lead[d].first()
        a_lead[d].first()
    b_lead[0].second()
    a_lead[0].second()
    for k in range(6):
        if k < 2:
            stage_copy(k, mixed.at[0]).wait()
        else:
            mate_copy(k - 2).wait_send()
        stage[k % 2] = chunk(1 - place["core"], k)
        mate_copy(k).start()
        own = chunk(place["core"], k)
        if k < 4:
            gu_sums[k] = own
        else:
            down_sums[2 * k - 8] = own[:128]
            down_sums[2 * k - 7] = own[128:]
        if k == 4:
            for d in (2, 1, -1):
                b_lead[d].second()
                a_lead[d].second()
    for k in range(6):
        mate_copy(k).wait_recv()

        @pl.loop(0, 4)
        def _(n):
            other = mate_rows[pl.ds(pl.multiple_of(k * 256 + n * 64, 64), 64)].astype(jnp.float32)
            if k < 4:
                at = (k, pl.ds(pl.multiple_of(n * 64, 64), 64))
                gu_sums[at] = (gu_sums[at].astype(jnp.float32) + other).astype(jnp.bfloat16)
            else:
                at = (2 * k - 8 + n // 2, pl.ds(pl.multiple_of(n % 2 * 64, 64), 64))
                down_sums[at] = (down_sums[at].astype(jnp.float32) + other).astype(jnp.bfloat16)

    for one in rings:
        one.first()
    for one in rings:
        one.second()
    for d in order:
        b_lead[d].third()
        a_lead[d].third()
        if d == 2:
            b_last.first()
            a_last.first()
    b_last.second()
    a_last.second()

    def put(at, total):
        ret[at] = total

    b_last.third(put)
    a_last.third(put)

    def put_gu(at, total):
        own_gu[at] = total.astype(jnp.bfloat16)

    def put_down(at, total):
        own_down[at] = total.astype(jnp.bfloat16)

    rings[0].third(put_gu)
    rings[1].third(put_down)
    for one in [*a_lead.values(), *b_lead.values(), a_last, b_last, *rings]:
        one.drain()
    for k in (4, 5):
        mate_copy(k).wait_send()


def moe(ffn_in, cot_all, own_cot, router_rows, w_gate, w_up, w_down):
    vmem, hbm = pl.BlockSpec(memory_space=pltpu.VMEM), pl.BlockSpec(memory_space=pl.ANY)
    low, total = jnp.bfloat16, 4 * GROUP
    return pl.pallas_call(
        moe_kernel,
        name="moe",
        out_shape=(
            jax.ShapeDtypeStruct((FULL, 1024), jnp.float32),
            jax.ShapeDtypeStruct((16, ROWS, 1024), low),
            jax.ShapeDtypeStruct((256, 1024), low),
            jax.ShapeDtypeStruct((128, 1024), low),
        ),
        in_specs=[vmem, hbm, hbm, vmem, hbm, hbm, hbm],
        out_specs=(vmem, hbm, vmem, vmem),
        scratch_shapes=[
            pltpu.VMEM((16 * BOTH, 1024), low),
            pltpu.VMEM((16, FULL, 1024), low),
            pltpu.VMEM((2, 1024, 1024), low),
            pltpu.VMEM((2, 512, 1024), low),
            pltpu.VMEM((2, total, 1024), low),
            pltpu.VMEM((2, total, 1024), low),
            pltpu.VMEM((2, total, 512), low),
            pltpu.VMEM((2, total, 1024), low),
            pltpu.VMEM((2, GROUP, 1024), low),
            pltpu.VMEM((2, GROUP, 1024), low),
            pltpu.VMEM((4 * SENT, 1024), low),
            pltpu.VMEM((ROWS, ROWS), low),
            pltpu.VMEM((4, 2 * CAP, ROWS), low),
            pltpu.VMEM((2, GROUP, 128), jnp.float32),
            pltpu.VMEM((2, GROUP, 128), jnp.float32),
            pltpu.VMEM((2, ROWS, 1024), low),
            pltpu.VMEM((6 * 256, 1024), low),
            pltpu.VMEM((4, 256, 1024), low),
            pltpu.VMEM((4, 128, 1024), low),
            pltpu.SemaphoreType.DMA((10, 4)),
            pltpu.SemaphoreType.DMA((10, 4)),
            pltpu.SemaphoreType.DMA((10, 4)),
            pltpu.SemaphoreType.DMA((10, 4)),
            pltpu.SemaphoreType.DMA((3,)),
            pltpu.SemaphoreType.DMA((4,)),
            pltpu.SemaphoreType.DMA,
            pltpu.SemaphoreType.DMA((2,)),
            pltpu.SemaphoreType.DMA((6,)),
            pltpu.SemaphoreType.DMA((6,)),
            pltpu.SemaphoreType.DMA((2, 4)),
            pltpu.SemaphoreType.DMA((2, 4)),
            pltpu.SemaphoreType.REGULAR,
        ],
        compiler_params=pltpu.CompilerParams(
            collective_id=1, has_side_effects=True, vmem_limit_bytes=63 * 2**20
        ),
        cost_estimate=pl.CostEstimate(flops=50 * 10**9, bytes_accessed=40 * 10**6, transcendentals=2 * 10**6),
    )(ffn_in, cot_all, own_cot, router_rows, w_gate, w_up, w_down)


def everywhere():
    dp, expert = lax.axis_index("dp"), lax.axis_index("expert")
    here = {"x": dp // 2, "core": dp % 2, "z": expert // RING, "y": expert % RING}

    def device(axis, step):
        there = dict(here)
        size = 2 if axis == "core" else RING
        there[axis] = (here[axis] + step + size) % size
        return (there["x"] * 2 + there["core"], there["z"] * RING + there["y"])

    return here, device


def rms_scale(values):
    return lax.rsqrt(jnp.mean(values * values, axis=-1, keepdims=True) + epsilon)


def as_row(gain):
    return gain[...].astype(jnp.float32).reshape(1, -1)


def turned_rows(values, cosine, sine):
    front, back = values[: HEAD_DIM // 2], values[HEAD_DIM // 2 :]
    return jnp.concatenate([front * cosine - back * sine, back * cosine + front * sine], axis=0)


def kv_order(here, step):
    turn = step // 2
    return (turn % 2) * (3 - turn // 2) + (1 - turn % 2) * (turn // 2)


class Keys:
    def __init__(self, here, device, blocks, send, recv, origin=None):
        self.here, self.device, self.blocks, self.send, self.recv = here, device, blocks, send, recv
        self.origin = origin
        self.lines = blocks.shape[1]

    def copy(self, which):
        half = self.lines // 2
        offset, start, size, axis, step = (
            (0, 0, self.lines, "core", 1),
            (0, 0, self.lines, "x", 1),
            (0, 0, self.lines, "x", -1),
            (-1, 0, half, "x", 1),
            (1, half, half, "x", -1),
            (-1, 0, self.lines, "core", 1),
            (1, 0, self.lines, "core", 1),
            (2, 0, self.lines, "core", 1),
        )[which]
        block = (self.here["x"] + offset + RING) % RING * 2 + self.here["core"]
        part = self.blocks.at[block, pl.ds(start, size)]
        return pltpu.make_async_remote_copy(
            src_ref=part if which > 2 or self.origin is None else self.origin,
            dst_ref=part,
            send_sem=self.send.at[which],
            recv_sem=self.recv.at[which],
            device_id=self.device(axis, step),
            device_id_type=MESH,
        )

    def start(self, *which):
        for one in which:
            self.copy(one).start()

    def arrive(self, *which):
        for one in which:
            self.copy(one).wait_recv()

    def drain(self):
        for one in range(8):
            self.copy(one).wait_send()


def forward_kernel(
    tokens, cot, routes_t, length, cosine, sine, attn_gain, query_gain, key_gain, ffn_gain,
    w_query, w_key, w_value, w_output,
    ffn_in, hidden, mixed_t, queries, log_total, normed, query_raw, key_raw, kv_all, cot_all,
    wq, wk, wv, wo, kv, turned, most, total, mixed, packed,
    ag_send, ag_recv, kv_send, kv_recv, w_sem, kv_sem, own_sem,
):
    torus = Torus()
    here, device = everywhere()
    me = here["x"] * 2 + here["core"]
    barrier = pltpu.get_barrier_semaphore()
    peers = [*torus.neighbours(), device("core", 1), device("x", 1), device("x", -1)]
    for peer in peers:
        pl.semaphore_signal(barrier, inc=1, device_id=peer, device_id_type=MESH)
    loads = [
        pltpu.make_async_copy(source, target, w_sem.at[n])
        for n, (source, target) in enumerate(((w_query, wq), (w_key, wk), (w_value, wv), (w_output, wo)))
    ]
    for load in loads:
        load.start()

    expert_rows = lax.broadcasted_iota(jnp.int32, (EXPERTS, ROWS), 0)
    member = jnp.zeros((EXPERTS, ROWS), jnp.float32)
    for k in range(TOPK):
        member = member + jnp.where(expert_rows == routes_t[pl.ds(k, 1), :], 1.0, 0.0)
    laid = jnp.concatenate([member[8 * q : 8 * q + 8] for q in range(4)], axis=1)
    packed[...] = jnp.concatenate([laid, jnp.zeros_like(laid)], axis=0).astype(jnp.bfloat16)
    first_row = pl.multiple_of(torus.expert * SENT, 16)
    owns = [
        pltpu.make_async_copy(packed, cot_all.at[pl.ds(first_row, EXTRA)], own_sem.at[0]),
        pltpu.make_async_copy(
            cot.at[pl.ds(0, SENT - EXTRA)],
            cot_all.at[pl.ds(pl.multiple_of(first_row + EXTRA, 16), SENT - EXTRA)],
            own_sem.at[1],
        ),
    ]
    for copy in owns:
        copy.start()
    for copy in owns:
        copy.wait()
    pl.semaphore_wait(barrier, len(peers))

    def gather(number, axis, other, low, first, second):
        return Gather(torus, cot_all, ag_send, ag_recv, number, axis, other, low, first, second, SENT)

    a_first = gather(0, "y", 0, 0, 48, 48)
    b_first = gather(1, "z", 0, 96, 48, 48)
    a_second = {d: gather(2 + d % RING, "z", d, 0, 48, 48) for d in (0, 1, -1, 2)}
    b_second = {d: gather(6 + d % RING, "y", d, 96, 48, 48) for d in (0, 1, -1, 2)}
    gathers = [a_first, b_first, *a_second.values(), *b_second.values()]
    a_first.first()
    b_first.first()
    b_second[0].first()
    a_second[0].first()

    @pl.loop(0, 4)
    def _(n):
        at = pl.ds(pl.multiple_of(n * 64, 64), 64)
        rows = tokens[at].astype(jnp.float32)
        normed[at] = (rows * rms_scale(rows) * as_row(attn_gain)).astype(jnp.bfloat16)

    for load in loads:
        load.wait()

    keys = Keys(here, device, kv, kv_send, kv_recv)
    key_raw[...] = dot_nn(normed[...], wk[...])
    scaled = key_raw[...]
    scaled = (scaled * rms_scale(scaled) * as_row(key_gain)).T
    for j in range(KV_HEADS):
        head = turned_rows(scaled[j * 64 : j * 64 + 64], cosine[...], sine[...])
        kv[me, pl.ds(j * 64, 64)] = head.astype(jnp.bfloat16)
    kv[me, pl.ds(512, 512)] = dot_nn(normed[...], wv[...]).T.astype(jnp.bfloat16)
    keys.start(0, 1, 2)
    query_raw[...] = dot_nn(normed[...], wq[...])
    scaled = query_raw[...]
    turned[...] = (scaled * rms_scale(scaled) * as_row(query_gain)).T

    for j in range(KV_HEADS):
        for r in range(2):
            head = turned[j * 128 + r * 64 : j * 128 + r * 64 + 64]
            head = turned_rows(head, cosine[...], sine[...])
            queries[j, :, r * ROWS : (r + 1) * ROWS] = (head * HEAD_DIM**-0.5).astype(jnp.bfloat16)

    a_first.second()
    b_first.second()
    for d in (1, -1):
        b_second[d].first()
        a_second[d].first()

    key_at = lax.broadcasted_iota(jnp.int32, (ROWS, 2 * ROWS), 0)
    query_at = lax.broadcasted_iota(jnp.int32, (ROWS, 2 * ROWS), 1) % ROWS
    valid = (key_at <= query_at) & (key_at + me * ROWS < length[...])

    def heads_of(block):
        keys_here = [kv[block, j * 64 : j * 64 + 64] for j in range(KV_HEADS)]
        values_here = [kv[block, 512 + j * 64 : 576 + j * 64] for j in range(KV_HEADS)]
        return keys_here, values_here

    keys_here, values_here = heads_of(me)
    scores = [jnp.where(valid, dot_tn(keys_here[j], queries[j]), -1e30) for j in range(KV_HEADS)]
    tops = [jnp.max(one, axis=0, keepdims=True) for one in scores]
    probs = [jnp.exp(one - top) for one, top in zip(scores, tops)]
    parts = [dot_nn(one, prob.astype(jnp.bfloat16)) for one, prob in zip(values_here, probs)]
    for j in range(KV_HEADS):
        most[j] = tops[j]
        total[j] = jnp.sum(probs[j], axis=0, keepdims=True)
        mixed[j] = parts[j]

    @pl.loop(1, 8)
    def _(step):
        @pl.when(step == 1)
        def _():
            a_first.third()
            b_first.third()
            b_second[2].first()
            a_second[2].first()
            keys.arrive(0)

        @pl.when(step == 2)
        def _():
            b_second[0].second()
            a_second[0].second()
            keys.arrive(1)
            keys.start(3, 5)
            keys.arrive(2)
            keys.start(4, 6)

        @pl.when(step == 3)
        def _():
            for d in (1, -1):
                b_second[d].second()
                a_second[d].second()
            keys.arrive(5)

        @pl.when(step == 5)
        def _():
            keys.arrive(3, 4)
            keys.start(7)
            b_second[2].second()
            a_second[2].second()
            keys.arrive(6)

        @pl.when(step == 7)
        def _():
            keys.arrive(7)

        block = (here["x"] + kv_order(here, step) + RING) % RING * 2 + (here["core"] + step) % 2

        @pl.when(block < me)
        def _():
            keys_here, values_here = heads_of(block)
            before = [most[j] for j in range(KV_HEADS)]
            shares = [total[j] for j in range(KV_HEADS)]
            sums = [mixed[j] for j in range(KV_HEADS)]
            scores = [dot_tn(keys_here[j], queries[j]) for j in range(KV_HEADS)]
            tops = [jnp.maximum(old, jnp.max(one, axis=0, keepdims=True)) for old, one in zip(before, scores)]
            probs = [jnp.exp(one - top) for one, top in zip(scores, tops)]
            less = [jnp.exp(old - top) for old, top in zip(before, tops)]
            parts = [dot_nn(one, prob.astype(jnp.bfloat16)) for one, prob in zip(values_here, probs)]
            for j in range(KV_HEADS):
                most[j] = tops[j]
                total[j] = shares[j] * less[j] + jnp.sum(probs[j], axis=0, keepdims=True)
                mixed[j] = sums[j] * less[j] + parts[j]

    save = pltpu.make_async_copy(kv, kv_all, kv_sem)
    save.start()

    for j in range(KV_HEADS):
        share = total[j]
        log_total[j] = most[j] + jnp.log(share)
        head = (mixed[j] * (1.0 / share)).astype(jnp.bfloat16)
        for r in range(2):
            mixed_t[j * 128 + r * 64 : j * 128 + r * 64 + 64, :] = head[:, r * ROWS : (r + 1) * ROWS]

    hidden[...] = dot_tn(mixed_t[...], wo[...])

    @pl.loop(0, 4)
    def _(n):
        at = pl.ds(pl.multiple_of(n * 64, 64), 64)
        rows = hidden[at] + tokens[at].astype(jnp.float32)
        hidden[at] = rows
        ffn_in[at] = (rows * rms_scale(rows) * as_row(ffn_gain)).astype(jnp.bfloat16)

    for d in (0, 1, -1, 2):
        a_second[d].third()
        b_second[d].third()
    save.wait()
    keys.drain()
    for one in gathers:
        one.drain()


def forward(tokens, cot, routes_t, length, cosine, sine, gains, weights):
    vmem, hbm = pl.BlockSpec(memory_space=pltpu.VMEM), pl.BlockSpec(memory_space=pl.ANY)
    low, wide = jnp.bfloat16, jnp.float32
    shape = jax.ShapeDtypeStruct
    return pl.pallas_call(
        forward_kernel,
        name="forward",
        out_shape=(
            shape((ROWS, 1024), low),
            shape((ROWS, 1024), wide),
            shape((1024, ROWS), low),
            shape((KV_HEADS, HEAD_DIM, 2 * ROWS), low),
            shape((KV_HEADS, 1, 2 * ROWS), wide),
            shape((ROWS, 1024), low),
            shape((ROWS, 1024), wide),
            shape((ROWS, 512), wide),
            shape((8, 1024, ROWS), low),
            shape((16 * SENT, 1024), low),
        ),
        in_specs=[vmem] * 10 + [hbm] * 4,
        out_specs=(vmem,) * 8 + (hbm, hbm),
        scratch_shapes=[
            pltpu.VMEM((1024, 1024), low),
            pltpu.VMEM((1024, 512), low),
            pltpu.VMEM((1024, 512), low),
            pltpu.VMEM((1024, 1024), low),
            pltpu.VMEM((8, 1024, ROWS), low),
            pltpu.VMEM((1024, ROWS), wide),
            pltpu.VMEM((KV_HEADS, 1, 2 * ROWS), wide),
            pltpu.VMEM((KV_HEADS, 1, 2 * ROWS), wide),
            pltpu.VMEM((KV_HEADS, HEAD_DIM, 2 * ROWS), wide),
            pltpu.VMEM((EXTRA, 1024), low),
            pltpu.SemaphoreType.DMA((10, 4)),
            pltpu.SemaphoreType.DMA((10, 4)),
            pltpu.SemaphoreType.DMA((8,)),
            pltpu.SemaphoreType.DMA((8,)),
            pltpu.SemaphoreType.DMA((4,)),
            pltpu.SemaphoreType.DMA,
            pltpu.SemaphoreType.DMA((2,)),
        ],
        compiler_params=pltpu.CompilerParams(
            collective_id=3, has_side_effects=True, vmem_limit_bytes=56 * 2**20
        ),
    )(tokens, cot, routes_t, length, cosine, sine, *gains, *weights)


ORDERS = (("x", "y", "z"), ("y", "z", "x"), ("z", "x", "y"))
STREAMS = {2048: ((0, 768), (768, 768), (1536, 512)), 2304: ((0, 768), (768, 768), (1536, 768))}


class Total:
    def __init__(self, here, device, buffer, shift, final, landing, work, send, recv, number, stream, half, begin=0):
        self.here, self.device, self.buffer, self.shift, self.final = here, device, buffer, shift, final
        self.landing, self.work = landing, work
        self.send, self.recv, self.number, self.order = send, recv, number, ORDERS[(stream + number // 3) % 3]
        self.half = half
        self.start, self.rows = STREAMS[half][stream]
        self.stages = range(begin, 7)
        r, own = self.rows, 0 if begin else self.rows
        first = self.start * 9 // 8 + (0 if begin else self.start)
        self.lands = (first, first + own, first + own + 3 * (r // 4), first + own + 3 * (r // 4) + 3 * (r // 16))

    def own(self):
        return self.here["core"] * self.half + self.start

    def copy(self, which, source, target, axis, step):
        return pltpu.make_async_remote_copy(
            src_ref=source,
            dst_ref=target,
            send_sem=self.send.at[self.number, which],
            recv_sem=self.recv.at[self.number, which],
            device_id=self.device(axis, step),
            device_id_type=MESH,
        )

    def held(self, at, size):
        return self.buffer.at[pl.ds(pl.multiple_of(at + self.shift, 16), size)]

    def ready(self, at, size):
        return self.final.at[pl.ds(pl.multiple_of(at, 16), size)]

    def land(self, stage, n, size):
        return self.landing.at[pl.ds(self.lands[stage] + n * size, size)]

    def copies(self, stage):
        r, own = self.rows, self.own()
        a, b, c = self.order
        ia, ib = self.here[a], self.here[b]
        second = own + ia * (r // 4)
        third = second + ib * (r // 16)
        if stage == 0:
            there = (1 - self.here["core"]) * self.half + self.start
            return [self.copy(0, self.held(there, r), self.land(0, 0, r), "core", 1)]
        if stage == 6:
            return [self.copy(16, self.ready(own, r), self.ready(own, r), "core", 1)]
        found = []
        for d in (1, 2, 3):
            if stage == 1:
                source, target, axis = self.held(own + (ia + d) % RING * (r // 4), r // 4), self.land(1, d - 1, r // 4), a
            elif stage == 2:
                source = self.held(second + (ib + d) % RING * (r // 16), r // 16)
                target, axis = self.land(2, d - 1, r // 16), b
            elif stage == 3:
                source = self.work.at[self.number, pl.ds(0, r // 16)]
                target, axis = self.land(3, d - 1, r // 16), c
            elif stage == 4:
                source, target, axis = self.ready(third, r // 16), self.ready(third, r // 16), b
            else:
                source, target, axis = self.ready(second, r // 4), self.ready(second, r // 4), a
            found.append(self.copy(1 + (stage - 1) * 3 + d - 1, source, target, axis, d))
        return found

    def begin(self, stage):
        for copy in self.copies(stage):
            copy.start()

    def add(self, stage, load, store, size, count):
        step = 64 if size % 64 == 0 else 16

        @pl.loop(0, size // step)
        def _(k):
            at = k * step
            total = load(at, step).astype(jnp.float32)
            for n in range(count):
                land = pl.ds(pl.multiple_of(self.lands[stage] + n * size + at, 16), step)
                total = total + self.landing[land].astype(jnp.float32)
            store(at, step, total.astype(jnp.bfloat16))

    def finish(self, stage):
        for copy in self.copies(stage):
            copy.wait_recv()
        if stage > 3:
            return
        r, own = self.rows, self.own()
        a, b, _ = self.order
        second = own + self.here[a] * (r // 4)
        third = second + self.here[b] * (r // 16)
        first = (own, second, third, third)[stage] + self.shift

        def in_place(at, step, *value):
            lines = pl.ds(pl.multiple_of(first + at, 16), step)
            if not value:
                return self.buffer[lines]
            self.buffer[lines] = value[0]

        def in_work(at, step, *value):
            lines = pl.ds(pl.multiple_of(at, 16), step)
            if not value:
                return self.work[self.number, lines]
            self.work[self.number, lines] = value[0]

        def in_final(at, step, value):
            self.final[pl.ds(pl.multiple_of(third + at, 16), step)] = value

        if stage == 0:
            self.add(0, in_place, in_place, r, 1)
        elif stage == 1:
            self.add(1, in_place, in_place, r // 4, 3)
        elif stage == 2:
            self.add(2, in_place, in_work, r // 16, 3)
        else:
            self.add(3, in_work, in_final, r // 16, 3)

    def drain(self):
        for stage in self.stages:
            for copy in self.copies(stage):
                copy.wait_send()


class Small:
    STAGES = (("core", (1,)), ("x", (1, 2, 3)), ("y", (1, 2, 3)), ("z", (1, 2, 3)))

    def __init__(self, device, value, landing, send, recv):
        self.device, self.value, self.landing, self.send, self.recv = device, value, landing, send, recv

    def copies(self, stage):
        axis, steps = self.STAGES[stage]
        first = sum(len(s) for _, s in self.STAGES[:stage])
        return [
            pltpu.make_async_remote_copy(
                src_ref=self.value.at[stage],
                dst_ref=self.landing.at[first + n],
                send_sem=self.send.at[first + n],
                recv_sem=self.recv.at[first + n],
                device_id=self.device(axis, step),
                device_id_type=MESH,
            )
            for n, step in enumerate(steps)
        ]

    def begin(self, stage):
        for copy in self.copies(stage):
            copy.start()

    def finish(self, stage):
        for copy in self.copies(stage):
            copy.wait_recv()
        first = sum(len(s) for _, s in self.STAGES[:stage])
        total = self.value[stage]
        for n in range(len(self.STAGES[stage][1])):
            total = total + self.landing[first + n]
        self.value[stage + 1] = total

    def drain(self):
        for stage in range(4):
            for copy in self.copies(stage):
                copy.wait_send()


class Line:
    def __init__(self, here, device):
        self.here, self.device = here, device

    def along(self, axis, other, step):
        return (self.here["x"] + step + RING) % RING

    def near(self, axis, step):
        return self.device("x", step)


def rms_back(values, gain, grad):
    scale = rms_scale(values)
    lifted = gain * grad
    inner = jnp.mean(values * lifted, axis=-1, keepdims=True)
    return scale * lifted - values * (scale * scale * scale) * inner, jnp.sum(
        grad * values * scale, axis=0, keepdims=True
    )


def turned_back(grads, cosine, sine):
    front, back = grads[: HEAD_DIM // 2], grads[HEAD_DIM // 2 :]
    return jnp.concatenate([front * cosine + back * sine, back * cosine - front * sine], axis=0)


def backward_kernel(
    routes_t, length, cosine, sine, attn_gain, query_gain, key_gain, ffn_gain, router_rows,
    hidden_all, ffn_in_all, cot_all, tokens_all, normed_all, key_raw_all, mixed_t_all, queries_all, log_total_all,
    own_gu, own_down, returned_all, query_raw_all, mixed_parts, kv_all, w_query, w_key, w_value, w_output,
    mixed_out, token_grad, early_small, late_small, query_sum, key_sum, value_sum, output_sum, all_gu, all_down,
    sums, rows, returned, square, kv, hidden_grad, result, branch, grads, delta, query_grad, turned,
    for_mate, from_mate, kv_sums, kv_rows, key_value, normed_other, query_other, key_value_other,
    hidden, ffn_in, cot, tokens, normed, key_raw, mixed_t, queries, log_total, share_gu, share_down,
    held, final_output, final_query, final_keys, land_output, land_query, land_keys, work, late_values, late_rows,
    rs_send, rs_recv, mate_send, mate_recv, kv_send, kv_recv, ar_send, ar_recv, small_send, small_recv, load_sem, out_sem, ex_send, ex_recv, pair_send, pair_recv,
):
    torus = Torus()
    here, device = everywhere()
    me = here["x"] * 2 + here["core"]
    barrier = pltpu.get_barrier_semaphore()
    peers = [device("core", 1)] + [device(axis, d) for axis in "xyz" for d in (1, 2, 3)]
    for peer in peers:
        pl.semaphore_signal(barrier, inc=1, device_id=peer, device_id_type=MESH)
    wanted = (
        ((returned_all, returned), (ffn_in_all, ffn_in), (hidden_all, hidden), (cot_all, cot)),
        ((w_output, square), (mixed_t_all, mixed_t), (queries_all, queries), (log_total_all, log_total)),
        ((normed_all, normed), (kv_all, kv), (own_gu, share_gu), (own_down, share_down)),
        ((mixed_parts, sums), (tokens_all, tokens), (key_raw_all, key_raw)),
    )
    loads, number = [], 0
    for group in wanted:
        loads.append([])
        for source, target in group:
            loads[-1].append(pltpu.make_async_copy(source, target, load_sem.at[number]))
            loads[-1][-1].start()
            number += 1

    order = (2, 1, -1, 0)
    leads = []
    for n, d in enumerate(order):
        leads.append(Scatter(torus, sums, rows, rs_send, rs_recv, n, n * 384, "z", d, 0, 64, 64, mixed_parts))
        leads.append(Scatter(torus, sums, rows, rs_send, rs_recv, 4 + n, (5 + n) * 384, "y", d, 128, 64, 64, mixed_parts))
    lasts = [
        Scatter(torus, sums, rows, rs_send, rs_recv, 8, 4 * 384, "y", 0, 0, 64, 64),
        Scatter(torus, sums, rows, rs_send, rs_recv, 9, 9 * 384, "z", 0, 128, 64, 64),
    ]
    ring = Scatter(Line(here, device), kv_sums, kv_rows, kv_send, kv_recv, 0, 0, "x", 0, 0, 512, 512)
    experts = [
        Keys(here, device, blocks, ex_send.at[n], ex_recv.at[n], origin)
        for n, (blocks, origin) in enumerate(((all_gu, own_gu), (all_down, own_down)))
    ]
    pl.semaphore_wait(barrier, len(peers))
    for one in leads:
        one.first()
    for one in experts:
        one.start(0, 1, 2)

    def to_other(number, source, target):
        return pltpu.make_async_remote_copy(
            src_ref=source,
            dst_ref=target,
            send_sem=pair_send.at[number],
            recv_sem=pair_recv.at[number],
            device_id=device("core", 1),
            device_id_type=MESH,
        )

    own_half = pl.ds(pl.multiple_of(here["core"] * 512, 512), 512)
    other_half = pl.ds(pl.multiple_of((1 - here["core"]) * 512, 512), 512)
    pairs = [
        to_other(0, normed, normed_other),
        to_other(1, branch.at[:, other_half], query_other),
        to_other(2, key_value.at[:, other_half], key_value_other),
    ]
    for load in loads[0]:
        load.wait()

    expert_rows = lax.broadcasted_iota(jnp.int32, (EXPERTS, ROWS), 0)
    member = jnp.zeros((EXPERTS, ROWS), jnp.float32)
    for k in range(TOPK):
        member = member + jnp.where(expert_rows == routes_t[pl.ds(k, 1), :], 1.0, 0.0)
    named = member > 0.5
    logits = jnp.where(named, dot_nt(router_rows[...], ffn_in[...]), -1e30)
    weight = jnp.where(named, jnp.exp(logits - jnp.max(logits, axis=0, keepdims=True)), 0.0)
    gates = weight / jnp.sum(weight, axis=0, keepdims=True)
    gate_grad = jnp.concatenate([returned[:8, q * ROWS : (q + 1) * ROWS] for q in range(4)], axis=0)
    logit_grad = (gates * (gate_grad - jnp.sum(gates * gate_grad, axis=0, keepdims=True))).astype(jnp.bfloat16)
    result[...] = dot_tn(logit_grad, router_rows[...])
    router_grad = dot_nn(logit_grad, ffn_in[...]).astype(jnp.bfloat16)
    for q in range(4):
        held[2048 + q * EXPERTS : 2048 + (q + 1) * EXPERTS] = router_grad[:, q * 256 : (q + 1) * 256]

    def ffn_part(n, gain_grad):
        at = pl.ds(pl.multiple_of(n * 64, 64), 64)
        grad = result[at] + returned[pl.ds(pl.multiple_of(n * 64 + EXTRA, 16), 64)]
        part, more = rms_back(hidden[at], as_row(ffn_gain), grad)
        part = part + cot[at].astype(jnp.float32)
        hidden_grad[at] = part
        branch[at] = part.astype(jnp.bfloat16)
        return gain_grad + more

    gain_grad = lax.fori_loop(0, 4, ffn_part, jnp.zeros((1, 1024), jnp.float32))
    gain_lines = [gain_grad[:, q * 256 : (q + 1) * 256] for q in range(4)] + [jnp.zeros((124, 256), jnp.float32)]
    held[2176:2304] = jnp.concatenate(gain_lines, axis=0).astype(jnp.bfloat16)
    held[4352:4608] = jnp.zeros((256, 256), jnp.bfloat16)

    for load in [*loads[1], *loads[2]]:
        load.wait()
    pairs[0].start()
    owns = [
        pltpu.make_async_copy(share_gu, all_gu.at[me], load_sem.at[19]),
        pltpu.make_async_copy(share_down, all_down.at[me], load_sem.at[20]),
    ]
    for copy in owns:
        copy.start()
    turned[...] = dot_nt(square[...], branch[...])
    next_load = pltpu.make_async_copy(w_query, square, load_sem.at[15])
    next_load.start()
    query_raw = returned.at[pl.ds(0, ROWS)]
    raw_load = pltpu.make_async_copy(query_raw_all, query_raw, load_sem.at[16])
    raw_load.start()

    for j in range(KV_HEADS):
        for r in range(2):
            at = slice(j * 128 + r * 64, j * 128 + r * 64 + 64)
            low = turned[at].astype(jnp.bfloat16)
            grads[j, :, r * ROWS : (r + 1) * ROWS] = low
            delta[j, :, r * ROWS : (r + 1) * ROWS] = jnp.sum(
                low.astype(jnp.float32) * mixed_t[at].astype(jnp.float32), axis=0, keepdims=True
            )
        query_grad[j] = jnp.zeros((HEAD_DIM, 2 * ROWS), jnp.float32)

    @pl.loop(0, 4)
    def _(n):
        at = pl.ds(pl.multiple_of(n * 256, 256), 256)
        part = dot_nn(mixed_t[at], branch[...]).astype(jnp.bfloat16)
        for q in range(4):
            held[pl.ds(pl.multiple_of(q * 1024 + q // 2 * 256 + n * 256, 256), 256)] = part[:, q * 256 : (q + 1) * 256]

    def reduction(number, buffer, shift, final, land, half, begin):
        return [
            Total(here, device, buffer, shift, final, land, work, ar_send, ar_recv, 3 * number + s, s, half, begin)
            for s in range(3)
        ]

    early = reduction(0, held, 0, final_output, land_output, 2304, 0)
    of_query = reduction(1, kv, 0, final_query, land_query, 2048, 1)
    of_keys = reduction(2, kv, 4096, final_keys, land_keys, 2048, 1)
    late_few = Small(device, late_values, late_rows, small_send, small_recv)
    for one in early:
        one.begin(0)
    def onward(streams, stage):
        for one in streams:
            one.finish(stage)
            if stage < 6:
                one.begin(stage + 1)

    def write_out(number, final, first, target, at):
        block = final.at[pl.ds(first, 1024)]
        return pltpu.make_async_copy(block, target.at[:, pl.ds(at * 256, 256)], out_sem.at[number])

    outs = [write_out(q, final_output, q * 1024 + q // 2 * 256, output_sum, q) for q in range(4)]
    outs += [write_out(4 + q, final_query, q * 1024, query_sum, q) for q in range(4)]
    outs += [write_out(8 + q, final_keys, q * 1024, key_sum, q) for q in range(2)]
    outs += [write_out(10 + q, final_keys, (2 + q) * 1024, value_sum, q) for q in range(2)]

    def mate_copy(turn, at):
        return pltpu.make_async_remote_copy(
            src_ref=for_mate.at[turn % 2],
            dst_ref=from_mate.at[at],
            send_sem=mate_send.at[turn],
            recv_sem=mate_recv.at[turn],
            device_id=device("core", 1),
            device_id_type=MESH,
        )

    key_at = lax.broadcasted_iota(jnp.int32, (ROWS, 2 * ROWS), 0)
    query_at = lax.broadcasted_iota(jnp.int32, (ROWS, 2 * ROWS), 1) % ROWS
    valid = (key_at <= query_at) & (key_at + me * ROWS < length[...])

    def block_grads(block, target, at, masked):
        for group in range(2):
            heads = range(4 * group, 4 * group + 4)
            key_heads = [kv[pl.ds(pl.multiple_of(block * 1024 + j * 64, 64), 64)] for j in heads]
            value_heads = [kv[pl.ds(pl.multiple_of(block * 1024 + 512 + j * 64, 64), 64)] for j in heads]
            probs = [jnp.exp(dot_tn(one, queries[j]) - log_total[j]) for one, j in zip(key_heads, heads)]
            if masked:
                probs = [jnp.where(valid, one, 0.0) for one in probs]
            probs_grads = [dot_tn(one, grads[j]) for one, j in zip(value_heads, heads)]
            lows = [
                (one * (grad - delta[j])).astype(jnp.bfloat16) for one, grad, j in zip(probs, probs_grads, heads)
            ]
            key_parts = [dot_nt(queries[j], low).astype(jnp.bfloat16) for low, j in zip(lows, heads)]
            value_parts = [
                dot_nt(grads[j], one.astype(jnp.bfloat16)).astype(jnp.bfloat16) for one, j in zip(probs, heads)
            ]
            query_parts = [dot_nn(one, low) for one, low in zip(key_heads, lows)]
            for n, j in enumerate(heads):
                target[at, j * 64 : j * 64 + 64] = key_parts[n]
                target[at, 512 + j * 64 : 576 + j * 64] = value_parts[n]
                query_grad[j] += query_parts[n]

    def from_other(turn, at):
        mate_copy(turn, at).wait_recv()

        @pl.loop(0, 16)
        def _(n):
            lines = pl.ds(pl.multiple_of(n * 64, 64), 64)
            total = kv_sums[at, lines].astype(jnp.float32) + from_mate[at, lines].astype(jnp.float32)
            kv_sums[at, lines] = total.astype(jnp.bfloat16)

    def turn_x(turn):
        offset = (1 - turn % 2) * (2 + turn // 2) + (turn % 2) * (1 - turn // 2)
        return (here["x"] + offset + RING) % RING

    @pl.loop(0, 4)
    def _(turn):
        @pl.when(turn == 1)
        def _():
            for load in loads[3]:
                load.wait()
            for one in leads:
                one.second()
            for one in experts:
                one.arrive(1)
                one.start(3, 5)
                one.arrive(2)
                one.start(4, 6)

        @pl.when(turn == 2)
        def _():
            onward(early, 0)

        @pl.when(turn == 3)
        def _():
            onward(early, 1)

        at = turn_x(turn)
        other = at * 2 + 1 - here["core"]

        @pl.when(turn >= 2)
        def _():
            mate_copy(turn - 2, at).wait_send()

        @pl.when(other < me)
        def _():
            block_grads(other, for_mate, turn % 2, False)

        @pl.when(other >= me)
        def _():
            for_mate[turn % 2] = jnp.zeros((1024, ROWS), jnp.bfloat16)

        mate_copy(turn, at).start()

        own = at * 2 + here["core"]

        @pl.when(own < me)
        def _():
            block_grads(own, kv_sums, at, False)

        @pl.when(own > me)
        def _():
            kv_sums[at] = jnp.zeros((1024, ROWS), jnp.bfloat16)

        @pl.when(own == me)
        def _():
            block_grads(own, kv_sums, at, True)

        from_other(turn, at)

        @pl.when(turn == 0)
        def _():
            ring.first()

        @pl.when(turn == 2)
        def _():
            ring.second()

    for j in range(KV_HEADS):
        for r in range(2):
            head = query_grad[j, :, r * ROWS : (r + 1) * ROWS] * HEAD_DIM**-0.5
            turned[j * 128 + r * 64 : j * 128 + r * 64 + 64] = turned_back(head, cosine[...], sine[...])

    raw_load.wait()
    result[...] = turned[...].T

    def query_part(n, gain_grad):
        at = pl.ds(pl.multiple_of(n * 64, 64), 64)
        part, more = rms_back(query_raw[at], as_row(query_gain), result[at])
        branch[at] = part.astype(jnp.bfloat16)
        return gain_grad + more

    query_gain_grad = lax.fori_loop(0, 4, query_part, jnp.zeros((1, 1024), jnp.float32))

    def half_of_columns(raw, raw_other, shift):
        both = jnp.concatenate([raw[:, own_half], raw_other[...]], axis=0)

        @pl.loop(0, 4)
        def _(n):
            columns = pl.ds(pl.multiple_of(n * 256, 256), 256)
            left = jnp.concatenate([normed[:, columns], normed_other[:, columns]], axis=0)
            part = dot_tn(left, both).astype(jnp.bfloat16)
            for q in range(2):
                first = shift + (here["core"] * 2 + q) * 1024 + n * 256
                kv[pl.ds(pl.multiple_of(first, 256), 256)] = part[:, q * 256 : (q + 1) * 256]

    pairs[1].start()
    onward(early, 2)
    for one in experts:
        one.arrive(3, 4)
        one.start(7)
    pairs[0].wait_recv()
    pairs[1].wait_recv()
    half_of_columns(branch, query_other, 0)
    for one in of_query:
        one.begin(1)

    def put(at, total):
        turned[at] = total

    ring.third(put)
    for j in range(KV_HEADS):
        turned[j * 64 : j * 64 + 64] = turned_back(turned[j * 64 : j * 64 + 64], cosine[...], sine[...])
    part, key_gain_grad = rms_back(key_raw[...], as_row(key_gain), turned[:512].T)
    key_value[:, :512] = part.astype(jnp.bfloat16)
    key_value[:, 512:] = turned[512:].T.astype(jnp.bfloat16)
    pairs[2].start()
    pairs[2].wait_recv()
    half_of_columns(key_value, key_value_other, 4096)
    for one in of_keys:
        one.begin(1)

    next_load.wait()
    result[...] = dot_nt(branch[...], square[...])
    last_loads = [
        pltpu.make_async_copy(w_key, square.at[:, pl.ds(0, 512)], load_sem.at[17]),
        pltpu.make_async_copy(w_value, square.at[:, pl.ds(512, 512)], load_sem.at[18]),
    ]
    for load in last_loads:
        load.start()
    onward(of_query, 1)
    for load in last_loads:
        load.wait()
    result[...] += dot_nt(key_value[...], square[...])

    def token_part(n, gain_grad):
        at = pl.ds(pl.multiple_of(n * 64, 64), 64)
        part, more = rms_back(tokens[at].astype(jnp.float32), as_row(attn_gain), result[at])
        token_grad[at] = (hidden_grad[at] + part).astype(jnp.bfloat16)
        return gain_grad + more

    attn_gain_grad = lax.fori_loop(0, 4, token_part, jnp.zeros((1, 1024), jnp.float32))
    key_wide = jnp.concatenate([key_gain_grad, jnp.zeros((1, 512), jnp.float32)], axis=1)
    late_values[0] = jnp.concatenate(
        [attn_gain_grad, query_gain_grad, key_wide, jnp.zeros((5, 1024), jnp.float32)], axis=0
    )
    late_few.begin(0)
    onward(of_keys, 1)
    onward(early, 3)
    for stage in range(2, 5):
        onward(of_keys, stage)
        onward(of_query, stage)
        late_few.finish(stage - 2)
        late_few.begin(stage - 1)
        onward(early, stage + 2)
        if stage == 2:
            for one in leads:
                one.third()
            for one in lasts:
                one.first()
        if stage == 4:
            for one in lasts:
                one.second()
    for q in range(4):
        outs[q].start()
    late_few.finish(3)
    late_small[...] = late_values[4]
    router = [final_output[2048 + q * EXPERTS : 2048 + (q + 1) * EXPERTS].astype(jnp.float32) for q in range(4)]
    lines = final_output[2176:2192].astype(jnp.float32)
    lines = jnp.concatenate([lines[q : q + 1] for q in range(4)], axis=1)
    early_small[...] = jnp.concatenate(
        [jnp.concatenate(router, axis=1), lines, jnp.zeros((7, 1024), jnp.float32)], axis=0
    )

    def put_mixed(at, total):
        mixed_out[at] = (hidden[at] + total).astype(jnp.bfloat16)

    for stage in range(5, 7):
        onward(of_query, stage)
        onward(of_keys, stage)
        if stage == 6:
            for one in lasts:
                one.third(put_mixed)
    for q in range(4, 12):
        outs[q].start()
    for one in experts:
        one.arrive(0, 5, 6, 7)
    for one in [*experts, *leads, *lasts, ring, *early, *of_query, *of_keys, late_few]:
        one.drain()
    for turn in (2, 3):
        mate_copy(turn, 0).wait_send()
    for pair in pairs:
        pair.wait_send()
    for out in [*outs, *owns]:
        out.wait()


def backward(smalls, larges):
    vmem, hbm = pl.BlockSpec(memory_space=pltpu.VMEM), pl.BlockSpec(memory_space=pl.ANY)
    low, wide = jnp.bfloat16, jnp.float32
    shape = jax.ShapeDtypeStruct
    dma = pltpu.SemaphoreType.DMA
    return pl.pallas_call(
        backward_kernel,
        name="backward",
        out_shape=(
            shape((ROWS, 1024), low),
            shape((ROWS, 1024), low),
            shape((40, 1024), wide),
            shape((8, 1024), wide),
            shape((1024, 1024), low),
            shape((1024, 512), low),
            shape((1024, 512), low),
            shape((1024, 1024), low),
            shape((8, 256, 1024), low),
            shape((8, 128, 1024), low),
        ),
        in_specs=[vmem] * len(smalls) + [hbm] * len(larges),
        out_specs=(vmem,) * 4 + (hbm,) * 6,
        scratch_shapes=[
            pltpu.VMEM((16, ROWS, 1024), low),
            pltpu.VMEM((10 * 384, 1024), low),
            pltpu.VMEM((FULL, 1024), wide),
            pltpu.VMEM((1024, 1024), low),
            pltpu.VMEM((8 * 1024, ROWS), low),
            pltpu.VMEM((ROWS, 1024), wide),
            pltpu.VMEM((ROWS, 1024), wide),
            pltpu.VMEM((ROWS, 1024), low),
            pltpu.VMEM((KV_HEADS, HEAD_DIM, 2 * ROWS), low),
            pltpu.VMEM((KV_HEADS, 1, 2 * ROWS), wide),
            pltpu.VMEM((KV_HEADS, HEAD_DIM, 2 * ROWS), wide),
            pltpu.VMEM((1024, ROWS), wide),
            pltpu.VMEM((2, 1024, ROWS), low),
            pltpu.VMEM((4, 1024, ROWS), low),
            pltpu.VMEM((4, 1024, ROWS), low),
            pltpu.VMEM((3072, ROWS), low),
            pltpu.VMEM((ROWS, 1024), low),
            pltpu.VMEM((ROWS, 1024), low),
            pltpu.VMEM((ROWS, 512), low),
            pltpu.VMEM((ROWS, 512), low),
            pltpu.VMEM((ROWS, 1024), wide),
            pltpu.VMEM((ROWS, 1024), low),
            pltpu.VMEM((ROWS, 1024), low),
            pltpu.VMEM((ROWS, 1024), low),
            pltpu.VMEM((ROWS, 1024), low),
            pltpu.VMEM((ROWS, 512), wide),
            pltpu.VMEM((1024, ROWS), low),
            pltpu.VMEM((KV_HEADS, HEAD_DIM, 2 * ROWS), low),
            pltpu.VMEM((KV_HEADS, 1, 2 * ROWS), wide),
            pltpu.VMEM((256, 1024), low),
            pltpu.VMEM((128, 1024), low),
            pltpu.VMEM((4608, 256), low),
            pltpu.VMEM((4608, 256), low),
            pltpu.VMEM((4096, 256), low),
            pltpu.VMEM((4096, 256), low),
            pltpu.VMEM((4896, 256), low),
            pltpu.VMEM((2304, 256), low),
            pltpu.VMEM((2304, 256), low),
            pltpu.VMEM((9, 48, 256), low),
            pltpu.VMEM((5, 8, 1024), wide),
            pltpu.VMEM((10, 8, 1024), wide),
            dma((10, 4)),
            dma((10, 4)),
            dma((4,)),
            dma((4,)),
            dma((1, 4)),
            dma((1, 4)),
            dma((9, 17)),
            dma((9, 17)),
            dma((10,)),
            dma((10,)),
            dma((21,)),
            dma((12,)),
            dma((2, 8)),
            dma((2, 8)),
            dma((3,)),
            dma((3,)),
        ],
        compiler_params=pltpu.CompilerParams(
            collective_id=4, has_side_effects=True, vmem_limit_bytes=66000000
        ),
        cost_estimate=pl.CostEstimate(flops=100 * 10**9, bytes_accessed=60 * 10**6, transcendentals=8 * 10**6),
    )(*smalls, *larges)


def widen_kernel(
    early, late, mixed, tokens, query, key, value, output, gate_up, down,
    ffn_gain, attn_gain, query_gain, key_gain, router,
    mixed_out, token_out, query_out, key_out, value_out, output_out, gate_out, up_out, down_out,
    query_in, key_in, value_in, output_in, gate_up_in, down_in,
    query_wide, key_wide, value_wide, output_wide, gate_up_wide, down_wide,
    in_sem, out_sem,
):
    arrays = (
        (query, query_in, query_wide, query_out),
        (output, output_in, output_wide, output_out),
        (key, key_in, key_wide, key_out),
        (value, value_in, value_wide, value_out),
    )
    parts = []
    for source, low, wide, target in arrays:
        for n in range(0, 1024, 512):
            at = pl.ds(n, 512)
            parts.append((source.at[at], low.at[at], wide.at[at], [(wide.at[at], target.at[at])]))
    for block in range(8):
        rows, e = pl.ds(block // 2 * 256, 256), block % 2
        wide = gate_up_wide.at[block]
        targets = [
            (wide.at[:, pl.ds(0, 512)], gate_out.at[e, rows]),
            (wide.at[:, pl.ds(512, 512)], up_out.at[e, rows]),
        ]
        parts.append((gate_up.at[block], gate_up_in.at[block], wide, targets))
    for block in range(8):
        wide = down_wide.at[block]
        target = down_out.at[block % 2, pl.ds(block // 2 * 128, 128)]
        parts.append((down.at[block], down_in.at[block], wide, [(wide, target)]))
    loads = [pltpu.make_async_copy(source, low, in_sem.at[n]) for n, (source, low, _, _) in enumerate(parts)]
    for load in loads:
        load.start()
    ffn_gain[...] = early[EXPERTS]
    attn_gain[...] = late[0]
    query_gain[...] = late[1]
    key_gain[...] = late[2, :512]
    router[...] = early[:EXPERTS]
    mixed_out[...] = mixed[...]
    token_out[...] = tokens[...]
    stores = []
    for load, (_, low, wide, targets) in zip(loads, parts):
        load.wait()

        @pl.loop(0, low.shape[0] // 32)
        def _(n):
            at = pl.ds(pl.multiple_of(n * 32, 32), 32)
            wide[at] = low[at].astype(jnp.float32)

        for source, target in targets:
            stores.append(pltpu.make_async_copy(source, target, out_sem.at[len(stores)]))
            stores[-1].start()
    for copy in stores:
        copy.wait()


def widen(arrays):
    vmem, hbm = pl.BlockSpec(memory_space=pltpu.VMEM), pl.BlockSpec(memory_space=pl.ANY)
    low, wide = jnp.bfloat16, jnp.float32
    shape = jax.ShapeDtypeStruct
    held = ((1024, 1024), (1024, 512), (1024, 512), (1024, 1024), (8, 256, 1024), (8, 128, 1024))
    return pl.pallas_call(
        widen_kernel,
        name="widen",
        out_shape=(
            shape((1024,), wide),
            shape((1024,), wide),
            shape((1024,), wide),
            shape((512,), wide),
            shape((EXPERTS, 1024), wide),
            shape((ROWS, 1024), low),
            shape((ROWS, 1024), low),
            shape((1024, 1024), wide),
            shape((1024, 512), wide),
            shape((1024, 512), wide),
            shape((1024, 1024), wide),
            shape((2, 1024, 512), wide),
            shape((2, 1024, 512), wide),
            shape((2, 512, 1024), wide),
        ),
        in_specs=[vmem] * 4 + [hbm] * 6,
        out_specs=(vmem,) * 7 + (hbm,) * 7,
        scratch_shapes=[
            *[pltpu.VMEM(size, low) for size in held],
            *[pltpu.VMEM(size, wide) for size in held],
            pltpu.SemaphoreType.DMA((24,)),
            pltpu.SemaphoreType.DMA((32,)),
        ],
        compiler_params=pltpu.CompilerParams(vmem_limit_bytes=56 * 2**20),
    )(*arrays)


def body(
    tokens,
    cotangent,
    lengths,
    routes,
    attn_gain,
    w_query,
    w_key,
    w_value,
    query_gain,
    key_gain,
    w_output,
    ffn_gain,
    w_router,
    w_gate,
    w_up,
    w_down,
):
    query_pos = lax.axis_index("dp") * ROWS + jnp.arange(ROWS, dtype=jnp.int32)
    cosine, sine_table = rope_tables(query_pos)
    cosine, sine_table = cosine.T, sine_table.T
    routes_t, length = routes[0].T, lengths.reshape(1, 1)
    gains = [attn_gain, query_gain, key_gain, ffn_gain]
    weights = (w_query, w_key, w_value, w_output)
    router_rows = w_router.T
    ffn_in, hidden, mixed_t, queries, log_total, normed, query_raw, key_raw, kv_all, cot_all = forward(
        tokens[0], cotangent[0], routes_t, length, cosine, sine_table, gains, weights
    )
    returned, mixed_parts, own_gu, own_down = moe(
        ffn_in, cot_all, cotangent[0], router_rows, w_gate, w_up, w_down
    )
    mixed_low, token_low, early_small, late_small, *sums = backward(
        (routes_t, length, cosine, sine_table, *gains, router_rows),
        (
            hidden, ffn_in, cotangent[0], tokens[0], normed, key_raw, mixed_t, queries, log_total, own_gu, own_down,
            returned, query_raw, mixed_parts, kv_all.reshape(8 * 1024, ROWS), *weights,
        ),
    )
    (
        ffn_gain_sum, attn_gain_sum, query_gain_sum, key_gain_sum, router_sum, mixed_out, token_grad,
        query_w_sum, key_w_sum, value_w_sum, output_w_sum, gate_w_sum, up_w_sum, down_w_sum,
    ) = widen((early_small, late_small, mixed_low, token_low, *sums))
    return (
        mixed_out[None],
        token_grad[None],
        attn_gain_sum,
        query_w_sum,
        key_w_sum,
        value_w_sum,
        query_gain_sum,
        key_gain_sum,
        output_w_sum,
        ffn_gain_sum,
        router_sum.T,
        gate_w_sum,
        up_w_sum,
        down_w_sum,
    )


def solution(mesh):
    return jax.shard_map(
        body,
        mesh=mesh,
        in_specs=(
            P("expert", "dp", None),
            P("expert", "dp", None),
            P("expert"),
            P("expert", "dp", None),
            P(),
            P(),
            P(),
            P(),
            P(),
            P(),
            P(),
            P(),
            P(),
            P("expert", None, None),
            P("expert", None, None),
            P("expert", None, None),
        ),
        out_specs=(
            P("expert", "dp", None),
            P("expert", "dp", None),
            P(),
            P(),
            P(),
            P(),
            P(),
            P(),
            P(),
            P(),
            P(),
            P("expert", None, None),
            P("expert", None, None),
            P("expert", None, None),
        ),
        check_vma=False,
    )
```
